32 devices in a mesh: section: 2 (over y), fsdp: 4 (over z), dp: 4 (over x, core).
Axes of the slice: x: 2, y: 2, z: 4, core: 2. Of those that a mesh axis runs over, the one named last changes fastest.
Arguments:
- inputs: bfloat16 [2, 4, 1024, 1536], P(None, 'dp', 'fsdp'), may hold values from -6 to 6
- segment: int32 [2, 4, 1024], P(None, 'dp', 'fsdp'), may hold values from 0 to 2, as said below
- cotangent: bfloat16 [2, 4, 1024, 1536], P(None, 'dp', 'fsdp'), may hold values from -6 to 6
- norm_gain: float32 [2, 1, 1536], P('section'), may hold values from 0.5 to 1.5
- in_weight: bfloat16 [2, 1, 1536, 6448], P('section', None, 'fsdp'), may hold values from -0.15625 to 0.15625
- conv_weight: float32 [2, 1, 4, 3328], P('section'), may hold values from -3 to 3
- conv_bias: float32 [2, 1, 3328], P('section'), may hold values from -3 to 3
- dt_bias: float32 [2, 1, 48], P('section'), may hold values from -7 to -2
- a_log: float32 [2, 1, 48], P('section'), may hold values from -4 to 1
- d_skip: float32 [2, 1, 48], P('section'), may hold values from 0.5 to 1.5
- gate_gain: float32 [2, 1, 3072], P('section'), may hold values from 0.5 to 1.5
- out_weight: bfloat16 [2, 1, 3072, 1536], P('section', None, 'fsdp'), may hold values from -0.109375 to 0.109375
Outputs:
- final: bfloat16 [2, 4, 1024, 1536], P('section', 'dp', 'fsdp')
- input_grad: bfloat16 [2, 4, 1024, 1536], P('section', 'dp', 'fsdp')
- norm_gain_grad: float32 [2, 1, 1536], P('section')
- in_weight_grad: float32 [2, 1, 1536, 6448], P('section', None, 'fsdp')
- conv_weight_grad: float32 [2, 1, 4, 3328], P('section')
- conv_bias_grad: float32 [2, 1, 3328], P('section')
- dt_bias_grad: float32 [2, 1, 48], P('section')
- a_log_grad: float32 [2, 1, 48], P('section')
- d_skip_grad: float32 [2, 1, 48], P('section')
- gate_gain_grad: float32 [2, 1, 3072], P('section')
- out_weight_grad: float32 [2, 1, 3072, 1536], P('section', None, 'fsdp')
The draws below stay inside these ranges and needn't reach their ends.
Inputs may be any that keep to these rules, and one draw needn't show every extreme that they name: Along each sequence the segment numbers never fall; they start at 0 and end at 2, and segment 1 starts among the first 256 tokens and ends among the last 256.
All inputs are finite; a program needn't handle non-finite values.
Results may differ from the reference program's by a relative error of at most 0.01575.
The reference program's roundings to bfloat16 on the way count: a program that leaves them out, or rounds other values in their place, can miss the bound.
Values may be sent and summed in bfloat16 or wider, within the bound.
A program may use at most 384 MiB of HBM per device.

```python
import math
import jax
import jax.numpy as jnp
from jax import lax

D = 1536
H = 48
P_SIZE = 64
N = 128
K = 4
DI = 3072
DC = 3328
DIN = 6448
LAYERS = 1
MB = 2
SEQ = 1024
TOK_DEV = 256
SEQS = 4
SECTIONS = 2
N_SECTION = 2


def draw_segment(key, part):
    key = jax.random.fold_in(key, 11)
    first_key, second_key = jax.random.split(key)
    begin = jax.random.randint(first_key, (MB, SEQS, 1), 1, TOK_DEV)
    finish = jax.random.randint(second_key, (MB, SEQS, 1), SEQ - TOK_DEV + 1, SEQ)
    place = lax.broadcasted_iota(jnp.int32, (MB, SEQS, SEQ), 2)
    return (place >= begin).astype(jnp.int32) + (place >= finish).astype(jnp.int32)


def block_levels(rng, dims, shards, smallest, largest):
    level = 1.0
    for dim, blocks in shards:
        heights = jax.random.uniform(jax.random.fold_in(jax.random.fold_in(rng, 6), dim), (blocks,), jnp.float32, smallest / len(shards), largest / len(shards))
        level = level * jnp.repeat(jnp.exp(heights), dims[dim] // blocks).reshape((-1,) + (1,) * (len(dims) - 1 - dim))
    return level


def scatter_about(key, shape, deviation, limit, cuts=(), kind=jnp.bfloat16):
    entries = jax.random.normal(key, shape, jnp.float32) * deviation
    if len(cuts) > 0:
        entries = block_levels(key, shape, cuts, -0.22, 0.18) * entries
    return jnp.clip(entries, min=-limit, max=limit).astype(kind)


def setup_inputs(seed: int = 0) -> dict:
    keys = jax.random.split(jax.random.key(seed), 13)
    inputs = scatter_about(keys[0], (MB, SEQS, SEQ, D), 1.0, 6.0, ((1, 4), (2, 4)))
    segment = draw_segment(jax.random.fold_in(keys[12], 71), 0)
    cotangent = scatter_about(keys[2], (MB, SEQS, SEQ, D), 1.0, 6.0, ((1, 4), (2, 4)))
    norm_gain = jnp.clip(1.0 + 0.1 * jax.random.normal(keys[3], (SECTIONS, LAYERS, D), jnp.float32), 0.5, 1.5)
    in_weight = scatter_about(keys[4], (SECTIONS, LAYERS, D, DIN), D ** -0.5, 0.15625, ((0, 2), (2, 4)))
    conv_weight = scatter_about(keys[5], (SECTIONS, LAYERS, K, DC), 0.5, 3.0, ((0, 2),), jnp.float32)
    conv_bias = scatter_about(keys[6], (SECTIONS, LAYERS, DC), 0.5, 3.0, ((0, 2),), jnp.float32)
    dt_bias = jnp.clip(-7.0 + 5.0 * jax.random.uniform(keys[7], (SECTIONS, LAYERS, H), jnp.float32) ** block_levels(keys[7], (SECTIONS, LAYERS, H), ((0, 2),), -0.2, 0.2), -7.0, -2.0)
    a_log = jnp.clip(-4.0 + 5.0 * jax.random.uniform(keys[8], (SECTIONS, LAYERS, H), jnp.float32) ** block_levels(keys[8], (SECTIONS, LAYERS, H), ((0, 2),), -0.2, 0.2), -4.0, 1.0)
    d_skip = jnp.clip(0.5 + 1.0 * jax.random.uniform(keys[9], (SECTIONS, LAYERS, H), jnp.float32) ** block_levels(keys[9], (SECTIONS, LAYERS, H), ((0, 2),), -0.2, 0.2), 0.5, 1.5)
    gate_gain = jnp.clip(1.0 + 0.1 * jax.random.normal(keys[10], (SECTIONS, LAYERS, DI), jnp.float32), 0.5, 1.5)
    out_weight = scatter_about(keys[11], (SECTIONS, LAYERS, DI, D), DI ** -0.5, 0.109375, ((0, 2), (2, 4)))
    return dict(inputs=inputs, segment=segment, cotangent=cotangent, norm_gain=norm_gain, in_weight=in_weight, conv_weight=conv_weight, conv_bias=conv_bias, dt_bias=dt_bias, a_log=a_log, d_skip=d_skip, gate_gain=gate_gain, out_weight=out_weight)


EPSILON = 1e-05
HIGHEST = lax.Precision.HIGHEST

@jax.custom_vjp
def low(v):
    return lax.optimization_barrier(v.astype(jnp.bfloat16)).astype(jnp.float32)

@jax.custom_vjp
def low_back(v):
    return v

def low_keep(v):
    return (low(v), None)

def low_pass(kept, grad):
    return (grad,)

def back_keep(v):
    return (v, None)

def back_low(kept, grad):
    return (low(grad),)
low.defvjp(low_keep, low_pass)
low_back.defvjp(back_keep, back_low)

def rms_scale(values, scale_gain):
    return values * lax.rsqrt(lax.optimization_barrier(jnp.mean(values * values, axis=-1, keepdims=True)) + EPSILON) * scale_gain

def conv_mix(raw_rows, seg_row, conv_w, conv_b):
    row_count = raw_rows.shape[0]
    mixed = conv_b
    for offset in range(K):
        lag_rows = K - 1 - offset
        earlier = jnp.concatenate([jnp.zeros((lag_rows, raw_rows.shape[1]), jnp.float32), raw_rows[:row_count - lag_rows]], axis=0)
        seg_earlier = jnp.concatenate([jnp.full((lag_rows,), -1, jnp.int32), seg_row[:row_count - lag_rows]])
        keep_mask = jnp.where(seg_earlier == seg_row, 1.0, 0.0)
        mixed = mixed + conv_w[offset] * earlier * keep_mask[:, None]
    return jax.nn.silu(mixed)

def scan_states(values, step_size, log_decay, b_matrix, c_matrix, seg_row):
    length = values.shape[0]
    block_rows = math.gcd(length, 256)
    block_count = length // block_rows

    def to_blocks(array):
        return array.reshape((block_count, block_rows) + array.shape[1:])

    @jax.checkpoint
    def one_block(carry, pieces):
        state, last_seg = carry
        block_vals, block_steps, block_logs, b_part, c_part, block_segs = pieces
        cumulative = jnp.cumsum(block_logs, axis=0)
        position = lax.broadcasted_iota(jnp.int32, (block_rows, block_rows), 0)
        source = lax.broadcasted_iota(jnp.int32, (block_rows, block_rows), 1)
        linked = (block_segs[:, None] == block_segs[None, :]) & (position >= source)
        spread = jnp.where(linked[:, :, None], cumulative[:, None, :] - cumulative[None, :, :], 0.0)
        decay_mat = jnp.where(linked[:, :, None], jnp.exp(spread), 0.0)
        inner = jnp.dot(c_part, b_part.T, precision=HIGHEST)
        mixing = inner[:, :, None] * decay_mat * block_steps[None, :, :]
        output = jnp.einsum('tsh,shp->thp', mixing, block_vals, precision=HIGHEST)
        entry = jnp.where(block_segs == last_seg, 1.0, 0.0)[:, None] * jnp.exp(cumulative)
        output = output + entry[:, :, None] * jnp.einsum('tn,hpn->thp', c_part, state, precision=HIGHEST)
        weight_out = jnp.where(block_segs == block_segs[-1], 1.0, 0.0)[:, None] * jnp.exp(cumulative[-1][None, :] - cumulative) * block_steps
        new_state = entry[-1][:, None, None] * state + jnp.einsum('sh,shp,sn->hpn', weight_out, block_vals, b_part, precision=HIGHEST)
        return ((new_state, block_segs[-1]), output)
    begin = (jnp.zeros((H, P_SIZE, N), jnp.float32), jnp.array(-1, jnp.int32))
    final_carry, outputs = lax.scan(one_block, begin, (to_blocks(values), to_blocks(step_size), to_blocks(log_decay), to_blocks(b_matrix), to_blocks(c_matrix), to_blocks(seg_row)))
    return outputs.reshape(values.shape)

def mixer_layer(hidden, seg_row, norm_scale, in_w, conv_w, conv_b, dt_shift, a_logs, skip_gain, gate_scale, out_w):
    length = hidden.shape[0]
    normed = rms_scale(hidden, norm_scale)
    projected = low_back(jnp.dot(low(normed), in_w, precision=HIGHEST))
    conv_out = conv_mix(projected[:, DI:DI + DC], seg_row, conv_w, conv_b)
    values = conv_out[:, :DI].reshape(length, H, P_SIZE)
    step_size = jax.nn.softplus(projected[:, DI + DC:] + dt_shift)
    log_decay = -step_size * jnp.exp(a_logs)
    mixed = scan_states(values, step_size, log_decay, conv_out[:, DI:DI + N], conv_out[:, DI + N:], seg_row) + skip_gain[:, None] * values
    gated = mixed.reshape(length, DI) * jax.nn.silu(projected[:, :DI])
    normed_out = rms_scale(gated, gate_scale)
    return hidden + low_back(jnp.dot(low(normed_out), out_w, precision=HIGHEST))

def run_sections(start_hidden, seg_row, params):
    hidden = start_hidden
    for section_number in range(N_SECTION):
        for depth_index in range(LAYERS):
            hidden = mixer_layer(hidden, seg_row, *[param[section_number, depth_index] for param in params])
        if section_number < N_SECTION - 1:
            hidden = low_back(low(hidden))
    return hidden

def reference(inputs, segment, cotangent, norm_gain, in_weight, conv_weight, conv_bias, dt_bias, a_log, d_skip, gate_gain, out_weight):
    params = tuple((param.astype(jnp.float32) for param in (norm_gain, in_weight, conv_weight, conv_bias, dt_bias, a_log, d_skip, gate_gain, out_weight)))
    flat_in = inputs.reshape(MB * SEQS, SEQ, D)
    flat_seg = segment.reshape(MB * SEQS, SEQ)
    flat_cot = cotangent.reshape(MB * SEQS, SEQ, D)

    def one_sequence(totals, pieces):
        seq_in, seq_seg, seq_cot = pieces

        def forward(start_hidden, *weights):
            return run_sections(start_hidden, seq_seg, weights)
        final_hidden, backward = jax.vjp(forward, seq_in.astype(jnp.float32), *params)
        grads = backward(seq_cot.astype(jnp.float32))
        totals = tuple((total + grad for total, grad in zip(totals, grads[1:])))
        return (totals, (final_hidden.astype(jnp.bfloat16), grads[0].astype(jnp.bfloat16)))
    zero_totals = tuple((jnp.zeros_like(param) for param in params))
    totals, (finals, in_grads) = lax.scan(one_sequence, zero_totals, (flat_in, flat_seg, flat_cot))
    return (finals.reshape(MB, SEQS, SEQ, D), in_grads.reshape(MB, SEQS, SEQ, D), totals[0], totals[1], totals[2], totals[3], totals[4], totals[5], totals[6], totals[7], totals[8])
```

```python
import functools

import jax
import jax.numpy as jnp
from jax import lax
from jax.experimental import pallas as pl
from jax.experimental.pallas import tpu as pltpu
from jax.sharding import PartitionSpec as P

D = 1536
H = 48
P_SIZE = 64
N = 128
K = 4
DI = 3072
DC = 3328
DIN = 6448
EPSILON = 1e-05
HIGHEST = lax.Precision.HIGHEST
BF16 = jnp.bfloat16
F32 = jnp.float32
Q = 128
LANES = 128


def dot(a, b, dims=((1,), (0,)), precision=None):
    return lax.dot_general(a, b, (dims, ((), ())), preferred_element_type=F32, precision=precision)


def low_dot(a, b, dims=((1,), (0,))):
    return dot(a.astype(BF16), b.astype(BF16), dims)


def fine_dot(a, b, dims=((1,), (0,))):
    return dot(a, b, dims, HIGHEST)


def pair_lanes(table, first, low_half):
    return jnp.where(low_half, table[:, first : first + 1], table[:, first + 1 : first + 2])


def decay_tables(proj_dt, dt_bias, a_row, tri):
    shifted = proj_dt + dt_bias
    step = jnp.maximum(shifted, 0.0) + jnp.log1p(jnp.exp(-jnp.abs(shifted)))
    log_decay = -step * jnp.exp(a_row)
    cumulative = fine_dot(tri, log_decay)
    return shifted, step, log_decay, cumulative


def triangles():
    row = lax.broadcasted_iota(jnp.int32, (Q, Q), 0)
    column = lax.broadcasted_iota(jnp.int32, (Q, Q), 1)
    return row, column


MESH_ID = pl.DeviceIdType.MESH
VMEM_LIMIT = 60 * 1024 * 1024


def remote(src, dst, send_sem, recv_sem, device):
    return pltpu.make_async_remote_copy(
        src_ref=src, dst_ref=dst, send_sem=send_sem, recv_sem=recv_sem, device_id=device, device_id_type=MESH_ID
    )


def greet(devices):
    barrier = pltpu.get_barrier_semaphore()
    count = 0
    for condition, device in devices:
        if condition is None:
            pl.semaphore_signal(barrier, inc=1, device_id=device, device_id_type=MESH_ID)
            count = count + 1
        else:

            @pl.when(condition)
            def _():
                pl.semaphore_signal(barrier, inc=1, device_id=device, device_id_type=MESH_ID)

            count = count + condition.astype(jnp.int32)
    pl.semaphore_wait(barrier, count)


def bits_of(peers):
    return [1 << k for k in range(peers.bit_length() - 1)]


def has_bit(value, bit):
    return (value // bit) % 2


def flip(value, bits):
    bit = 1
    out = value
    while bit <= bits:
        if bits & bit:
            out = out + bit * (1 - 2 * has_bit(value, bit))
        bit = bit * 2
    return out


def to_column(row):
    down, across = triangles()
    return jnp.sum(jnp.where(down == across, jnp.broadcast_to(row, (Q, Q)), 0.0), axis=1, keepdims=True)


def to_row(column):
    down, across = triangles()
    return jnp.sum(jnp.where(down == across, jnp.broadcast_to(column, (Q, Q)), 0.0), axis=0, keepdims=True)


def group_tiles(tiles, send_sem, recv_sem, here, peers):
    copies = [
        remote(tiles.at[0], tiles.at[j], send_sem.at[j], recv_sem.at[j], {"dp": flip(here, j)})
        for j in range(1, peers)
    ]
    for copy in copies:
        copy.start()
    for copy in copies:
        copy.wait()
    total = tiles[0]
    for j in range(1, peers):
        total = total + tiles[j]
    return total


class GroupRows:

    def __init__(self, where, here, peers, send_sem, recv_sem):
        self.where, self.here, self.peers = where, here, peers
        self.send_sem, self.recv_sem = send_sem, recv_sem

    def part(self, j):
        return self.where(flip(self.here, j))

    def copy(self, j, bit, source=None):
        part = self.part(j)
        return remote(
            part if source is None else source, part, self.send_sem.at[j ^ bit], self.recv_sem.at[j ^ bit],
            {"dp": flip(self.here, bit)},
        )

    def begin(self, source=None):
        for bit in bits_of(self.peers)[::-1]:
            self.copy(0, bit, source).start()

    def finish(self):
        for bit in bits_of(self.peers)[::-1]:
            for j in range(bit, self.peers, 2 * bit):
                self.copy(j ^ bit, bit).wait_send()
                landing = self.part(j)
                remote(
                    landing, landing, self.send_sem.at[j], self.recv_sem.at[j], {"dp": flip(self.here, bit)}
                ).wait_recv()
                for lower in bits_of(bit)[::-1]:
                    self.copy(j, lower).start()


def rows_of(whole, rows):
    return lambda device: whole.at[pl.ds(pl.multiple_of(device * rows, 8), rows)]


class GroupSum:

    def __init__(self, partial, landed, per_rank, here, peers, send_sem, recv_sem):
        self.partial, self.landed, self.per_rank = partial, landed, per_rank
        self.here, self.bits = here, bits_of(peers)
        self.send_sem, self.recv_sem = send_sem, recv_sem

    def leaves_by(self, k, piece):
        owner = piece // self.per_rank
        fits = has_bit(owner, self.bits[k]) != has_bit(self.here, self.bits[k])
        for bit in self.bits[:k]:
            fits = fits & (has_bit(owner, bit) == has_bit(self.here, bit))
        return fits

    def copy(self, k, piece):
        rows = pl.ds(pl.multiple_of(piece * Q, Q), Q)
        return remote(
            self.partial.at[rows], self.landed.at[k, rows], self.send_sem.at[k, piece], self.recv_sem.at[k, piece],
            {"dp": flip(self.here, self.bits[k])},
        )

    def send(self, k, piece):
        @pl.when(self.leaves_by(k, piece))
        def _():
            if k > 0:
                rows = pl.ds(pl.multiple_of(piece * Q, Q), Q)
                total = self.partial[rows, :].astype(F32)
                for m in range(k):
                    self.copy(m, piece).wait_recv()
                    total = total + self.landed[m, rows, :].astype(F32)
                self.partial[rows, :] = total.astype(BF16)
            self.copy(k, piece).start()

    def own(self, piece):
        rows = pl.ds(pl.multiple_of(piece * Q, Q), Q)
        total = self.partial[rows, :].astype(F32)
        for m in range(len(self.bits)):
            self.copy(m, piece).wait_recv()
            total = total + self.landed[m, rows, :].astype(F32)
        return total

    def settle(self, pieces):
        for k in range(len(self.bits)):
            for piece in range(pieces):

                @pl.when(self.leaves_by(k, piece))
                def _():
                    self.copy(k, piece).wait_send()


def rms_parts(values):
    return lax.rsqrt(jnp.mean(values * values, axis=-1, keepdims=True) + EPSILON)


class SectionGather:

    def __init__(self, held, section, nf, y, z, sems):
        self.held, self.section, self.nf, self.y, self.z, self.sems = held, section, nf, y, z, sems
        width = held.shape[1]
        first = -(-width // 32) * 16
        self.spans = [(0, first), (first, width - first)]
        self.peer = {"section": 1 - y}

    def block(self, b, part):
        start, size = self.spans[part]
        return self.held.at[b, pl.ds(start, size)]

    def each(self, body):
        for part in range(2):
            owner = self.y == self.section

            @pl.when(owner if part == 0 else jnp.logical_not(owner))
            def _():
                body(part)

    def send(self, b, part, row, k, landed, device):
        here = self.block(b, part)
        return remote(here, here, self.sems.at[row, k], self.sems.at[landed, k], device)

    def right(self, k, b, part):
        return self.send(b, part, 0, k, 2, {"fsdp": self.z + 1})

    def left(self, k, b, part):
        return self.send(b, part, 1, k, 3, {"fsdp": self.z - 1})

    def over(self, k, b, part):
        return self.send(b, part, 4, k, 5, self.peer)

    def cross(self):
        here = self.block(self.z, 1)
        return remote(here, here, self.sems.at[6, 0], self.sems.at[6, 1], self.peer)

    def has_right(self):
        return self.z < self.nf - 1

    def has_left(self):
        return self.z > 0

    def start_cross(self):
        @pl.when(self.y == self.section)
        def _():
            self.cross().start()

    def begin(self):
        def body(part):
            if part == 1:
                self.cross().wait_recv()

            @pl.when(self.has_right())
            def _():
                self.right(1, self.z, part).start()

            @pl.when(self.has_left())
            def _():
                self.left(1, self.z, part).start()

            if part == 0:
                self.cross().wait_send()
                self.over(0, self.z, 0).start()

        self.each(body)

    def settle_begin(self):
        def body(part):
            @pl.when(self.has_right())
            def _():
                self.right(1, self.z, part).wait_send()

            @pl.when(self.has_left())
            def _():
                self.left(1, self.z, part).wait_send()

            if part == 0:
                self.over(0, self.z, 0).wait_send()
            else:
                self.over(0, self.z, 0).wait_recv()

        self.each(body)

    def sides(self, k, body):
        @pl.when(self.z >= k)
        def _():
            body(self.z - k, k, True)

        @pl.when(self.z + k < self.nf)
        def _():
            body(self.z + k, self.nf + k, False)

    def arrive(self, k):
        def body(part):
            def one(b, index, from_left):
                if from_left:
                    self.right(k, b, part).wait_recv()
                else:
                    self.left(k, b, part).wait_recv()

            self.sides(k, one)

        self.each(body)

    def relay(self, k):
        def body(part):
            def one(b, index, from_left):
                if k < self.nf - 1:
                    if from_left:

                        @pl.when(self.has_right())
                        def _():
                            self.right(k + 1, b, part).start()

                    else:

                        @pl.when(self.has_left())
                        def _():
                            self.left(k + 1, b, part).start()

                self.over(index, b, part).start()

            self.sides(k, one)

        self.each(body)

    def settle(self, k):
        def body(part):
            def one(b, index, from_left):
                self.over(index, b, part).wait_send()
                self.over(index, b, 1 - part).wait_recv()
                if k < self.nf - 1:
                    if from_left:

                        @pl.when(self.has_right())
                        def _():
                            self.right(k + 1, b, part).wait_send()

                    else:

                        @pl.when(self.has_left())
                        def _():
                            self.left(k + 1, b, part).wait_send()

            self.sides(k, one)

        self.each(body)


class OutGather:

    def __init__(self, source, held, section, nf, y, z, d, sems):
        self.source, self.held, self.section, self.nf = source, held, section, nf
        self.y, self.z, self.d, self.sems = y, z, d, sems
        self.pieces = sems.shape[1]
        self.rows = source.shape[0] // self.pieces
        self.columns = source.shape[1] // 2
        self.peer = {"section": 1 - y}
        self.source_here = z == d

    def owner(self):
        return self.y == self.section

    def piece(self, ref, part, i):
        return ref.at[pl.ds(i * self.rows, self.rows), pl.ds(part * self.columns, self.columns)]

    def send(self, i, part, row, landed, device, source=None):
        target = self.piece(self.held, part, i)
        return remote(
            target if source is None else self.piece(source, part, i), target, self.sems.at[row, i],
            self.sems.at[landed, i], device,
        )

    def right(self, i, part, source=None):
        return self.send(i, part, 0, 2, {"fsdp": self.z + 1}, source)

    def left(self, i, part, source=None):
        return self.send(i, part, 1, 2, {"fsdp": self.z - 1}, source)

    def over(self, i, part, source=None):
        return self.send(i, part, 3, 4, self.peer, source)

    def cross(self):
        columns = pl.ds(self.columns, self.columns)
        return remote(
            self.source.at[:, columns], self.held.at[:, columns], self.sems.at[5, 0], self.sems.at[5, 1], self.peer
        )

    def keep(self):
        return pltpu.make_async_copy(self.source, self.held, self.sems.at[5, 2])

    def goes_right(self):
        return (self.z >= self.d) & (self.z < self.nf - 1)

    def goes_left(self):
        return (self.z <= self.d) & (self.z > 0)

    def each(self, condition, body):
        for part in range(2):
            mine = self.owner() if part == 0 else jnp.logical_not(self.owner())

            @pl.when(condition & mine)
            def _():
                body(part)

    def along(self, i, part, action, source=None):
        @pl.when(self.goes_right())
        def _():
            action(self.right(i, part, source))

        @pl.when(self.goes_left())
        def _():
            action(self.left(i, part, source))

    def begin(self):
        @pl.when(self.source_here & self.owner())
        def _():
            self.cross().start()
            self.keep().start()
            for i in range(self.pieces):
                self.along(i, 0, lambda copy: copy.start(), self.source)
            for i in range(self.pieces):
                self.over(i, 0, self.source).start()

    def begin_other(self):
        @pl.when(self.source_here & jnp.logical_not(self.owner()))
        def _():
            self.cross().wait_recv()
            for i in range(self.pieces):
                self.along(i, 1, lambda copy: copy.start())

    def hops(self, distance):
        def body(part):
            for i in range(self.pieces):
                self.right(i, part).wait_recv()
                self.along(i, part, lambda copy: copy.start())
                self.over(i, part).start()

        self.each((self.z == self.d + distance) | (self.z == self.d - distance), body)

    def settle(self):
        @pl.when(self.source_here & self.owner())
        def _():
            self.cross().wait_send()
            self.keep().wait()

        def at_source(part):
            for i in range(self.pieces):
                self.along(i, part, lambda copy: copy.wait_send())
                if part == 0:
                    self.over(i, 0).wait_send()
                else:
                    self.over(i, 0).wait_recv()

        def elsewhere(part):
            for i in range(self.pieces):
                self.along(i, part, lambda copy: copy.wait_send())
                self.over(i, part).wait_send()
                self.over(i, 1 - part).wait_recv()

        self.each(self.source_here, at_source)
        self.each(jnp.logical_not(self.source_here), elsewhere)


def line_neighbours(nf, y, z):
    return [
        (None, {"section": 1 - y}),
        (z < nf - 1, {"fsdp": z + 1}),
        (z > 0, {"fsdp": z - 1}),
    ]


def start_kernel(
    nf, nd, rows, x_ref, seg_ref, in_ref, out_ref, conv_w_ref, conv_b_ref, norm_ref, gate_ref, head_ref,
    hidden_ref, normed_all, w_in0, w_in1, w_out0, seg_out,
    conv_w_out, conv_b_out, dtb_out, alog_out, skip_out, gain_out, norm_out, meta_out,
    table, x_low, normed_low, seg_all, local_sem, swap_send, swap_recv, small_sem, in_sems0, in_sems1, out_sems,
    own_sem, group_send, group_recv,
):
    y, z, d = lax.axis_index("section"), lax.axis_index("fsdp"), lax.axis_index("dp")
    ch = DI // nd
    heads = H // nd
    lines = rows // Q * 8
    length = rows * nd
    twin = {"fsdp": d, "dp": z}
    peer = {"section": 1 - y}
    home = z == d
    away = z != d
    greet(line_neighbours(nf, y, z) + [(away, twin)] + [(None, {"dp": flip(d, bit)}) for bit in bits_of(nd)])
    gathers = [SectionGather(w_in0, 0, nf, y, z, in_sems0), SectionGather(w_in1, 1, nf, y, z, in_sems1)]
    outs = OutGather(out_ref, w_out0, 0, nf, y, z, d, out_sems)

    def own(held):
        return [
            pltpu.make_async_copy(
                in_ref.at[pl.ds(pl.multiple_of(begin, 16), count)], held.at[z, pl.ds(place, count)], own_sem.at[k]
            )
            for k, (begin, place, count) in enumerate(
                [(d * ch, 0, ch), (DI + d * ch, ch, ch), (2 * DI, 2 * ch, DIN - 2 * DI)]
            )
        ]

    for section, held in enumerate((w_in0, w_in1)):

        @pl.when(y == section)
        def _():
            for copy in own(held):
                copy.start()
            for copy in own(held):
                copy.wait()

    gathers[0].start_cross()
    gathers[1].start_cross()

    table[y, 0:4, :] = conv_w_ref[...]
    table[y, 4:5, :] = conv_b_ref[...]
    table[y, 5:6, 0:D] = norm_ref[...]
    table[y, 6:7, 0:DI] = gate_ref[...]
    for k in range(3):
        table[y, 7:8, k * LANES : (k + 1) * LANES] = head_ref[k : k + 1, :]
    small_copy = remote(table.at[y], table.at[y], small_sem.at[0], small_sem.at[1], peer)
    small_copy.start()

    def seg_rows(device):
        return seg_all.at[pl.ds(pl.multiple_of(device * lines, 8), lines)]

    swaps = [
        remote(x_ref.at[y], hidden_ref, swap_send.at[0], swap_recv.at[0], twin),
        remote(seg_ref, seg_rows(z), swap_send.at[1], swap_recv.at[1], twin),
    ]
    stays = [
        pltpu.make_async_copy(x_ref.at[y], hidden_ref, local_sem.at[1]),
        pltpu.make_async_copy(seg_ref, seg_rows(d), local_sem.at[2]),
    ]

    @pl.when(away)
    def _():
        for copy in swaps:
            copy.start()

    @pl.when(home)
    def _():
        for copy in stays:
            copy.start()

    gathers[0].begin()
    outs.begin()

    def settle_swap(k):
        @pl.when(away)
        def _():
            swaps[k].wait()

        @pl.when(home)
        def _():
            stays[k].wait()

    small_copy.wait()
    settle_swap(0)
    x_copy = pltpu.make_async_copy(hidden_ref, x_low, local_sem.at[1])
    x_copy.start()
    x_copy.wait()
    values = x_low[...].astype(F32)
    normed_low[...] = (values * rms_parts(values) * table[0, 5:6, 0:D]).astype(BF16)
    normed_group = GroupRows(rows_of(normed_all, rows), d, nd, group_send.at[0], group_recv.at[0])
    normed_own = pltpu.make_async_copy(normed_low, normed_group.part(0), local_sem.at[0])
    normed_own.start()
    normed_group.begin(normed_low)
    settle_swap(1)
    seg_group = GroupRows(seg_rows, d, nd, group_send.at[1], group_recv.at[1])
    seg_group.begin()

    turn = d * heads
    low_half = lax.broadcasted_iota(jnp.int32, (1, LANES), 1) < P_SIZE
    channels = pl.ds(pl.multiple_of(d * ch, LANES), ch)
    for section in range(2):
        conv_w_out[section, :, 0:ch] = table[section, 0:4, channels]
        conv_w_out[section, :, ch:] = table[section, 0:4, DI:DC]
        conv_b_out[section, :, 0:ch] = table[section, 4:5, channels]
        conv_b_out[section, :, ch:] = table[section, 4:5, DI:DC]
        norm_out[section] = table[section, 5:6, 0:D]
        gain_out[section] = table[section, 6:7, channels]
        head_rows = [
            pltpu.roll(table[section, :, k * LANES : (k + 1) * LANES], LANES - turn, 1)[7:8, :] for k in range(3)
        ]
        dtb_out[section] = head_rows[0]
        alog_out[section] = head_rows[1]
        for pair in range(ch // LANES):
            skip_out[section, :, pair * LANES : (pair + 1) * LANES] = pair_lanes(head_rows[2], 2 * pair, low_half)

    gathers[0].arrive(1)
    gathers[0].relay(1)
    outs.begin_other()
    outs.hops(1)
    for k in range(2, nf):
        gathers[0].arrive(k)
        gathers[0].relay(k)
        if k == 2:
            gathers[1].begin()
            normed_group.finish()
            seg_group.finish()
            normed_own.wait()
        outs.hops(k)

    seg_copy = pltpu.make_async_copy(seg_all, seg_out, local_sem.at[0])
    seg_copy.start()
    lane = lax.broadcasted_iota(jnp.int32, (8, LANES), 1)
    sub_lane = lax.broadcasted_iota(jnp.int32, (Q, LANES), 1)
    before = jnp.full((8, LANES), -1.0, F32)
    for chunk in range(length // Q):
        now = seg_all[chunk * 8 : chunk * 8 + 8, :]
        columns = [now[0:1, :]]
        for lag in range(1, K):
            earlier = jnp.where(lane < lag, pltpu.roll(before, lag, 1), pltpu.roll(now, lag, 1))
            columns.append(jnp.where(earlier == now, 1.0, 0.0)[0:1, :])
        columns.append(jnp.where(now == before[:, Q - 1 : Q], 1.0, 0.0)[0:1, :])
        columns.append(jnp.where(now == now[:, Q - 1 : Q], 1.0, 0.0)[0:1, :])
        block = jnp.zeros((Q, LANES), F32)
        for k, row in enumerate(columns):
            block = jnp.where(sub_lane == k, to_column(row), block)
        meta_out[chunk * Q : (chunk + 1) * Q, :] = block
        before = now

    gathers[1].arrive(1)
    for k in range(1, nf):
        gathers[0].settle(k)
    gathers[0].settle_begin()
    gathers[1].settle_begin()
    outs.settle()
    seg_copy.wait()


def run_start(nf, nd, rows, x, seg, in_rows, out_rows, conv_w, conv_b, norm_gain, gate_gain, head_table):
    length = rows * nd
    ch = DI // nd
    conv_width = ch + 2 * N
    block = in_rows.shape[1]
    width = 2 * ch + DIN - 2 * DI
    lines = seg.shape[0]
    anywhere = pl.BlockSpec(memory_space=pl.ANY)
    local = pl.BlockSpec(memory_space=pltpu.VMEM)
    dma = pltpu.SemaphoreType.DMA
    return pl.pallas_call(
        functools.partial(start_kernel, nf, nd, rows),
        in_specs=[anywhere] * 4 + [local] * 5,
        out_specs=[anywhere] * 6 + [local] * 8,
        out_shape=[
            jax.ShapeDtypeStruct((rows, D), BF16),
            jax.ShapeDtypeStruct((length, D), BF16),
            jax.ShapeDtypeStruct((nf, width, block), BF16),
            jax.ShapeDtypeStruct((nf, width, block), BF16),
            jax.ShapeDtypeStruct((ch, D), BF16),
            jax.ShapeDtypeStruct((lines * nd, LANES), F32),
            jax.ShapeDtypeStruct((2, K, conv_width), F32),
            jax.ShapeDtypeStruct((2, 1, conv_width), F32),
            jax.ShapeDtypeStruct((2, 1, LANES), F32),
            jax.ShapeDtypeStruct((2, 1, LANES), F32),
            jax.ShapeDtypeStruct((2, 1, ch), F32),
            jax.ShapeDtypeStruct((2, 1, ch), F32),
            jax.ShapeDtypeStruct((2, 1, D), F32),
            jax.ShapeDtypeStruct((length, LANES), F32),
        ],
        scratch_shapes=[
            pltpu.VMEM((2, 8, DC), F32),
            pltpu.VMEM((rows, D), BF16),
            pltpu.VMEM((rows, D), BF16),
            pltpu.VMEM((lines * nd, LANES), F32),
            dma((3,)),
            dma((2,)),
            dma((2,)),
            dma((2,)),
            dma((7, 2 * nf)),
            dma((7, 2 * nf)),
            dma((6, 4)),
            dma((3,)),
            dma((2, nd)),
            dma((2, nd)),
        ],
        compiler_params=pltpu.CompilerParams(
            vmem_limit_bytes=VMEM_LIMIT, collective_id=1, has_side_effects=True
        ),
        name="gather_start",
    )(x, seg, in_rows, out_rows, conv_w, conv_b, norm_gain, gate_gain, head_table)


class SectionSum:

    def __init__(self, view, nf, y, z, own, landed, chain, sems, result):
        self.view, self.nf, self.y, self.z, self.result = view, nf, y, z, result
        self.own, self.landed, self.chain = own, landed, chain
        self.load_sem, self.over_send, self.over_recv, self.chain_send, self.chain_recv = (
            sems.at[0], sems.at[1], sems.at[2], sems.at[3], sems.at[4]
        )
        self.part_rows = own.shape[1]

    def load(self, block):
        return pltpu.make_async_copy(self.view(block, self.y), self.own.at[block], self.load_sem.at[block])

    def over(self, block):
        return remote(
            self.view(block, 1 - self.y), self.landed.at[block], self.over_send.at[block], self.over_recv.at[block],
            {"section": 1 - self.y},
        )

    def right(self, block):
        return remote(
            self.own.at[block], self.chain.at[block], self.chain_send.at[block], self.chain_recv.at[block],
            {"fsdp": self.z + 1},
        )

    def left(self, block, arrives):
        slot = self.nf if arrives else block
        return remote(
            self.own.at[block], self.chain.at[slot], self.chain_send.at[block], self.chain_recv.at[slot],
            {"fsdp": self.z - 1},
        )

    def at(self, k, body):
        if k == 0:
            body(self.z, False)
            return

        @pl.when(self.z + k < self.nf)
        def _():
            body(self.z + k, True)

        @pl.when(self.z - k >= 0)
        def _():
            body(self.z - k, False)

    def begin(self):
        self.at(self.nf - 1, lambda block, rightward: self.over(block).start())
        for k in range(self.nf - 1, -1, -1):
            self.at(k, lambda block, rightward: self.load(block).start())

    def add(self, block, sources, target):
        step = 32

        def some(i, carry):
            rows = pl.ds(pl.multiple_of(i * step, 16), step)
            total = self.own[block, rows, :].astype(F32)
            for ref, slot in sources:
                total = total + ref[slot, rows, :].astype(F32)
            if target is None:
                self.own[block, rows, :] = total.astype(BF16)
            else:
                target[rows, :] = total.astype(BF16)
            return carry

        lax.fori_loop(0, self.part_rows // step, some, 0)

    def ready(self, block):
        self.load(block).wait()
        self.over(block).wait_recv()

    def stage(self, k):
        z, nf = self.z, self.nf
        self.at(k, lambda block, rightward: self.ready(block))
        self.at(k - 1, lambda block, rightward: self.over(block).start())

        def one(block, rightward):
            far_end = z == 0 if rightward else z == nf - 1
            arrived = self.right(block) if rightward else self.left(block, False)
            leaving = self.right(block) if rightward else self.left(block, k == 1)

            @pl.when(jnp.logical_not(far_end))
            def _():
                arrived.wait_recv()
                self.add(block, [(self.landed, block), (self.chain, block)], None)

            @pl.when(far_end)
            def _():
                self.add(block, [(self.landed, block)], None)

            leaving.start()

        self.at(k, one)

    def finish(self):
        z, nf, target = self.z, self.nf, self.result
        self.ready(z)

        @pl.when(z > 0)
        def _():
            self.right(z).wait_recv()

        @pl.when(z < nf - 1)
        def _():
            self.left(z, True).wait_recv()

        @pl.when(z == 0)
        def _():
            self.add(z, [(self.landed, z), (self.chain, nf)], target)

        @pl.when(z == nf - 1)
        def _():
            self.add(z, [(self.landed, z), (self.chain, z)], target)

        @pl.when((z > 0) & (z < nf - 1))
        def _():
            self.add(z, [(self.landed, z), (self.chain, z), (self.chain, nf)], target)

    def settle(self):
        z, nf = self.z, self.nf
        self.over(z).wait_send()
        for k in range(nf - 1, 0, -1):

            @pl.when(z + k < nf)
            def _():
                self.over(z + k).wait_send()
                self.right(z + k).wait_send()

            @pl.when(z - k >= 0)
            def _():
                self.over(z - k).wait_send()
                self.left(z - k, k == 1).wait_send()


def in_parts(width):
    rows = -(-width // 64) * 32
    return rows, width - rows


def in_view(source, nf):
    rows, second = in_parts(source.shape[-2])

    def view(block, part):
        here = pl.ds(pl.multiple_of(part * second, 16), rows)
        if len(source.shape) == 3:
            return source.at[block, here]
        columns = source.shape[1] // nf
        return source.at[here, pl.ds(pl.multiple_of(block * columns, LANES), columns)]

    return view


def out_view(source, nf):
    rows, columns = source.shape[0] // nf, source.shape[1] // 2

    def view(block, part):
        here = pl.ds(pl.multiple_of(block * rows, 16), rows)
        return source.at[here, pl.ds(pl.multiple_of(part * columns, LANES), columns)]

    return view


def in_part_shape(nf, source):
    columns = source.shape[2] if len(source.shape) == 3 else source.shape[1] // nf
    return in_parts(source.shape[-2])[0], columns


def out_part_shape(nf, source):
    return source.shape[0] // nf, source.shape[1] // 2


def section_sum_scratch(nf, part):
    return [
        pltpu.VMEM((nf,) + part, BF16),
        pltpu.VMEM((nf,) + part, BF16),
        pltpu.VMEM((nf + 1,) + part, BF16),
        pltpu.SemaphoreType.DMA((5, nf + 1)),
        pltpu.VMEM(part, BF16),
    ]


class SectionReturn:

    def __init__(self, piece, place, owner, y, sems):
        self.piece, self.place, self.owner, self.y, self.sems = piece, place, owner, y, sems

    def keep(self):
        return pltpu.make_async_copy(self.piece(self.owner), self.place(self.owner), self.sems.at[2])

    def send(self):
        other = 1 - self.owner
        return remote(
            self.piece(other), self.place(other), self.sems.at[0], self.sems.at[1], {"section": 1 - self.y}
        )

    def begin(self):
        @pl.when(self.y == self.owner)
        def _():
            self.keep().start()

        @pl.when(self.y != self.owner)
        def _():
            self.send().start()

    def finish(self):
        @pl.when(self.y == self.owner)
        def _():
            self.keep().wait()
            self.send().wait_recv()

        @pl.when(self.y != self.owner)
        def _():
            self.send().wait_send()


def end_kernel(
    nf, nd,
    in_ref, in_part1_ref, out_part0_ref, out_part1_ref, small_ref,
    in_all, out_all, small_all,
    in_own, in_landed, in_chain, in_sems, in_part,
    in_final, out_final, small_slots, small_total, local_sem, swap_sem, back_sem, small_sems, group_send, group_recv,
):
    y, z, d = lax.axis_index("section"), lax.axis_index("fsdp"), lax.axis_index("dp")
    away = z != d
    twin = {"fsdp": d, "dp": z}
    peer = {"section": 1 - y}
    lines = small_ref.shape[1]
    wide = lambda k: {"fsdp": (z + k) % nf}
    greet(
        [(None, peer), (away, twin)]
        + [(None, wide(k)) for k in range(1, nf)]
        + [(None, {"dp": flip(d, bit)}) for bit in bits_of(nd)]
    )
    in_sum = SectionSum(in_view(in_ref, nf), nf, y, z, in_own, in_landed, in_chain, in_sems, in_part)
    in_sum.begin()
    small_over = remote(small_ref.at[1 - y], small_slots.at[nf], small_sems.at[0, 0], small_sems.at[1, 0], peer)
    small_over.start()
    small_load = pltpu.make_async_copy(small_ref.at[y], small_slots.at[0], local_sem.at[0])
    small_load.start()
    width = in_final.shape[0]
    part_rows, second = in_parts(width)
    overlap = part_rows - second
    out_rows, out_columns = out_part0_ref.shape
    in_piece = lambda ref: lambda p: ref if p == 0 else ref.at[pl.ds(overlap, width - part_rows)]
    in_place = lambda p: in_final.at[pl.ds(p * part_rows, width - part_rows if p else part_rows)]
    out_place = lambda p: out_final.at[:, pl.ds(p * out_columns, out_columns)]
    out_returns = [
        SectionReturn(lambda p: out_part0_ref, out_place, 0, y, back_sem.at[0]),
        SectionReturn(lambda p: out_part1_ref, out_place, 1, y, back_sem.at[1]),
    ]
    in_returns = [
        SectionReturn(in_piece(in_part), in_place, 0, y, back_sem.at[2]),
        SectionReturn(in_piece(in_part1_ref), in_place, 1, y, back_sem.at[3]),
    ]
    in_groups = [
        GroupRows(
            lambda device, p=p: in_all.at[device, pl.ds(p * part_rows, width - part_rows if p else part_rows)],
            d, nd, group_send.at[p], group_recv.at[p],
        )
        for p in range(2)
    ]
    out_group = GroupRows(rows_of(out_all, out_rows), d, nd, group_send.at[2], group_recv.at[2])
    small_group = GroupRows(rows_of(small_all, lines), d, nd, group_send.at[3], group_recv.at[3])

    small_load.wait()
    small_over.wait()
    small_slots[0] = small_slots[0] + small_slots[nf]
    small_copies = [
        remote(small_slots.at[0], small_slots.at[k], small_sems.at[0, k], small_sems.at[1, k], wide(k))
        for k in range(1, nf)
    ]
    for copy in small_copies:
        copy.start()
    for copy in small_copies:
        copy.wait()
    total = small_slots[0]
    for k in range(1, nf):
        total = total + small_slots[k]
    small_total[...] = total
    small_own = pltpu.make_async_copy(small_total, small_group.part(0), local_sem.at[0])
    small_own.start()
    small_group.begin(small_total)

    swap_target = out_all.at[pl.ds(pl.multiple_of(z * out_rows, 16), out_rows)]
    swap = remote(out_final, swap_target, swap_sem.at[0], swap_sem.at[1], twin)
    stay = pltpu.make_async_copy(out_final, out_group.part(0), swap_sem.at[2])
    for k in range(nf - 1, 0, -1):
        in_sum.stage(k)
        if k == nf - 1:
            for back in out_returns:
                back.begin()
            small_group.finish()
            small_own.wait()
        if k == nf - 2:
            for back in out_returns:
                back.finish()

            @pl.when(away)
            def _():
                swap.start()

            @pl.when(jnp.logical_not(away))
            def _():
                stay.start()

        if k == 1:
            in_returns[1].begin()

            @pl.when(away)
            def _():
                swap.wait()

            @pl.when(jnp.logical_not(away))
            def _():
                stay.wait()

            out_group.begin()
    in_returns[1].finish()
    out_group.finish()
    in_sum.finish()
    in_returns[0].begin()

    @pl.when(y == 0)
    def _():
        in_returns[0].keep().wait()

    def own_copy(p):
        return pltpu.make_async_copy(in_place(p), in_groups[p].part(0), local_sem.at[1 + p])

    own_copy(0).start()
    in_groups[0].begin(in_place(0))

    @pl.when(y == 0)
    def _():
        in_returns[0].send().wait_recv()

    own_copy(1).start()
    in_groups[1].begin(in_place(1))
    in_groups[0].finish()
    in_groups[1].finish()
    own_copy(0).wait()
    own_copy(1).wait()

    @pl.when(y == 1)
    def _():
        in_returns[0].send().wait_send()

    in_sum.settle()


def run_end(nf, nd, in_grad, in_part1, out_part0, out_part1, small):
    anywhere = pl.BlockSpec(memory_space=pl.ANY)
    dma = pltpu.SemaphoreType.DMA
    lines = small.shape[1]
    width = in_grad.shape[-2]
    out_rows = out_part0.shape[0]
    return pl.pallas_call(
        functools.partial(end_kernel, nf, nd),
        in_specs=[anywhere] * 5,
        out_specs=[anywhere] * 3,
        out_shape=[
            jax.ShapeDtypeStruct((nd, width, in_part1.shape[1]), BF16),
            jax.ShapeDtypeStruct((nd * out_rows, D), BF16),
            jax.ShapeDtypeStruct((nd * lines, LANES), F32),
        ],
        scratch_shapes=section_sum_scratch(nf, in_part1.shape)
        + [
            pltpu.VMEM((width, in_part1.shape[1]), BF16),
            pltpu.VMEM((out_rows, D), BF16),
            pltpu.VMEM((nf + 1, lines, LANES), F32),
            pltpu.VMEM((lines, LANES), F32),
            dma((3,)),
            dma((3,)),
            dma((4, 3)),
            dma((2, nf)),
            dma((4, nd)),
            dma((4, nd)),
        ],
        compiler_params=pltpu.CompilerParams(
            vmem_limit_bytes=VMEM_LIMIT, collective_id=6, has_side_effects=True
        ),
        name="sum_end",
    )(in_grad, in_part1, out_part0, out_part1, small)


class Weights:

    def __init__(self, source, held, sems):
        self.source, self.held, self.sems = source, held, sems
        self.blocks = source.shape[0]
        self.columns = source.shape[2]

    def copies(self):
        out = []
        for k in range(self.blocks):
            if len(self.held.shape) == 3:
                target = self.held.at[k]
            else:
                target = self.held.at[:, pl.ds(k * self.columns, self.columns)]
            out.append(pltpu.make_async_copy(self.source.at[k], target, self.sems.at[k]))
        return out

    def forward(self, rows):
        if len(self.held.shape) == 2:
            return dot(rows, self.held[...], ((1,), (1,)))
        total = 0.0
        for k in range(self.blocks):
            total = total + dot(
                rows[:, k * self.columns : (k + 1) * self.columns], self.held[k], ((1,), (1,))
            )
        return total

    def backward(self, rows):
        if len(self.held.shape) == 2:
            return dot(rows, self.held[...])
        return jnp.concatenate([dot(rows, self.held[k]) for k in range(self.blocks)], axis=1)


def held_shape(w_in):
    blocks, width, columns = w_in.shape
    return (width, blocks * columns) if columns % LANES == 0 else (blocks, width, columns)


def own_steps(steps, turn):
    padded = jnp.concatenate([steps, jnp.zeros((steps.shape[0], LANES - H), F32)], axis=1)
    return pltpu.roll(padded, LANES - turn, 1)


def mix_forward(
    ch, proj_ref, meta_ref, segrow_ref, conv_w_ref, conv_b_ref, dtb_ref, alog_ref, skip_ref, gain_ref,
    gated_ref, square_ref, mixed_ref, pre_ref, state_out_ref, pad, state, sub, chunk, turn,
):
    conv_width = ch + 2 * N
    rows = pl.ds(pl.multiple_of(sub * Q, Q), Q)
    meta = meta_ref[rows, :]
    pad[8:, :] = proj_ref[rows, ch : ch + conv_width]
    pre = conv_b_ref[...] + conv_w_ref[3:4, :] * pad[8:, :]
    for lag in range(1, K):
        pre = pre + (conv_w_ref[3 - lag : 4 - lag, :] * meta[:, lag : lag + 1]) * pad[8 - lag : 8 - lag + Q, :]
    pad[0:8, :] = pad[Q : Q + 8, :]
    pre_ref[rows, :] = pre
    conv_out = pre * jax.nn.sigmoid(pre)
    values = conv_out[:, :ch]
    b_part = conv_out[:, ch : ch + N]
    c_part = conv_out[:, ch + N :]
    row, column = triangles()
    tri = jnp.where(row >= column, 1.0, 0.0)
    shifted, step, log_decay, cumulative = decay_tables(
        own_steps(proj_ref[rows, ch + conv_width :], turn), dtb_ref[...], alog_ref[...], tri
    )
    linked = (row >= column) & (meta[:, 0:1] == segrow_ref[sub])
    inner = jnp.where(linked, low_dot(c_part, b_part, ((1,), (1,))), 0.0)
    cum_t = cumulative.T
    step_t = step.T
    last = cumulative[Q - 1 : Q, :]
    entry = meta[:, 4:5] * jnp.exp(cumulative)
    weight = meta[:, 5:6] * jnp.exp(last - cumulative) * step
    state_in = state[...]
    state_out_ref[sub] = state_in
    carried = low_dot(c_part, state_in)
    low_half = lax.broadcasted_iota(jnp.int32, (Q, LANES), 1) < P_SIZE
    squares = jnp.zeros((Q, 1), F32)
    weighted = []
    entries = []
    for pair in range(ch // LANES):
        lanes = slice(pair * LANES, (pair + 1) * LANES)
        values_pair = values[:, lanes]
        mats = []
        for head in (2 * pair, 2 * pair + 1):
            spread = jnp.minimum(cumulative[:, head : head + 1] - cum_t[head : head + 1, :], 0.0)
            mats.append((inner * jnp.exp(spread) * step_t[head : head + 1, :]).astype(BF16))
        zero = jnp.zeros_like(values_pair)
        stacked = jnp.concatenate(
            [jnp.where(low_half, values_pair, zero), jnp.where(low_half, zero, values_pair)], axis=0
        ).astype(BF16)
        out = dot(jnp.concatenate(mats, axis=1), stacked)
        entry_pair = pair_lanes(entry, 2 * pair, low_half)
        out = out + entry_pair * carried[:, lanes] + skip_ref[:, lanes] * values_pair
        mixed_ref[rows, lanes] = out
        gate = proj_ref[rows, lanes]
        gated = out * (gate * jax.nn.sigmoid(gate))
        squares = squares + jnp.sum(gated * gated, axis=1, keepdims=True)
        gated_ref[rows, lanes] = (gated * gain_ref[:, lanes]).astype(BF16)
        weighted.append((pair_lanes(weight, 2 * pair, low_half) * values_pair).astype(BF16))
        entries.append(entry_pair[Q - 1 : Q, :])
    square_ref[0, pl.ds(chunk, 1), :] = to_row(squares)
    state[...] = jnp.concatenate(entries, axis=1) * state_in + dot(
        b_part.T.astype(BF16), jnp.concatenate(weighted, axis=1)
    )


def layer_kernel(
    ch, rows, nf, nd, final,
    normed_ref, meta_ref, segrow_ref, conv_w_ref, conv_b_ref, dtb_ref, alog_ref, skip_ref, gain_ref,
    w_in_ref, w_out_ref, hidden_ref, extra_ref, *refs,
):
    if not final:
        cot_ref, out_ref, _ = refs[:3]
        refs = refs[3:]
    (
        proj_ref, gated_ref, mixed_ref, pre_ref, state_out_ref, branch_ref, next_ref, ratio_ref, pull_ref, moved_ref,
        *refs,
    ) = refs
    if final:
        cot_all, refs = refs[0], refs[1:]
    else:
        w_in1, w_out1, cot_own = refs[:3]
        in_sems, out_sems = refs[-2:]
        refs = refs[3:-2]
    (
        held, w_out, pad, state, partial, landed, squares, pulls, low,
        sum_send, sum_recv, tile_send, tile_recv, group_send, group_recv, local_sem, load_sem, cot_sem,
    ) = refs
    step = pl.program_id(0)
    y, z, d = lax.axis_index("section"), lax.axis_index("fsdp"), lax.axis_index("dp")
    block = normed_ref.shape[0]
    subs = block // Q
    steps = pl.num_programs(0)
    pieces = partial.shape[0] // Q
    step_count = pieces // subs
    per_rank = rows // Q
    bits = bits_of(nd)
    away = z != d
    twin = {"fsdp": d, "dp": z}
    group = GroupSum(partial, landed, per_rank, d, nd, sum_send, sum_recv)
    weights = Weights(w_in_ref, held, load_sem)
    out_load = pltpu.make_async_copy(w_out_ref, w_out, local_sem.at[3])
    if final:
        cot_group = GroupRows(rows_of(cot_all, rows), d, nd, cot_sem.at[0], cot_sem.at[1])
        cot_keep = pltpu.make_async_copy(extra_ref, cot_group.part(0), local_sem.at[4])
    else:
        gather = SectionGather(w_in1, 1, nf, y, z, in_sems)
        outs = OutGather(out_ref, w_out1, 1, nf, y, z, d, out_sems)
        cot_swap = remote(cot_ref.at[y], cot_own, cot_sem.at[0, 0], cot_sem.at[1, 0], twin)
        cot_stay = pltpu.make_async_copy(cot_ref.at[y], cot_own, cot_sem.at[0, 0])

    @pl.when(step == 0)
    def _():
        for copy in weights.copies():
            copy.start()
        out_load.start()
        greet(
            [(None, {"dp": flip(d, j)}) for j in range(1, nd)]
            + [(away, twin)]
            + ([] if final else line_neighbours(nf, y, z))
        )
        if final:
            cot_keep.start()
            cot_group.begin(extra_ref)
        else:
            gather.relay(1)
            outs.begin()

            @pl.when(away)
            def _():
                cot_swap.start()

            @pl.when(jnp.logical_not(away))
            def _():
                cot_stay.start()

        pad[0:8, :] = jnp.zeros((8, pad.shape[1]), F32)
        state[...] = jnp.zeros_like(state)
        for copy in weights.copies():
            copy.wait()
        out_load.wait()

    proj_ref[...] = weights.forward(normed_ref[...])

    def one_chunk(sub, carry):
        mix_forward(
            ch, proj_ref, meta_ref, segrow_ref, conv_w_ref, conv_b_ref, dtb_ref, alog_ref, skip_ref, gain_ref,
            gated_ref, squares, mixed_ref, pre_ref, state_out_ref, pad, state, sub, step * subs + sub, d * (H // nd),
        )
        return carry

    lax.fori_loop(0, subs, one_chunk, 0)
    here_rows = pl.ds(pl.multiple_of(step * block, block), block)
    partial[here_rows, :] = dot(gated_ref[...], w_out[...]).astype(BF16)

    for k in range(len(bits)):

        @pl.when(step >= k)
        def _():
            for sub in range(subs):
                group.send(k, (step - k) * subs + sub)

    if final:

        @pl.when(step == min(2, step_count - 1))
        def _():
            cot_group.finish()

    else:
        for k in range(1, nf):

            @pl.when(step == min(k, step_count - 1))
            def _():
                if k == 1:
                    outs.begin_other()
                else:
                    gather.arrive(k)
                    gather.relay(k)
                outs.hops(k)

    @pl.when(step == steps - 1)
    def _():
        for k in range(1, len(bits)):
            for late in range(k):
                for sub in range(subs):
                    group.send(k, pieces - (late + 1) * subs + sub)
        total = group_tiles(squares, tile_send, tile_recv, d, nd)
        ratio = lax.rsqrt(total * (1.0 / DI) + EPSILON)
        ratio_ref[...] = ratio
        pulls[0] = jnp.zeros(pulls.shape[1:], F32)
        for part in range(per_rank):
            piece = d * per_rank + part
            here = slice(part * Q, (part + 1) * Q)
            branch = group.own(piece) * to_column(ratio_ref[pl.ds(piece, 1), :])
            branch_ref[here, :] = branch
            moved = (hidden_ref[here, :].astype(F32) + branch).astype(BF16)
            next_ref[here, :] = moved
            if final:
                low[here, :] = moved
                pulls[0, pl.ds(piece, 1), :] = to_row(
                    jnp.sum(extra_ref[here, :].astype(F32) * branch, axis=1, keepdims=True)
                )
            else:
                values = moved.astype(F32)
                low[here, :] = (values * rms_parts(values) * extra_ref[...]).astype(BF16)
        if final:
            swap = remote(low, moved_ref, local_sem.at[0], local_sem.at[1], twin)
            stay = pltpu.make_async_copy(low, moved_ref, local_sem.at[2])

            @pl.when(away)
            def _():
                swap.start()

            @pl.when(jnp.logical_not(away))
            def _():
                stay.start()

            pull_ref[...] = group_tiles(pulls, group_send, group_recv, d, nd)

            @pl.when(away)
            def _():
                swap.wait()

            @pl.when(jnp.logical_not(away))
            def _():
                stay.wait()
        else:
            pull_ref[...] = jnp.zeros_like(pull_ref)
            every = GroupRows(rows_of(moved_ref, rows), d, nd, group_send, group_recv)
            mine = pltpu.make_async_copy(low, every.part(0), local_sem.at[0])
            mine.start()
            every.begin(low)
            every.finish()
            mine.wait()

            for k in range(1, nf):
                gather.settle(k)
            outs.settle()

            @pl.when(away)
            def _():
                cot_swap.wait()

            @pl.when(jnp.logical_not(away))
            def _():
                cot_stay.wait()

        if final:
            cot_keep.wait()
        group.settle(pieces)


def once(shape):
    return pl.BlockSpec(shape, lambda s: (0,) * len(shape), pipeline_mode=pl.Buffered(buffer_count=1))


def pick(part, layer):
    return pl.BlockSpec(
        (None,) + part.shape[1:], lambda s: (layer, 0, 0), pipeline_mode=pl.Buffered(buffer_count=1)
    )


def run_layer(
    ch, rows, nf, nd, final, normed_all, meta, segrow, small, w_in, w_out, hidden, extra, identity, *more
):
    length, width = normed_all.shape[0], w_in.shape[1]
    layer = 1 if final else 0
    conv_width = ch + 2 * N
    block = 2 * Q
    steps = length // block
    pieces = length // Q
    subs = block // Q
    bits = len(bits_of(nd))
    dma = pltpu.SemaphoreType.DMA
    anywhere = pl.BlockSpec(memory_space=pl.ANY)
    ordered = lambda s: (s, 0)
    ordered3 = lambda s: (s, 0, 0)
    return pl.pallas_call(
        functools.partial(layer_kernel, ch, rows, nf, nd, final),
        grid=(steps,),
        in_specs=[
            pl.BlockSpec((block, D), ordered),
            pl.BlockSpec((block, LANES), ordered),
            pl.BlockSpec((subs, 1, Q), ordered3),
        ]
        + [pick(part, layer) for part in small]
        + [
            anywhere,
            anywhere,
            once((rows, D)),
            once((rows, D)) if final else pick(extra, 1),
        ]
        + [anywhere] * len(more),
        out_specs=[
            pl.BlockSpec((block, width), ordered),
            pl.BlockSpec((block, ch), ordered),
            pl.BlockSpec((block, ch), ordered),
            pl.BlockSpec((block, conv_width), ordered),
            pl.BlockSpec((subs, N, ch), ordered3),
            once((rows, D)),
            once((rows, D)),
            once((pieces, Q)),
            once((pieces, Q)),
            anywhere,
        ]
        + [anywhere] * (1 if final else 3),
        out_shape=[
            jax.ShapeDtypeStruct((length, width), F32),
            jax.ShapeDtypeStruct((length, ch), BF16),
            jax.ShapeDtypeStruct((length, ch), F32),
            jax.ShapeDtypeStruct((length, conv_width), F32),
            jax.ShapeDtypeStruct((pieces, N, ch), F32),
            jax.ShapeDtypeStruct((rows, D), F32),
            jax.ShapeDtypeStruct((rows, D), BF16),
            jax.ShapeDtypeStruct((pieces, Q), F32),
            jax.ShapeDtypeStruct((pieces, Q), F32),
            jax.ShapeDtypeStruct((rows if final else length, D), BF16),
        ]
        + (
            [jax.ShapeDtypeStruct((length, D), BF16)]
            if final
            else [
                jax.ShapeDtypeStruct(w_in.shape, BF16),
                jax.ShapeDtypeStruct((ch, D), BF16),
                jax.ShapeDtypeStruct((rows, D), BF16),
            ]
        ),
        scratch_shapes=[
            pltpu.VMEM(held_shape(w_in), BF16),
            pltpu.VMEM((ch, D), BF16),
            pltpu.VMEM((Q + 8, conv_width), F32),
            pltpu.VMEM((N, ch), F32),
            pltpu.VMEM((length, D), BF16),
            pltpu.VMEM((bits, length, D), BF16),
            pltpu.VMEM((nd, pieces, Q), F32),
            pltpu.VMEM((nd, pieces, Q), F32),
            pltpu.VMEM((rows, D), BF16),
            dma((bits, pieces)),
            dma((bits, pieces)),
            dma((nd,)),
            dma((nd,)),
            dma((nd,)),
            dma((nd,)),
            dma((5,)),
            dma((nf,)),
            dma((2, nd)),
        ]
        + ([] if final else [dma((7, 2 * nf)), dma((6, 4))]),
        input_output_aliases={} if final else {15: 10},
        compiler_params=pltpu.CompilerParams(
            vmem_limit_bytes=VMEM_LIMIT, collective_id=identity, has_side_effects=True
        ),
        name="layer_last" if final else "layer_first",
    )(normed_all, meta, segrow, *small, w_in, w_out, hidden, extra, *more)


def mix_backward(
    ch, proj_ref, pre_ref, mixed_ref, state_ref, grad_ref, ratio_ref, pull_ref, meta_ref, segrow_ref,
    conv_w_ref, dtb_ref, alog_ref, skip_ref, gain_ref,
    dproj_ref, dconv_w_ref, dchan_ref, ddecay_ref, tail, dstate, sub, chunk, turn,
):
    conv_width = ch + 2 * N
    rows = pl.ds(pl.multiple_of(sub * Q, Q), Q)
    meta = meta_ref[rows, :]
    pre = pre_ref[rows, :]
    sig = jax.nn.sigmoid(pre)
    conv_out = pre * sig
    values = conv_out[:, :ch]
    b_part = conv_out[:, ch : ch + N]
    c_part = conv_out[:, ch + N :]
    row, column = triangles()
    tri = jnp.where(row >= column, 1.0, 0.0)
    shifted, step, log_decay, cumulative = decay_tables(
        own_steps(proj_ref[rows, ch + conv_width :], turn), dtb_ref[...], alog_ref[...], tri
    )
    linked = (row <= column) & (meta[:, 0:1] == segrow_ref[sub])
    b_low = b_part.astype(BF16)
    c_low = c_part.astype(BF16)
    inner = jnp.where(linked, dot(b_low, c_low, ((1,), (1,))), 0.0)
    cum_t = cumulative.T
    last = cumulative[Q - 1 : Q, :]
    entry = meta[:, 4:5] * jnp.exp(cumulative)
    weight = meta[:, 5:6] * jnp.exp(last - cumulative)
    state_in = state_ref[sub]
    dstate_in = dstate[...]
    state_low = state_in.astype(BF16)
    dstate_low = dstate_in.astype(BF16)
    carried = dot(c_low, state_low)
    carried_back = dot(b_low, dstate_low)
    low_half = lax.broadcasted_iota(jnp.int32, (Q, LANES), 1) < P_SIZE
    lane = lax.broadcasted_iota(jnp.int32, (Q, LANES), 1)
    ratio = to_column(ratio_ref[pl.ds(chunk, 1), :])
    pull = ratio * ratio * to_column(pull_ref[pl.ds(chunk, 1), :]) * (1.0 / DI)
    dinner = jnp.zeros((Q, Q), F32)
    dcum = jnp.zeros((Q, LANES), F32)
    dcum_rows = []
    dexit = jnp.zeros((Q, LANES), F32)
    dstep = jnp.zeros((Q, LANES), F32)
    dcum_entry = jnp.zeros((Q, LANES), F32)
    weighted = []
    entered = []
    entry_rows = []
    dpre_parts = []
    for pair in range(ch // LANES):
        lanes = slice(pair * LANES, (pair + 1) * LANES)
        values_pair = values[:, lanes]
        gate = proj_ref[rows, lanes]
        mixed = mixed_ref[rows, lanes]
        gate_sig = jax.nn.sigmoid(gate)
        gate_silu = gate * gate_sig
        gated = mixed * gate_silu
        scaled = grad_ref[rows, lanes] * ratio
        dchan_ref[0:1, lanes] += jnp.sum(scaled * gated, axis=0, keepdims=True)
        dgated = scaled * gain_ref[:, lanes] - gated * pull
        dproj_ref[rows, lanes] = (dgated * mixed * (gate_sig + gate_silu * (1.0 - gate_sig))).astype(BF16)
        dmixed = dgated * gate_silu
        dchan_ref[1:2, lanes] += jnp.sum(dmixed * values_pair, axis=0, keepdims=True)
        zero = jnp.zeros_like(values_pair)
        dmixed_halves = [jnp.where(low_half, dmixed, zero).astype(BF16), jnp.where(low_half, zero, dmixed).astype(BF16)]
        values_low = values_pair.astype(BF16)
        step_pair = pair_lanes(step, 2 * pair, low_half)
        mats = []
        for half, head in enumerate((2 * pair, 2 * pair + 1)):
            spread = jnp.minimum(cum_t[head : head + 1, :] - cumulative[:, head : head + 1], 0.0)
            plain = jnp.exp(spread)
            decay = plain * step[:, head : head + 1]
            product = dot(values_low, dmixed_halves[half], ((1,), (1,)))
            mats.append((inner * plain).astype(BF16))
            spreaded = product * decay
            dinner = dinner + spreaded
            turned = spreaded * inner
            dcum = dcum - jnp.where(lane == head, jnp.sum(turned, axis=1, keepdims=True), 0.0)
            dcum_rows.append(jnp.sum(turned, axis=0, keepdims=True))
        back = dot(jnp.concatenate(mats, axis=1), jnp.concatenate(dmixed_halves, axis=0))
        weight_pair = pair_lanes(weight, 2 * pair, low_half)
        through = weight_pair * carried_back[:, lanes]
        total = back + through
        dvalues = step_pair * total + skip_ref[:, lanes] * dmixed
        step_terms = total * values_pair
        exit_terms = through * values_pair * step_pair
        entry_pair = pair_lanes(entry, 2 * pair, low_half)
        entry_grad = entry_pair * dmixed
        entry_terms = entry_grad * carried[:, lanes]
        for half, head in enumerate((2 * pair, 2 * pair + 1)):
            own = lane == head
            mask = low_half if half == 0 else ~low_half
            dstep = dstep + jnp.where(own, jnp.sum(jnp.where(mask, step_terms, 0.0), axis=1, keepdims=True), 0.0)
            dexit = dexit + jnp.where(own, jnp.sum(jnp.where(mask, exit_terms, 0.0), axis=1, keepdims=True), 0.0)
            dcum_entry = dcum_entry + jnp.where(own, jnp.sum(jnp.where(mask, entry_terms, 0.0), axis=1, keepdims=True), 0.0)
        weighted.append((weight_pair * step_pair * values_pair).astype(BF16))
        entered.append(entry_grad.astype(BF16))
        entry_rows.append(entry_pair[Q - 1 : Q, :])
        dpre_parts.append(dvalues)
    weighted = jnp.concatenate(weighted, axis=1)
    entered = jnp.concatenate(entered, axis=1)
    entry_rows = jnp.concatenate(entry_rows, axis=1)
    dinner_low = jnp.where(linked, dinner, 0.0).astype(BF16)
    db = dot(dinner_low, c_low) + dot(weighted, dstate_low, ((1,), (1,)))
    dc = dot(dinner_low.T, b_low) + dot(entered, state_low, ((1,), (1,)))
    state_terms = jnp.sum(state_in * dstate_in, axis=0, keepdims=True) * entry_rows
    head_lane = lax.broadcasted_iota(jnp.int32, (1, LANES), 1)
    state_sum = jnp.zeros((1, LANES), F32)
    for head in range(ch // P_SIZE):
        part = jnp.sum(state_terms[:, head * P_SIZE : (head + 1) * P_SIZE], axis=1, keepdims=True)
        state_sum = state_sum + jnp.where(head_lane == head, part, 0.0)
    by_row = jnp.concatenate(dcum_rows + [jnp.zeros((LANES - len(dcum_rows), Q), F32)], axis=0)
    dcum = dcum + by_row.T + dcum_entry
    later = jnp.where(row <= column, 1.0, 0.0)
    before = jnp.where(row > column, 1.0, 0.0)
    dlog = fine_dot(later, dcum) + fine_dot(before, dexit) + state_sum
    growth = jnp.exp(alog_ref[...])
    dstep = dstep - dlog * growth
    ddt = dstep * jax.nn.sigmoid(shifted)
    ddecay_ref[0:1, :] += jnp.sum(ddt, axis=0, keepdims=True)
    ddecay_ref[1:2, :] += jnp.sum(dlog * log_decay, axis=0, keepdims=True)
    heads = ch // P_SIZE
    dproj_ref[rows, ch + conv_width :] = pltpu.roll(jnp.where(lane < heads, ddt, 0.0), turn, 1)[:, :H].astype(BF16)
    dstate[...] = entry_rows * dstate_in + dot(c_part.T.astype(BF16), entered)
    dconv_out = jnp.concatenate(dpre_parts + [db, dc], axis=1)
    dpre = dconv_out * (sig + conv_out * (1.0 - sig))
    raw = proj_ref[rows, ch : ch + conv_width]
    dchan_ref[2:3, :] += jnp.sum(dpre, axis=0, keepdims=True)
    draw = conv_w_ref[3:4, :] * dpre
    dconv_w_ref[3:4, :] += jnp.sum(raw * dpre, axis=0, keepdims=True)
    for lag in range(1, K):
        kept = meta[:, lag : lag + 1] * dpre
        tail[lag - 1, 0:Q, :] = kept
        moved = tail[lag - 1, lag : lag + Q, :]
        tail[lag - 1, Q : Q + 8, :] = kept[0:8, :]
        draw = draw + conv_w_ref[3 - lag : 4 - lag, :] * moved
        dconv_w_ref[3 - lag : 4 - lag, :] += jnp.sum(raw * moved, axis=0, keepdims=True)
    dproj_ref[rows, ch : ch + conv_width] = draw.astype(BF16)


def layer_back_kernel(
    ch, rows, nf, nd, last,
    grad_all_ref, proj_ref, pre_ref, mixed_ref, state_ref, meta_ref, segrow_ref, ratio_ref, pull_ref,
    conv_w_ref, dtb_ref, alog_ref, skip_ref, gain_ref, w_in_ref, w_out_ref,
    hidden_ref, grad_own_ref, norm_gain_ref, branch_ref, *refs,
):
    count = 2 if last else 1
    sources, refs = refs[:count], refs[count:]
    (
        dproj_ref, dconv_w_ref, dchan_ref, ddecay_ref, dgain_ref, next_ref, next_pull_ref, moved_ref,
    ) = refs[:8]
    results, refs = refs[8 : 8 + count], refs[8 + count :]
    (
        held, w_out, tail, dstate, dnout, partial, landed, pulls, low,
        sum_send, sum_recv, tile_send, tile_recv, group_send, group_recv, local_sem, load_sem,
    ) = refs[:17]
    refs = refs[17:]
    step = pl.program_id(0)
    y, z, d = lax.axis_index("section"), lax.axis_index("fsdp"), lax.axis_index("dp")
    block = grad_all_ref.shape[0]
    subs = block // Q
    steps = pl.num_programs(0)
    pieces = partial.shape[0] // Q
    per_rank = rows // Q
    bits = bits_of(nd)
    away = z != d
    twin = {"fsdp": d, "dp": z}
    group = GroupSum(partial, landed, per_rank, d, nd, sum_send, sum_recv)
    place = steps - 1 - step
    step_count = pieces // subs
    sums = [
        SectionSum(make(source, nf), nf, y, z, *refs[5 * k : 5 * k + 5])
        for k, (make, source) in enumerate(zip((out_view, in_view), sources))
    ]
    weights = Weights(w_in_ref, held, load_sem)
    out_load = pltpu.make_async_copy(w_out_ref, w_out, local_sem.at[3])

    @pl.when(step == 0)
    def _():
        for copy in weights.copies():
            copy.start()
        out_load.start()
        greet(
            [(None, {"dp": flip(d, j)}) for j in range(1, nd)]
            + line_neighbours(nf, y, z)
            + ([(away, twin)] if last else [])
        )
        for one in sums:
            one.begin()
        tail[...] = jnp.zeros_like(tail)
        dstate[...] = jnp.zeros_like(dstate)
        dconv_w_ref[...] = jnp.zeros_like(dconv_w_ref)
        dchan_ref[...] = jnp.zeros_like(dchan_ref)
        ddecay_ref[...] = jnp.zeros_like(ddecay_ref)
        for copy in weights.copies():
            copy.wait()
        out_load.wait()

    dnout[...] = dot(grad_all_ref[...], w_out[...], ((1,), (1,)))

    def one_chunk(turn, carry):
        sub = subs - 1 - turn
        mix_backward(
            ch, proj_ref, pre_ref, mixed_ref, state_ref, dnout, ratio_ref, pull_ref, meta_ref, segrow_ref,
            conv_w_ref, dtb_ref, alog_ref, skip_ref, gain_ref,
            dproj_ref, dconv_w_ref, dchan_ref, ddecay_ref, tail, dstate, sub, place * subs + sub, d * (H // nd),
        )
        return carry

    lax.fori_loop(0, subs, one_chunk, 0)
    partial[pl.ds(pl.multiple_of(place * block, block), block), :] = weights.backward(
        dproj_ref[...]
    ).astype(BF16)

    for k in range(len(bits)):

        @pl.when(step >= k)
        def _():
            for sub in range(subs):
                group.send(k, (place + k) * subs + sub)

    for k in range(nf - 1, 0, -1):

        @pl.when(step == min(nf - 1 - k, step_count - 1))
        def _():
            for one in sums:
                one.stage(k)

    @pl.when(step == steps - 1)
    def _():
        for k in range(1, len(bits)):
            for late in range(k):
                for sub in range(subs):
                    group.send(k, late * subs + sub)
        pulls[0] = jnp.zeros(pulls.shape[1:], F32)
        dgain = jnp.zeros((1, D), F32)
        for part in range(per_rank):
            piece = d * per_rank + part
            here = slice(part * Q, (part + 1) * Q)
            dnormed = group.own(piece)
            hidden = hidden_ref[here, :].astype(F32)
            inverse = rms_parts(hidden)
            dgain = dgain + jnp.sum(dnormed * hidden * inverse, axis=0, keepdims=True)
            scaled = dnormed * norm_gain_ref[...]
            dhidden = inverse * (
                scaled - hidden * (inverse * inverse) * jnp.mean(scaled * hidden, axis=1, keepdims=True)
            )
            moved = (grad_own_ref[here, :].astype(F32) + dhidden).astype(BF16)
            low[here, :] = moved
            next_ref[here, :] = moved
            if not last:
                pulls[0, pl.ds(piece, 1), :] = to_row(
                    jnp.sum(moved.astype(F32) * branch_ref[here, :], axis=1, keepdims=True)
                )
        dgain_ref[...] = dgain
        if last:
            swap = remote(low, moved_ref, local_sem.at[0], local_sem.at[1], twin)
            stay = pltpu.make_async_copy(low, moved_ref, local_sem.at[2])

            @pl.when(away)
            def _():
                swap.start()
                swap.wait()

            @pl.when(jnp.logical_not(away))
            def _():
                stay.start()
                stay.wait()

            next_pull_ref[...] = jnp.zeros_like(next_pull_ref)
        else:
            every = GroupRows(rows_of(moved_ref, rows), d, nd, group_send, group_recv)
            mine = pltpu.make_async_copy(low, every.part(0), local_sem.at[0])
            mine.start()
            every.begin(low)
            next_pull_ref[...] = group_tiles(pulls, tile_send, tile_recv, d, nd)
            every.finish()
            mine.wait()
        group.settle(pieces)
        for one, result in zip(sums, results):
            one.finish()
            copy = pltpu.make_async_copy(one.result, result, local_sem.at[1])
            copy.start()
            copy.wait()
            one.settle()


def run_layer_back(
    ch, rows, nf, nd, last, grad_all, proj, pre, mixed, states, meta, segrow, ratio, pull, small, w_in, w_out,
    hidden, grad_own, norm_gain, branch, identity, *sums,
):
    length, width = proj.shape
    shapes = [make(nf, g) for make, g in zip((out_part_shape, in_part_shape), sums)]
    conv_width = ch + 2 * N
    block = 2 * Q
    steps = length // block
    pieces = length // Q
    subs = block // Q
    bits = len(bits_of(nd))
    dma = pltpu.SemaphoreType.DMA
    ordered = lambda s: (steps - 1 - s, 0)
    ordered3 = lambda s: (steps - 1 - s, 0, 0)
    layer = 0 if last else 1
    conv_w, conv_b, dtb, alog, skip, gain = small
    return pl.pallas_call(
        functools.partial(layer_back_kernel, ch, rows, nf, nd, last),
        grid=(steps,),
        in_specs=[
            pl.BlockSpec((block, D), ordered),
            pl.BlockSpec((block, width), ordered),
            pl.BlockSpec((block, conv_width), ordered),
            pl.BlockSpec((block, ch), ordered),
            pl.BlockSpec((subs, N, ch), ordered3),
            pl.BlockSpec((block, LANES), ordered),
            pl.BlockSpec((subs, 1, Q), ordered3),
            once((pieces, Q)),
            once((pieces, Q)),
        ]
        + [pick(part, layer) for part in (conv_w, dtb, alog, skip, gain)]
        + [
            pl.BlockSpec(memory_space=pl.ANY),
            pl.BlockSpec(memory_space=pl.ANY),
            once((rows, D)),
            once((rows, D)),
            pick(norm_gain, layer),
            once((rows, D)),
        ]
        + [pl.BlockSpec(memory_space=pl.ANY)] * len(sums),
        out_specs=[
            pl.BlockSpec((block, width), ordered),
            once((K, conv_width)),
            once((8, conv_width)),
            once((8, LANES)),
            once((1, D)),
            once((rows, D)),
            once((pieces, Q)),
            pl.BlockSpec(memory_space=pl.ANY),
        ]
        + [pl.BlockSpec(memory_space=pl.ANY)] * len(sums),
        out_shape=[
            jax.ShapeDtypeStruct((length, width), BF16),
            jax.ShapeDtypeStruct((K, conv_width), F32),
            jax.ShapeDtypeStruct((8, conv_width), F32),
            jax.ShapeDtypeStruct((8, LANES), F32),
            jax.ShapeDtypeStruct((1, D), F32),
            jax.ShapeDtypeStruct((rows, D), BF16),
            jax.ShapeDtypeStruct((pieces, Q), F32),
            jax.ShapeDtypeStruct((rows if last else length, D), BF16),
        ]
        + [jax.ShapeDtypeStruct(shape, BF16) for shape in shapes],
        scratch_shapes=[
            pltpu.VMEM(held_shape(w_in), BF16),
            pltpu.VMEM((ch, D), BF16),
            pltpu.VMEM((K - 1, Q + 8, conv_width), F32),
            pltpu.VMEM((N, ch), F32),
            pltpu.VMEM((block, ch), F32),
            pltpu.VMEM((length, D), BF16),
            pltpu.VMEM((bits, length, D), BF16),
            pltpu.VMEM((nd, pieces, Q), F32),
            pltpu.VMEM((rows, D), BF16),
            dma((bits, pieces)),
            dma((bits, pieces)),
            dma((nd,)),
            dma((nd,)),
            dma((nd,)),
            dma((nd,)),
            dma((4,)),
            dma((nf,)),
        ]
        + [part for shape in shapes for part in section_sum_scratch(nf, shape)],
        compiler_params=pltpu.CompilerParams(
            vmem_limit_bytes=VMEM_LIMIT, collective_id=identity, has_side_effects=True
        ),
        name="layer_back_last" if last else "layer_back_first",
    )(
        grad_all, proj, pre, mixed, states, meta, segrow, ratio, pull, conv_w, dtb, alog, skip, gain, w_in, w_out,
        hidden, grad_own, norm_gain, branch, *sums,
    )


def shards(
    inputs, segment, cotangent, norm_gain, in_weight, conv_weight, conv_bias, dt_bias, a_log, d_skip,
    gate_gain, out_weight,
):
    fsdp, dp = lax.axis_size("fsdp"), lax.axis_size("dp")
    section, here = lax.axis_index("section"), lax.axis_index("dp")
    rows = inputs.shape[2]
    ch = DI // dp
    heads = H // dp
    conv_width = ch + 2 * N
    seg_mine = lax.dynamic_index_in_dim(segment, section, 0, keepdims=False)[0].astype(F32)
    seg_mine = jnp.broadcast_to(seg_mine.reshape(rows // Q, 1, Q), (rows // Q, 8, Q)).reshape(-1, Q)
    head_table = jnp.pad(
        jnp.concatenate([dt_bias[0], a_log[0], d_skip[0]], axis=0), ((0, 0), (0, LANES - H))
    )
    hidden, normed_all, w_in0, w_in1, w_out0, seg_all, *table = run_start(
        fsdp, dp, rows, inputs[:, 0], seg_mine, in_weight[0, 0].T, out_weight[0, 0], conv_weight[0, 0], conv_bias[0],
        norm_gain[0], gate_gain[0], head_table,
    )
    *small, gains, meta = table
    length = meta.shape[0]
    segrow = seg_all.reshape(-1, 8, Q)[:, :1]
    saved = []
    for layer in range(2):
        last = layer == 1
        proj, gated, mixed, pre, states, branch, after, ratio, pull, moved, *more = run_layer(
            ch, rows, fsdp, dp, last, normed_all, meta, segrow, small, full_in if last else w_in0,
            full_out if last else w_out0, hidden, cot_own if last else gains, 2 + layer,
            *(() if last else (cotangent[:, 0], out_weight[0, 0], w_in1)),
        )
        saved.append((normed_all, hidden, proj, gated, mixed, pre, states, branch, ratio))
        normed_all, hidden = moved, after
        if last:
            (cot_all,) = more
        else:
            full_in, full_out, cot_own = more
    final = moved

    grad_all, grad_own = cot_all, cot_own
    in_grad, small_grads, parts = (), [None, None], []
    for layer in (1, 0):
        last = layer == 0
        normed_all, hidden, proj, gated, mixed, pre, states, branch, ratio = saved[layer]
        out_grad = dot((gated.astype(F32) * ratio.reshape(length, 1)).astype(BF16), grad_all, ((0,), (0,)))
        dproj, dconv_w, dchan, ddecay, dgain, after, next_pull, moved, *done = run_layer_back(
            ch, rows, fsdp, dp, last, grad_all, proj, pre, mixed, states, meta, segrow, ratio, pull, small,
            w_in0 if last else full_in, w_out0 if last else full_out, hidden, grad_own, gains, saved[0][7], 4 + layer,
            out_grad.astype(BF16), *in_grad,
        )
        parts += done
        grad = dot(dproj, normed_all, ((0,), (0,))).astype(BF16)
        if D // fsdp % LANES:
            grad = jnp.swapaxes(grad.reshape(-1, fsdp, D // fsdp), 0, 1)
        in_grad = (grad,)
        small_grads[layer] = (dgain[0], dconv_w, dchan, ddecay)
        grad_all, grad_own, pull = moved, after, next_pull
    input_grad = moved

    def pack_small(grads):
        dgain, dconv_w, dchan, ddecay = grads
        skip = jnp.sum(dchan[1, :ch].reshape(heads, P_SIZE), axis=1)
        pieces = [dgain, dconv_w.reshape(-1), dchan[2], dchan[0, :ch], ddecay[0, :heads], ddecay[1, :heads], skip]
        flat = jnp.concatenate(pieces)
        return jnp.pad(flat, (0, -flat.shape[0] % 1024)).reshape(-1, LANES)

    packed = jnp.stack([pack_small(grads) for grads in small_grads])
    in_all, out_all, small_sum = run_end(fsdp, dp, in_grad[0], parts[2], parts[1], parts[0], packed)
    in_total = jnp.concatenate(
        [
            in_all[:, :ch].reshape(DI, -1).astype(F32),
            in_all[:, ch : 2 * ch].reshape(DI, -1).astype(F32),
            jnp.sum(in_all[:, 2 * ch :].astype(F32), axis=0),
        ],
        axis=0,
    ).T
    out_total = out_all.astype(F32)
    everything = small_sum.reshape(dp, -1)
    offset = 0
    pieces = []
    for size in (D, K * conv_width, conv_width, ch, heads, heads, heads):
        pieces.append(everything[:, offset : offset + size])
        offset += size
    gain_total = jnp.sum(pieces[0], axis=0)
    convw = pieces[1].reshape(dp, K, conv_width)
    convw_total = jnp.concatenate(
        [jnp.moveaxis(convw[:, :, :ch], 0, 1).reshape(K, DI), jnp.sum(convw[:, :, ch:], axis=0)], axis=1
    )
    convb = pieces[2]
    convb_total = jnp.concatenate([convb[:, :ch].reshape(DI), jnp.sum(convb[:, ch:], axis=0)])
    gate_total = pieces[3].reshape(DI)
    dtb_total, alog_total, skip_total = (piece.reshape(H) for piece in pieces[4:])
    return (
        final[None, None],
        input_grad[None, None],
        gain_total[None, None],
        in_total[None, None],
        convw_total[None, None],
        convb_total[None, None],
        dtb_total[None, None],
        alog_total[None, None],
        skip_total[None, None],
        gate_total[None, None],
        out_total[None, None],
    )


def solution(mesh):
    return jax.shard_map(
        shards,
        mesh=mesh,
        in_specs=(
            P(None, "dp", "fsdp", None),
            P(None, "dp", "fsdp"),
            P(None, "dp", "fsdp", None),
            P("section", None, None),
            P("section", None, "fsdp", None),
            P("section", None, None, None),
            P("section", None, None),
            P("section", None, None),
            P("section", None, None),
            P("section", None, None),
            P("section", None, None),
            P("section", None, "fsdp", None),
        ),
        out_specs=(
            P("section", "dp", "fsdp", None),
            P("section", "dp", "fsdp", None),
            P("section", None, None),
            P("section", None, "fsdp", None),
            P("section", None, None, None),
            P("section", None, None),
            P("section", None, None),
            P("section", None, None),
            P("section", None, None),
            P("section", None, None),
            P("section", None, "fsdp", None),
        ),
        check_vma=False,
    )
```

```python
import functools

import jax
import jax.numpy as jnp
from jax import lax
from jax.experimental import pallas as pl
from jax.experimental.pallas import tpu as pltpu
from jax.sharding import PartitionSpec as P

D = 1536
H = 48
P_SIZE = 64
N = 128
K = 4
DI = 3072
DC = 3328
DIN = 6448
EPSILON = 1e-05
HIGHEST = lax.Precision.HIGHEST
BF16 = jnp.bfloat16
F32 = jnp.float32
Q = 128
LANES = 128


def dot(a, b, dims=((1,), (0,)), precision=None):
    return lax.dot_general(a, b, (dims, ((), ())), preferred_element_type=F32, precision=precision)


def low_dot(a, b, dims=((1,), (0,))):
    return dot(a.astype(BF16), b.astype(BF16), dims)


def fine_dot(a, b, dims=((1,), (0,))):
    return dot(a, b, dims, HIGHEST)


def halves(value):
    high = value.astype(BF16)
    return high, (value - high.astype(F32)).astype(BF16)


def split_dot(a, b, dims=((1,), (0,))):
    (a_high, a_low), (b_high, b_low) = halves(a), halves(b)
    return dot(a_high, b_high, dims) + (dot(a_high, b_low, dims) + dot(a_low, b_high, dims))


def pair_lanes(table, first, low_half):
    return jnp.where(low_half, table[:, first : first + 1], table[:, first + 1 : first + 2])


def decay_tables(proj_dt, dt_bias, a_row, tri):
    shifted = proj_dt + dt_bias
    step = jnp.maximum(shifted, 0.0) + jnp.log1p(jnp.exp(-jnp.abs(shifted)))
    log_decay = -step * jnp.exp(a_row)
    cumulative = fine_dot(tri, log_decay)
    return shifted, step, log_decay, cumulative


def triangles():
    row = lax.broadcasted_iota(jnp.int32, (Q, Q), 0)
    column = lax.broadcasted_iota(jnp.int32, (Q, Q), 1)
    return row, column


MESH_ID = pl.DeviceIdType.MESH
VMEM_LIMIT = 60 * 1024 * 1024


def remote(src, dst, send_sem, recv_sem, device):
    return pltpu.make_async_remote_copy(
        src_ref=src, dst_ref=dst, send_sem=send_sem, recv_sem=recv_sem, device_id=device, device_id_type=MESH_ID
    )


def greet(devices):
    barrier = pltpu.get_barrier_semaphore()
    count = 0
    for condition, device in devices:
        if condition is None:
            pl.semaphore_signal(barrier, inc=1, device_id=device, device_id_type=MESH_ID)
            count = count + 1
        else:

            @pl.when(condition)
            def _():
                pl.semaphore_signal(barrier, inc=1, device_id=device, device_id_type=MESH_ID)

            count = count + condition.astype(jnp.int32)
    pl.semaphore_wait(barrier, count)


def bits_of(peers):
    return [1 << k for k in range(peers.bit_length() - 1)]


def has_bit(value, bit):
    return (value // bit) % 2


def flip(value, bits):
    bit = 1
    out = value
    while bit <= bits:
        if bits & bit:
            out = out + bit * (1 - 2 * has_bit(value, bit))
        bit = bit * 2
    return out


def to_column(row):
    down, across = triangles()
    return jnp.sum(jnp.where(down == across, jnp.broadcast_to(row, (Q, Q)), 0.0), axis=1, keepdims=True)


def to_row(column, offset=0):
    shape = (column.shape[0], Q)
    down = lax.broadcasted_iota(jnp.int32, shape, 0)
    across = lax.broadcasted_iota(jnp.int32, shape, 1)
    return jnp.sum(jnp.where(across == down + offset, jnp.broadcast_to(column, shape), 0.0), axis=0, keepdims=True)


class GroupTiles:

    def __init__(self, tiles, send_sem, recv_sem, here, peers):
        self.tiles, self.send_sem, self.recv_sem, self.here, self.peers = tiles, send_sem, recv_sem, here, peers

    def copies(self):
        return [
            remote(
                self.tiles.at[0], self.tiles.at[j], self.send_sem.at[j], self.recv_sem.at[j],
                {"dp": flip(self.here, j)},
            )
            for j in range(1, self.peers)
        ]

    def begin(self):
        for copy in self.copies():
            copy.start()

    def finish(self):
        for copy in self.copies():
            copy.wait()
        total = self.tiles[0]
        for j in range(1, self.peers):
            total = total + self.tiles[j]
        return total


def group_tiles(tiles, send_sem, recv_sem, here, peers):
    group = GroupTiles(tiles, send_sem, recv_sem, here, peers)
    group.begin()
    return group.finish()


class GroupRows:

    def __init__(self, where, here, peers, send_sem, recv_sem):
        self.where, self.here, self.peers = where, here, peers
        self.send_sem, self.recv_sem = send_sem, recv_sem

    def part(self, j):
        return self.where(flip(self.here, j))

    def copy(self, j, bit, source=None):
        part = self.part(j)
        return remote(
            part if source is None else source, part, self.send_sem.at[j ^ bit], self.recv_sem.at[j ^ bit],
            {"dp": flip(self.here, bit)},
        )

    def begin(self, source=None):
        for bit in bits_of(self.peers)[::-1]:
            self.copy(0, bit, source).start()

    def phase(self, bit):
        for j in range(bit, self.peers, 2 * bit):
            self.copy(j ^ bit, bit).wait_send()
            landing = self.part(j)
            remote(
                landing, landing, self.send_sem.at[j], self.recv_sem.at[j], {"dp": flip(self.here, bit)}
            ).wait_recv()
            for lower in bits_of(bit)[::-1]:
                self.copy(j, lower).start()

    def relay(self):
        for bit in bits_of(self.peers)[:0:-1]:
            self.phase(bit)

    def close(self):
        self.phase(1)

    def finish(self):
        self.relay()
        self.close()


def rows_of(whole, rows):
    return lambda device: whole.at[pl.ds(pl.multiple_of(device * rows, 8), rows)]


def rms_parts(values):
    return lax.rsqrt(jnp.mean(values * values, axis=-1, keepdims=True) + EPSILON)


class BlockSum:

    def __init__(self, partial, landed, here, peers, send_sem, recv_sem):
        self.partial, self.landed, self.here, self.peers = partial, landed, here, peers
        self.bits = bits_of(peers)
        self.send_sem, self.recv_sem = send_sem, recv_sem

    def copy(self, k, block, owner):
        return remote(
            self.partial.at[block, owner], self.landed.at[k, block, owner // 2], self.send_sem.at[k, block, owner],
            self.recv_sem.at[k, block, owner], {"dp": flip(self.here, self.bits[k])},
        )

    def total(self, block, owner, stages):
        total = self.partial[block, owner].astype(F32)
        for m in range(stages):
            self.copy(m, block, owner).wait_recv()
            total = total + self.landed[m, block, owner // 2].astype(F32)
        return total

    def leaving(self, k):
        return [flip(self.here, j) for j in range(self.bits[k], self.peers, 2 * self.bits[k])]

    def send(self, k, block):
        for owner in self.leaving(k):
            if k > 0:
                self.partial[block, owner] = self.total(block, owner, k).astype(self.partial.dtype)
            self.copy(k, block, owner).start()

    def own(self, block):
        return self.total(block, self.here, len(self.bits))

    def settle(self, blocks):
        for block in range(blocks):
            for k in range(len(self.bits)):
                for owner in self.leaving(k):
                    self.copy(k, block, owner).wait_send()


class Deal:

    def __init__(self, chunk, own, nf, nd, z, d, send_sem, recv_sem, outward):
        self.chunk, self.own, self.nf, self.nd, self.z, self.d = chunk, own, nf, nd, z, d
        self.send_sem, self.recv_sem, self.outward = send_sem, recv_sem, outward
        self.rows = chunk.shape[0] // nd

    def part(self, o):
        return self.chunk.at[pl.ds(pl.multiple_of(o * self.rows, 16), self.rows)]

    def holder(self, b):
        return {"fsdp": b, "dp": self.z}

    def worker(self, o):
        return {"fsdp": self.d, "dp": o}

    def at_home(self, k):
        return (self.z == self.d) & (self.z == k)

    def send(self, k):
        if self.outward:
            return remote(
                self.own.at[k], self.part(self.d), self.send_sem.at[k], self.recv_sem.at[self.d], self.holder(k)
            )
        return remote(
            self.part(k), self.own.at[self.z], self.send_sem.at[k], self.recv_sem.at[self.z], self.worker(k)
        )

    def recv(self, k):
        if self.outward:
            part = self.part(k)
            return remote(part, part, self.send_sem.at[k], self.recv_sem.at[k], self.worker(k))
        part = self.own.at[k]
        return remote(part, part, self.send_sem.at[k], self.recv_sem.at[k], self.holder(k))

    def keep(self, k):
        if self.outward:
            return pltpu.make_async_copy(self.own.at[k], self.part(k), self.send_sem.at[k])
        return pltpu.make_async_copy(self.part(k), self.own.at[k], self.send_sem.at[k])

    def start(self, k):
        @pl.when(self.at_home(k))
        def _():
            self.keep(k).start()

        @pl.when(jnp.logical_not(self.at_home(k)))
        def _():
            self.send(k).start()

    def start_all(self):
        for k in range(self.nf):
            self.start(k)

    def arrive(self):
        for k in range(self.nf):

            @pl.when(self.at_home(k))
            def _():
                self.keep(k).wait()

            @pl.when(jnp.logical_not(self.at_home(k)))
            def _():
                self.recv(k).wait_recv()

    def settle(self):
        for k in range(self.nf):

            @pl.when(jnp.logical_not(self.at_home(k)))
            def _():
                self.send(k).wait_send()


def deal_partners(nf, nd, z, d):
    out = []
    for k in range(nf):
        elsewhere = (z != d) | (z != k)
        out += [(elsewhere, {"fsdp": k, "dp": z}), (elsewhere, {"fsdp": d, "dp": k})]
    return out


class SectionGather:

    def __init__(self, held, section, nf, y, z, sems, own=None):
        self.own = own
        self.held, self.section, self.nf, self.y, self.z, self.sems = held, section, nf, y, z, sems
        width = held.shape[1]
        first = -(-width // 32) * 16
        self.spans = [(0, first), (first, width - first)]
        self.peer = {"section": 1 - y}

    def block(self, b, part):
        start, size = self.spans[part]
        return self.held.at[b, pl.ds(start, size)]

    def each(self, body):
        for part in range(2):
            owner = self.y == self.section

            @pl.when(owner if part == 0 else jnp.logical_not(owner))
            def _():
                body(part)

    def own_part(self, part):
        start, size = self.spans[part]
        return self.own.at[pl.ds(start, size)]

    def send(self, b, part, row, k, landed, device, source=None):
        here = self.block(b, part)
        return remote(
            here if source is None else source, here, self.sems.at[row, k], self.sems.at[landed, k], device
        )

    def right(self, k, b, part, source=None):
        return self.send(b, part, 0, k, 2, {"fsdp": self.z + 1}, source)

    def left(self, k, b, part, source=None):
        return self.send(b, part, 1, k, 3, {"fsdp": self.z - 1}, source)

    def over(self, k, b, part, source=None):
        return self.send(b, part, 4, k, 5, self.peer, source)

    def cross(self):
        here = self.block(self.z, 1)
        return remote(self.own_part(1), here, self.sems.at[6, 0], self.sems.at[6, 1], self.peer)

    def keep(self):
        return pltpu.make_async_copy(self.own, self.held.at[self.z], self.sems.at[6, 2])

    def has_right(self):
        return self.z < self.nf - 1

    def has_left(self):
        return self.z > 0

    def start_cross(self):
        @pl.when(self.y == self.section)
        def _():
            self.cross().start()
            self.keep().start()

    def begin(self):
        def body(part):
            source = None
            if part == 1:
                self.cross().wait_recv()
            else:
                source = self.own_part(0)

            @pl.when(self.has_right())
            def _():
                self.right(1, self.z, part, source).start()

            @pl.when(self.has_left())
            def _():
                self.left(1, self.z, part, source).start()

            if part == 0:
                self.cross().wait_send()
                self.over(0, self.z, 0, source).start()

        self.each(body)

    def settle_begin(self):
        def body(part):
            @pl.when(self.has_right())
            def _():
                self.right(1, self.z, part).wait_send()

            @pl.when(self.has_left())
            def _():
                self.left(1, self.z, part).wait_send()

            if part == 0:
                self.over(0, self.z, 0).wait_send()
                self.keep().wait()
            else:
                self.over(0, self.z, 0).wait_recv()

        self.each(body)

    def sides(self, k, body):
        @pl.when(self.z >= k)
        def _():
            body(self.z - k, k, True)

        @pl.when(self.z + k < self.nf)
        def _():
            body(self.z + k, self.nf + k, False)

    def arrive(self, k):
        def body(part):
            def one(b, index, from_left):
                if from_left:
                    self.right(k, b, part).wait_recv()
                else:
                    self.left(k, b, part).wait_recv()

            self.sides(k, one)

        self.each(body)

    def relay(self, k):
        def body(part):
            def one(b, index, from_left):
                if k < self.nf - 1:
                    if from_left:

                        @pl.when(self.has_right())
                        def _():
                            self.right(k + 1, b, part).start()

                    else:

                        @pl.when(self.has_left())
                        def _():
                            self.left(k + 1, b, part).start()

                self.over(index, b, part).start()

            self.sides(k, one)

        self.each(body)

    def settle(self, k):
        def body(part):
            def one(b, index, from_left):
                self.over(index, b, part).wait_send()
                self.over(index, b, 1 - part).wait_recv()
                if k < self.nf - 1:
                    if from_left:

                        @pl.when(self.has_right())
                        def _():
                            self.right(k + 1, b, part).wait_send()

                    else:

                        @pl.when(self.has_left())
                        def _():
                            self.left(k + 1, b, part).wait_send()

            self.sides(k, one)

        self.each(body)


class OutGather:

    def __init__(self, source, held, section, nf, y, z, d, sems, staged):
        self.staged = staged
        self.source, self.held, self.section, self.nf = source, held, section, nf
        self.y, self.z, self.d, self.sems = y, z, d, sems
        self.pieces = sems.shape[1]
        self.rows = source.shape[0] // self.pieces
        self.columns = source.shape[1] // 2
        self.peer = {"section": 1 - y}
        self.source_here = z == d

    def owner(self):
        return self.y == self.section

    def piece(self, ref, part, i):
        return ref.at[pl.ds(i * self.rows, self.rows), pl.ds(part * self.columns, self.columns)]

    def send(self, i, part, row, landed, device, source=None):
        target = self.piece(self.held, part, i)
        return remote(
            target if source is None else self.piece(source, part, i), target, self.sems.at[row, i],
            self.sems.at[landed, i], device,
        )

    def right(self, i, part, source=None):
        return self.send(i, part, 0, 2, {"fsdp": self.z + 1}, source)

    def left(self, i, part, source=None):
        return self.send(i, part, 1, 2, {"fsdp": self.z - 1}, source)

    def over(self, i, part, source=None):
        return self.send(i, part, 3, 4, self.peer, source)

    def cross(self):
        columns = pl.ds(self.columns, self.columns)
        return remote(
            self.source.at[:, columns], self.held.at[:, columns], self.sems.at[5, 0], self.sems.at[5, 1], self.peer
        )

    def stage(self):
        return pltpu.make_async_copy(self.source, self.staged, self.sems.at[5, 2])

    def keep(self):
        return pltpu.make_async_copy(self.staged, self.held, self.sems.at[5, 3])

    def goes_right(self):
        return (self.z >= self.d) & (self.z < self.nf - 1)

    def goes_left(self):
        return (self.z <= self.d) & (self.z > 0)

    def each(self, condition, body):
        for part in range(2):
            mine = self.owner() if part == 0 else jnp.logical_not(self.owner())

            @pl.when(condition & mine)
            def _():
                body(part)

    def along(self, i, part, action, source=None):
        @pl.when(self.goes_right())
        def _():
            action(self.right(i, part, source))

        @pl.when(self.goes_left())
        def _():
            action(self.left(i, part, source))

    def begin(self):
        @pl.when(self.source_here & self.owner())
        def _():
            self.cross().start()
            self.stage().start()
            for i in range(self.pieces):
                self.along(i, 0, lambda copy: copy.start(), self.source)

    def begin_other(self):
        @pl.when(self.source_here & jnp.logical_not(self.owner()))
        def _():
            self.cross().wait_recv()
            for i in range(self.pieces):
                self.along(i, 1, lambda copy: copy.start())

    def hops(self, distance):
        def body(part):
            for i in range(self.pieces):
                self.right(i, part).wait_recv()
                self.along(i, part, lambda copy: copy.start())

        self.each((self.z == self.d + distance) | (self.z == self.d - distance), body)

    def hand_over(self):
        @pl.when(self.source_here & self.owner())
        def _():
            self.stage().wait()
            self.keep().start()
            for i in range(self.pieces):
                self.over(i, 0, self.source).start()

        def body(part):
            for i in range(self.pieces):
                self.over(i, part).start()

        self.each(jnp.logical_not(self.source_here), body)

    def settle(self):
        @pl.when(self.source_here & self.owner())
        def _():
            self.cross().wait_send()
            self.keep().wait()

        def at_source(part):
            for i in range(self.pieces):
                self.along(i, part, lambda copy: copy.wait_send())
                if part == 0:
                    self.over(i, 0).wait_send()
                else:
                    self.over(i, 0).wait_recv()

        def elsewhere(part):
            for i in range(self.pieces):
                self.along(i, part, lambda copy: copy.wait_send())
                self.over(i, part).wait_send()
                self.over(i, 1 - part).wait_recv()

        self.each(self.source_here, at_source)
        self.each(jnp.logical_not(self.source_here), elsewhere)


def line_neighbours(nf, y, z):
    return [
        (None, {"section": 1 - y}),
        (z < nf - 1, {"fsdp": z + 1}),
        (z > 0, {"fsdp": z - 1}),
    ]


class SectionSum:

    def __init__(self, view, nf, y, z, own, landed, chain, sems, result):
        self.view, self.nf, self.y, self.z, self.result = view, nf, y, z, result
        self.own, self.landed, self.chain = own, landed, chain
        self.load_sem, self.over_send, self.over_recv, self.chain_send, self.chain_recv = (
            sems.at[0], sems.at[1], sems.at[2], sems.at[3], sems.at[4]
        )
        self.part_rows = own.shape[1]

    def load(self, block):
        return pltpu.make_async_copy(self.view(block, self.y), self.own.at[block], self.load_sem.at[block])

    def over(self, block):
        return remote(
            self.view(block, 1 - self.y), self.landed.at[block], self.over_send.at[block], self.over_recv.at[block],
            {"section": 1 - self.y},
        )

    def right(self, block):
        return remote(
            self.own.at[block], self.chain.at[block], self.chain_send.at[block], self.chain_recv.at[block],
            {"fsdp": self.z + 1},
        )

    def left(self, block, arrives):
        slot = self.nf if arrives else block
        return remote(
            self.own.at[block], self.chain.at[slot], self.chain_send.at[block], self.chain_recv.at[slot],
            {"fsdp": self.z - 1},
        )

    def at(self, k, body):
        if k == 0:
            body(self.z, False)
            return

        @pl.when(self.z + k < self.nf)
        def _():
            body(self.z + k, True)

        @pl.when(self.z - k >= 0)
        def _():
            body(self.z - k, False)

    def begin(self):
        self.at(self.nf - 1, lambda block, rightward: self.over(block).start())
        for k in range(self.nf - 1, -1, -1):
            self.at(k, lambda block, rightward: self.load(block).start())

    def add(self, block, sources, target):
        step = 32

        def some(i, carry):
            rows = pl.ds(pl.multiple_of(i * step, 16), step)
            total = self.own[block, rows, :].astype(F32)
            for ref, slot in sources:
                total = total + ref[slot, rows, :].astype(F32)
            if target is None:
                self.own[block, rows, :] = total.astype(BF16)
            else:
                target[rows, :] = total.astype(BF16)
            return carry

        lax.fori_loop(0, self.part_rows // step, some, 0)

    def ready(self, block):
        self.load(block).wait()
        self.over(block).wait_recv()

    def stage(self, k):
        z, nf = self.z, self.nf
        self.at(k, lambda block, rightward: self.ready(block))
        self.at(k - 1, lambda block, rightward: self.over(block).start())

        def one(block, rightward):
            far_end = z == 0 if rightward else z == nf - 1
            arrived = self.right(block) if rightward else self.left(block, False)
            leaving = self.right(block) if rightward else self.left(block, k == 1)

            @pl.when(jnp.logical_not(far_end))
            def _():
                arrived.wait_recv()
                self.add(block, [(self.landed, block), (self.chain, block)], None)

            @pl.when(far_end)
            def _():
                self.add(block, [(self.landed, block)], None)

            leaving.start()

        self.at(k, one)

    def finish(self):
        z, nf, target = self.z, self.nf, self.result
        self.ready(z)

        @pl.when(z > 0)
        def _():
            self.right(z).wait_recv()

        @pl.when(z < nf - 1)
        def _():
            self.left(z, True).wait_recv()

        @pl.when(z == 0)
        def _():
            self.add(z, [(self.landed, z), (self.chain, nf)], target)

        @pl.when(z == nf - 1)
        def _():
            self.add(z, [(self.landed, z), (self.chain, z)], target)

        @pl.when((z > 0) & (z < nf - 1))
        def _():
            self.add(z, [(self.landed, z), (self.chain, z), (self.chain, nf)], target)

    def settle(self):
        z, nf = self.z, self.nf
        self.over(z).wait_send()
        for k in range(nf - 1, 0, -1):

            @pl.when(z + k < nf)
            def _():
                self.over(z + k).wait_send()
                self.right(z + k).wait_send()

            @pl.when(z - k >= 0)
            def _():
                self.over(z - k).wait_send()
                self.left(z - k, k == 1).wait_send()


def in_parts(width):
    rows = -(-width // 64) * 32
    return rows, width - rows


def in_view(source, nf):
    rows, second = in_parts(source.shape[-2])

    def view(block, part):
        here = pl.ds(pl.multiple_of(part * second, 16), rows)
        if len(source.shape) == 3:
            return source.at[block, here]
        columns = source.shape[1] // nf
        return source.at[here, pl.ds(pl.multiple_of(block * columns, LANES), columns)]

    return view


def out_view(source, nf):
    rows, columns = source.shape[0] // nf, source.shape[1] // 2

    def view(block, part):
        here = pl.ds(pl.multiple_of(block * rows, 16), rows)
        return source.at[here, pl.ds(pl.multiple_of(part * columns, LANES), columns)]

    return view


def in_part_shape(nf, source):
    columns = source.shape[2] if len(source.shape) == 3 else source.shape[1] // nf
    return in_parts(source.shape[-2])[0], columns


def out_part_shape(nf, source):
    return source.shape[0] // nf, source.shape[1] // 2


def section_sum_scratch(nf, part):
    return [
        pltpu.VMEM((nf,) + part, BF16),
        pltpu.VMEM((nf,) + part, BF16),
        pltpu.VMEM((nf + 1,) + part, BF16),
        pltpu.SemaphoreType.DMA((5, nf + 1)),
        pltpu.VMEM(part, BF16),
    ]


class SectionReturn:

    def __init__(self, piece, place, owner, y, sems):
        self.piece, self.place, self.owner, self.y, self.sems = piece, place, owner, y, sems

    def keep(self):
        return pltpu.make_async_copy(self.piece(self.owner), self.place(self.owner), self.sems.at[2])

    def send(self):
        other = 1 - self.owner
        return remote(
            self.piece(other), self.place(other), self.sems.at[0], self.sems.at[1], {"section": 1 - self.y}
        )

    def begin(self):
        @pl.when(self.y == self.owner)
        def _():
            self.keep().start()

        @pl.when(self.y != self.owner)
        def _():
            self.send().start()

    def finish(self):
        @pl.when(self.y == self.owner)
        def _():
            self.keep().wait()
            self.send().wait_recv()

        @pl.when(self.y != self.owner)
        def _():
            self.send().wait_send()


def end_kernel(
    nf, nd,
    in_ref, in_part1_ref, out_part0_ref, out_part1_ref, small_ref,
    in_all, out_all, small_all,
    in_own, in_landed, in_chain, in_sems, in_part,
    in_final, out_final, small_slots, small_total, local_sem, swap_sem, back_sem, small_sems, group_send, group_recv,
):
    y, z, d = lax.axis_index("section"), lax.axis_index("fsdp"), lax.axis_index("dp")
    away = z != d
    twin = {"fsdp": d, "dp": z}
    peer = {"section": 1 - y}
    lines = small_ref.shape[1]
    wide = lambda k: {"fsdp": (z + k) % nf}
    greet(
        [(None, peer), (away, twin)]
        + [(None, wide(k)) for k in range(1, nf)]
        + [(None, {"dp": flip(d, bit)}) for bit in bits_of(nd)]
    )
    in_sum = SectionSum(in_view(in_ref, nf), nf, y, z, in_own, in_landed, in_chain, in_sems, in_part)
    in_sum.begin()
    small_over = remote(small_ref.at[1 - y], small_slots.at[nf], small_sems.at[0, 0], small_sems.at[1, 0], peer)
    small_over.start()
    small_load = pltpu.make_async_copy(small_ref.at[y], small_slots.at[0], local_sem.at[0])
    small_load.start()
    width = in_final.shape[0]
    part_rows, second = in_parts(width)
    overlap = part_rows - second
    out_rows, out_columns = out_part0_ref.shape
    in_piece = lambda ref: lambda p: ref if p == 0 else ref.at[pl.ds(overlap, width - part_rows)]
    in_place = lambda p: in_final.at[pl.ds(p * part_rows, width - part_rows if p else part_rows)]
    out_place = lambda p: out_final.at[:, pl.ds(p * out_columns, out_columns)]
    out_returns = [
        SectionReturn(lambda p: out_part0_ref, out_place, 0, y, back_sem.at[0]),
        SectionReturn(lambda p: out_part1_ref, out_place, 1, y, back_sem.at[1]),
    ]
    in_returns = [
        SectionReturn(in_piece(in_part), in_place, 0, y, back_sem.at[2]),
        SectionReturn(in_piece(in_part1_ref), in_place, 1, y, back_sem.at[3]),
    ]
    in_groups = [
        GroupRows(
            lambda device, p=p: in_all.at[device, pl.ds(p * part_rows, width - part_rows if p else part_rows)],
            d, nd, group_send.at[p], group_recv.at[p],
        )
        for p in range(2)
    ]
    out_group = GroupRows(rows_of(out_all, out_rows), d, nd, group_send.at[2], group_recv.at[2])
    small_group = GroupRows(rows_of(small_all, lines), d, nd, group_send.at[3], group_recv.at[3])

    small_load.wait()
    small_over.wait()
    small_slots[0] = small_slots[0] + small_slots[nf]
    small_copies = [
        remote(small_slots.at[0], small_slots.at[k], small_sems.at[0, k], small_sems.at[1, k], wide(k))
        for k in range(1, nf)
    ]
    for copy in small_copies:
        copy.start()
    for copy in small_copies:
        copy.wait()
    total = small_slots[0]
    for k in range(1, nf):
        total = total + small_slots[k]
    small_total[...] = total
    small_own = pltpu.make_async_copy(small_total, small_group.part(0), local_sem.at[0])
    small_own.start()
    small_group.begin(small_total)

    swap_target = out_all.at[pl.ds(pl.multiple_of(z * out_rows, 16), out_rows)]
    swap = remote(out_final, swap_target, swap_sem.at[0], swap_sem.at[1], twin)
    stay = pltpu.make_async_copy(out_final, out_group.part(0), swap_sem.at[2])
    for k in range(nf - 1, 0, -1):
        in_sum.stage(k)
        if k == nf - 1:
            for back in out_returns:
                back.begin()
            small_group.finish()
            small_own.wait()
        if k == nf - 2:
            for back in out_returns:
                back.finish()

            @pl.when(away)
            def _():
                swap.start()

            @pl.when(jnp.logical_not(away))
            def _():
                stay.start()

        if k == 1:
            in_returns[1].begin()

            @pl.when(away)
            def _():
                swap.wait()

            @pl.when(jnp.logical_not(away))
            def _():
                stay.wait()

            out_group.begin()
    in_returns[1].finish()
    out_group.finish()
    in_sum.finish()
    in_returns[0].begin()

    @pl.when(y == 0)
    def _():
        in_returns[0].keep().wait()

    def own_copy(p):
        return pltpu.make_async_copy(in_place(p), in_groups[p].part(0), local_sem.at[1 + p])

    own_copy(0).start()
    in_groups[0].begin(in_place(0))

    @pl.when(y == 0)
    def _():
        in_returns[0].send().wait_recv()

    own_copy(1).start()
    in_groups[1].begin(in_place(1))
    in_groups[0].finish()
    in_groups[1].finish()
    own_copy(0).wait()
    own_copy(1).wait()

    @pl.when(y == 1)
    def _():
        in_returns[0].send().wait_send()

    in_sum.settle()


def run_end(nf, nd, in_grad, in_part1, out_part0, out_part1, small):
    anywhere = pl.BlockSpec(memory_space=pl.ANY)
    dma = pltpu.SemaphoreType.DMA
    lines = small.shape[1]
    width = in_grad.shape[-2]
    out_rows = out_part0.shape[0]
    return pl.pallas_call(
        functools.partial(end_kernel, nf, nd),
        in_specs=[anywhere] * 5,
        out_specs=[anywhere] * 3,
        out_shape=[
            jax.ShapeDtypeStruct((nd, width, in_part1.shape[1]), BF16),
            jax.ShapeDtypeStruct((nd * out_rows, D), BF16),
            jax.ShapeDtypeStruct((nd * lines, LANES), F32),
        ],
        scratch_shapes=section_sum_scratch(nf, in_part1.shape)
        + [
            pltpu.VMEM((width, in_part1.shape[1]), BF16),
            pltpu.VMEM((out_rows, D), BF16),
            pltpu.VMEM((nf + 1, lines, LANES), F32),
            pltpu.VMEM((lines, LANES), F32),
            dma((3,)),
            dma((3,)),
            dma((4, 3)),
            dma((2, nf)),
            dma((4, nd)),
            dma((4, nd)),
        ],
        compiler_params=pltpu.CompilerParams(
            vmem_limit_bytes=VMEM_LIMIT, collective_id=6, has_side_effects=True
        ),
        name="sum_end",
    )(in_grad, in_part1, out_part0, out_part1, small)


class Weights:

    def __init__(self, source, held, sems):
        self.source, self.held, self.sems = source, held, sems
        self.blocks = source.shape[0]
        self.columns = source.shape[2]

    def copies(self):
        out = []
        for k in range(self.blocks):
            if len(self.held.shape) == 3:
                target = self.held.at[k]
            else:
                target = self.held.at[:, pl.ds(k * self.columns, self.columns)]
            out.append(pltpu.make_async_copy(self.source.at[k], target, self.sems.at[k]))
        return out

    def forward(self, rows):
        if len(self.held.shape) == 2:
            return dot(rows, self.held[...], ((1,), (1,)))
        total = 0.0
        for k in range(self.blocks):
            total = total + dot(
                rows[:, k * self.columns : (k + 1) * self.columns], self.held[k], ((1,), (1,))
            )
        return total

    def backward(self, rows):
        if len(self.held.shape) == 2:
            return dot(rows, self.held[...])
        return jnp.concatenate([dot(rows, self.held[k]) for k in range(self.blocks)], axis=1)


def held_shape(w_in):
    blocks, width, columns = w_in.shape
    return (width, blocks * columns) if columns % LANES == 0 else (blocks, width, columns)


def own_steps(steps, turn):
    padded = jnp.concatenate([steps, jnp.zeros((steps.shape[0], LANES - H), F32)], axis=1)
    return pltpu.roll(padded, LANES - turn, 1)


def mix_forward(
    ch, proj_ref, meta_ref, segrow_ref, conv_w_ref, conv_b_ref, dtb_ref, alog_ref, skip_ref,
    gated_ref, square_ref, mixed_ref, pre_ref, state_out_ref, pad, state, sub, turn,
):
    conv_width = ch + 2 * N
    rows = pl.ds(pl.multiple_of(sub * Q, Q), Q)
    meta = meta_ref[rows, :]
    pad[8:, :] = proj_ref[rows, ch : ch + conv_width]
    pre = conv_b_ref[...] + conv_w_ref[3:4, :] * pad[8:, :]
    for lag in range(1, K):
        pre = pre + (conv_w_ref[3 - lag : 4 - lag, :] * meta[:, lag : lag + 1]) * pad[8 - lag : 8 - lag + Q, :]
    pad[0:8, :] = pad[Q : Q + 8, :]
    pre_ref[rows, :] = pre
    conv_out = pre * jax.nn.sigmoid(pre)
    values = conv_out[:, :ch]
    b_part = conv_out[:, ch : ch + N]
    c_part = conv_out[:, ch + N :]
    row, column = triangles()
    tri = jnp.where(row >= column, 1.0, 0.0)
    shifted, step, log_decay, cumulative = decay_tables(
        own_steps(proj_ref[rows, ch + conv_width :], turn), dtb_ref[...], alog_ref[...], tri
    )
    linked = (row >= column) & (meta[:, 0:1] == segrow_ref[sub])
    inner = jnp.where(linked, split_dot(c_part, b_part, ((1,), (1,))), 0.0)
    cum_t = cumulative.T
    step_t = step.T
    last = cumulative[Q - 1 : Q, :]
    entry = meta[:, 4:5] * jnp.exp(cumulative)
    weight = meta[:, 5:6] * jnp.exp(last - cumulative) * step
    state_in = state[...]
    state_out_ref[sub] = state_in
    carried = split_dot(c_part, state_in)
    low_half = lax.broadcasted_iota(jnp.int32, (Q, LANES), 1) < P_SIZE
    squares = jnp.zeros((Q, 1), F32)
    weighted = []
    entries = []
    for pair in range(ch // LANES):
        lanes = slice(pair * LANES, (pair + 1) * LANES)
        values_pair = values[:, lanes]
        mats = []
        for head in (2 * pair, 2 * pair + 1):
            spread = jnp.minimum(cumulative[:, head : head + 1] - cum_t[head : head + 1, :], 0.0)
            mats.append(inner * jnp.exp(spread) * step_t[head : head + 1, :])
        zero = jnp.zeros_like(values_pair)
        stacked = jnp.concatenate(
            [jnp.where(low_half, values_pair, zero), jnp.where(low_half, zero, values_pair)], axis=0
        )
        out = split_dot(jnp.concatenate(mats, axis=1), stacked)
        entry_pair = pair_lanes(entry, 2 * pair, low_half)
        out = out + entry_pair * carried[:, lanes] + skip_ref[:, lanes] * values_pair
        mixed_ref[rows, lanes] = out
        gate = proj_ref[rows, lanes]
        gated = out * (gate * jax.nn.sigmoid(gate))
        squares = squares + jnp.sum(gated * gated, axis=1, keepdims=True)
        gated_ref[rows, lanes] = gated
        weighted.append(pair_lanes(weight, 2 * pair, low_half) * values_pair)
        entries.append(entry_pair[Q - 1 : Q, :])
    square_ref[0, pl.ds(sub, 1), :] = to_row(squares)
    state[...] = jnp.concatenate(entries, axis=1) * state_in + split_dot(
        b_part.T, jnp.concatenate(weighted, axis=1)
    )


def first_kernel(
    ch, nf, nd,
    x_ref, cot_ref, seg_ref, in_ref, out_ref, conv_w_ref, conv_b_ref, norm_ref, gate_ref, head_ref,
    proj_ref, mixed_ref, pre_ref, state_out_ref, nout_ref, branch_ref, next_ref, ratio_ref,
    conv_w_out, conv_b_out, dtb_out, alog_out, skip_out, gain_out, norm_out, meta_out, segrow_out,
    normed_all, moved_ref, hidden_out, cot_own, w_in0, w_in1, w_out0, w_out1,
    held, w_out, pad, state, gated, partial, landed, squares, low, normed, x_low, table, seg_all, own_block, staged,
    sum_send, sum_recv, tile_send, tile_recv, group_send, group_recv, start_send, start_recv, deal_send, deal_recv,
    in_sems0, in_sems1, out_sems0, out_sems1, local_sem, load_sem, small_sem, swap_sem, own_sem,
):
    step = pl.program_id(0)
    y, z, d = lax.axis_index("section"), lax.axis_index("fsdp"), lax.axis_index("dp")
    block = proj_ref.shape[0]
    subs = block // Q
    rows = block // nd
    length = block * nf
    lines = block // Q * 8
    heads = H // nd
    bits = bits_of(nd)
    twin = {"fsdp": d, "dp": z}
    home = z == d
    away = z != d
    peer = {"section": 1 - y}
    blocks = BlockSum(partial, landed, d, nd, sum_send, sum_recv)
    weights = Weights(w_in0, held, load_sem)
    out_load = pltpu.make_async_copy(w_out0, w_out, local_sem.at[0])
    gathers = [SectionGather(w_in0, 0, nf, y, z, in_sems0, own_block), SectionGather(w_in1, 1, nf, y, z, in_sems1, own_block)]
    outs = [
        OutGather(out_ref, w_out0, 0, nf, y, z, d, out_sems0, staged),
        OutGather(out_ref, w_out1, 1, nf, y, z, d, out_sems1, staged),
    ]
    enter = Deal(x_ref.at[y], x_low, nf, nd, z, d, deal_send.at[0], deal_recv.at[0], False)
    enter_cot = Deal(cot_ref.at[y], cot_own, nf, nd, z, d, deal_send.at[1], deal_recv.at[1], False)
    first_group = GroupRows(lambda device: normed.at[:, device], d, nd, start_send.at[0], start_recv.at[0])
    normed_copy = pltpu.make_async_copy(normed, normed_all, local_sem.at[1])
    hidden_copy = pltpu.make_async_copy(x_low, hidden_out, local_sem.at[2])

    def seg_rows(device):
        return seg_all.at[pl.ds(pl.multiple_of(device * lines, 8), lines)]

    seg_group = GroupRows(seg_rows, d, nd, start_send.at[1], start_recv.at[1])

    def every(place):
        return GroupRows(lambda device: moved_ref.at[place, device], d, nd, group_send.at[place], group_recv.at[place])

    def mine(place):
        return pltpu.make_async_copy(low.at[place], moved_ref.at[place, d], local_sem.at[3 + place])

    def stage(gather, k):
        gather.arrive(k)
        gather.relay(k)

    @pl.when(step == 0)
    def _():
        greet(
            line_neighbours(nf, y, z)
            + [(away, twin)]
            + deal_partners(nf, nd, z, d)
            + [(None, {"dp": flip(d, j)}) for j in range(1, nd)]
        )

        own_copies = [
            pltpu.make_async_copy(
                in_ref.at[pl.ds(pl.multiple_of(begin, 16), count)], own_block.at[pl.ds(spot, count)], own_sem.at[k]
            )
            for k, (begin, spot, count) in enumerate(
                [(d * ch, 0, ch), (DI + d * ch, ch, ch), (2 * DI, 2 * ch, DIN - 2 * DI)]
            )
        ]
        for copy in own_copies:
            copy.start()
        for copy in own_copies:
            copy.wait()
        gathers[0].start_cross()
        gathers[1].start_cross()
        table[y, 0:4, :] = conv_w_ref[...]
        table[y, 4:5, :] = conv_b_ref[...]
        table[y, 5:6, 0:D] = norm_ref[...]
        table[y, 6:7, 0:DI] = gate_ref[...]
        for k in range(3):
            table[y, 7:8, k * LANES : (k + 1) * LANES] = head_ref[k : k + 1, :]
        small_copy = remote(table.at[y], table.at[y], small_sem.at[0], small_sem.at[1], peer)
        small_copy.start()
        seg_swap = remote(seg_ref, seg_rows(z), swap_sem.at[0], swap_sem.at[1], twin)
        seg_stay = pltpu.make_async_copy(seg_ref, seg_rows(d), swap_sem.at[0])

        @pl.when(away)
        def _():
            seg_swap.start()

        @pl.when(home)
        def _():
            seg_stay.start()

        gathers[0].begin()
        enter.start_all()
        outs[0].begin()
        stage(gathers[0], 1)
        outs[0].begin_other()
        outs[0].hops(1)

        small_copy.wait()
        enter.arrive()
        hidden_copy.start()
        values = x_low[...].astype(F32)
        low[...] = (values * rms_parts(values) * table[0, 5:6, 0:D]).astype(BF16)
        for place in range(nf):
            normed[place, d] = low[place]
        first_group.begin(low)

        @pl.when(away)
        def _():
            seg_swap.wait()

        @pl.when(home)
        def _():
            seg_stay.wait()

        seg_group.begin()
        for k in range(2, nf - 1):
            stage(gathers[0], k)
            outs[0].hops(k)

        turn = d * heads
        low_half = lax.broadcasted_iota(jnp.int32, (1, LANES), 1) < P_SIZE
        channels = pl.ds(pl.multiple_of(d * ch, LANES), ch)
        for section in range(2):
            conv_w_out[section, :, 0:ch] = table[section, 0:4, channels]
            conv_w_out[section, :, ch:] = table[section, 0:4, DI:DC]
            conv_b_out[section, :, 0:ch] = table[section, 4:5, channels]
            conv_b_out[section, :, ch:] = table[section, 4:5, DI:DC]
            norm_out[section] = table[section, 5:6, 0:D]
            gain_out[section] = table[section, 6:7, channels]
            head_rows = [
                pltpu.roll(table[section, :, k * LANES : (k + 1) * LANES], LANES - turn, 1)[7:8, :] for k in range(3)
            ]
            dtb_out[section] = head_rows[0]
            alog_out[section] = head_rows[1]
            for pair in range(ch // LANES):
                skip_out[section, :, pair * LANES : (pair + 1) * LANES] = pair_lanes(head_rows[2], 2 * pair, low_half)

        seg_group.finish()

        lane = lax.broadcasted_iota(jnp.int32, (8, LANES), 1)
        sub_lane = lax.broadcasted_iota(jnp.int32, (Q, LANES), 1)
        before = jnp.full((8, LANES), -1.0, F32)
        for chunk in range(length // Q):
            now = seg_all[chunk * 8 : chunk * 8 + 8, :]
            segrow_out[chunk] = now[0:1, :]
            columns = [now[0:1, :]]
            for lag in range(1, K):
                earlier = jnp.where(lane < lag, pltpu.roll(before, lag, 1), pltpu.roll(now, lag, 1))
                columns.append(jnp.where(earlier == now, 1.0, 0.0)[0:1, :])
            columns.append(jnp.where(now == before[:, Q - 1 : Q], 1.0, 0.0)[0:1, :])
            columns.append(jnp.where(now == now[:, Q - 1 : Q], 1.0, 0.0)[0:1, :])
            masks = jnp.zeros((Q, LANES), F32)
            for j, row in enumerate(columns):
                masks = jnp.where(sub_lane == j, to_column(row), masks)
            meta_out[chunk * Q : (chunk + 1) * Q, :] = masks
            before = now

        stage(gathers[0], nf - 1)
        outs[0].hops(nf - 1)
        outs[0].hand_over()
        gathers[1].begin()
        first_group.finish()
        normed_copy.start()
        pad[0:8, :] = jnp.zeros((8, pad.shape[1]), F32)
        state[...] = jnp.zeros_like(state)
        for k in range(1, nf):
            gathers[0].settle(k)
        gathers[0].settle_begin()
        for copy in weights.copies():
            copy.start()
        for copy in weights.copies():
            copy.wait()

    def tile(place):
        return GroupTiles(squares.at[place], tile_send.at[place], tile_recv.at[place], d, nd)

    def project(place):
        ratio = lax.rsqrt(tile(place).finish() * (1.0 / DI) + EPSILON)
        for sub in range(subs):
            piece = place * subs + sub
            ratio_ref[pl.ds(piece, 1), :] = ratio[sub : sub + 1, :]
            normed_out = gated[place % 2, sub * Q : (sub + 1) * Q, :] * to_column(ratio[sub : sub + 1, :])
            nout_ref[pl.ds(pl.multiple_of(piece * Q, Q), Q), :] = (normed_out * gain_out[0]).astype(BF16)
        here_rows = pl.ds(pl.multiple_of(place * block, Q), block)
        product = dot(nout_ref[here_rows, :], w_out[...])
        for o in range(nd):
            partial[place, o] = product[o * rows : (o + 1) * rows, :]
        blocks.send(0, place)

    def pass_on(place):
        for k in range(1, len(bits)):
            blocks.send(k, place)

    def conclude(place):
        branch = blocks.own(place)
        branch_ref[place] = branch
        moved = (x_low[place].astype(F32) + branch).astype(BF16)
        next_ref[place] = moved
        values = moved.astype(F32)
        low[place] = (values * rms_parts(values) * norm_out[1]).astype(BF16)
        mine(place).start()
        every(place).begin(low.at[place])

    proj_ref[...] = weights.forward(normed[step].reshape(block, D))

    @pl.when(step == 0)
    def _():
        stage(gathers[1], 1)

    @pl.when(step == 1)
    def _():
        outs[0].settle()
        out_load.start()
        out_load.wait()

    @pl.when(step >= 1)
    def _():
        project(step - 1)

    meta = meta_out.at[pl.ds(pl.multiple_of(step * block, Q), block)]
    segrow = segrow_out.at[pl.ds(step * subs, subs)]

    def one_chunk(sub, carry):
        mix_forward(
            ch, proj_ref, meta, segrow, conv_w_out.at[0], conv_b_out.at[0], dtb_out.at[0], alog_out.at[0],
            skip_out.at[0], gated.at[step % 2], squares.at[step], mixed_ref, pre_ref, state_out_ref, pad, state, sub,
            d * heads,
        )

        @pl.when(sub == 0)
        def _():
            @pl.when(step >= 2)
            def _():
                conclude(step - 2)

            @pl.when(step >= 1)
            def _():
                pass_on(step - 1)

            @pl.when(step >= 3)
            def _():
                every(step - 3).relay()

            for k in range(2, nf):

                @pl.when(step == k - 1)
                def _():
                    stage(gathers[1], k)

        return carry

    lax.fori_loop(0, subs, one_chunk, 0)
    tile(step).begin()

    @pl.when(step == 1)
    def _():
        outs[1].begin()

    @pl.when(step == nf - 2)
    def _():
        enter_cot.start_all()

    @pl.when(step == 2)
    def _():
        outs[1].begin_other()

    for k in range(1, nf):

        @pl.when(step == min(k + 1, nf - 1))
        def _():
            outs[1].hops(k)
            if k == nf - 1:
                outs[1].hand_over()

    @pl.when(step == nf - 1)
    def _():
        project(nf - 1)
        pass_on(nf - 1)
        conclude(nf - 2)
        every(nf - 3).relay()
        conclude(nf - 1)
        every(nf - 2).relay()
        for k in range(1, nf):
            gathers[1].settle(k)
        gathers[1].settle_begin()
        outs[1].settle()
        enter.settle()
        enter_cot.arrive()
        enter_cot.settle()
        normed_copy.wait()
        hidden_copy.wait()
        every(nf - 1).relay()
        for place in range(nf):
            every(place).close()
            mine(place).wait()
        blocks.settle(nf)


def run_first(ch, nf, nd, x, cot, seg, in_rows, out_rows, conv_w, conv_b, norm_gain, gate_gain, head_table, identity):
    block = x.shape[1]
    length = block * nf
    conv_width = ch + 2 * N
    columns = in_rows.shape[1]
    width = 2 * ch + DIN - 2 * DI
    pieces = length // Q
    subs = block // Q
    bits = len(bits_of(nd))
    own = (nf, block // nd, D)
    every = (nf, nd, block // nd, D)
    w_in = jax.ShapeDtypeStruct((nf, width, columns), BF16)
    anywhere = pl.BlockSpec(memory_space=pl.ANY)
    dma = pltpu.SemaphoreType.DMA
    ordered = lambda s: (s, 0)
    small = [(2, K, conv_width), (2, 1, conv_width), (2, 1, LANES), (2, 1, LANES), (2, 1, ch), (2, 1, ch), (2, 1, D)]
    resident = small + [(length, LANES), (pieces, 1, Q)]
    return pl.pallas_call(
        functools.partial(first_kernel, ch, nf, nd),
        grid=(nf,),
        in_specs=[anywhere] * 5 + [once(part.shape) for part in (conv_w, conv_b, norm_gain, gate_gain, head_table)],
        out_specs=[
            pl.BlockSpec((block, width), ordered),
            pl.BlockSpec((block, ch), ordered),
            pl.BlockSpec((block, conv_width), ordered),
            pl.BlockSpec((subs, N, ch), lambda s: (s, 0, 0)),
            once((length, ch)),
            once(own),
            once(own),
            once((pieces, Q)),
        ]
        + [once(shape) for shape in resident]
        + [anywhere] * 8,
        out_shape=[
            jax.ShapeDtypeStruct((length, width), F32),
            jax.ShapeDtypeStruct((length, ch), F32),
            jax.ShapeDtypeStruct((length, conv_width), F32),
            jax.ShapeDtypeStruct((pieces, N, ch), F32),
            jax.ShapeDtypeStruct((length, ch), BF16),
            jax.ShapeDtypeStruct(own, F32),
            jax.ShapeDtypeStruct(own, BF16),
            jax.ShapeDtypeStruct((pieces, Q), F32),
        ]
        + [jax.ShapeDtypeStruct(shape, F32) for shape in resident]
        + [
            jax.ShapeDtypeStruct(every, BF16),
            jax.ShapeDtypeStruct(every, BF16),
            jax.ShapeDtypeStruct(own, BF16),
            jax.ShapeDtypeStruct(own, BF16),
            w_in,
            w_in,
            jax.ShapeDtypeStruct((ch, D), BF16),
            jax.ShapeDtypeStruct((ch, D), BF16),
        ],
        scratch_shapes=[
            pltpu.VMEM(held_shape(w_in), BF16),
            pltpu.VMEM((ch, D), BF16),
            pltpu.VMEM((Q + 8, conv_width), F32),
            pltpu.VMEM((N, ch), F32),
            pltpu.VMEM((2, block, ch), F32),
            pltpu.VMEM(every, F32),
            pltpu.VMEM((bits, nf, nd // 2, block // nd, D), F32),
            pltpu.VMEM((nf, nd, 8, LANES), F32),
            pltpu.VMEM(own, BF16),
            pltpu.VMEM(every, BF16),
            pltpu.VMEM(own, BF16),
            pltpu.VMEM((2, 8, DC), F32),
            pltpu.VMEM((pieces * 8, LANES), F32),
            pltpu.VMEM((width, columns), BF16),
            pltpu.VMEM((ch, D), BF16),
            dma((bits, nf, nd)),
            dma((bits, nf, nd)),
            dma((nf, nd)),
            dma((nf, nd)),
            dma((nf, nd)),
            dma((nf, nd)),
            dma((2, nd)),
            dma((2, nd)),
            dma((2, nf)),
            dma((2, nf)),
            dma((7, 2 * nf)),
            dma((7, 2 * nf)),
            dma((6, 4)),
            dma((6, 4)),
            dma((3 + nf,)),
            dma((nf,)),
            dma((2,)),
            dma((2,)),
            dma((3,)),
        ],
        compiler_params=pltpu.CompilerParams(
            vmem_limit_bytes=VMEM_LIMIT, collective_id=identity, has_side_effects=True
        ),
        name="layer_first",
    )(x, cot, seg, in_rows, out_rows, conv_w, conv_b, norm_gain, gate_gain, head_table)


def layer_kernel(
    ch, nf, nd,
    normed_ref, meta_ref, segrow_ref, conv_w_ref, conv_b_ref, dtb_ref, alog_ref, skip_ref, gain_ref,
    w_in_ref, w_out_ref, hidden_ref, extra_ref,
    proj_ref, nout_ref, mixed_ref, pre_ref, state_out_ref, branch_ref, next_ref, ratio_ref, pull_ref, moved_ref,
    cot_all,
    held, w_out, pad, state, gated, partial, landed, squares, pulls, low,
    sum_send, sum_recv, tile_send, tile_recv, group_send, group_recv, local_sem, load_sem, deal_send, deal_recv,
):
    step = pl.program_id(0)
    y, z, d = lax.axis_index("section"), lax.axis_index("fsdp"), lax.axis_index("dp")
    block = normed_ref.shape[0]
    subs = block // Q
    rows = block // nd
    bits = bits_of(nd)
    blocks = BlockSum(partial, landed, d, nd, sum_send, sum_recv)
    weights = Weights(w_in_ref, held, load_sem)
    out_load = pltpu.make_async_copy(w_out_ref, w_out, local_sem.at[0])
    cot_group = GroupRows(lambda device: cot_all.at[:, device], d, nd, group_send.at[0], group_recv.at[0])
    cot_keep = pltpu.make_async_copy(extra_ref, cot_group.part(0), local_sem.at[1])
    leave = Deal(moved_ref, low, nf, nd, z, d, deal_send, deal_recv, True)

    @pl.when(step == 0)
    def _():
        for copy in weights.copies():
            copy.start()
        out_load.start()
        greet([(None, {"dp": flip(d, j)}) for j in range(1, nd)] + deal_partners(nf, nd, z, d))
        cot_keep.start()
        cot_group.begin(extra_ref)
        pad[0:8, :] = jnp.zeros((8, pad.shape[1]), F32)
        state[...] = jnp.zeros_like(state)
        pulls[0] = jnp.zeros(pulls.shape[1:], F32)
        for copy in weights.copies():
            copy.wait()
        out_load.wait()

    def tile(place):
        return GroupTiles(squares.at[place], tile_send.at[place], tile_recv.at[place], d, nd)

    def project(place):
        ratio = lax.rsqrt(tile(place).finish() * (1.0 / DI) + EPSILON)
        for sub in range(subs):
            piece = place * subs + sub
            ratio_ref[pl.ds(piece, 1), :] = ratio[sub : sub + 1, :]
            normed_out = gated[place % 2, sub * Q : (sub + 1) * Q, :] * to_column(ratio[sub : sub + 1, :])
            nout_ref[pl.ds(pl.multiple_of(piece * Q, Q), Q), :] = (normed_out * gain_ref[...]).astype(BF16)
        here_rows = pl.ds(pl.multiple_of(place * block, Q), block)
        product = dot(nout_ref[here_rows, :], w_out[...]).astype(partial.dtype)
        for o in range(nd):
            partial[place, o] = product[o * rows : (o + 1) * rows, :]
        blocks.send(0, place)

    def pass_on(place):
        for k in range(1, len(bits)):
            blocks.send(k, place)

    def conclude(place):
        branch = blocks.own(place)
        branch_ref[place] = branch
        moved = (hidden_ref[place].astype(F32) + branch).astype(BF16)
        next_ref[place] = moved
        low[place] = moved
        first = place * block + d * rows
        pulls[0, pl.ds(first // Q, 1), :] += to_row(
            jnp.sum(extra_ref[place].astype(F32) * branch, axis=1, keepdims=True), first % Q
        )
        leave.start(place)

    proj_ref[...] = weights.forward(normed_ref[...])

    @pl.when(step >= 1)
    def _():
        project(step - 1)

    def one_chunk(sub, carry):
        mix_forward(
            ch, proj_ref, meta_ref, segrow_ref, conv_w_ref, conv_b_ref, dtb_ref, alog_ref, skip_ref,
            gated.at[step % 2], squares.at[step], mixed_ref, pre_ref, state_out_ref, pad, state, sub, d * (H // nd),
        )

        @pl.when(sub == 0)
        def _():
            @pl.when(step >= 2)
            def _():
                conclude(step - 2)

            @pl.when(step >= 1)
            def _():
                pass_on(step - 1)

        return carry

    lax.fori_loop(0, subs, one_chunk, 0)
    tile(step).begin()

    @pl.when(step == min(2, nf - 1))
    def _():
        cot_group.finish()

    @pl.when(step == nf - 1)
    def _():
        project(nf - 1)
        pass_on(nf - 1)
        conclude(nf - 2)
        conclude(nf - 1)
        pull_ref[...] = group_tiles(pulls, group_send.at[1], group_recv.at[1], d, nd)
        leave.arrive()
        leave.settle()
        cot_keep.wait()
        blocks.settle(nf)


def once(shape):
    return pl.BlockSpec(shape, lambda s: (0,) * len(shape), pipeline_mode=pl.Buffered(buffer_count=1))


def pick(part, layer):
    return pl.BlockSpec(
        (None,) + part.shape[1:], lambda s: (layer, 0, 0), pipeline_mode=pl.Buffered(buffer_count=1)
    )


def run_layer(
    ch, rows, nf, nd, normed_all, meta, segrow, small, w_in, w_out, hidden, extra, identity
):
    length, width = normed_all.shape[0], w_in.shape[1]
    layer = 1
    conv_width = ch + 2 * N
    block = rows
    steps = nf
    pieces = length // Q
    subs = block // Q
    own = (nf, rows // nd, D)
    every = (nf, nd, rows // nd, D)
    bits = len(bits_of(nd))
    dma = pltpu.SemaphoreType.DMA
    anywhere = pl.BlockSpec(memory_space=pl.ANY)
    ordered = lambda s: (s, 0)
    ordered3 = lambda s: (s, 0, 0)
    return pl.pallas_call(
        functools.partial(layer_kernel, ch, nf, nd),
        grid=(steps,),
        in_specs=[
            pl.BlockSpec((block, D), ordered),
            pl.BlockSpec((block, LANES), ordered),
            pl.BlockSpec((subs, 1, Q), ordered3),
        ]
        + [pick(part, layer) for part in small]
        + [
            anywhere,
            anywhere,
            once(own),
            once(own),
        ],
        out_specs=[
            pl.BlockSpec((block, width), ordered),
            once((length, ch)),
            pl.BlockSpec((block, ch), ordered),
            pl.BlockSpec((block, conv_width), ordered),
            pl.BlockSpec((subs, N, ch), ordered3),
            once(own),
            once(own),
            once((pieces, Q)),
            once((pieces, Q)),
            anywhere,
            anywhere,
        ],
        out_shape=[
            jax.ShapeDtypeStruct((length, width), F32),
            jax.ShapeDtypeStruct((length, ch), BF16),
            jax.ShapeDtypeStruct((length, ch), F32),
            jax.ShapeDtypeStruct((length, conv_width), F32),
            jax.ShapeDtypeStruct((pieces, N, ch), F32),
            jax.ShapeDtypeStruct(own, F32),
            jax.ShapeDtypeStruct(own, BF16),
            jax.ShapeDtypeStruct((pieces, Q), F32),
            jax.ShapeDtypeStruct((pieces, Q), F32),
            jax.ShapeDtypeStruct((rows, D), BF16),
            jax.ShapeDtypeStruct(every, BF16),
        ],
        scratch_shapes=[
            pltpu.VMEM(held_shape(w_in), BF16),
            pltpu.VMEM((ch, D), BF16),
            pltpu.VMEM((Q + 8, conv_width), F32),
            pltpu.VMEM((N, ch), F32),
            pltpu.VMEM((2, block, ch), F32),
            pltpu.VMEM(every, BF16),
            pltpu.VMEM((bits, nf, nd // 2, rows // nd, D), BF16),
            pltpu.VMEM((steps, nd, 8, LANES), F32),
            pltpu.VMEM((nd, pieces, Q), F32),
            pltpu.VMEM(own, BF16),
            dma((bits, nf, nd)),
            dma((bits, nf, nd)),
            dma((steps, nd)),
            dma((steps, nd)),
            dma((nf, nd)),
            dma((nf, nd)),
            dma((2 + nf,)),
            dma((nf,)),
            dma((nf,)),
            dma((nf,)),
        ],
        compiler_params=pltpu.CompilerParams(
            vmem_limit_bytes=VMEM_LIMIT, collective_id=identity, has_side_effects=True
        ),
        name="layer_last",
    )(normed_all, meta, segrow, *small, w_in, w_out, hidden, extra)


def mix_backward(
    ch, proj_ref, pre_ref, mixed_ref, state_ref, grad_ref, ratio_ref, pull_ref, meta_ref, segrow_ref,
    conv_w_ref, dtb_ref, alog_ref, skip_ref, gain_ref,
    dproj_ref, dconv_w_ref, dchan_ref, ddecay_ref, tail, dstate, sub, chunk, turn,
):
    conv_width = ch + 2 * N
    rows = pl.ds(pl.multiple_of(sub * Q, Q), Q)
    meta = meta_ref[rows, :]
    pre = pre_ref[rows, :]
    sig = jax.nn.sigmoid(pre)
    conv_out = pre * sig
    values = conv_out[:, :ch]
    b_part = conv_out[:, ch : ch + N]
    c_part = conv_out[:, ch + N :]
    row, column = triangles()
    tri = jnp.where(row >= column, 1.0, 0.0)
    shifted, step, log_decay, cumulative = decay_tables(
        own_steps(proj_ref[rows, ch + conv_width :], turn), dtb_ref[...], alog_ref[...], tri
    )
    linked = (row <= column) & (meta[:, 0:1] == segrow_ref[sub])
    b_low = b_part.astype(BF16)
    c_low = c_part.astype(BF16)
    inner = jnp.where(linked, dot(b_low, c_low, ((1,), (1,))), 0.0)
    cum_t = cumulative.T
    last = cumulative[Q - 1 : Q, :]
    entry = meta[:, 4:5] * jnp.exp(cumulative)
    weight = meta[:, 5:6] * jnp.exp(last - cumulative)
    state_in = state_ref[sub]
    dstate_in = dstate[...]
    state_low = state_in.astype(BF16)
    dstate_low = dstate_in.astype(BF16)
    carried = dot(c_low, state_low)
    carried_back = dot(b_low, dstate_low)
    low_half = lax.broadcasted_iota(jnp.int32, (Q, LANES), 1) < P_SIZE
    lane = lax.broadcasted_iota(jnp.int32, (Q, LANES), 1)
    ratio = to_column(ratio_ref[pl.ds(chunk, 1), :])
    pull = ratio * ratio * to_column(pull_ref[pl.ds(chunk, 1), :]) * (1.0 / DI)
    dinner = jnp.zeros((Q, Q), F32)
    dcum = jnp.zeros((Q, LANES), F32)
    dcum_rows = []
    dexit = jnp.zeros((Q, LANES), F32)
    dstep = jnp.zeros((Q, LANES), F32)
    dcum_entry = jnp.zeros((Q, LANES), F32)
    weighted = []
    entered = []
    entry_rows = []
    dpre_parts = []
    for pair in range(ch // LANES):
        lanes = slice(pair * LANES, (pair + 1) * LANES)
        values_pair = values[:, lanes]
        gate = proj_ref[rows, lanes]
        mixed = mixed_ref[rows, lanes]
        gate_sig = jax.nn.sigmoid(gate)
        gate_silu = gate * gate_sig
        gated = mixed * gate_silu
        scaled = grad_ref[rows, lanes] * ratio
        dchan_ref[0:1, lanes] += jnp.sum(scaled * gated, axis=0, keepdims=True)
        dgated = scaled * gain_ref[:, lanes] - gated * pull
        dproj_ref[rows, lanes] = (dgated * mixed * (gate_sig + gate_silu * (1.0 - gate_sig))).astype(BF16)
        dmixed = dgated * gate_silu
        dchan_ref[1:2, lanes] += jnp.sum(dmixed * values_pair, axis=0, keepdims=True)
        zero = jnp.zeros_like(values_pair)
        dmixed_halves = [jnp.where(low_half, dmixed, zero).astype(BF16), jnp.where(low_half, zero, dmixed).astype(BF16)]
        values_low = values_pair.astype(BF16)
        step_pair = pair_lanes(step, 2 * pair, low_half)
        mats = []
        for half, head in enumerate((2 * pair, 2 * pair + 1)):
            spread = jnp.minimum(cum_t[head : head + 1, :] - cumulative[:, head : head + 1], 0.0)
            plain = jnp.exp(spread)
            decay = plain * step[:, head : head + 1]
            product = dot(values_low, dmixed_halves[half], ((1,), (1,)))
            mats.append((inner * plain).astype(BF16))
            spreaded = product * decay
            dinner = dinner + spreaded
            turned = spreaded * inner
            dcum = dcum - jnp.where(lane == head, jnp.sum(turned, axis=1, keepdims=True), 0.0)
            dcum_rows.append(jnp.sum(turned, axis=0, keepdims=True))
        back = dot(jnp.concatenate(mats, axis=1), jnp.concatenate(dmixed_halves, axis=0))
        weight_pair = pair_lanes(weight, 2 * pair, low_half)
        through = weight_pair * carried_back[:, lanes]
        total = back + through
        dvalues = step_pair * total + skip_ref[:, lanes] * dmixed
        step_terms = total * values_pair
        exit_terms = through * values_pair * step_pair
        entry_pair = pair_lanes(entry, 2 * pair, low_half)
        entry_grad = entry_pair * dmixed
        entry_terms = entry_grad * carried[:, lanes]
        for half, head in enumerate((2 * pair, 2 * pair + 1)):
            own = lane == head
            mask = low_half if half == 0 else ~low_half
            dstep = dstep + jnp.where(own, jnp.sum(jnp.where(mask, step_terms, 0.0), axis=1, keepdims=True), 0.0)
            dexit = dexit + jnp.where(own, jnp.sum(jnp.where(mask, exit_terms, 0.0), axis=1, keepdims=True), 0.0)
            dcum_entry = dcum_entry + jnp.where(own, jnp.sum(jnp.where(mask, entry_terms, 0.0), axis=1, keepdims=True), 0.0)
        weighted.append((weight_pair * step_pair * values_pair).astype(BF16))
        entered.append(entry_grad.astype(BF16))
        entry_rows.append(entry_pair[Q - 1 : Q, :])
        dpre_parts.append(dvalues)
    weighted = jnp.concatenate(weighted, axis=1)
    entered = jnp.concatenate(entered, axis=1)
    entry_rows = jnp.concatenate(entry_rows, axis=1)
    dinner_low = jnp.where(linked, dinner, 0.0).astype(BF16)
    db = dot(dinner_low, c_low) + dot(weighted, dstate_low, ((1,), (1,)))
    dc = dot(dinner_low.T, b_low) + dot(entered, state_low, ((1,), (1,)))
    state_terms = jnp.sum(state_in * dstate_in, axis=0, keepdims=True) * entry_rows
    head_lane = lax.broadcasted_iota(jnp.int32, (1, LANES), 1)
    state_sum = jnp.zeros((1, LANES), F32)
    for head in range(ch // P_SIZE):
        part = jnp.sum(state_terms[:, head * P_SIZE : (head + 1) * P_SIZE], axis=1, keepdims=True)
        state_sum = state_sum + jnp.where(head_lane == head, part, 0.0)
    by_row = jnp.concatenate(dcum_rows + [jnp.zeros((LANES - len(dcum_rows), Q), F32)], axis=0)
    dcum = dcum + by_row.T + dcum_entry
    later = jnp.where(row <= column, 1.0, 0.0)
    before = jnp.where(row > column, 1.0, 0.0)
    dlog = fine_dot(later, dcum) + fine_dot(before, dexit) + state_sum
    growth = jnp.exp(alog_ref[...])
    dstep = dstep - dlog * growth
    ddt = dstep * jax.nn.sigmoid(shifted)
    ddecay_ref[0:1, :] += jnp.sum(ddt, axis=0, keepdims=True)
    ddecay_ref[1:2, :] += jnp.sum(dlog * log_decay, axis=0, keepdims=True)
    heads = ch // P_SIZE
    dproj_ref[rows, ch + conv_width :] = pltpu.roll(jnp.where(lane < heads, ddt, 0.0), turn, 1)[:, :H].astype(BF16)
    dstate[...] = entry_rows * dstate_in + dot(c_part.T.astype(BF16), entered)
    dconv_out = jnp.concatenate(dpre_parts + [db, dc], axis=1)
    dpre = dconv_out * (sig + conv_out * (1.0 - sig))
    raw = proj_ref[rows, ch : ch + conv_width]
    dchan_ref[2:3, :] += jnp.sum(dpre, axis=0, keepdims=True)
    draw = conv_w_ref[3:4, :] * dpre
    dconv_w_ref[3:4, :] += jnp.sum(raw * dpre, axis=0, keepdims=True)
    for lag in range(1, K):
        kept = meta[:, lag : lag + 1] * dpre
        tail[lag - 1, 0:Q, :] = kept
        moved = tail[lag - 1, lag : lag + Q, :]
        tail[lag - 1, Q : Q + 8, :] = kept[0:8, :]
        draw = draw + conv_w_ref[3 - lag : 4 - lag, :] * moved
        dconv_w_ref[3 - lag : 4 - lag, :] += jnp.sum(raw * moved, axis=0, keepdims=True)
    dproj_ref[rows, ch : ch + conv_width] = draw.astype(BF16)


def layer_back_kernel(
    ch, nf, nd, last,
    grad_all_ref, proj_ref, pre_ref, mixed_ref, state_ref, meta_ref, segrow_ref, ratio_ref, pull_ref,
    conv_w_ref, dtb_ref, alog_ref, skip_ref, gain_ref, w_in_ref, w_out_ref,
    hidden_ref, grad_own_ref, norm_gain_ref, branch_ref, *refs,
):
    count = 2 if last else 1
    sources, refs = refs[:count], refs[count:]
    (
        dproj_ref, dconv_w_ref, dchan_ref, ddecay_ref, dgain_ref, next_ref, next_pull_ref, moved_ref,
    ) = refs[:8]
    results, refs = refs[8 : 8 + count], refs[8 + count :]
    (
        held, w_out, tail, dstate, dnout, partial, landed, pulls, low,
        sum_send, sum_recv, tile_send, tile_recv, group_send, group_recv, local_sem, load_sem, deal_send, deal_recv,
    ) = refs[:19]
    refs = refs[19:]
    step = pl.program_id(0)
    y, z, d = lax.axis_index("section"), lax.axis_index("fsdp"), lax.axis_index("dp")
    block = grad_all_ref.shape[0]
    subs = block // Q
    rows = block // nd
    bits = bits_of(nd)
    place = nf - 1 - step
    blocks = BlockSum(partial, landed, d, nd, sum_send, sum_recv)
    sums = [
        SectionSum(make(source, nf), nf, y, z, *refs[5 * k : 5 * k + 5])
        for k, (make, source) in enumerate(zip((out_view, in_view), sources))
    ]
    weights = Weights(w_in_ref, held, load_sem)
    out_load = pltpu.make_async_copy(w_out_ref, w_out, local_sem.at[0])
    if last:
        leave = Deal(moved_ref, low, nf, nd, z, d, deal_send, deal_recv, True)

    def every(place):
        return GroupRows(lambda device: moved_ref.at[place, device], d, nd, group_send.at[place], group_recv.at[place])

    def mine(place):
        return pltpu.make_async_copy(low.at[place], moved_ref.at[place, d], local_sem.at[2 + place])

    @pl.when(step == 0)
    def _():
        for copy in weights.copies():
            copy.start()
        out_load.start()
        greet(
            [(None, {"dp": flip(d, j)}) for j in range(1, nd)]
            + line_neighbours(nf, y, z)
            + (deal_partners(nf, nd, z, d) if last else [])
        )
        for one in sums:
            one.begin()
        tail[...] = jnp.zeros_like(tail)
        dstate[...] = jnp.zeros_like(dstate)
        dconv_w_ref[...] = jnp.zeros_like(dconv_w_ref)
        dchan_ref[...] = jnp.zeros_like(dchan_ref)
        ddecay_ref[...] = jnp.zeros_like(ddecay_ref)
        dgain_ref[...] = jnp.zeros_like(dgain_ref)
        pulls[0] = jnp.zeros(pulls.shape[1:], F32)
        for copy in weights.copies():
            copy.wait()
        out_load.wait()

    def pass_on(place):
        for k in range(1, len(bits)):
            blocks.send(k, place)

    def conclude(place):
        dnormed = blocks.own(place)
        hidden = hidden_ref[place].astype(F32)
        inverse = rms_parts(hidden)
        dgain_ref[...] += jnp.sum(dnormed * hidden * inverse, axis=0, keepdims=True)
        scaled = dnormed * norm_gain_ref[...]
        dhidden = inverse * (
            scaled - hidden * (inverse * inverse) * jnp.mean(scaled * hidden, axis=1, keepdims=True)
        )
        moved = (grad_own_ref[place].astype(F32) + dhidden).astype(BF16)
        low[place] = moved
        next_ref[place] = moved
        if last:
            leave.start(place)
        else:
            first = place * block + d * rows
            pulls[0, pl.ds(first // Q, 1), :] += to_row(
                jnp.sum(moved.astype(F32) * branch_ref[place], axis=1, keepdims=True), first % Q
            )
            mine(place).start()
            every(place).begin(low.at[place])

    dnout[...] = dot(grad_all_ref[...], w_out[...], ((1,), (1,)))

    @pl.when(step >= 1)
    def _():
        pass_on(place + 1)

    def one_chunk(turn, carry):
        sub = subs - 1 - turn
        mix_backward(
            ch, proj_ref, pre_ref, mixed_ref, state_ref, dnout, ratio_ref, pull_ref, meta_ref, segrow_ref,
            conv_w_ref, dtb_ref, alog_ref, skip_ref, gain_ref,
            dproj_ref, dconv_w_ref, dchan_ref, ddecay_ref, tail, dstate, sub, place * subs + sub, d * (H // nd),
        )

        @pl.when((turn == 0) & (step >= 1))
        def _():
            conclude(place + 1)

        return carry

    lax.fori_loop(0, subs, one_chunk, 0)
    product = weights.backward(dproj_ref[...]).astype(BF16)
    for o in range(nd):
        partial[place, o] = product[o * rows : (o + 1) * rows, :]
    blocks.send(0, place)
    if not last:

        @pl.when(step >= 1)
        def _():
            every(place + 1).relay()

    for k in range(nf - 1, 0, -1):

        @pl.when(step == nf - 1 - k)
        def _():
            for one in sums:
                one.stage(k)

    @pl.when(step == nf - 1)
    def _():
        pass_on(0)
        conclude(0)
        if last:
            next_pull_ref[...] = jnp.zeros_like(next_pull_ref)
        else:
            next_pull_ref[...] = group_tiles(pulls, tile_send, tile_recv, d, nd)
        for one, result in zip(sums, results):
            one.finish()
            copy = pltpu.make_async_copy(one.result, result, local_sem.at[1])
            copy.start()
            copy.wait()
            one.settle()
        if last:
            leave.arrive()
            leave.settle()
        else:
            every(0).relay()
            for k in range(nf):
                every(k).close()
                mine(k).wait()
        blocks.settle(nf)


def run_layer_back(
    ch, rows, nf, nd, last, grad_all, proj, pre, mixed, states, meta, segrow, ratio, pull, small, w_in, w_out,
    hidden, grad_own, norm_gain, branch, identity, *sums,
):
    length, width = proj.shape
    shapes = [make(nf, g) for make, g in zip((out_part_shape, in_part_shape), sums)]
    conv_width = ch + 2 * N
    block = rows
    steps = nf
    own = (nf, rows // nd, D)
    every = (nf, nd, rows // nd, D)
    pieces = length // Q
    subs = block // Q
    bits = len(bits_of(nd))
    dma = pltpu.SemaphoreType.DMA
    ordered = lambda s: (steps - 1 - s, 0)
    ordered3 = lambda s: (steps - 1 - s, 0, 0)
    layer = 0 if last else 1
    conv_w, conv_b, dtb, alog, skip, gain = small
    return pl.pallas_call(
        functools.partial(layer_back_kernel, ch, nf, nd, last),
        grid=(steps,),
        in_specs=[
            pl.BlockSpec((block, D), ordered),
            pl.BlockSpec((block, width), ordered),
            pl.BlockSpec((block, conv_width), ordered),
            pl.BlockSpec((block, ch), ordered),
            pl.BlockSpec((subs, N, ch), ordered3),
            pl.BlockSpec((block, LANES), ordered),
            pl.BlockSpec((subs, 1, Q), ordered3),
            once((pieces, Q)),
            once((pieces, Q)),
        ]
        + [pick(part, layer) for part in (conv_w, dtb, alog, skip, gain)]
        + [
            pl.BlockSpec(memory_space=pl.ANY),
            pl.BlockSpec(memory_space=pl.ANY),
            once(own),
            once(own),
            pick(norm_gain, layer),
            once(own),
        ]
        + [pl.BlockSpec(memory_space=pl.ANY)] * len(sums),
        out_specs=[
            pl.BlockSpec((block, width), ordered),
            once((K, conv_width)),
            once((8, conv_width)),
            once((8, LANES)),
            once((1, D)),
            once(own),
            once((pieces, Q)),
            pl.BlockSpec(memory_space=pl.ANY),
        ]
        + [pl.BlockSpec(memory_space=pl.ANY)] * len(sums),
        out_shape=[
            jax.ShapeDtypeStruct((length, width), BF16),
            jax.ShapeDtypeStruct((K, conv_width), F32),
            jax.ShapeDtypeStruct((8, conv_width), F32),
            jax.ShapeDtypeStruct((8, LANES), F32),
            jax.ShapeDtypeStruct((1, D), F32),
            jax.ShapeDtypeStruct(own, BF16),
            jax.ShapeDtypeStruct((pieces, Q), F32),
            jax.ShapeDtypeStruct((rows, D) if last else every, BF16),
        ]
        + [jax.ShapeDtypeStruct(shape, BF16) for shape in shapes],
        scratch_shapes=[
            pltpu.VMEM(held_shape(w_in), BF16),
            pltpu.VMEM((ch, D), BF16),
            pltpu.VMEM((K - 1, Q + 8, conv_width), F32),
            pltpu.VMEM((N, ch), F32),
            pltpu.VMEM((block, ch), F32),
            pltpu.VMEM(every, BF16),
            pltpu.VMEM((bits, nf, nd // 2, rows // nd, D), BF16),
            pltpu.VMEM((nd, pieces, Q), F32),
            pltpu.VMEM(own, BF16),
            dma((bits, nf, nd)),
            dma((bits, nf, nd)),
            dma((nd,)),
            dma((nd,)),
            dma((nf, nd)),
            dma((nf, nd)),
            dma((2 + nf,)),
            dma((nf,)),
            dma((nf,)),
            dma((nf,)),
        ]
        + [part for shape in shapes for part in section_sum_scratch(nf, shape)],
        compiler_params=pltpu.CompilerParams(
            vmem_limit_bytes=VMEM_LIMIT, collective_id=identity, has_side_effects=True
        ),
        name="layer_back_last" if last else "layer_back_first",
    )(
        grad_all, proj, pre, mixed, states, meta, segrow, ratio, pull, conv_w, dtb, alog, skip, gain, w_in, w_out,
        hidden, grad_own, norm_gain, branch, *sums,
    )


def shards(
    inputs, segment, cotangent, norm_gain, in_weight, conv_weight, conv_bias, dt_bias, a_log, d_skip,
    gate_gain, out_weight,
):
    fsdp, dp = lax.axis_size("fsdp"), lax.axis_size("dp")
    section, here = lax.axis_index("section"), lax.axis_index("dp")
    rows = inputs.shape[2]
    ch = DI // dp
    heads = H // dp
    conv_width = ch + 2 * N
    seg_mine = lax.dynamic_index_in_dim(segment, section, 0, keepdims=False)[0].astype(F32)
    seg_mine = jnp.broadcast_to(seg_mine.reshape(rows // Q, 1, Q), (rows // Q, 8, Q)).reshape(-1, Q)
    head_table = jnp.pad(
        jnp.concatenate([dt_bias[0], a_log[0], d_skip[0]], axis=0), ((0, 0), (0, LANES - H))
    )
    (
        proj, mixed, pre, states, nout, branch, after, ratio, conv_w, conv_b, dtb, alog, skip, gain, gains, meta, segrow,
        normed_all, moved, hidden, cot_own, w_in0, w_in1, w_out0, w_out1,
    ) = run_first(
        ch, fsdp, dp, inputs[:, 0], cotangent[:, 0], seg_mine, in_weight[0, 0].T, out_weight[0, 0], conv_weight[0, 0],
        conv_bias[0], norm_gain[0], gate_gain[0], head_table, 2,
    )
    small = (conv_w, conv_b, dtb, alog, skip, gain)
    length = meta.shape[0]
    saved = [(normed_all.reshape(length, D), hidden, proj, nout, mixed, pre, states, branch, ratio)]
    normed_all, hidden = moved.reshape(length, D), after
    proj, nout, mixed, pre, states, branch, after, ratio, pull, final, cot_all = run_layer(
        ch, rows, fsdp, dp, normed_all, meta, segrow, small, w_in1, w_out1, hidden, cot_own, 3
    )
    saved.append((normed_all, hidden, proj, nout, mixed, pre, states, branch, ratio))

    grad_all, grad_own = cot_all.reshape(length, D), cot_own
    in_grad, small_grads, parts = (), [None, None], []
    for layer in (1, 0):
        last = layer == 0
        normed_all, hidden, proj, gated, mixed, pre, states, branch, ratio = saved[layer]
        out_grad = dot(gated, grad_all, ((0,), (0,)))
        dproj, dconv_w, dchan, ddecay, dgain, after, next_pull, moved, *done = run_layer_back(
            ch, rows, fsdp, dp, last, grad_all, proj, pre, mixed, states, meta, segrow, ratio, pull, small,
            w_in0 if last else w_in1, w_out0 if last else w_out1, hidden, grad_own, gains, saved[0][7], 4 + layer,
            out_grad.astype(BF16), *in_grad,
        )
        parts += done
        grad = dot(dproj, normed_all, ((0,), (0,))).astype(BF16)
        if D // fsdp % LANES:
            grad = jnp.swapaxes(grad.reshape(-1, fsdp, D // fsdp), 0, 1)
        in_grad = (grad,)
        small_grads[layer] = (dgain[0], dconv_w, dchan, ddecay)
        if not last:
            grad_all, grad_own, pull = moved.reshape(length, D), after, next_pull
    input_grad = moved

    def pack_small(grads):
        dgain, dconv_w, dchan, ddecay = grads
        skip = jnp.sum(dchan[1, :ch].reshape(heads, P_SIZE), axis=1)
        pieces = [dgain, dconv_w.reshape(-1), dchan[2], dchan[0, :ch], ddecay[0, :heads], ddecay[1, :heads], skip]
        flat = jnp.concatenate(pieces)
        return jnp.pad(flat, (0, -flat.shape[0] % 1024)).reshape(-1, LANES)

    packed = jnp.stack([pack_small(grads) for grads in small_grads])
    in_all, out_all, small_sum = run_end(fsdp, dp, in_grad[0], parts[2], parts[1], parts[0], packed)
    in_total = jnp.concatenate(
        [
            in_all[:, :ch].reshape(DI, -1).astype(F32),
            in_all[:, ch : 2 * ch].reshape(DI, -1).astype(F32),
            jnp.sum(in_all[:, 2 * ch :].astype(F32), axis=0),
        ],
        axis=0,
    ).T
    out_total = out_all.astype(F32)
    everything = small_sum.reshape(dp, -1)
    offset = 0
    pieces = []
    for size in (D, K * conv_width, conv_width, ch, heads, heads, heads):
        pieces.append(everything[:, offset : offset + size])
        offset += size
    gain_total = jnp.sum(pieces[0], axis=0)
    convw = pieces[1].reshape(dp, K, conv_width)
    convw_total = jnp.concatenate(
        [jnp.moveaxis(convw[:, :, :ch], 0, 1).reshape(K, DI), jnp.sum(convw[:, :, ch:], axis=0)], axis=1
    )
    convb = pieces[2]
    convb_total = jnp.concatenate([convb[:, :ch].reshape(DI), jnp.sum(convb[:, ch:], axis=0)])
    gate_total = pieces[3].reshape(DI)
    dtb_total, alog_total, skip_total = (piece.reshape(H) for piece in pieces[4:])
    return (
        final[None, None],
        input_grad[None, None],
        gain_total[None, None],
        in_total[None, None],
        convw_total[None, None],
        convb_total[None, None],
        dtb_total[None, None],
        alog_total[None, None],
        skip_total[None, None],
        gate_total[None, None],
        out_total[None, None],
    )


def solution(mesh):
    return jax.shard_map(
        shards,
        mesh=mesh,
        in_specs=(
            P(None, "dp", "fsdp", None),
            P(None, "dp", "fsdp"),
            P(None, "dp", "fsdp", None),
            P("section", None, None),
            P("section", None, "fsdp", None),
            P("section", None, None, None),
            P("section", None, None),
            P("section", None, None),
            P("section", None, None),
            P("section", None, None),
            P("section", None, None),
            P("section", None, "fsdp", None),
        ),
        out_specs=(
            P("section", "dp", "fsdp", None),
            P("section", "dp", "fsdp", None),
            P("section", None, None),
            P("section", None, "fsdp", None),
            P("section", None, None, None),
            P("section", None, None),
            P("section", None, None),
            P("section", None, None),
            P("section", None, None),
            P("section", None, None),
            P("section", None, "fsdp", None),
        ),
        check_vma=False,
    )
```

```python
import functools

import jax
import jax.numpy as jnp
from jax import lax
from jax.experimental import pallas as pl
from jax.experimental.pallas import tpu as pltpu
from jax.sharding import PartitionSpec as P

D = 1536
H = 48
P_SIZE = 64
N = 128
K = 4
DI = 3072
DC = 3328
DIN = 6448
EPSILON = 1e-05
HIGHEST = lax.Precision.HIGHEST
BF16 = jnp.bfloat16
F32 = jnp.float32
Q = 128
LANES = 128


def dot(a, b, dims=((1,), (0,)), precision=None):
    return lax.dot_general(a, b, (dims, ((), ())), preferred_element_type=F32, precision=precision)


def low_dot(a, b, dims=((1,), (0,))):
    return dot(a.astype(BF16), b.astype(BF16), dims)


def fine_dot(a, b, dims=((1,), (0,))):
    return dot(a, b, dims, HIGHEST)


def halves(value):
    high = value.astype(BF16)
    return high, (value - high.astype(F32)).astype(BF16)


def split_dot(a, b, dims=((1,), (0,))):
    (a_high, a_low), (b_high, b_low) = halves(a), halves(b)
    a_axis, b_axis = dims[0][0], dims[1][0]
    both = dot(
        jnp.concatenate([a_high, a_low], axis=a_axis), jnp.concatenate([b_high, b_high], axis=b_axis), dims
    )
    return both + dot(a_high, b_low, dims)


def pair_lanes(table, first, low_half):
    return jnp.where(low_half, table[:, first : first + 1], table[:, first + 1 : first + 2])


def decay_tables(proj_dt, dt_bias, a_row, tri):
    shifted = proj_dt + dt_bias
    step = jnp.maximum(shifted, 0.0) + jnp.log1p(jnp.exp(-jnp.abs(shifted)))
    log_decay = -step * jnp.exp(a_row)
    cumulative = fine_dot(tri, log_decay)
    return shifted, step, log_decay, cumulative


def triangles():
    row = lax.broadcasted_iota(jnp.int32, (Q, Q), 0)
    column = lax.broadcasted_iota(jnp.int32, (Q, Q), 1)
    return row, column


MESH_ID = pl.DeviceIdType.MESH
VMEM_LIMIT = 60 * 1024 * 1024


def remote(src, dst, send_sem, recv_sem, device):
    return pltpu.make_async_remote_copy(
        src_ref=src, dst_ref=dst, send_sem=send_sem, recv_sem=recv_sem, device_id=device, device_id_type=MESH_ID
    )


def greet(devices):
    barrier = pltpu.get_barrier_semaphore()
    count = 0
    for condition, device in devices:
        if condition is None:
            pl.semaphore_signal(barrier, inc=1, device_id=device, device_id_type=MESH_ID)
            count = count + 1
        else:

            @pl.when(condition)
            def _():
                pl.semaphore_signal(barrier, inc=1, device_id=device, device_id_type=MESH_ID)

            count = count + condition.astype(jnp.int32)
    pl.semaphore_wait(barrier, count)


def bits_of(peers):
    return [1 << k for k in range(peers.bit_length() - 1)]


def has_bit(value, bit):
    return (value // bit) % 2


def flip(value, bits):
    bit = 1
    out = value
    while bit <= bits:
        if bits & bit:
            out = out + bit * (1 - 2 * has_bit(value, bit))
        bit = bit * 2
    return out


def to_column(row):
    down, across = triangles()
    return jnp.sum(jnp.where(down == across, jnp.broadcast_to(row, (Q, Q)), 0.0), axis=1, keepdims=True)


def to_row(column, offset=0):
    shape = (column.shape[0], Q)
    down = lax.broadcasted_iota(jnp.int32, shape, 0)
    across = lax.broadcasted_iota(jnp.int32, shape, 1)
    return jnp.sum(jnp.where(across == down + offset, jnp.broadcast_to(column, shape), 0.0), axis=0, keepdims=True)


class GroupTiles:

    def __init__(self, tiles, send_sem, recv_sem, here, peers):
        self.tiles, self.send_sem, self.recv_sem, self.here, self.peers = tiles, send_sem, recv_sem, here, peers

    def copies(self):
        return [
            remote(
                self.tiles.at[0], self.tiles.at[j], self.send_sem.at[j], self.recv_sem.at[j],
                {"dp": flip(self.here, j)},
            )
            for j in range(1, self.peers)
        ]

    def begin(self):
        for copy in self.copies():
            copy.start()

    def finish(self):
        for copy in self.copies():
            copy.wait()
        total = self.tiles[0]
        for j in range(1, self.peers):
            total = total + self.tiles[j]
        return total


def group_tiles(tiles, send_sem, recv_sem, here, peers):
    group = GroupTiles(tiles, send_sem, recv_sem, here, peers)
    group.begin()
    return group.finish()


class GroupRows:

    def __init__(self, where, here, peers, send_sem, recv_sem):
        self.where, self.here, self.peers = where, here, peers
        self.send_sem, self.recv_sem = send_sem, recv_sem

    def part(self, j):
        return self.where(flip(self.here, j))

    def copy(self, j, bit, source=None):
        part = self.part(j)
        return remote(
            part if source is None else source, part, self.send_sem.at[j ^ bit], self.recv_sem.at[j ^ bit],
            {"dp": flip(self.here, bit)},
        )

    def begin(self, source=None):
        for bit in bits_of(self.peers)[::-1]:
            self.copy(0, bit, source).start()

    def phase(self, bit):
        for j in range(bit, self.peers, 2 * bit):
            self.copy(j ^ bit, bit).wait_send()
            landing = self.part(j)
            remote(
                landing, landing, self.send_sem.at[j], self.recv_sem.at[j], {"dp": flip(self.here, bit)}
            ).wait_recv()
            for lower in bits_of(bit)[::-1]:
                self.copy(j, lower).start()

    def relay(self):
        for bit in bits_of(self.peers)[:0:-1]:
            self.phase(bit)

    def close(self):
        self.phase(1)

    def finish(self):
        self.relay()
        self.close()


def rows_of(whole, rows):
    return lambda device: whole.at[pl.ds(pl.multiple_of(device * rows, 8), rows)]


def rms_parts(values):
    return lax.rsqrt(jnp.mean(values * values, axis=-1, keepdims=True) + EPSILON)


class BlockSum:

    def __init__(self, partial, landed, here, peers, send_sem, recv_sem):
        self.partial, self.landed, self.here, self.peers = partial, landed, here, peers
        self.bits = bits_of(peers)
        self.send_sem, self.recv_sem = send_sem, recv_sem

    def copy(self, k, block, owner):
        return remote(
            self.partial.at[block, owner], self.landed.at[k, block, owner // 2], self.send_sem.at[k, block, owner],
            self.recv_sem.at[k, block, owner], {"dp": flip(self.here, self.bits[k])},
        )

    def total(self, block, owner, stages):
        total = self.partial[block, owner].astype(F32)
        for m in range(stages):
            self.copy(m, block, owner).wait_recv()
            total = total + self.landed[m, block, owner // 2].astype(F32)
        return total

    def leaving(self, k):
        return [flip(self.here, j) for j in range(self.bits[k], self.peers, 2 * self.bits[k])]

    def send(self, k, block):
        for owner in self.leaving(k):
            if k > 0:
                self.partial[block, owner] = self.total(block, owner, k).astype(self.partial.dtype)
            self.copy(k, block, owner).start()

    def own(self, block):
        return self.total(block, self.here, len(self.bits))

    def settle(self, blocks):
        for block in range(blocks):
            for k in range(len(self.bits)):
                for owner in self.leaving(k):
                    self.copy(k, block, owner).wait_send()


class Deal:

    def __init__(self, chunk, own, nf, nd, z, d, send_sem, recv_sem, outward):
        self.chunk, self.own, self.nf, self.nd, self.z, self.d = chunk, own, nf, nd, z, d
        self.send_sem, self.recv_sem, self.outward = send_sem, recv_sem, outward
        self.rows = chunk.shape[0] // nd

    def part(self, o):
        return self.chunk.at[pl.ds(pl.multiple_of(o * self.rows, 16), self.rows)]

    def holder(self, b):
        return {"fsdp": b, "dp": self.z}

    def worker(self, o):
        return {"fsdp": self.d, "dp": o}

    def at_home(self, k):
        return (self.z == self.d) & (self.z == k)

    def send(self, k):
        if self.outward:
            return remote(
                self.own.at[k], self.part(self.d), self.send_sem.at[k], self.recv_sem.at[self.d], self.holder(k)
            )
        return remote(
            self.part(k), self.own.at[self.z], self.send_sem.at[k], self.recv_sem.at[self.z], self.worker(k)
        )

    def recv(self, k):
        if self.outward:
            part = self.part(k)
            return remote(part, part, self.send_sem.at[k], self.recv_sem.at[k], self.worker(k))
        part = self.own.at[k]
        return remote(part, part, self.send_sem.at[k], self.recv_sem.at[k], self.holder(k))

    def keep(self, k):
        if self.outward:
            return pltpu.make_async_copy(self.own.at[k], self.part(k), self.send_sem.at[k])
        return pltpu.make_async_copy(self.part(k), self.own.at[k], self.send_sem.at[k])

    def start(self, k):
        @pl.when(self.at_home(k))
        def _():
            self.keep(k).start()

        @pl.when(jnp.logical_not(self.at_home(k)))
        def _():
            self.send(k).start()

    def start_all(self):
        for k in range(self.nf):
            self.start(k)

    def arrive(self):
        for k in range(self.nf):

            @pl.when(self.at_home(k))
            def _():
                self.keep(k).wait()

            @pl.when(jnp.logical_not(self.at_home(k)))
            def _():
                self.recv(k).wait_recv()

    def settle(self):
        for k in range(self.nf):

            @pl.when(jnp.logical_not(self.at_home(k)))
            def _():
                self.send(k).wait_send()


def deal_partners(nf, nd, z, d):
    out = []
    for k in range(nf):
        elsewhere = (z != d) | (z != k)
        out += [(elsewhere, {"fsdp": k, "dp": z}), (elsewhere, {"fsdp": d, "dp": k})]
    return out


class SectionGather:

    def __init__(self, held, section, nf, y, z, sems, own=None):
        self.own = own
        self.held, self.section, self.nf, self.y, self.z, self.sems = held, section, nf, y, z, sems
        width = held.shape[1]
        first = -(-width // 32) * 16
        self.spans = [(0, first), (first, width - first)]
        self.peer = {"section": 1 - y}

    def block(self, b, part):
        start, size = self.spans[part]
        return self.held.at[b, pl.ds(start, size)]

    def each(self, body):
        for part in range(2):
            owner = self.y == self.section

            @pl.when(owner if part == 0 else jnp.logical_not(owner))
            def _():
                body(part)

    def own_part(self, part):
        start, size = self.spans[part]
        return self.own.at[pl.ds(start, size)]

    def send(self, b, part, row, k, landed, device, source=None):
        here = self.block(b, part)
        return remote(
            here if source is None else source, here, self.sems.at[row, k], self.sems.at[landed, k], device
        )

    def right(self, k, b, part, source=None):
        return self.send(b, part, 0, k, 2, {"fsdp": self.z + 1}, source)

    def left(self, k, b, part, source=None):
        return self.send(b, part, 1, k, 3, {"fsdp": self.z - 1}, source)

    def over(self, k, b, part, source=None):
        return self.send(b, part, 4, k, 5, self.peer, source)

    def cross(self):
        here = self.block(self.z, 1)
        return remote(self.own_part(1), here, self.sems.at[6, 0], self.sems.at[6, 1], self.peer)

    def keep(self):
        return pltpu.make_async_copy(self.own, self.held.at[self.z], self.sems.at[6, 2])

    def has_right(self):
        return self.z < self.nf - 1

    def has_left(self):
        return self.z > 0

    def start_cross(self):
        @pl.when(self.y == self.section)
        def _():
            self.cross().start()
            self.keep().start()

    def begin(self):
        def body(part):
            source = None
            if part == 1:
                self.cross().wait_recv()
            else:
                source = self.own_part(0)

            @pl.when(self.has_right())
            def _():
                self.right(1, self.z, part, source).start()

            @pl.when(self.has_left())
            def _():
                self.left(1, self.z, part, source).start()

            if part == 0:
                self.cross().wait_send()
                self.over(0, self.z, 0, source).start()

        self.each(body)

    def settle_begin(self):
        def body(part):
            @pl.when(self.has_right())
            def _():
                self.right(1, self.z, part).wait_send()

            @pl.when(self.has_left())
            def _():
                self.left(1, self.z, part).wait_send()

            if part == 0:
                self.over(0, self.z, 0).wait_send()
                self.keep().wait()
            else:
                self.over(0, self.z, 0).wait_recv()

        self.each(body)

    def sides(self, k, body):
        @pl.when(self.z >= k)
        def _():
            body(self.z - k, k, True)

        @pl.when(self.z + k < self.nf)
        def _():
            body(self.z + k, self.nf + k, False)

    def arrive(self, k):
        def body(part):
            def one(b, index, from_left):
                if from_left:
                    self.right(k, b, part).wait_recv()
                else:
                    self.left(k, b, part).wait_recv()

            self.sides(k, one)

        self.each(body)

    def relay(self, k):
        def body(part):
            def one(b, index, from_left):
                if k < self.nf - 1:
                    if from_left:

                        @pl.when(self.has_right())
                        def _():
                            self.right(k + 1, b, part).start()

                    else:

                        @pl.when(self.has_left())
                        def _():
                            self.left(k + 1, b, part).start()

                self.over(index, b, part).start()

            self.sides(k, one)

        self.each(body)

    def settle(self, k):
        def body(part):
            def one(b, index, from_left):
                self.over(index, b, part).wait_send()
                self.over(index, b, 1 - part).wait_recv()
                if k < self.nf - 1:
                    if from_left:

                        @pl.when(self.has_right())
                        def _():
                            self.right(k + 1, b, part).wait_send()

                    else:

                        @pl.when(self.has_left())
                        def _():
                            self.left(k + 1, b, part).wait_send()

            self.sides(k, one)

        self.each(body)


class OutGather:

    def __init__(self, source, held, section, nf, y, z, d, sems, staged):
        self.staged = staged
        self.source, self.held, self.section, self.nf = source, held, section, nf
        self.y, self.z, self.d, self.sems = y, z, d, sems
        self.pieces = sems.shape[1]
        self.rows = source.shape[0] // self.pieces
        self.columns = source.shape[1] // 2
        self.peer = {"section": 1 - y}
        self.source_here = z == d

    def owner(self):
        return self.y == self.section

    def piece(self, ref, part, i):
        return ref.at[pl.ds(i * self.rows, self.rows), pl.ds(part * self.columns, self.columns)]

    def send(self, i, part, row, landed, device, source=None):
        target = self.piece(self.held, part, i)
        return remote(
            target if source is None else self.piece(source, part, i), target, self.sems.at[row, i],
            self.sems.at[landed, i], device,
        )

    def right(self, i, part, source=None):
        return self.send(i, part, 0, 2, {"fsdp": self.z + 1}, source)

    def left(self, i, part, source=None):
        return self.send(i, part, 1, 2, {"fsdp": self.z - 1}, source)

    def over(self, i, part, source=None):
        return self.send(i, part, 3, 4, self.peer, source)

    def cross(self):
        columns = pl.ds(self.columns, self.columns)
        return remote(
            self.source.at[:, columns], self.held.at[:, columns], self.sems.at[5, 0], self.sems.at[5, 1], self.peer
        )

    def stage(self):
        return pltpu.make_async_copy(self.source, self.staged, self.sems.at[5, 2])

    def keep(self):
        return pltpu.make_async_copy(self.staged, self.held, self.sems.at[5, 3])

    def goes_right(self):
        return (self.z >= self.d) & (self.z < self.nf - 1)

    def goes_left(self):
        return (self.z <= self.d) & (self.z > 0)

    def each(self, condition, body):
        for part in range(2):
            mine = self.owner() if part == 0 else jnp.logical_not(self.owner())

            @pl.when(condition & mine)
            def _():
                body(part)

    def along(self, i, part, action, source=None):
        @pl.when(self.goes_right())
        def _():
            action(self.right(i, part, source))

        @pl.when(self.goes_left())
        def _():
            action(self.left(i, part, source))

    def begin(self):
        @pl.when(self.source_here & self.owner())
        def _():
            self.cross().start()
            self.stage().start()
            for i in range(self.pieces):
                self.along(i, 0, lambda copy: copy.start(), self.source)

    def begin_other(self):
        @pl.when(self.source_here & jnp.logical_not(self.owner()))
        def _():
            self.cross().wait_recv()
            for i in range(self.pieces):
                self.along(i, 1, lambda copy: copy.start())

    def hops(self, distance):
        def body(part):
            for i in range(self.pieces):
                self.right(i, part).wait_recv()
                self.along(i, part, lambda copy: copy.start())

        self.each((self.z == self.d + distance) | (self.z == self.d - distance), body)

    def hand_over(self):
        @pl.when(self.source_here & self.owner())
        def _():
            self.stage().wait()
            self.keep().start()
            for i in range(self.pieces):
                self.over(i, 0, self.source).start()

        def body(part):
            for i in range(self.pieces):
                self.over(i, part).start()

        self.each(jnp.logical_not(self.source_here), body)

    def settle(self):
        @pl.when(self.source_here & self.owner())
        def _():
            self.cross().wait_send()
            self.keep().wait()

        def at_source(part):
            for i in range(self.pieces):
                self.along(i, part, lambda copy: copy.wait_send())
                if part == 0:
                    self.over(i, 0).wait_send()
                else:
                    self.over(i, 0).wait_recv()

        def elsewhere(part):
            for i in range(self.pieces):
                self.along(i, part, lambda copy: copy.wait_send())
                self.over(i, part).wait_send()
                self.over(i, 1 - part).wait_recv()

        self.each(self.source_here, at_source)
        self.each(jnp.logical_not(self.source_here), elsewhere)


def line_neighbours(nf, y, z):
    return [
        (None, {"section": 1 - y}),
        (z < nf - 1, {"fsdp": z + 1}),
        (z > 0, {"fsdp": z - 1}),
    ]


class SectionSum:

    def __init__(self, view, nf, y, z, own, landed, chain, sems, result):
        self.view, self.nf, self.y, self.z, self.result = view, nf, y, z, result
        self.own, self.landed, self.chain = own, landed, chain
        self.load_sem, self.over_send, self.over_recv, self.chain_send, self.chain_recv = (
            sems.at[0], sems.at[1], sems.at[2], sems.at[3], sems.at[4]
        )
        self.part_rows = own.shape[1]

    def load(self, block):
        return pltpu.make_async_copy(self.view(block, self.y), self.own.at[block], self.load_sem.at[block])

    def over(self, block):
        return remote(
            self.view(block, 1 - self.y), self.landed.at[block], self.over_send.at[block], self.over_recv.at[block],
            {"section": 1 - self.y},
        )

    def right(self, block):
        return remote(
            self.own.at[block], self.chain.at[block], self.chain_send.at[block], self.chain_recv.at[block],
            {"fsdp": self.z + 1},
        )

    def left(self, block, arrives):
        slot = self.nf if arrives else block
        return remote(
            self.own.at[block], self.chain.at[slot], self.chain_send.at[block], self.chain_recv.at[slot],
            {"fsdp": self.z - 1},
        )

    def at(self, k, body):
        if k == 0:
            body(self.z, False)
            return

        @pl.when(self.z + k < self.nf)
        def _():
            body(self.z + k, True)

        @pl.when(self.z - k >= 0)
        def _():
            body(self.z - k, False)

    def begin(self):
        self.at(self.nf - 1, lambda block, rightward: self.over(block).start())
        for k in range(self.nf - 1, -1, -1):
            self.at(k, lambda block, rightward: self.load(block).start())

    def add(self, block, sources, target):
        step = 32

        def some(i, carry):
            rows = pl.ds(pl.multiple_of(i * step, 16), step)
            total = self.own[block, rows, :].astype(F32)
            for ref, slot in sources:
                total = total + ref[slot, rows, :].astype(F32)
            if target is None:
                self.own[block, rows, :] = total.astype(BF16)
            else:
                target[rows, :] = total.astype(BF16)
            return carry

        lax.fori_loop(0, self.part_rows // step, some, 0)

    def ready(self, block):
        self.load(block).wait()
        self.over(block).wait_recv()

    def stage(self, k):
        z, nf = self.z, self.nf
        self.at(k, lambda block, rightward: self.ready(block))
        self.at(k - 1, lambda block, rightward: self.over(block).start())

        def one(block, rightward):
            far_end = z == 0 if rightward else z == nf - 1
            arrived = self.right(block) if rightward else self.left(block, False)
            leaving = self.right(block) if rightward else self.left(block, k == 1)

            @pl.when(jnp.logical_not(far_end))
            def _():
                arrived.wait_recv()
                self.add(block, [(self.landed, block), (self.chain, block)], None)

            @pl.when(far_end)
            def _():
                self.add(block, [(self.landed, block)], None)

            leaving.start()

        self.at(k, one)

    def finish(self):
        z, nf, target = self.z, self.nf, self.result
        self.ready(z)

        @pl.when(z > 0)
        def _():
            self.right(z).wait_recv()

        @pl.when(z < nf - 1)
        def _():
            self.left(z, True).wait_recv()

        @pl.when(z == 0)
        def _():
            self.add(z, [(self.landed, z), (self.chain, nf)], target)

        @pl.when(z == nf - 1)
        def _():
            self.add(z, [(self.landed, z), (self.chain, z)], target)

        @pl.when((z > 0) & (z < nf - 1))
        def _():
            self.add(z, [(self.landed, z), (self.chain, z), (self.chain, nf)], target)

    def settle(self):
        z, nf = self.z, self.nf
        self.over(z).wait_send()
        for k in range(nf - 1, 0, -1):

            @pl.when(z + k < nf)
            def _():
                self.over(z + k).wait_send()
                self.right(z + k).wait_send()

            @pl.when(z - k >= 0)
            def _():
                self.over(z - k).wait_send()
                self.left(z - k, k == 1).wait_send()


def in_parts(width):
    rows = -(-width // 64) * 32
    return rows, width - rows


def in_view(source, nf):
    rows, second = in_parts(source.shape[-2])

    def view(block, part):
        here = pl.ds(pl.multiple_of(part * second, 16), rows)
        if len(source.shape) == 3:
            return source.at[block, here]
        columns = source.shape[1] // nf
        return source.at[here, pl.ds(pl.multiple_of(block * columns, LANES), columns)]

    return view


def out_view(source, nf):
    rows, columns = source.shape[0] // nf, source.shape[1] // 2

    def view(block, part):
        here = pl.ds(pl.multiple_of(block * rows, 16), rows)
        return source.at[here, pl.ds(pl.multiple_of(part * columns, LANES), columns)]

    return view


def in_part_shape(nf, source):
    columns = source.shape[2] if len(source.shape) == 3 else source.shape[1] // nf
    return in_parts(source.shape[-2])[0], columns


def out_part_shape(nf, source):
    return source.shape[0] // nf, source.shape[1] // 2


def section_sum_scratch(nf, part):
    return [
        pltpu.VMEM((nf,) + part, BF16),
        pltpu.VMEM((nf,) + part, BF16),
        pltpu.VMEM((nf + 1,) + part, BF16),
        pltpu.SemaphoreType.DMA((5, nf + 1)),
        pltpu.VMEM(part, BF16),
    ]


class SectionReturn:

    def __init__(self, piece, place, owner, y, sems):
        self.piece, self.place, self.owner, self.y, self.sems = piece, place, owner, y, sems

    def keep(self):
        return pltpu.make_async_copy(self.piece(self.owner), self.place(self.owner), self.sems.at[2])

    def send(self):
        other = 1 - self.owner
        return remote(
            self.piece(other), self.place(other), self.sems.at[0], self.sems.at[1], {"section": 1 - self.y}
        )

    def begin(self):
        @pl.when(self.y == self.owner)
        def _():
            self.keep().start()

        @pl.when(self.y != self.owner)
        def _():
            self.send().start()

    def finish(self):
        @pl.when(self.y == self.owner)
        def _():
            self.keep().wait()
            self.send().wait_recv()

        @pl.when(self.y != self.owner)
        def _():
            self.send().wait_send()


def end_kernel(
    nf, nd,
    in_ref, in_part1_ref, out_part0_ref, out_part1_ref, small0_ref, small1_ref,
    in_all, out_all, small_all,
    in_own, in_landed, in_chain, in_sems, in_part,
    in_final, out_final, small_slots, small_total, local_sem, swap_sem, back_sem, small_sems, group_send, group_recv,
):
    y, z, d = lax.axis_index("section"), lax.axis_index("fsdp"), lax.axis_index("dp")
    away = z != d
    twin = {"fsdp": d, "dp": z}
    peer = {"section": 1 - y}
    wide = lambda k: {"fsdp": (z + k) % nf}
    greet(
        [(None, peer), (away, twin)]
        + [(None, wide(k)) for k in range(1, nf)]
        + [(None, {"dp": flip(d, bit)}) for bit in bits_of(nd)]
    )
    in_sum = SectionSum(in_view(in_ref, nf), nf, y, z, in_own, in_landed, in_chain, in_sems, in_part)
    width = in_final.shape[0]
    part_rows, second = in_parts(width)
    overlap = part_rows - second
    out_rows, out_columns = out_part0_ref.shape
    in_piece = lambda ref: lambda p: ref if p == 0 else ref.at[pl.ds(overlap, width - part_rows)]
    in_place = lambda p: in_final.at[pl.ds(p * part_rows, width - part_rows if p else part_rows)]
    out_place = lambda p: out_final.at[:, pl.ds(p * out_columns, out_columns)]
    out_returns = [
        SectionReturn(lambda p: out_part0_ref, out_place, 0, y, back_sem.at[0]),
        SectionReturn(lambda p: out_part1_ref, out_place, 1, y, back_sem.at[1]),
    ]
    in_returns = [
        SectionReturn(in_piece(in_part), in_place, 0, y, back_sem.at[2]),
        SectionReturn(in_piece(in_part1_ref), in_place, 1, y, back_sem.at[3]),
    ]
    in_groups = [
        GroupRows(
            lambda device, p=p: in_all.at[device, pl.ds(p * part_rows, width - part_rows if p else part_rows)],
            d, nd, group_send.at[p], group_recv.at[p],
        )
        for p in range(2)
    ]
    out_group = GroupRows(rows_of(out_all, out_rows), d, nd, group_send.at[2], group_recv.at[2])
    small_group = GroupRows(lambda device: small_all.at[device], d, nd, group_send.at[3], group_recv.at[3])

    def small_over(ref):
        return remote(ref, small_slots.at[nf], small_sems.at[0, 0], small_sems.at[1, 0], peer)

    def small_load(ref):
        return pltpu.make_async_copy(ref, small_slots.at[0], local_sem.at[0])

    small_copies = [
        remote(small_slots.at[0], small_slots.at[k], small_sems.at[0, k], small_sems.at[1, k], wide(k))
        for k in range(1, nf)
    ]
    small_own = pltpu.make_async_copy(small_total, small_group.part(0), local_sem.at[0])
    swap_target = out_all.at[pl.ds(pl.multiple_of(z * out_rows, 16), out_rows)]
    swap = remote(out_final, swap_target, swap_sem.at[0], swap_sem.at[1], twin)
    stay = pltpu.make_async_copy(out_final, out_group.part(0), swap_sem.at[2])

    def own_copy(p):
        return pltpu.make_async_copy(in_place(p), in_groups[p].part(0), local_sem.at[1 + p])

    def spread(p):
        own_copy(p).start()
        in_groups[p].begin(in_place(p))

    for back in out_returns:
        back.begin()
    in_sum.begin()
    for section, (mine, other) in enumerate(((small0_ref, small1_ref), (small1_ref, small0_ref))):

        @pl.when(y == section)
        def _():
            small_over(other).start()
            small_load(mine).start()


    @pl.when(y == 1)
    def _():
        in_returns[1].keep().start()
        in_returns[1].keep().wait()
        spread(1)

    for back in out_returns:
        back.finish()

    @pl.when(away)
    def _():
        swap.start()

    @pl.when(jnp.logical_not(away))
    def _():
        stay.start()

    for k in range(nf - 1, 0, -1):
        in_sum.stage(k)
        if k == nf - 1:
            small_load(small0_ref).wait()
            small_over(small0_ref).wait()
            small_slots[0] = small_slots[0] + small_slots[nf]
            for copy in small_copies:
                copy.start()

            @pl.when(away)
            def _():
                swap.wait()

            @pl.when(jnp.logical_not(away))
            def _():
                stay.wait()

            out_group.begin()
        if k == nf - 2:
            for copy in small_copies:
                copy.wait()
            total = small_slots[0]
            for j in range(1, nf):
                total = total + small_slots[j]
            small_total[...] = total
            small_own.start()
            small_group.begin(small_total)
            out_group.relay()
        if k == 1:
            small_group.finish()
            small_own.wait()
            out_group.close()
    in_sum.finish()

    @pl.when(y == 0)
    def _():
        in_returns[0].keep().start()
        in_returns[1].send().start()
        in_returns[0].keep().wait()
        spread(0)
        in_returns[0].send().wait_recv()
        spread(1)
        in_returns[1].send().wait_send()

    @pl.when(y == 1)
    def _():
        in_returns[0].send().start()
        in_returns[1].send().wait_recv()
        spread(0)
        in_returns[0].send().wait_send()

    for p in range(2):
        in_groups[p].finish()
        own_copy(p).wait()
    in_sum.settle()


def run_end(nf, nd, in_grad, in_part1, out_part0, out_part1, small0, small1):
    anywhere = pl.BlockSpec(memory_space=pl.ANY)
    dma = pltpu.SemaphoreType.DMA
    width = in_grad.shape[-2]
    out_rows = out_part0.shape[0]
    return pl.pallas_call(
        functools.partial(end_kernel, nf, nd),
        in_specs=[anywhere] * 6,
        out_specs=[anywhere] * 3,
        out_shape=[
            jax.ShapeDtypeStruct((nd, width, in_part1.shape[1]), BF16),
            jax.ShapeDtypeStruct((nd * out_rows, D), BF16),
            jax.ShapeDtypeStruct((nd,) + small0.shape, F32),
        ],
        scratch_shapes=section_sum_scratch(nf, in_part1.shape)
        + [
            pltpu.VMEM((width, in_part1.shape[1]), BF16),
            pltpu.VMEM((out_rows, D), BF16),
            pltpu.VMEM((nf + 1,) + small0.shape, F32),
            pltpu.VMEM(small0.shape, F32),
            dma((3,)),
            dma((3,)),
            dma((4, 3)),
            dma((2, nf)),
            dma((4, nd)),
            dma((4, nd)),
        ],
        compiler_params=pltpu.CompilerParams(
            vmem_limit_bytes=VMEM_LIMIT, collective_id=6, has_side_effects=True
        ),
        name="sum_end",
    )(in_grad, in_part1, out_part0, out_part1, small0, small1)


def finish_kernel(
    ch, nd, in_ref, shared_ref, out_ref, small_ref,
    in_total, out_total, gain_ref, convw_ref, convb_ref, dtb_ref, alog_ref, skip_ref, gate_ref, shared, sems,
):
    step = pl.program_id(0)
    heads = H // nd
    count = DIN - 2 * DI

    def copy(j):
        return pltpu.make_async_copy(shared_ref.at[j, pl.ds(2 * ch, count)], shared.at[j], sems.at[j])

    @pl.when(step == 0)
    def _():
        for j in range(nd):
            copy(j).start()
        for row, (start, size) in enumerate(gain_rows(small_ref.shape[2])):
            gain_ref[:, start : start + size] = jnp.sum(small_ref[:, 8 + row : 9 + row, 0:size], axis=0)
        both = jnp.sum(small_ref[:, 0:8, ch:], axis=0)
        convw_ref[:, DI:] = both[0:4, :]
        convb_ref[:, DI:] = both[4:5, :]
        rows = lax.broadcasted_iota(jnp.int32, (ch, LANES), 0)
        columns = lax.broadcasted_iota(jnp.int32, (ch, LANES), 1)
        by_head = jnp.where(rows // P_SIZE == columns, 1.0, 0.0)
        decays, skips = [[], []], []
        for j in range(nd):
            here = slice(j * ch, (j + 1) * ch)
            convw_ref[:, here] = small_ref[j, 0:4, :ch]
            convb_ref[:, here] = small_ref[j, 4:5, :ch]
            gate_ref[:, here] = small_ref[j, 5:6, :ch]
            skips.append(fine_dot(small_ref[j, 0:8, :ch], by_head)[6:7, :heads])
            for k in range(2):
                decays[k].append(small_ref[j, 7:8, k * LANES : k * LANES + heads])
        dtb_ref[...] = jnp.concatenate(decays[0], axis=1)
        alog_ref[...] = jnp.concatenate(decays[1], axis=1)
        skip_ref[...] = jnp.concatenate(skips, axis=1)

    @pl.when(step < 2 * nd)
    def _():
        in_total[...] = in_ref[...].astype(F32)
        out_total[...] = out_ref[...].astype(F32)

    @pl.when(step == 2 * nd)
    def _():
        for j in range(nd):
            copy(j).wait()
        total = shared[0].astype(F32)
        for j in range(1, nd):
            total = total + shared[j].astype(F32)
        in_total[0:count, :] = total


def run_finish(ch, nd, in_all, out_all, small_all):
    columns = in_all.shape[2]
    rows = out_all.shape[0]
    piece = rows // (2 * nd)
    final = lambda s: (jnp.minimum(s, 2 * nd - 1), 0)

    def in_block(s):
        s = jnp.minimum(s, 2 * nd - 1)
        return (s % nd, s // nd, 0)

    smalls = [(1, D), (K, DC), (1, DC), (1, H), (1, H), (1, H), (1, DI)]
    return pl.pallas_call(
        functools.partial(finish_kernel, ch, nd),
        grid=(2 * nd + 1,),
        in_specs=[
            pl.BlockSpec((None, ch, columns), in_block),
            pl.BlockSpec(memory_space=pl.ANY),
            pl.BlockSpec((piece, D), final),
            once(small_all.shape),
        ],
        out_specs=[pl.BlockSpec((ch, columns), lambda s: (s, 0)), pl.BlockSpec((piece, D), final)]
        + [once(shape) for shape in smalls],
        out_shape=[jax.ShapeDtypeStruct((DIN, columns), F32), jax.ShapeDtypeStruct((rows, D), F32)]
        + [jax.ShapeDtypeStruct(shape, F32) for shape in smalls],
        scratch_shapes=[pltpu.VMEM((nd, DIN - 2 * DI, columns), BF16), pltpu.SemaphoreType.DMA((nd,))],
        compiler_params=pltpu.CompilerParams(vmem_limit_bytes=VMEM_LIMIT),
        name="finish",
    )(in_all, in_all, out_all, small_all)


class Weights:

    def __init__(self, source, held, sems):
        self.source, self.held, self.sems = source, held, sems
        self.blocks = source.shape[0]
        self.columns = source.shape[2]

    def copies(self):
        out = []
        for k in range(self.blocks):
            if len(self.held.shape) == 3:
                target = self.held.at[k]
            else:
                target = self.held.at[:, pl.ds(k * self.columns, self.columns)]
            out.append(pltpu.make_async_copy(self.source.at[k], target, self.sems.at[k]))
        return out

    def forward(self, rows):
        if len(self.held.shape) == 2:
            return dot(rows, self.held[...], ((1,), (1,)))
        total = 0.0
        for k in range(self.blocks):
            total = total + dot(
                rows[:, k * self.columns : (k + 1) * self.columns], self.held[k], ((1,), (1,))
            )
        return total

    def backward(self, rows):
        if len(self.held.shape) == 2:
            return dot(rows, self.held[...])
        return jnp.concatenate([dot(rows, self.held[k]) for k in range(self.blocks)], axis=1)


def held_shape(w_in):
    blocks, width, columns = w_in.shape
    return (width, blocks * columns) if columns % LANES == 0 else (blocks, width, columns)


def own_steps(steps, turn):
    padded = jnp.concatenate([steps, jnp.zeros((steps.shape[0], LANES - H), F32)], axis=1)
    return pltpu.roll(padded, LANES - turn, 1)


def mix_forward(
    ch, proj_ref, meta_ref, segrow_ref, conv_w_ref, conv_b_ref, dtb_ref, alog_ref, skip_ref,
    gated_ref, square_ref, mixed_ref, pre_ref, state_out_ref, pad, state, sub, turn,
):
    conv_width = ch + 2 * N
    rows = pl.ds(pl.multiple_of(sub * Q, Q), Q)
    meta = meta_ref[rows, :]
    pad[8:, :] = proj_ref[rows, ch : ch + conv_width]
    pre = conv_b_ref[...] + conv_w_ref[3:4, :] * pad[8:, :]
    for lag in range(1, K):
        pre = pre + (conv_w_ref[3 - lag : 4 - lag, :] * meta[:, lag : lag + 1]) * pad[8 - lag : 8 - lag + Q, :]
    pad[0:8, :] = pad[Q : Q + 8, :]
    pre_ref[rows, :] = pre
    conv_out = pre * jax.nn.sigmoid(pre)
    values = conv_out[:, :ch]
    b_part = conv_out[:, ch : ch + N]
    c_part = conv_out[:, ch + N :]
    row, column = triangles()
    tri = jnp.where(row >= column, 1.0, 0.0)
    shifted, step, log_decay, cumulative = decay_tables(
        own_steps(proj_ref[rows, ch + conv_width :], turn), dtb_ref[...], alog_ref[...], tri
    )
    linked = (row >= column) & (meta[:, 0:1] == segrow_ref[sub])
    inner = jnp.where(linked, split_dot(c_part, b_part, ((1,), (1,))), 0.0)
    cum_t = cumulative.T
    step_t = step.T
    last = cumulative[Q - 1 : Q, :]
    entry = meta[:, 4:5] * jnp.exp(cumulative)
    weight = meta[:, 5:6] * jnp.exp(last - cumulative) * step
    state_in = state[...]
    state_out_ref[sub] = state_in
    carried = split_dot(c_part, state_in)
    low_half = lax.broadcasted_iota(jnp.int32, (Q, LANES), 1) < P_SIZE
    squares = jnp.zeros((Q, 1), F32)
    weighted = []
    entries = []
    values_high, values_low = halves(values)
    for pair in range(ch // LANES):
        lanes = slice(pair * LANES, (pair + 1) * LANES)
        values_pair = values[:, lanes]
        mats = []
        for head in (2 * pair, 2 * pair + 1):
            spread = jnp.minimum(cumulative[:, head : head + 1] - cum_t[head : head + 1, :], 0.0)
            mats.append((inner * jnp.exp(spread) * step_t[head : head + 1, :]).astype(BF16))
        parts = [values_high[:, lanes], values_low[:, lanes]]
        zero = jnp.zeros_like(parts[0])
        stacked = jnp.concatenate(
            [
                jnp.concatenate([jnp.where(low_half, part, zero) for part in parts], axis=1),
                jnp.concatenate([jnp.where(low_half, zero, part) for part in parts], axis=1),
            ],
            axis=0,
        )
        both = dot(jnp.concatenate(mats, axis=1), stacked)
        out = both[:, :LANES] + both[:, LANES:]
        entry_pair = pair_lanes(entry, 2 * pair, low_half)
        out = out + entry_pair * carried[:, lanes] + skip_ref[:, lanes] * values_pair
        mixed_ref[rows, lanes] = out
        gate = proj_ref[rows, lanes]
        gated = out * (gate * jax.nn.sigmoid(gate))
        squares = squares + jnp.sum(gated * gated, axis=1, keepdims=True)
        gated_ref[rows, lanes] = gated
        weighted.append(pair_lanes(weight, 2 * pair, low_half) * values_pair)
        entries.append(entry_pair[Q - 1 : Q, :])
    square_ref[0, pl.ds(sub, 1), :] = to_row(squares)
    state[...] = jnp.concatenate(entries, axis=1) * state_in + split_dot(
        b_part.T, jnp.concatenate(weighted, axis=1)
    )


def first_kernel(
    ch, nf, nd,
    x_ref, cot_ref, seg_ref, in_ref, out_ref, conv_w_ref, conv_b_ref, norm_ref, gate_ref, head_ref,
    proj_ref, mixed_ref, pre_ref, state_out_ref, nout_ref, branch_ref, next_ref, ratio_ref,
    conv_w_out, conv_b_out, dtb_out, alog_out, skip_out, gain_out, norm_out, meta_out, segrow_out,
    normed_all, moved_ref, hidden_out, cot_own, w_in0, w_in1, w_out0, w_out1,
    held, w_out, pad, state, gated, partial, landed, squares, low, normed, x_low, table, seg_all, own_block, staged,
    sum_send, sum_recv, tile_send, tile_recv, group_send, group_recv, start_send, start_recv, deal_send, deal_recv,
    in_sems0, in_sems1, out_sems0, out_sems1, local_sem, load_sem, small_sem, swap_sem, own_sem,
):
    step = pl.program_id(0)
    y, z, d = lax.axis_index("section"), lax.axis_index("fsdp"), lax.axis_index("dp")
    block = proj_ref.shape[0]
    subs = block // Q
    rows = block // nd
    length = block * nf
    lines = block // Q * 8
    heads = H // nd
    bits = bits_of(nd)
    twin = {"fsdp": d, "dp": z}
    home = z == d
    away = z != d
    peer = {"section": 1 - y}
    blocks = BlockSum(partial, landed, d, nd, sum_send, sum_recv)
    weights = Weights(w_in0, held, load_sem)
    out_load = pltpu.make_async_copy(w_out0, w_out, local_sem.at[0])
    gathers = [SectionGather(w_in0, 0, nf, y, z, in_sems0, own_block), SectionGather(w_in1, 1, nf, y, z, in_sems1, own_block)]
    outs = [
        OutGather(out_ref, w_out0, 0, nf, y, z, d, out_sems0, staged),
        OutGather(out_ref, w_out1, 1, nf, y, z, d, out_sems1, staged),
    ]
    enter = Deal(x_ref.at[y], x_low, nf, nd, z, d, deal_send.at[0], deal_recv.at[0], False)
    enter_cot = Deal(cot_ref.at[y], cot_own, nf, nd, z, d, deal_send.at[1], deal_recv.at[1], False)
    first_group = GroupRows(lambda device: normed.at[:, device], d, nd, start_send.at[0], start_recv.at[0])
    normed_copy = pltpu.make_async_copy(normed, normed_all, local_sem.at[1])
    hidden_copy = pltpu.make_async_copy(x_low, hidden_out, local_sem.at[2])

    def seg_rows(device):
        return seg_all.at[pl.ds(pl.multiple_of(device * lines, 8), lines)]

    seg_group = GroupRows(seg_rows, d, nd, start_send.at[1], start_recv.at[1])

    def every(place):
        return GroupRows(lambda device: moved_ref.at[place, device], d, nd, group_send.at[place], group_recv.at[place])

    def mine(place):
        return pltpu.make_async_copy(low.at[place], moved_ref.at[place, d], local_sem.at[3 + place])

    def stage(gather, k):
        gather.arrive(k)
        gather.relay(k)

    @pl.when(step == 0)
    def _():
        greet(
            line_neighbours(nf, y, z)
            + [(away, twin)]
            + deal_partners(nf, nd, z, d)
            + [(None, {"dp": flip(d, j)}) for j in range(1, nd)]
        )

        own_copies = [
            pltpu.make_async_copy(
                in_ref.at[pl.ds(pl.multiple_of(begin, 16), count)], own_block.at[pl.ds(spot, count)], own_sem.at[k]
            )
            for k, (begin, spot, count) in enumerate(
                [(d * ch, 0, ch), (DI + d * ch, ch, ch), (2 * DI, 2 * ch, DIN - 2 * DI)]
            )
        ]
        for copy in own_copies:
            copy.start()
        for copy in own_copies:
            copy.wait()
        gathers[0].start_cross()
        gathers[1].start_cross()
        table[y, 0:4, :] = conv_w_ref[...]
        table[y, 4:5, :] = conv_b_ref[...]
        table[y, 5:6, 0:D] = norm_ref[...]
        table[y, 6:7, 0:DI] = gate_ref[...]
        for k in range(3):
            table[y, 7:8, k * LANES : (k + 1) * LANES] = head_ref[k : k + 1, :]
        small_copy = remote(table.at[y], table.at[y], small_sem.at[0], small_sem.at[1], peer)
        small_copy.start()
        seg_swap = remote(seg_ref, seg_rows(z), swap_sem.at[0], swap_sem.at[1], twin)
        seg_stay = pltpu.make_async_copy(seg_ref, seg_rows(d), swap_sem.at[0])

        @pl.when(away)
        def _():
            seg_swap.start()

        @pl.when(home)
        def _():
            seg_stay.start()

        gathers[0].begin()
        enter.start_all()
        outs[0].begin()
        stage(gathers[0], 1)
        outs[0].begin_other()
        outs[0].hops(1)

        small_copy.wait()
        enter.arrive()
        hidden_copy.start()
        values = x_low[...].astype(F32)
        low[...] = (values * rms_parts(values) * table[0, 5:6, 0:D]).astype(BF16)
        for place in range(nf):
            normed[place, d] = low[place]
        first_group.begin(low)

        @pl.when(away)
        def _():
            seg_swap.wait()

        @pl.when(home)
        def _():
            seg_stay.wait()

        seg_group.begin()
        for k in range(2, nf - 1):
            stage(gathers[0], k)
            outs[0].hops(k)

        turn = d * heads
        low_half = lax.broadcasted_iota(jnp.int32, (1, LANES), 1) < P_SIZE
        channels = pl.ds(pl.multiple_of(d * ch, LANES), ch)
        for section in range(2):
            conv_w_out[section, :, 0:ch] = table[section, 0:4, channels]
            conv_w_out[section, :, ch:] = table[section, 0:4, DI:DC]
            conv_b_out[section, :, 0:ch] = table[section, 4:5, channels]
            conv_b_out[section, :, ch:] = table[section, 4:5, DI:DC]
            norm_out[section] = table[section, 5:6, 0:D]
            gain_out[section] = table[section, 6:7, channels]
            head_rows = [
                pltpu.roll(table[section, :, k * LANES : (k + 1) * LANES], LANES - turn, 1)[7:8, :] for k in range(3)
            ]
            dtb_out[section] = head_rows[0]
            alog_out[section] = head_rows[1]
            for pair in range(ch // LANES):
                skip_out[section, :, pair * LANES : (pair + 1) * LANES] = pair_lanes(head_rows[2], 2 * pair, low_half)

        seg_group.finish()

        lane = lax.broadcasted_iota(jnp.int32, (8, LANES), 1)
        sub_lane = lax.broadcasted_iota(jnp.int32, (Q, LANES), 1)
        before = jnp.full((8, LANES), -1.0, F32)
        for chunk in range(length // Q):
            now = seg_all[chunk * 8 : chunk * 8 + 8, :]
            segrow_out[chunk] = now[0:1, :]
            columns = [now[0:1, :]]
            for lag in range(1, K):
                earlier = jnp.where(lane < lag, pltpu.roll(before, lag, 1), pltpu.roll(now, lag, 1))
                columns.append(jnp.where(earlier == now, 1.0, 0.0)[0:1, :])
            columns.append(jnp.where(now == before[:, Q - 1 : Q], 1.0, 0.0)[0:1, :])
            columns.append(jnp.where(now == now[:, Q - 1 : Q], 1.0, 0.0)[0:1, :])
            masks = jnp.zeros((Q, LANES), F32)
            for j, row in enumerate(columns):
                masks = jnp.where(sub_lane == j, to_column(row), masks)
            meta_out[chunk * Q : (chunk + 1) * Q, :] = masks
            before = now

        stage(gathers[0], nf - 1)
        outs[0].hops(nf - 1)
        outs[0].hand_over()
        gathers[1].begin()
        first_group.finish()
        normed_copy.start()
        pad[0:8, :] = jnp.zeros((8, pad.shape[1]), F32)
        state[...] = jnp.zeros_like(state)
        for k in range(1, nf):
            gathers[0].settle(k)
        gathers[0].settle_begin()
        for copy in weights.copies():
            copy.start()
        for copy in weights.copies():
            copy.wait()

    def tile(place):
        return GroupTiles(squares.at[place], tile_send.at[place], tile_recv.at[place], d, nd)

    def project(place):
        ratio = lax.rsqrt(tile(place).finish() * (1.0 / DI) + EPSILON)
        for sub in range(subs):
            piece = place * subs + sub
            ratio_ref[pl.ds(piece, 1), :] = ratio[sub : sub + 1, :]
            normed_out = gated[place % 2, sub * Q : (sub + 1) * Q, :] * to_column(ratio[sub : sub + 1, :])
            nout_ref[pl.ds(pl.multiple_of(piece * Q, Q), Q), :] = (normed_out * gain_out[0]).astype(BF16)
        here_rows = pl.ds(pl.multiple_of(place * block, Q), block)
        product = dot(nout_ref[here_rows, :], w_out[...])
        for o in range(nd):
            partial[place, o] = product[o * rows : (o + 1) * rows, :]
        blocks.send(0, place)

    def pass_on(place):
        for k in range(1, len(bits)):
            blocks.send(k, place)

    def conclude(place):
        branch = blocks.own(place)
        branch_ref[place] = branch
        moved = (x_low[place].astype(F32) + branch).astype(BF16)
        next_ref[place] = moved
        values = moved.astype(F32)
        low[place] = (values * rms_parts(values) * norm_out[1]).astype(BF16)
        mine(place).start()
        every(place).begin(low.at[place])

    proj_ref[...] = weights.forward(normed[step].reshape(block, D))

    @pl.when(step == 0)
    def _():
        stage(gathers[1], 1)

    @pl.when(step == 1)
    def _():
        outs[0].settle()
        out_load.start()
        out_load.wait()

    @pl.when(step >= 1)
    def _():
        project(step - 1)

    meta = meta_out.at[pl.ds(pl.multiple_of(step * block, Q), block)]
    segrow = segrow_out.at[pl.ds(step * subs, subs)]

    def one_chunk(sub, carry):
        mix_forward(
            ch, proj_ref, meta, segrow, conv_w_out.at[0], conv_b_out.at[0], dtb_out.at[0], alog_out.at[0],
            skip_out.at[0], gated.at[step % 2], squares.at[step], mixed_ref, pre_ref, state_out_ref, pad, state, sub,
            d * heads,
        )

        @pl.when(sub == 0)
        def _():
            @pl.when(step >= 2)
            def _():
                conclude(step - 2)

            @pl.when(step >= 1)
            def _():
                pass_on(step - 1)

            @pl.when(step >= 3)
            def _():
                every(step - 3).relay()

            for k in range(2, nf):

                @pl.when(step == k - 1)
                def _():
                    stage(gathers[1], k)


        return carry

    lax.fori_loop(0, subs, one_chunk, 0)
    tile(step).begin()

    @pl.when(step == 1)
    def _():
        outs[1].begin()

    @pl.when(step == nf - 2)
    def _():
        enter_cot.start_all()

    @pl.when(step == 2)
    def _():
        outs[1].begin_other()

    for k in range(1, nf):

        @pl.when(step == min(k + 1, nf - 1))
        def _():
            outs[1].hops(k)
            if k == nf - 1:
                outs[1].hand_over()

    @pl.when(step == nf - 1)
    def _():
        project(nf - 1)
        pass_on(nf - 1)
        conclude(nf - 2)
        every(nf - 3).relay()
        conclude(nf - 1)
        every(nf - 2).relay()
        for k in range(1, nf):
            gathers[1].settle(k)
        gathers[1].settle_begin()
        outs[1].settle()
        enter.settle()
        enter_cot.arrive()
        enter_cot.settle()
        normed_copy.wait()
        hidden_copy.wait()
        every(nf - 1).relay()
        for place in range(nf):
            every(place).close()
            mine(place).wait()
        blocks.settle(nf)


def run_first(ch, nf, nd, x, cot, seg, in_rows, out_rows, conv_w, conv_b, norm_gain, gate_gain, head_table, identity):
    block = x.shape[1]
    length = block * nf
    conv_width = ch + 2 * N
    columns = in_rows.shape[1]
    width = 2 * ch + DIN - 2 * DI
    pieces = length // Q
    subs = block // Q
    bits = len(bits_of(nd))
    own = (nf, block // nd, D)
    every = (nf, nd, block // nd, D)
    w_in = jax.ShapeDtypeStruct((nf, width, columns), BF16)
    anywhere = pl.BlockSpec(memory_space=pl.ANY)
    dma = pltpu.SemaphoreType.DMA
    ordered = lambda s: (s, 0)
    small = [(2, K, conv_width), (2, 1, conv_width), (2, 1, LANES), (2, 1, LANES), (2, 1, ch), (2, 1, ch), (2, 1, D)]
    resident = small + [(length, LANES), (pieces, 1, Q)]
    return pl.pallas_call(
        functools.partial(first_kernel, ch, nf, nd),
        grid=(nf,),
        in_specs=[anywhere] * 5 + [once(part.shape) for part in (conv_w, conv_b, norm_gain, gate_gain, head_table)],
        out_specs=[
            pl.BlockSpec((block, width), ordered),
            pl.BlockSpec((block, ch), ordered),
            pl.BlockSpec((block, conv_width), ordered),
            pl.BlockSpec((subs, N, ch), lambda s: (s, 0, 0)),
            once((length, ch)),
            once(own),
            once(own),
            once((pieces, Q)),
        ]
        + [once(shape) for shape in resident]
        + [anywhere] * 8,
        out_shape=[
            jax.ShapeDtypeStruct((length, width), F32),
            jax.ShapeDtypeStruct((length, ch), F32),
            jax.ShapeDtypeStruct((length, conv_width), F32),
            jax.ShapeDtypeStruct((pieces, N, ch), F32),
            jax.ShapeDtypeStruct((length, ch), BF16),
            jax.ShapeDtypeStruct(own, F32),
            jax.ShapeDtypeStruct(own, BF16),
            jax.ShapeDtypeStruct((pieces, Q), F32),
        ]
        + [jax.ShapeDtypeStruct(shape, F32) for shape in resident]
        + [
            jax.ShapeDtypeStruct(every, BF16),
            jax.ShapeDtypeStruct(every, BF16),
            jax.ShapeDtypeStruct(own, BF16),
            jax.ShapeDtypeStruct(own, BF16),
            w_in,
            w_in,
            jax.ShapeDtypeStruct((ch, D), BF16),
            jax.ShapeDtypeStruct((ch, D), BF16),
        ],
        scratch_shapes=[
            pltpu.VMEM(held_shape(w_in), BF16),
            pltpu.VMEM((ch, D), BF16),
            pltpu.VMEM((Q + 8, conv_width), F32),
            pltpu.VMEM((N, ch), F32),
            pltpu.VMEM((2, block, ch), F32),
            pltpu.VMEM(every, F32),
            pltpu.VMEM((bits, nf, nd // 2, block // nd, D), F32),
            pltpu.VMEM((nf, nd, 8, LANES), F32),
            pltpu.VMEM(own, BF16),
            pltpu.VMEM(every, BF16),
            pltpu.VMEM(own, BF16),
            pltpu.VMEM((2, 8, DC), F32),
            pltpu.VMEM((pieces * 8, LANES), F32),
            pltpu.VMEM((width, columns), BF16),
            pltpu.VMEM((ch, D), BF16),
            dma((bits, nf, nd)),
            dma((bits, nf, nd)),
            dma((nf, nd)),
            dma((nf, nd)),
            dma((nf, nd)),
            dma((nf, nd)),
            dma((2, nd)),
            dma((2, nd)),
            dma((2, nf)),
            dma((2, nf)),
            dma((7, 2 * nf)),
            dma((7, 2 * nf)),
            dma((6, 4)),
            dma((6, 4)),
            dma((3 + nf,)),
            dma((nf,)),
            dma((2,)),
            dma((2,)),
            dma((3,)),
        ],
        compiler_params=pltpu.CompilerParams(
            vmem_limit_bytes=VMEM_LIMIT, collective_id=identity, has_side_effects=True
        ),
        name="layer_first",
    )(x, cot, seg, in_rows, out_rows, conv_w, conv_b, norm_gain, gate_gain, head_table)


def layer_kernel(
    ch, nf, nd,
    normed_ref, meta_ref, segrow_ref, conv_w_ref, conv_b_ref, dtb_ref, alog_ref, skip_ref, gain_ref,
    w_in_ref, w_out_ref, hidden_ref, extra_ref,
    proj_ref, nout_ref, mixed_ref, pre_ref, state_out_ref, branch_ref, next_ref, ratio_ref, pull_ref, cot_all,
    held, w_out, pad, state, gated, partial, landed, squares, pulls,
    sum_send, sum_recv, tile_send, tile_recv, group_send, group_recv, local_sem, load_sem,
):
    step = pl.program_id(0)
    y, z, d = lax.axis_index("section"), lax.axis_index("fsdp"), lax.axis_index("dp")
    block = normed_ref.shape[0]
    subs = block // Q
    rows = block // nd
    bits = bits_of(nd)
    blocks = BlockSum(partial, landed, d, nd, sum_send, sum_recv)
    weights = Weights(w_in_ref, held, load_sem)
    out_load = pltpu.make_async_copy(w_out_ref, w_out, local_sem.at[0])
    cot_group = GroupRows(lambda device: cot_all.at[:, device], d, nd, group_send.at[0], group_recv.at[0])
    cot_keep = pltpu.make_async_copy(extra_ref, cot_group.part(0), local_sem.at[1])

    @pl.when(step == 0)
    def _():
        for copy in weights.copies():
            copy.start()
        out_load.start()
        greet([(None, {"dp": flip(d, j)}) for j in range(1, nd)])
        cot_keep.start()
        cot_group.begin(extra_ref)
        pad[0:8, :] = jnp.zeros((8, pad.shape[1]), F32)
        state[...] = jnp.zeros_like(state)
        pulls[0] = jnp.zeros(pulls.shape[1:], F32)
        for copy in weights.copies():
            copy.wait()
        out_load.wait()

    def tile(place):
        return GroupTiles(squares.at[place], tile_send.at[place], tile_recv.at[place], d, nd)

    def project(place):
        ratio = lax.rsqrt(tile(place).finish() * (1.0 / DI) + EPSILON)
        for sub in range(subs):
            piece = place * subs + sub
            ratio_ref[pl.ds(piece, 1), :] = ratio[sub : sub + 1, :]
            normed_out = gated[place % 2, sub * Q : (sub + 1) * Q, :] * to_column(ratio[sub : sub + 1, :])
            nout_ref[pl.ds(pl.multiple_of(piece * Q, Q), Q), :] = (normed_out * gain_ref[...]).astype(BF16)
        here_rows = pl.ds(pl.multiple_of(place * block, Q), block)
        product = dot(nout_ref[here_rows, :], w_out[...]).astype(partial.dtype)
        for o in range(nd):
            partial[place, o] = product[o * rows : (o + 1) * rows, :]
        blocks.send(0, place)

    def pass_on(place):
        for k in range(1, len(bits)):
            blocks.send(k, place)

    def conclude(place):
        branch = blocks.own(place)
        branch_ref[place] = branch
        moved = (hidden_ref[place].astype(F32) + branch).astype(BF16)
        next_ref[place] = moved
        first = place * block + d * rows
        pulls[0, pl.ds(first // Q, 1), :] += to_row(
            jnp.sum(extra_ref[place].astype(F32) * branch, axis=1, keepdims=True), first % Q
        )

    proj_ref[...] = weights.forward(normed_ref[...])

    @pl.when(step >= 1)
    def _():
        project(step - 1)

    def one_chunk(sub, carry):
        mix_forward(
            ch, proj_ref, meta_ref, segrow_ref, conv_w_ref, conv_b_ref, dtb_ref, alog_ref, skip_ref,
            gated.at[step % 2], squares.at[step], mixed_ref, pre_ref, state_out_ref, pad, state, sub, d * (H // nd),
        )

        @pl.when(sub == 0)
        def _():
            @pl.when(step >= 2)
            def _():
                conclude(step - 2)

            @pl.when(step >= 1)
            def _():
                pass_on(step - 1)

        return carry

    lax.fori_loop(0, subs, one_chunk, 0)
    tile(step).begin()

    @pl.when(step == min(2, nf - 1))
    def _():
        cot_group.relay()

    @pl.when(step == nf - 1)
    def _():
        project(nf - 1)
        pass_on(nf - 1)
        conclude(nf - 2)
        conclude(nf - 1)
        pull_ref[...] = group_tiles(pulls, group_send.at[1], group_recv.at[1], d, nd)
        cot_group.close()
        cot_keep.wait()
        blocks.settle(nf)


def once(shape):
    return pl.BlockSpec(shape, lambda s: (0,) * len(shape), pipeline_mode=pl.Buffered(buffer_count=1))


def pick(part, layer):
    return pl.BlockSpec(
        (None,) + part.shape[1:], lambda s: (layer, 0, 0), pipeline_mode=pl.Buffered(buffer_count=1)
    )


def run_layer(
    ch, rows, nf, nd, normed_all, meta, segrow, small, w_in, w_out, hidden, extra, identity
):
    length, width = normed_all.shape[0], w_in.shape[1]
    layer = 1
    conv_width = ch + 2 * N
    block = rows
    steps = nf
    pieces = length // Q
    subs = block // Q
    own = (nf, rows // nd, D)
    every = (nf, nd, rows // nd, D)
    bits = len(bits_of(nd))
    dma = pltpu.SemaphoreType.DMA
    anywhere = pl.BlockSpec(memory_space=pl.ANY)
    ordered = lambda s: (s, 0)
    ordered3 = lambda s: (s, 0, 0)
    return pl.pallas_call(
        functools.partial(layer_kernel, ch, nf, nd),
        grid=(steps,),
        in_specs=[
            pl.BlockSpec((block, D), ordered),
            pl.BlockSpec((block, LANES), ordered),
            pl.BlockSpec((subs, 1, Q), ordered3),
        ]
        + [pick(part, layer) for part in small]
        + [
            anywhere,
            anywhere,
            once(own),
            once(own),
        ],
        out_specs=[
            pl.BlockSpec((block, width), ordered),
            once((length, ch)),
            pl.BlockSpec((block, ch), ordered),
            pl.BlockSpec((block, conv_width), ordered),
            pl.BlockSpec((subs, N, ch), ordered3),
            once(own),
            once(own),
            once((pieces, Q)),
            once((pieces, Q)),
            anywhere,
        ],
        out_shape=[
            jax.ShapeDtypeStruct((length, width), F32),
            jax.ShapeDtypeStruct((length, ch), BF16),
            jax.ShapeDtypeStruct((length, ch), F32),
            jax.ShapeDtypeStruct((length, conv_width), F32),
            jax.ShapeDtypeStruct((pieces, N, ch), F32),
            jax.ShapeDtypeStruct(own, F32),
            jax.ShapeDtypeStruct(own, BF16),
            jax.ShapeDtypeStruct((pieces, Q), F32),
            jax.ShapeDtypeStruct((pieces, Q), F32),
            jax.ShapeDtypeStruct(every, BF16),
        ],
        scratch_shapes=[
            pltpu.VMEM(held_shape(w_in), BF16),
            pltpu.VMEM((ch, D), BF16),
            pltpu.VMEM((Q + 8, conv_width), F32),
            pltpu.VMEM((N, ch), F32),
            pltpu.VMEM((2, block, ch), F32),
            pltpu.VMEM(every, BF16),
            pltpu.VMEM((bits, nf, nd // 2, rows // nd, D), BF16),
            pltpu.VMEM((steps, nd, 8, LANES), F32),
            pltpu.VMEM((nd, pieces, Q), F32),
            dma((bits, nf, nd)),
            dma((bits, nf, nd)),
            dma((steps, nd)),
            dma((steps, nd)),
            dma((nf, nd)),
            dma((nf, nd)),
            dma((2,)),
            dma((nf,)),
        ],
        compiler_params=pltpu.CompilerParams(
            vmem_limit_bytes=VMEM_LIMIT, collective_id=identity, has_side_effects=True
        ),
        name="layer_last",
    )(normed_all, meta, segrow, *small, w_in, w_out, hidden, extra)


def mix_backward(
    ch, proj_ref, pre_ref, mixed_ref, state_ref, grad_ref, ratio_ref, pull_ref, meta_ref, segrow_ref,
    conv_w_ref, dtb_ref, alog_ref, skip_ref, gain_ref,
    dproj_ref, small_ref, tail, dstate, sub, chunk, turn,
):
    conv_width = ch + 2 * N
    rows = pl.ds(pl.multiple_of(sub * Q, Q), Q)
    meta = meta_ref[rows, :]
    pre = pre_ref[rows, :]
    sig = jax.nn.sigmoid(pre)
    conv_out = pre * sig
    values = conv_out[:, :ch]
    b_part = conv_out[:, ch : ch + N]
    c_part = conv_out[:, ch + N :]
    row, column = triangles()
    tri = jnp.where(row >= column, 1.0, 0.0)
    shifted, step, log_decay, cumulative = decay_tables(
        own_steps(proj_ref[rows, ch + conv_width :], turn), dtb_ref[...], alog_ref[...], tri
    )
    linked = (row <= column) & (meta[:, 0:1] == segrow_ref[sub])
    b_low = b_part.astype(BF16)
    c_low = c_part.astype(BF16)
    inner = jnp.where(linked, dot(b_low, c_low, ((1,), (1,))), 0.0)
    cum_t = cumulative.T
    last = cumulative[Q - 1 : Q, :]
    entry = meta[:, 4:5] * jnp.exp(cumulative)
    weight = meta[:, 5:6] * jnp.exp(last - cumulative)
    state_in = state_ref[sub]
    dstate_in = dstate[...]
    state_low = state_in.astype(BF16)
    dstate_low = dstate_in.astype(BF16)
    carried = dot(c_low, state_low)
    carried_back = dot(b_low, dstate_low)
    low_half = lax.broadcasted_iota(jnp.int32, (Q, LANES), 1) < P_SIZE
    lane = lax.broadcasted_iota(jnp.int32, (Q, LANES), 1)
    ratio = to_column(ratio_ref[pl.ds(chunk, 1), :])
    pull = ratio * ratio * to_column(pull_ref[pl.ds(chunk, 1), :]) * (1.0 / DI)
    dinner = jnp.zeros((Q, Q), F32)
    turned_parts = []
    step_parts, exit_parts, entry_parts = [], [], []
    weighted = []
    entered = []
    entry_rows = []
    dpre_parts = []
    for pair in range(ch // LANES):
        lanes = slice(pair * LANES, (pair + 1) * LANES)
        values_pair = values[:, lanes]
        gate = proj_ref[rows, lanes]
        mixed = mixed_ref[rows, lanes]
        gate_sig = jax.nn.sigmoid(gate)
        gate_silu = gate * gate_sig
        gated = mixed * gate_silu
        scaled = grad_ref[rows, lanes] * ratio
        small_ref[5:6, lanes] += jnp.sum(scaled * gated, axis=0, keepdims=True)
        dgated = scaled * gain_ref[:, lanes] - gated * pull
        dproj_ref[rows, lanes] = (dgated * mixed * (gate_sig + gate_silu * (1.0 - gate_sig))).astype(BF16)
        dmixed = dgated * gate_silu
        small_ref[6:7, lanes] += jnp.sum(dmixed * values_pair, axis=0, keepdims=True)
        zero = jnp.zeros_like(values_pair)
        dmixed_halves = [jnp.where(low_half, dmixed, zero).astype(BF16), jnp.where(low_half, zero, dmixed).astype(BF16)]
        values_low = values_pair.astype(BF16)
        step_pair = pair_lanes(step, 2 * pair, low_half)
        mats = []
        for half, head in enumerate((2 * pair, 2 * pair + 1)):
            spread = jnp.minimum(cum_t[head : head + 1, :] - cumulative[:, head : head + 1], 0.0)
            plain = jnp.exp(spread)
            decay = plain * step[:, head : head + 1]
            product = dot(values_low, dmixed_halves[half], ((1,), (1,)))
            mats.append((inner * plain).astype(BF16))
            spreaded = product * decay
            dinner = dinner + spreaded
            turned_parts.append((spreaded * inner).astype(BF16))
        back = dot(jnp.concatenate(mats, axis=1), jnp.concatenate(dmixed_halves, axis=0))
        weight_pair = pair_lanes(weight, 2 * pair, low_half)
        through = weight_pair * carried_back[:, lanes]
        total = back + through
        dvalues = step_pair * total + skip_ref[:, lanes] * dmixed
        step_parts.append((total * values_pair).astype(BF16))
        exit_parts.append((through * values_pair * step_pair).astype(BF16))
        entry_pair = pair_lanes(entry, 2 * pair, low_half)
        entry_grad = entry_pair * dmixed
        entry_parts.append((entry_grad * carried[:, lanes]).astype(BF16))
        weighted.append((weight_pair * step_pair * values_pair).astype(BF16))
        entered.append(entry_grad.astype(BF16))
        entry_rows.append(entry_pair[Q - 1 : Q, :])
        dpre_parts.append(dvalues)
    weighted = jnp.concatenate(weighted, axis=1)
    entered = jnp.concatenate(entered, axis=1)
    entry_rows = jnp.concatenate(entry_rows, axis=1)
    dinner_low = jnp.where(linked, dinner, 0.0).astype(BF16)
    db = dot(dinner_low, c_low) + dot(weighted, dstate_low, ((1,), (1,)))
    dc = dot(dinner_low.T, b_low) + dot(entered, state_low, ((1,), (1,)))
    state_terms = jnp.sum(state_in * dstate_in, axis=0, keepdims=True) * entry_rows
    head_lane = lax.broadcasted_iota(jnp.int32, (1, LANES), 1)
    state_sum = jnp.zeros((1, LANES), F32)
    for head in range(ch // P_SIZE):
        part = jnp.sum(state_terms[:, head * P_SIZE : (head + 1) * P_SIZE], axis=1, keepdims=True)
        state_sum = state_sum + jnp.where(head_lane == head, part, 0.0)
    heads = ch // P_SIZE

    def marks(shape, place, index):
        return jnp.where(place(shape) == index(shape), 1.0, 0.0).astype(BF16)

    rows_of_shape = lambda shape: lax.broadcasted_iota(jnp.int32, shape, 0)
    columns_of_shape = lambda shape: lax.broadcasted_iota(jnp.int32, shape, 1)
    by_head = marks((ch, LANES), lambda shape: rows_of_shape(shape) // P_SIZE, columns_of_shape)
    dstep = dot(jnp.concatenate(step_parts, axis=1), by_head)
    dexit = dot(jnp.concatenate(exit_parts, axis=1), by_head)
    dcum = dot(jnp.concatenate(entry_parts, axis=1), by_head)
    by_target = marks((LANES, heads * Q), rows_of_shape, lambda shape: columns_of_shape(shape) // Q)
    by_source = marks((heads * Q, LANES), lambda shape: rows_of_shape(shape) // Q, columns_of_shape)
    dcum = dcum + dot(by_target, jnp.concatenate(turned_parts, axis=0)).T
    dcum = dcum - dot(jnp.concatenate(turned_parts, axis=1), by_source)
    later = jnp.where(row <= column, 1.0, 0.0)
    before = jnp.where(row > column, 1.0, 0.0)
    dlog = fine_dot(later, dcum) + fine_dot(before, dexit) + state_sum
    growth = jnp.exp(alog_ref[...])
    dstep = dstep - dlog * growth
    ddt = dstep * jax.nn.sigmoid(shifted)
    small_ref[7:8, 0:LANES] += jnp.sum(ddt, axis=0, keepdims=True)
    small_ref[7:8, LANES : 2 * LANES] += jnp.sum(dlog * log_decay, axis=0, keepdims=True)
    dproj_ref[rows, ch + conv_width :] = pltpu.roll(jnp.where(lane < heads, ddt, 0.0), turn, 1)[:, :H].astype(BF16)
    dstate[...] = entry_rows * dstate_in + dot(c_part.T.astype(BF16), entered)
    dconv_out = jnp.concatenate(dpre_parts + [db, dc], axis=1)
    dpre = dconv_out * (sig + conv_out * (1.0 - sig))
    raw = proj_ref[rows, ch : ch + conv_width]
    small_ref[4:5, :] += jnp.sum(dpre, axis=0, keepdims=True)
    draw = conv_w_ref[3:4, :] * dpre
    small_ref[3:4, :] += jnp.sum(raw * dpre, axis=0, keepdims=True)
    for lag in range(1, K):
        kept = meta[:, lag : lag + 1] * dpre
        tail[lag - 1, 0:Q, :] = kept
        moved = tail[lag - 1, lag : lag + Q, :]
        tail[lag - 1, Q : Q + 8, :] = kept[0:8, :]
        draw = draw + conv_w_ref[3 - lag : 4 - lag, :] * moved
        small_ref[3 - lag : 4 - lag, :] += jnp.sum(raw * moved, axis=0, keepdims=True)
    dproj_ref[rows, ch : ch + conv_width] = draw.astype(BF16)


def gain_rows(width):
    return [(start, min(width, D - start)) for start in range(0, D, width)]


def layer_back_kernel(
    ch, nf, nd, last,
    grad_all_ref, proj_ref, pre_ref, mixed_ref, state_ref, meta_ref, segrow_ref, ratio_ref, pull_ref,
    conv_w_ref, dtb_ref, alog_ref, skip_ref, gain_ref, w_in_ref, w_out_ref,
    hidden_ref, grad_own_ref, norm_gain_ref, branch_ref, *refs,
):
    count = 2 if last else 1
    sources, refs = refs[:count], refs[count:]
    if not last:
        rows_out, refs = refs[0], refs[1:]
    (
        dproj_ref, small_ref, next_ref, next_pull_ref, moved_ref,
    ) = refs[:5]
    results, refs = refs[5 : 5 + count], refs[5 + count :]
    if not last:
        final_ref, refs = refs[0], refs[1:]
    (
        held, w_out, tail, dstate, dnout, partial, landed, pulls, low, dgain,
        sum_send, sum_recv, tile_send, tile_recv, group_send, group_recv, local_sem, load_sem, deal_send, deal_recv,
    ) = refs[:20]
    refs = refs[20:]
    step = pl.program_id(0)
    y, z, d = lax.axis_index("section"), lax.axis_index("fsdp"), lax.axis_index("dp")
    block = grad_all_ref.shape[0]
    subs = block // Q
    rows = block // nd
    bits = bits_of(nd)
    place = nf - 1 - step
    blocks = BlockSum(partial, landed, d, nd, sum_send, sum_recv)
    sums = [
        SectionSum(make(source, nf), nf, y, z, *refs[5 * k : 5 * k + 5])
        for k, (make, source) in enumerate(zip((out_view, in_view), sources))
    ]
    weights = Weights(w_in_ref, held, load_sem)
    out_load = pltpu.make_async_copy(w_out_ref, w_out, local_sem.at[0])
    if last:
        leave = Deal(moved_ref, low, nf, nd, z, d, deal_send, deal_recv, True)
    else:
        leave = Deal(final_ref, rows_out, nf, nd, z, d, deal_send, deal_recv, True)

    def every(place):
        return GroupRows(lambda device: moved_ref.at[place, device], d, nd, group_send.at[place], group_recv.at[place])

    def mine(place):
        return pltpu.make_async_copy(low.at[place], moved_ref.at[place, d], local_sem.at[2 + place])

    @pl.when(step == 0)
    def _():
        for copy in weights.copies():
            copy.start()
        out_load.start()
        greet(
            [(None, {"dp": flip(d, j)}) for j in range(1, nd)]
            + line_neighbours(nf, y, z)
            + deal_partners(nf, nd, z, d)
        )
        for one in sums:
            one.begin()
        if not last:
            leave.start_all()
        tail[...] = jnp.zeros_like(tail)
        dstate[...] = jnp.zeros_like(dstate)
        small_ref[...] = jnp.zeros_like(small_ref)
        dgain[...] = jnp.zeros_like(dgain)
        pulls[0] = jnp.zeros(pulls.shape[1:], F32)
        for copy in weights.copies():
            copy.wait()
        out_load.wait()

    def pass_on(place):
        for k in range(1, len(bits)):
            blocks.send(k, place)

    def conclude(place):
        dnormed = blocks.own(place)
        hidden = hidden_ref[place].astype(F32)
        inverse = rms_parts(hidden)
        dgain[...] += jnp.sum(dnormed * hidden * inverse, axis=0, keepdims=True)
        scaled = dnormed * norm_gain_ref[...]
        dhidden = inverse * (
            scaled - hidden * (inverse * inverse) * jnp.mean(scaled * hidden, axis=1, keepdims=True)
        )
        moved = (grad_own_ref[place].astype(F32) + dhidden).astype(BF16)
        low[place] = moved
        next_ref[place] = moved
        if last:
            leave.start(place)
        else:
            first = place * block + d * rows
            pulls[0, pl.ds(first // Q, 1), :] += to_row(
                jnp.sum(moved.astype(F32) * branch_ref[place], axis=1, keepdims=True), first % Q
            )
            mine(place).start()
            every(place).begin(low.at[place])

    dnout[...] = dot(grad_all_ref[...], w_out[...], ((1,), (1,)))

    @pl.when(step >= 1)
    def _():
        pass_on(place + 1)

    def one_chunk(turn, carry):
        sub = subs - 1 - turn
        mix_backward(
            ch, proj_ref, pre_ref, mixed_ref, state_ref, dnout, ratio_ref, pull_ref, meta_ref, segrow_ref,
            conv_w_ref, dtb_ref, alog_ref, skip_ref, gain_ref,
            dproj_ref, small_ref, tail, dstate, sub, place * subs + sub, d * (H // nd),
        )

        @pl.when((turn == 0) & (step >= 1))
        def _():
            conclude(place + 1)

        return carry

    lax.fori_loop(0, subs, one_chunk, 0)
    product = weights.backward(dproj_ref[...]).astype(BF16)
    for o in range(nd):
        partial[place, o] = product[o * rows : (o + 1) * rows, :]
    blocks.send(0, place)
    if not last:

        @pl.when(step >= 1)
        def _():
            every(place + 1).relay()

    for k in range(nf - 1, 0, -1):

        @pl.when(step == nf - 1 - k)
        def _():
            for one in sums:
                one.stage(k)

    @pl.when(step == nf - 1)
    def _():
        pass_on(0)
        conclude(0)
        for row, (start, size) in enumerate(gain_rows(small_ref.shape[1])):
            small_ref[8 + row : 9 + row, 0:size] = dgain[:, start : start + size]
        if last:
            next_pull_ref[...] = jnp.zeros_like(next_pull_ref)
        else:
            next_pull_ref[...] = group_tiles(pulls, tile_send, tile_recv, d, nd)
        for one, result in zip(sums, results):
            one.finish()
            copy = pltpu.make_async_copy(one.result, result, local_sem.at[1])
            copy.start()
            copy.wait()
            one.settle()
        leave.arrive()
        leave.settle()
        if not last:
            every(0).relay()
            for k in range(nf):
                every(k).close()
                mine(k).wait()
        blocks.settle(nf)


def run_layer_back(
    ch, rows, nf, nd, last, grad_all, proj, pre, mixed, states, meta, segrow, ratio, pull, small, w_in, w_out,
    hidden, grad_own, norm_gain, branch, identity, sums, *leaving,
):
    length, width = proj.shape
    shapes = [make(nf, g) for make, g in zip((out_part_shape, in_part_shape), sums)]
    conv_width = ch + 2 * N
    block = rows
    steps = nf
    own = (nf, rows // nd, D)
    every = (nf, nd, rows // nd, D)
    pieces = length // Q
    subs = block // Q
    bits = len(bits_of(nd))
    dma = pltpu.SemaphoreType.DMA
    ordered = lambda s: (steps - 1 - s, 0)
    ordered3 = lambda s: (steps - 1 - s, 0, 0)
    layer = 0 if last else 1
    conv_w, conv_b, dtb, alog, skip, gain = small
    return pl.pallas_call(
        functools.partial(layer_back_kernel, ch, nf, nd, last),
        grid=(steps,),
        in_specs=[
            pl.BlockSpec((block, D), ordered),
            pl.BlockSpec((block, width), ordered),
            pl.BlockSpec((block, conv_width), ordered),
            pl.BlockSpec((block, ch), ordered),
            pl.BlockSpec((subs, N, ch), ordered3),
            pl.BlockSpec((block, LANES), ordered),
            pl.BlockSpec((subs, 1, Q), ordered3),
            once((pieces, Q)),
            once((pieces, Q)),
        ]
        + [pick(part, layer) for part in (conv_w, dtb, alog, skip, gain)]
        + [
            pl.BlockSpec(memory_space=pl.ANY),
            pl.BlockSpec(memory_space=pl.ANY),
            once(own),
            once(own),
            pick(norm_gain, layer),
            once(own),
        ]
        + [pl.BlockSpec(memory_space=pl.ANY)] * (len(sums) + len(leaving)),
        out_specs=[
            pl.BlockSpec((block, width), ordered),
            once((16, conv_width)),
            once(own),
            once((pieces, Q)),
            pl.BlockSpec(memory_space=pl.ANY),
        ]
        + [pl.BlockSpec(memory_space=pl.ANY)] * (len(sums) + len(leaving)),
        out_shape=[
            jax.ShapeDtypeStruct((length, width), BF16),
            jax.ShapeDtypeStruct((16, conv_width), F32),
            jax.ShapeDtypeStruct(own, BF16),
            jax.ShapeDtypeStruct((pieces, Q), F32),
            jax.ShapeDtypeStruct((rows, D) if last else every, BF16),
        ]
        + [jax.ShapeDtypeStruct(shape, BF16) for shape in shapes]
        + [jax.ShapeDtypeStruct((rows, D), BF16) for part in leaving],
        scratch_shapes=[
            pltpu.VMEM(held_shape(w_in), BF16),
            pltpu.VMEM((ch, D), BF16),
            pltpu.VMEM((K - 1, Q + 8, conv_width), F32),
            pltpu.VMEM((N, ch), F32),
            pltpu.VMEM((block, ch), F32),
            pltpu.VMEM(every, BF16),
            pltpu.VMEM((bits, nf, nd // 2, rows // nd, D), BF16),
            pltpu.VMEM((nd, pieces, Q), F32),
            pltpu.VMEM(own, BF16),
            pltpu.VMEM((1, D), F32),
            dma((bits, nf, nd)),
            dma((bits, nf, nd)),
            dma((nd,)),
            dma((nd,)),
            dma((nf, nd)),
            dma((nf, nd)),
            dma((2 + nf,)),
            dma((nf,)),
            dma((nf,)),
            dma((nf,)),
        ]
        + [part for shape in shapes for part in section_sum_scratch(nf, shape)],
        compiler_params=pltpu.CompilerParams(
            vmem_limit_bytes=VMEM_LIMIT, collective_id=identity, has_side_effects=True
        ),
        name="layer_back_last" if last else "layer_back_first",
    )(
        grad_all, proj, pre, mixed, states, meta, segrow, ratio, pull, conv_w, dtb, alog, skip, gain, w_in, w_out,
        hidden, grad_own, norm_gain, branch, *sums, *leaving,
    )


def shards(
    inputs, segment, cotangent, norm_gain, in_weight, conv_weight, conv_bias, dt_bias, a_log, d_skip,
    gate_gain, out_weight,
):
    fsdp, dp = lax.axis_size("fsdp"), lax.axis_size("dp")
    section, here = lax.axis_index("section"), lax.axis_index("dp")
    rows = inputs.shape[2]
    ch = DI // dp
    heads = H // dp
    conv_width = ch + 2 * N
    seg_mine = lax.dynamic_index_in_dim(segment, section, 0, keepdims=False)[0].astype(F32)
    seg_mine = jnp.broadcast_to(seg_mine.reshape(rows // Q, 1, Q), (rows // Q, 8, Q)).reshape(-1, Q)
    head_table = jnp.pad(
        jnp.concatenate([dt_bias[0], a_log[0], d_skip[0]], axis=0), ((0, 0), (0, LANES - H))
    )
    (
        proj, mixed, pre, states, nout, branch, after, ratio, conv_w, conv_b, dtb, alog, skip, gain, gains, meta, segrow,
        normed_all, moved, hidden, cot_own, w_in0, w_in1, w_out0, w_out1,
    ) = run_first(
        ch, fsdp, dp, inputs[:, 0], cotangent[:, 0], seg_mine, in_weight[0, 0].T, out_weight[0, 0], conv_weight[0, 0],
        conv_bias[0], norm_gain[0], gate_gain[0], head_table, 2,
    )
    small = (conv_w, conv_b, dtb, alog, skip, gain)
    length = meta.shape[0]
    saved = [(normed_all.reshape(length, D), hidden, proj, nout, mixed, pre, states, branch, ratio)]
    normed_all, hidden = moved.reshape(length, D), after
    proj, nout, mixed, pre, states, branch, final_rows, ratio, pull, cot_all = run_layer(
        ch, rows, fsdp, dp, normed_all, meta, segrow, small, w_in1, w_out1, hidden, cot_own, 3
    )
    saved.append((normed_all, hidden, proj, nout, mixed, pre, states, branch, ratio))

    grad_all, grad_own = cot_all.reshape(length, D), cot_own
    in_grad, small_grads, parts = (), [None, None], []
    for layer in (1, 0):
        last = layer == 0
        normed_all, hidden, proj, gated, mixed, pre, states, branch, ratio = saved[layer]
        out_grad = dot(gated, grad_all, ((0,), (0,)))
        dproj, small_grads[layer], after, next_pull, moved, *done = run_layer_back(
            ch, rows, fsdp, dp, last, grad_all, proj, pre, mixed, states, meta, segrow, ratio, pull, small,
            w_in0 if last else w_in1, w_out0 if last else w_out1, hidden, grad_own, gains, saved[0][7], 4 + layer,
            (out_grad.astype(BF16),) + in_grad, *(() if last else (final_rows,)),
        )
        if not last:
            *done, final = done
        parts += done
        grad = dot(dproj, normed_all, ((0,), (0,))).astype(BF16)
        if D // fsdp % LANES:
            grad = jnp.swapaxes(grad.reshape(-1, fsdp, D // fsdp), 0, 1)
        in_grad = (grad,)
        if not last:
            grad_all, grad_own, pull = moved.reshape(length, D), after, next_pull
    input_grad = moved

    in_all, out_all, small_all = run_end(
        fsdp, dp, in_grad[0], parts[2], parts[1], parts[0], small_grads[0], small_grads[1]
    )
    in_total, out_total, gain_total, convw_total, convb_total, dtb_total, alog_total, skip_total, gate_total = run_finish(
        ch, dp, in_all, out_all, small_all
    )
    return (
        final[None, None],
        input_grad[None, None],
        gain_total[None],
        in_total.T[None, None],
        convw_total[None, None],
        convb_total[None],
        dtb_total[None],
        alog_total[None],
        skip_total[None],
        gate_total[None],
        out_total[None, None],
    )


def solution(mesh):
    return jax.shard_map(
        shards,
        mesh=mesh,
        in_specs=(
            P(None, "dp", "fsdp", None),
            P(None, "dp", "fsdp"),
            P(None, "dp", "fsdp", None),
            P("section", None, None),
            P("section", None, "fsdp", None),
            P("section", None, None, None),
            P("section", None, None),
            P("section", None, None),
            P("section", None, None),
            P("section", None, None),
            P("section", None, None),
            P("section", None, "fsdp", None),
        ),
        out_specs=(
            P("section", "dp", "fsdp", None),
            P("section", "dp", "fsdp", None),
            P("section", None, None),
            P("section", None, "fsdp", None),
            P("section", None, None, None),
            P("section", None, None),
            P("section", None, None),
            P("section", None, None),
            P("section", None, None),
            P("section", None, None),
            P("section", None, "fsdp", None),
        ),
        check_vma=False,
    )
```

```python
import functools

import jax
import jax.numpy as jnp
from jax import lax
from jax.experimental import pallas as pl
from jax.experimental.pallas import tpu as pltpu
from jax.sharding import PartitionSpec as P

D = 1536
H = 48
P_SIZE = 64
N = 128
K = 4
DI = 3072
DC = 3328
DIN = 6448
EPSILON = 1e-05
HIGHEST = lax.Precision.HIGHEST
BF16 = jnp.bfloat16
F32 = jnp.float32
Q = 128
LANES = 128


def dot(a, b, dims=((1,), (0,)), precision=None):
    return lax.dot_general(a, b, (dims, ((), ())), preferred_element_type=F32, precision=precision)


def low_dot(a, b, dims=((1,), (0,))):
    return dot(a.astype(BF16), b.astype(BF16), dims)


def fine_dot(a, b, dims=((1,), (0,))):
    return dot(a, b, dims, HIGHEST)


def halves(value):
    high = value.astype(BF16)
    return high, (value - high.astype(F32)).astype(BF16)


def split_dot(a, b, dims=((1,), (0,))):
    (a_high, a_low), (b_high, b_low) = halves(a), halves(b)
    a_axis, b_axis = dims[0][0], dims[1][0]
    both = dot(
        jnp.concatenate([a_high, a_low], axis=a_axis), jnp.concatenate([b_high, b_high], axis=b_axis), dims
    )
    return both + dot(a_high, b_low, dims)


def pair_lanes(table, first, low_half):
    return jnp.where(low_half, table[:, first : first + 1], table[:, first + 1 : first + 2])


def decay_tables(proj_dt, dt_bias, a_row, tri):
    shifted = proj_dt + dt_bias
    step = jnp.maximum(shifted, 0.0) + jnp.log1p(jnp.exp(-jnp.abs(shifted)))
    log_decay = -step * jnp.exp(a_row)
    cumulative = fine_dot(tri, log_decay)
    return shifted, step, log_decay, cumulative


def triangles():
    row = lax.broadcasted_iota(jnp.int32, (Q, Q), 0)
    column = lax.broadcasted_iota(jnp.int32, (Q, Q), 1)
    return row, column


MESH_ID = pl.DeviceIdType.MESH
VMEM_LIMIT = 60 * 1024 * 1024


def remote(src, dst, send_sem, recv_sem, device):
    return pltpu.make_async_remote_copy(
        src_ref=src, dst_ref=dst, send_sem=send_sem, recv_sem=recv_sem, device_id=device, device_id_type=MESH_ID
    )


def greet(devices):
    barrier = pltpu.get_barrier_semaphore()
    count = 0
    for condition, device in devices:
        if condition is None:
            pl.semaphore_signal(barrier, inc=1, device_id=device, device_id_type=MESH_ID)
            count = count + 1
        else:

            @pl.when(condition)
            def _():
                pl.semaphore_signal(barrier, inc=1, device_id=device, device_id_type=MESH_ID)

            count = count + condition.astype(jnp.int32)
    pl.semaphore_wait(barrier, count)


def bits_of(peers):
    return [1 << k for k in range(peers.bit_length() - 1)]


def has_bit(value, bit):
    return (value // bit) % 2


def flip(value, bits):
    bit = 1
    out = value
    while bit <= bits:
        if bits & bit:
            out = out + bit * (1 - 2 * has_bit(value, bit))
        bit = bit * 2
    return out


def to_column(row):
    down, across = triangles()
    return jnp.sum(jnp.where(down == across, jnp.broadcast_to(row, (Q, Q)), 0.0), axis=1, keepdims=True)


def to_row(column, offset=0):
    shape = (column.shape[0], Q)
    down = lax.broadcasted_iota(jnp.int32, shape, 0)
    across = lax.broadcasted_iota(jnp.int32, shape, 1)
    return jnp.sum(jnp.where(across == down + offset, jnp.broadcast_to(column, shape), 0.0), axis=0, keepdims=True)


class GroupTiles:

    def __init__(self, tiles, send_sem, recv_sem, here, peers):
        self.tiles, self.send_sem, self.recv_sem, self.here, self.peers = tiles, send_sem, recv_sem, here, peers

    def copies(self):
        return [
            remote(
                self.tiles.at[0], self.tiles.at[j], self.send_sem.at[j], self.recv_sem.at[j],
                {"dp": flip(self.here, j)},
            )
            for j in range(1, self.peers)
        ]

    def begin(self):
        for copy in self.copies():
            copy.start()

    def finish(self):
        for copy in self.copies():
            copy.wait()
        total = self.tiles[0]
        for j in range(1, self.peers):
            total = total + self.tiles[j]
        return total


def group_tiles(tiles, send_sem, recv_sem, here, peers):
    group = GroupTiles(tiles, send_sem, recv_sem, here, peers)
    group.begin()
    return group.finish()


class GroupRows:

    def __init__(self, where, here, peers, send_sem, recv_sem):
        self.where, self.here, self.peers = where, here, peers
        self.send_sem, self.recv_sem = send_sem, recv_sem

    def part(self, j):
        return self.where(flip(self.here, j))

    def copy(self, j, bit, source=None):
        part = self.part(j)
        return remote(
            part if source is None else source, part, self.send_sem.at[j ^ bit], self.recv_sem.at[j ^ bit],
            {"dp": flip(self.here, bit)},
        )

    def begin(self, source=None):
        for bit in bits_of(self.peers)[::-1]:
            self.copy(0, bit, source).start()

    def phase(self, bit):
        for j in range(bit, self.peers, 2 * bit):
            self.copy(j ^ bit, bit).wait_send()
            landing = self.part(j)
            remote(
                landing, landing, self.send_sem.at[j], self.recv_sem.at[j], {"dp": flip(self.here, bit)}
            ).wait_recv()
            for lower in bits_of(bit)[::-1]:
                self.copy(j, lower).start()

    def relay(self):
        for bit in bits_of(self.peers)[:0:-1]:
            self.phase(bit)

    def close(self):
        self.phase(1)

    def finish(self):
        self.relay()
        self.close()


def rows_of(whole, rows):
    return lambda device: whole.at[pl.ds(pl.multiple_of(device * rows, 8), rows)]


def rms_parts(values):
    return lax.rsqrt(jnp.mean(values * values, axis=-1, keepdims=True) + EPSILON)


class BlockSum:

    def __init__(self, partial, landed, here, peers, send_sem, recv_sem):
        self.partial, self.landed, self.here, self.peers = partial, landed, here, peers
        self.bits = bits_of(peers)
        self.send_sem, self.recv_sem = send_sem, recv_sem

    def slot(self, k, owner):
        return self.peers - self.peers // self.bits[k] + owner // (2 * self.bits[k])

    def copy(self, k, block, owner):
        return remote(
            self.partial.at[block, owner], self.landed.at[self.slot(k, owner), block], self.send_sem.at[k, block, owner],
            self.recv_sem.at[k, block, owner], {"dp": flip(self.here, self.bits[k])},
        )

    def total(self, block, owner, stages):
        total = self.partial[block, owner].astype(F32)
        for m in range(stages):
            self.copy(m, block, owner).wait_recv()
            total = total + self.landed[self.slot(m, owner), block].astype(F32)
        return total

    def leaving(self, k):
        return [flip(self.here, j) for j in range(self.bits[k], self.peers, 2 * self.bits[k])]

    def send(self, k, block):
        for owner in self.leaving(k):
            if k > 0:
                self.partial[block, owner] = self.total(block, owner, k).astype(self.partial.dtype)
            self.copy(k, block, owner).start()

    def own(self, block):
        return self.total(block, self.here, len(self.bits))

    def settle(self, blocks):
        for block in range(blocks):
            for k in range(len(self.bits)):
                for owner in self.leaving(k):
                    self.copy(k, block, owner).wait_send()


class Deal:

    def __init__(self, chunk, own, nf, nd, z, d, send_sem, recv_sem, outward):
        self.chunk, self.own, self.nf, self.nd, self.z, self.d = chunk, own, nf, nd, z, d
        self.send_sem, self.recv_sem, self.outward = send_sem, recv_sem, outward
        self.rows = chunk.shape[0] // nd

    def part(self, o):
        return self.chunk.at[pl.ds(pl.multiple_of(o * self.rows, 16), self.rows)]

    def holder(self, b):
        return {"fsdp": b, "dp": self.z}

    def worker(self, o):
        return {"fsdp": self.d, "dp": o}

    def at_home(self, k):
        return (self.z == self.d) & (self.z == k)

    def send(self, k):
        if self.outward:
            return remote(
                self.own.at[k], self.part(self.d), self.send_sem.at[k], self.recv_sem.at[self.d], self.holder(k)
            )
        return remote(
            self.part(k), self.own.at[self.z], self.send_sem.at[k], self.recv_sem.at[self.z], self.worker(k)
        )

    def recv(self, k):
        if self.outward:
            part = self.part(k)
            return remote(part, part, self.send_sem.at[k], self.recv_sem.at[k], self.worker(k))
        part = self.own.at[k]
        return remote(part, part, self.send_sem.at[k], self.recv_sem.at[k], self.holder(k))

    def keep(self, k):
        if self.outward:
            return pltpu.make_async_copy(self.own.at[k], self.part(k), self.send_sem.at[k])
        return pltpu.make_async_copy(self.part(k), self.own.at[k], self.send_sem.at[k])

    def start(self, k):
        @pl.when(self.at_home(k))
        def _():
            self.keep(k).start()

        @pl.when(jnp.logical_not(self.at_home(k)))
        def _():
            self.send(k).start()

    def start_all(self):
        for k in range(self.nf):
            self.start(k)

    def arrive(self):
        for k in range(self.nf):

            @pl.when(self.at_home(k))
            def _():
                self.keep(k).wait()

            @pl.when(jnp.logical_not(self.at_home(k)))
            def _():
                self.recv(k).wait_recv()

    def settle(self):
        for k in range(self.nf):

            @pl.when(jnp.logical_not(self.at_home(k)))
            def _():
                self.send(k).wait_send()


def deal_partners(nf, nd, z, d):
    out = []
    for k in range(nf):
        elsewhere = (z != d) | (z != k)
        out += [(elsewhere, {"fsdp": k, "dp": z}), (elsewhere, {"fsdp": d, "dp": k})]
    return out


class SectionGather:

    def __init__(self, held, section, nf, y, z, sems, own=None):
        self.own = own
        self.held, self.section, self.nf, self.y, self.z, self.sems = held, section, nf, y, z, sems
        width = held.shape[1]
        first = -(-width // 32) * 16
        self.spans = [(0, first), (first, width - first)]
        self.peer = {"section": 1 - y}

    def block(self, b, part):
        start, size = self.spans[part]
        return self.held.at[b, pl.ds(start, size)]

    def each(self, body):
        for part in range(2):
            owner = self.y == self.section

            @pl.when(owner if part == 0 else jnp.logical_not(owner))
            def _():
                body(part)

    def own_part(self, part):
        start, size = self.spans[part]
        return self.own.at[pl.ds(start, size)]

    def send(self, b, part, row, k, landed, device, source=None):
        here = self.block(b, part)
        return remote(
            here if source is None else source, here, self.sems.at[row, k], self.sems.at[landed, k], device
        )

    def right(self, k, b, part, source=None):
        return self.send(b, part, 0, k, 2, {"fsdp": self.z + 1}, source)

    def left(self, k, b, part, source=None):
        return self.send(b, part, 1, k, 3, {"fsdp": self.z - 1}, source)

    def over(self, k, b, part, source=None):
        return self.send(b, part, 4, k, 5, self.peer, source)

    def cross(self):
        here = self.block(self.z, 1)
        return remote(self.own_part(1), here, self.sems.at[6, 0], self.sems.at[6, 1], self.peer)

    def keep(self):
        return pltpu.make_async_copy(self.own, self.held.at[self.z], self.sems.at[6, 2])

    def has_right(self):
        return self.z < self.nf - 1

    def has_left(self):
        return self.z > 0

    def start_cross(self):
        @pl.when(self.y == self.section)
        def _():
            self.cross().start()
            self.keep().start()

    def begin(self):
        def body(part):
            source = None
            if part == 1:
                self.cross().wait_recv()
            else:
                source = self.own_part(0)

            @pl.when(self.has_right())
            def _():
                self.right(1, self.z, part, source).start()

            @pl.when(self.has_left())
            def _():
                self.left(1, self.z, part, source).start()

            if part == 0:
                self.cross().wait_send()
                self.over(0, self.z, 0, source).start()

        self.each(body)

    def settle_begin(self):
        def body(part):
            @pl.when(self.has_right())
            def _():
                self.right(1, self.z, part).wait_send()

            @pl.when(self.has_left())
            def _():
                self.left(1, self.z, part).wait_send()

            if part == 0:
                self.over(0, self.z, 0).wait_send()
                self.keep().wait()
            else:
                self.over(0, self.z, 0).wait_recv()

        self.each(body)

    def sides(self, k, body):
        @pl.when(self.z >= k)
        def _():
            body(self.z - k, k, True)

        @pl.when(self.z + k < self.nf)
        def _():
            body(self.z + k, self.nf + k, False)

    def arrive(self, k):
        def body(part):
            def one(b, index, from_left):
                if from_left:
                    self.right(k, b, part).wait_recv()
                else:
                    self.left(k, b, part).wait_recv()

            self.sides(k, one)

        self.each(body)

    def relay(self, k):
        def body(part):
            def one(b, index, from_left):
                if k < self.nf - 1:
                    if from_left:

                        @pl.when(self.has_right())
                        def _():
                            self.right(k + 1, b, part).start()

                    else:

                        @pl.when(self.has_left())
                        def _():
                            self.left(k + 1, b, part).start()

                self.over(index, b, part).start()

            self.sides(k, one)

        self.each(body)

    def settle(self, k):
        def body(part):
            def one(b, index, from_left):
                self.over(index, b, part).wait_send()
                self.over(index, b, 1 - part).wait_recv()
                if k < self.nf - 1:
                    if from_left:

                        @pl.when(self.has_right())
                        def _():
                            self.right(k + 1, b, part).wait_send()

                    else:

                        @pl.when(self.has_left())
                        def _():
                            self.left(k + 1, b, part).wait_send()

            self.sides(k, one)

        self.each(body)


class OutGather:

    def __init__(self, source, held, section, nf, y, z, d, sems, staged):
        self.staged = staged
        self.source, self.held, self.section, self.nf = source, held, section, nf
        self.y, self.z, self.d, self.sems = y, z, d, sems
        self.pieces = sems.shape[1]
        self.rows = source.shape[0] // self.pieces
        self.columns = source.shape[1] // 2
        self.peer = {"section": 1 - y}
        self.source_here = z == d

    def owner(self):
        return self.y == self.section

    def piece(self, ref, part, i):
        return ref.at[pl.ds(i * self.rows, self.rows), pl.ds(part * self.columns, self.columns)]

    def send(self, i, part, row, landed, device, source=None):
        target = self.piece(self.held, part, i)
        return remote(
            target if source is None else self.piece(source, part, i), target, self.sems.at[row, i],
            self.sems.at[landed, i], device,
        )

    def right(self, i, part, source=None):
        return self.send(i, part, 0, 2, {"fsdp": self.z + 1}, source)

    def left(self, i, part, source=None):
        return self.send(i, part, 1, 2, {"fsdp": self.z - 1}, source)

    def over(self, i, part, source=None):
        return self.send(i, part, 3, 4, self.peer, source)

    def cross(self):
        columns = pl.ds(self.columns, self.columns)
        return remote(
            self.source.at[:, columns], self.held.at[:, columns], self.sems.at[5, 0], self.sems.at[5, 1], self.peer
        )

    def stage(self):
        return pltpu.make_async_copy(self.source, self.staged, self.sems.at[5, 2])

    def keep(self):
        return pltpu.make_async_copy(self.staged, self.held, self.sems.at[5, 3])

    def goes_right(self):
        return (self.z >= self.d) & (self.z < self.nf - 1)

    def goes_left(self):
        return (self.z <= self.d) & (self.z > 0)

    def each(self, condition, body):
        for part in range(2):
            mine = self.owner() if part == 0 else jnp.logical_not(self.owner())

            @pl.when(condition & mine)
            def _():
                body(part)

    def along(self, i, part, action, source=None):
        @pl.when(self.goes_right())
        def _():
            action(self.right(i, part, source))

        @pl.when(self.goes_left())
        def _():
            action(self.left(i, part, source))

    def begin(self):
        @pl.when(self.source_here & self.owner())
        def _():
            self.cross().start()
            self.stage().start()
            for i in range(self.pieces):
                self.along(i, 0, lambda copy: copy.start(), self.source)

    def begin_other(self):
        @pl.when(self.source_here & jnp.logical_not(self.owner()))
        def _():
            self.cross().wait_recv()
            for i in range(self.pieces):
                self.along(i, 1, lambda copy: copy.start())

    def hops(self, distance):
        def body(part):
            for i in range(self.pieces):
                self.right(i, part).wait_recv()
                self.along(i, part, lambda copy: copy.start())

        self.each((self.z == self.d + distance) | (self.z == self.d - distance), body)

    def hand_over(self):
        @pl.when(self.source_here & self.owner())
        def _():
            self.stage().wait()
            self.keep().start()
            for i in range(self.pieces):
                self.over(i, 0, self.source).start()

        def body(part):
            for i in range(self.pieces):
                self.over(i, part).start()

        self.each(jnp.logical_not(self.source_here), body)

    def settle(self):
        @pl.when(self.source_here & self.owner())
        def _():
            self.cross().wait_send()
            self.keep().wait()

        def at_source(part):
            for i in range(self.pieces):
                self.along(i, part, lambda copy: copy.wait_send())
                if part == 0:
                    self.over(i, 0).wait_send()
                else:
                    self.over(i, 0).wait_recv()

        def elsewhere(part):
            for i in range(self.pieces):
                self.along(i, part, lambda copy: copy.wait_send())
                self.over(i, part).wait_send()
                self.over(i, 1 - part).wait_recv()

        self.each(self.source_here, at_source)
        self.each(jnp.logical_not(self.source_here), elsewhere)


def line_neighbours(nf, y, z):
    return [
        (None, {"section": 1 - y}),
        (z < nf - 1, {"fsdp": z + 1}),
        (z > 0, {"fsdp": z - 1}),
    ]


class SectionSum:

    def __init__(self, view, nf, y, z, own, landed, chain, sems, result):
        self.view, self.nf, self.y, self.z, self.result = view, nf, y, z, result
        self.own, self.landed, self.chain = own, landed, chain
        self.load_sem, self.over_send, self.over_recv, self.chain_send, self.chain_recv = (
            sems.at[0], sems.at[1], sems.at[2], sems.at[3], sems.at[4]
        )
        self.part_rows = own.shape[1]

    def load(self, block):
        return pltpu.make_async_copy(self.view(block, self.y), self.own.at[block], self.load_sem.at[block])

    def over(self, block):
        return remote(
            self.view(block, 1 - self.y), self.landed.at[block], self.over_send.at[block], self.over_recv.at[block],
            {"section": 1 - self.y},
        )

    def right(self, block):
        return remote(
            self.own.at[block], self.chain.at[block], self.chain_send.at[block], self.chain_recv.at[block],
            {"fsdp": self.z + 1},
        )

    def left(self, block, arrives):
        slot = self.nf if arrives else block
        return remote(
            self.own.at[block], self.chain.at[slot], self.chain_send.at[block], self.chain_recv.at[slot],
            {"fsdp": self.z - 1},
        )

    def at(self, k, body):
        if k == 0:
            body(self.z, False)
            return

        @pl.when(self.z + k < self.nf)
        def _():
            body(self.z + k, True)

        @pl.when(self.z - k >= 0)
        def _():
            body(self.z - k, False)

    def begin(self):
        self.at(self.nf - 1, lambda block, rightward: self.over(block).start())
        for k in range(self.nf - 1, -1, -1):
            self.at(k, lambda block, rightward: self.load(block).start())

    def add(self, block, sources, target):
        step = 32

        def some(i, carry):
            rows = pl.ds(pl.multiple_of(i * step, 16), step)
            total = self.own[block, rows, :].astype(F32)
            for ref, slot in sources:
                total = total + ref[slot, rows, :].astype(F32)
            if target is None:
                self.own[block, rows, :] = total.astype(BF16)
            else:
                target[rows, :] = total.astype(BF16)
            return carry

        lax.fori_loop(0, self.part_rows // step, some, 0)

    def ready(self, block):
        self.load(block).wait()
        self.over(block).wait_recv()

    def stage(self, k):
        z, nf = self.z, self.nf
        self.at(k, lambda block, rightward: self.ready(block))
        self.at(k - 1, lambda block, rightward: self.over(block).start())

        def one(block, rightward):
            far_end = z == 0 if rightward else z == nf - 1
            arrived = self.right(block) if rightward else self.left(block, False)
            leaving = self.right(block) if rightward else self.left(block, k == 1)

            @pl.when(jnp.logical_not(far_end))
            def _():
                arrived.wait_recv()
                self.add(block, [(self.landed, block), (self.chain, block)], None)

            @pl.when(far_end)
            def _():
                self.add(block, [(self.landed, block)], None)

            leaving.start()

        self.at(k, one)

    def finish(self):
        z, nf, target = self.z, self.nf, self.result
        self.ready(z)

        @pl.when(z > 0)
        def _():
            self.right(z).wait_recv()

        @pl.when(z < nf - 1)
        def _():
            self.left(z, True).wait_recv()

        @pl.when(z == 0)
        def _():
            self.add(z, [(self.landed, z), (self.chain, nf)], target)

        @pl.when(z == nf - 1)
        def _():
            self.add(z, [(self.landed, z), (self.chain, z)], target)

        @pl.when((z > 0) & (z < nf - 1))
        def _():
            self.add(z, [(self.landed, z), (self.chain, z), (self.chain, nf)], target)

    def settle(self):
        z, nf = self.z, self.nf
        self.over(z).wait_send()
        for k in range(nf - 1, 0, -1):

            @pl.when(z + k < nf)
            def _():
                self.over(z + k).wait_send()
                self.right(z + k).wait_send()

            @pl.when(z - k >= 0)
            def _():
                self.over(z - k).wait_send()
                self.left(z - k, k == 1).wait_send()


def in_parts(width):
    rows = -(-width // 64) * 32
    return rows, width - rows


def in_view(source, nf):
    rows, second = in_parts(source.shape[-2])

    def view(block, part):
        here = pl.ds(pl.multiple_of(part * second, 16), rows)
        if len(source.shape) == 3:
            return source.at[block, here]
        columns = source.shape[1] // nf
        return source.at[here, pl.ds(pl.multiple_of(block * columns, LANES), columns)]

    return view


def out_view(source, nf):
    rows, columns = source.shape[0] // nf, source.shape[1] // 2

    def view(block, part):
        here = pl.ds(pl.multiple_of(block * rows, 16), rows)
        return source.at[here, pl.ds(pl.multiple_of(part * columns, LANES), columns)]

    return view


def in_part_shape(nf, source):
    columns = source.shape[2] if len(source.shape) == 3 else source.shape[1] // nf
    return in_parts(source.shape[-2])[0], columns


def out_part_shape(nf, source):
    return source.shape[0] // nf, source.shape[1] // 2


def section_sum_scratch(nf, part):
    return [
        pltpu.VMEM((nf,) + part, BF16),
        pltpu.VMEM((nf,) + part, BF16),
        pltpu.VMEM((nf + 1,) + part, BF16),
        pltpu.SemaphoreType.DMA((5, nf + 1)),
        pltpu.VMEM(part, BF16),
    ]


class SectionReturn:

    def __init__(self, piece, place, owner, y, sems):
        self.piece, self.place, self.owner, self.y, self.sems = piece, place, owner, y, sems

    def keep(self):
        return pltpu.make_async_copy(self.piece(self.owner), self.place(self.owner), self.sems.at[2])

    def send(self):
        other = 1 - self.owner
        return remote(
            self.piece(other), self.place(other), self.sems.at[0], self.sems.at[1], {"section": 1 - self.y}
        )

    def begin(self):
        @pl.when(self.y == self.owner)
        def _():
            self.keep().start()

        @pl.when(self.y != self.owner)
        def _():
            self.send().start()

    def finish(self):
        @pl.when(self.y == self.owner)
        def _():
            self.keep().wait()
            self.send().wait_recv()

        @pl.when(self.y != self.owner)
        def _():
            self.send().wait_send()


def end_kernel(
    nf, nd,
    in_ref, in_part1_ref, out_part0_ref, out_part1_ref, small0_ref, small1_ref,
    in_all, out_all, small_all,
    in_own, in_landed, in_chain, in_sems, in_part,
    in_final, out_final, small_slots, small_total, local_sem, swap_sem, back_sem, small_sems, group_send, group_recv,
):
    y, z, d = lax.axis_index("section"), lax.axis_index("fsdp"), lax.axis_index("dp")
    away = z != d
    twin = {"fsdp": d, "dp": z}
    peer = {"section": 1 - y}
    wide = lambda k: {"fsdp": (z + k) % nf}
    greet(
        [(None, peer), (away, twin)]
        + [(None, wide(k)) for k in range(1, nf)]
        + [(None, {"dp": flip(d, bit)}) for bit in bits_of(nd)]
    )
    in_sum = SectionSum(in_view(in_ref, nf), nf, y, z, in_own, in_landed, in_chain, in_sems, in_part)
    width = in_final.shape[0]
    part_rows, second = in_parts(width)
    overlap = part_rows - second
    out_rows, out_columns = out_part0_ref.shape
    in_piece = lambda ref: lambda p: ref if p == 0 else ref.at[pl.ds(overlap, width - part_rows)]
    in_place = lambda p: in_final.at[pl.ds(p * part_rows, width - part_rows if p else part_rows)]
    out_place = lambda p: out_final.at[:, pl.ds(p * out_columns, out_columns)]
    out_returns = [
        SectionReturn(lambda p: out_part0_ref, out_place, 0, y, back_sem.at[0]),
        SectionReturn(lambda p: out_part1_ref, out_place, 1, y, back_sem.at[1]),
    ]
    in_returns = [
        SectionReturn(in_piece(in_part), in_place, 0, y, back_sem.at[2]),
        SectionReturn(in_piece(in_part1_ref), in_place, 1, y, back_sem.at[3]),
    ]
    in_groups = [
        GroupRows(
            lambda device, p=p: in_all.at[device, pl.ds(p * part_rows, width - part_rows if p else part_rows)],
            d, nd, group_send.at[p], group_recv.at[p],
        )
        for p in range(2)
    ]
    out_group = GroupRows(rows_of(out_all, out_rows), d, nd, group_send.at[2], group_recv.at[2])
    small_group = GroupRows(lambda device: small_all.at[device], d, nd, group_send.at[3], group_recv.at[3])

    def small_over(ref):
        return remote(ref, small_slots.at[nf], small_sems.at[0, 0], small_sems.at[1, 0], peer)

    def small_load(ref):
        return pltpu.make_async_copy(ref, small_slots.at[0], local_sem.at[0])

    small_copies = [
        remote(small_slots.at[0], small_slots.at[k], small_sems.at[0, k], small_sems.at[1, k], wide(k))
        for k in range(1, nf)
    ]
    small_own = pltpu.make_async_copy(small_total, small_group.part(0), local_sem.at[0])
    swap_target = out_all.at[pl.ds(pl.multiple_of(z * out_rows, 16), out_rows)]
    swap = remote(out_final, swap_target, swap_sem.at[0], swap_sem.at[1], twin)
    stay = pltpu.make_async_copy(out_final, out_group.part(0), swap_sem.at[2])

    def own_copy(p):
        return pltpu.make_async_copy(in_place(p), in_groups[p].part(0), local_sem.at[1 + p])

    def spread(p):
        own_copy(p).start()
        in_groups[p].begin(in_place(p))

    for back in out_returns:
        back.begin()
    in_sum.begin()
    for section, (mine, other) in enumerate(((small0_ref, small1_ref), (small1_ref, small0_ref))):

        @pl.when(y == section)
        def _():
            small_over(other).start()
            small_load(mine).start()


    @pl.when(y == 1)
    def _():
        in_returns[1].keep().start()
        in_returns[1].keep().wait()
        spread(1)

    for back in out_returns:
        back.finish()

    @pl.when(away)
    def _():
        swap.start()

    @pl.when(jnp.logical_not(away))
    def _():
        stay.start()

    for k in range(nf - 1, 0, -1):
        in_sum.stage(k)
        if k == nf - 1:
            small_load(small0_ref).wait()
            small_over(small0_ref).wait()
            small_slots[0] = small_slots[0] + small_slots[nf]
            for copy in small_copies:
                copy.start()

            @pl.when(away)
            def _():
                swap.wait()

            @pl.when(jnp.logical_not(away))
            def _():
                stay.wait()

            out_group.begin()
        if k == nf - 2:
            for copy in small_copies:
                copy.wait()
            total = small_slots[0]
            for j in range(1, nf):
                total = total + small_slots[j]
            small_total[...] = total
            small_own.start()
            small_group.begin(small_total)
            out_group.relay()
        if k == 1:
            small_group.finish()
            small_own.wait()
            out_group.close()
    in_sum.finish()

    @pl.when(y == 0)
    def _():
        in_returns[0].keep().start()
        in_returns[1].send().start()
        in_returns[0].keep().wait()
        spread(0)
        in_returns[0].send().wait_recv()
        spread(1)
        in_returns[1].send().wait_send()

    @pl.when(y == 1)
    def _():
        in_returns[0].send().start()
        in_returns[1].send().wait_recv()
        spread(0)
        in_returns[0].send().wait_send()

    for p in range(2):
        in_groups[p].finish()
        own_copy(p).wait()
    in_sum.settle()


def run_end(nf, nd, in_grad, in_part1, out_part0, out_part1, small0, small1):
    anywhere = pl.BlockSpec(memory_space=pl.ANY)
    dma = pltpu.SemaphoreType.DMA
    width = in_grad.shape[-2]
    out_rows = out_part0.shape[0]
    return pl.pallas_call(
        functools.partial(end_kernel, nf, nd),
        in_specs=[anywhere] * 6,
        out_specs=[anywhere] * 3,
        out_shape=[
            jax.ShapeDtypeStruct((nd, width, in_part1.shape[1]), BF16),
            jax.ShapeDtypeStruct((nd * out_rows, D), BF16),
            jax.ShapeDtypeStruct((nd,) + small0.shape, F32),
        ],
        scratch_shapes=section_sum_scratch(nf, in_part1.shape)
        + [
            pltpu.VMEM((width, in_part1.shape[1]), BF16),
            pltpu.VMEM((out_rows, D), BF16),
            pltpu.VMEM((nf + 1,) + small0.shape, F32),
            pltpu.VMEM(small0.shape, F32),
            dma((3,)),
            dma((3,)),
            dma((4, 3)),
            dma((2, nf)),
            dma((4, nd)),
            dma((4, nd)),
        ],
        compiler_params=pltpu.CompilerParams(
            vmem_limit_bytes=VMEM_LIMIT, collective_id=6, has_side_effects=True
        ),
        name="sum_end",
    )(in_grad, in_part1, out_part0, out_part1, small0, small1)


def finish_kernel(
    ch, nd, in_ref, shared_ref, out_ref, small_ref,
    in_total, out_total, gain_ref, convw_ref, convb_ref, dtb_ref, alog_ref, skip_ref, gate_ref, shared, sems,
):
    step = pl.program_id(0)
    heads = H // nd
    count = DIN - 2 * DI

    def copy(j):
        return pltpu.make_async_copy(shared_ref.at[j, pl.ds(2 * ch, count)], shared.at[j], sems.at[j])

    @pl.when(step == 0)
    def _():
        for j in range(nd):
            copy(j).start()
        for row, (start, size) in enumerate(gain_rows(small_ref.shape[2])):
            gain_ref[:, start : start + size] = jnp.sum(small_ref[:, 8 + row : 9 + row, 0:size], axis=0)
        both = jnp.sum(small_ref[:, 0:8, ch:], axis=0)
        convw_ref[:, DI:] = both[0:4, :]
        convb_ref[:, DI:] = both[4:5, :]
        rows = lax.broadcasted_iota(jnp.int32, (ch, LANES), 0)
        columns = lax.broadcasted_iota(jnp.int32, (ch, LANES), 1)
        by_head = jnp.where(rows // P_SIZE == columns, 1.0, 0.0)
        decays, skips = [[], []], []
        for j in range(nd):
            here = slice(j * ch, (j + 1) * ch)
            convw_ref[:, here] = small_ref[j, 0:4, :ch]
            convb_ref[:, here] = small_ref[j, 4:5, :ch]
            gate_ref[:, here] = small_ref[j, 5:6, :ch]
            skips.append(fine_dot(small_ref[j, 0:8, :ch], by_head)[6:7, :heads])
            for k in range(2):
                decays[k].append(small_ref[j, 7:8, k * LANES : k * LANES + heads])
        dtb_ref[...] = jnp.concatenate(decays[0], axis=1)
        alog_ref[...] = jnp.concatenate(decays[1], axis=1)
        skip_ref[...] = jnp.concatenate(skips, axis=1)

    @pl.when(step < 2 * nd)
    def _():
        in_total[...] = in_ref[...].astype(F32)
        out_total[...] = out_ref[...].astype(F32)

    @pl.when(step == 2 * nd)
    def _():
        for j in range(nd):
            copy(j).wait()
        total = shared[0].astype(F32)
        for j in range(1, nd):
            total = total + shared[j].astype(F32)
        in_total[0:count, :] = total


def run_finish(ch, nd, in_all, out_all, small_all):
    columns = in_all.shape[2]
    rows = out_all.shape[0]
    piece = rows // (2 * nd)
    final = lambda s: (jnp.minimum(s, 2 * nd - 1), 0)

    def in_block(s):
        s = jnp.minimum(s, 2 * nd - 1)
        return (s % nd, s // nd, 0)

    smalls = [(1, D), (K, DC), (1, DC), (1, H), (1, H), (1, H), (1, DI)]
    return pl.pallas_call(
        functools.partial(finish_kernel, ch, nd),
        grid=(2 * nd + 1,),
        in_specs=[
            pl.BlockSpec((None, ch, columns), in_block),
            pl.BlockSpec(memory_space=pl.ANY),
            pl.BlockSpec((piece, D), final),
            once(small_all.shape),
        ],
        out_specs=[pl.BlockSpec((ch, columns), lambda s: (s, 0)), pl.BlockSpec((piece, D), final)]
        + [once(shape) for shape in smalls],
        out_shape=[jax.ShapeDtypeStruct((DIN, columns), F32), jax.ShapeDtypeStruct((rows, D), F32)]
        + [jax.ShapeDtypeStruct(shape, F32) for shape in smalls],
        scratch_shapes=[pltpu.VMEM((nd, DIN - 2 * DI, columns), BF16), pltpu.SemaphoreType.DMA((nd,))],
        compiler_params=pltpu.CompilerParams(vmem_limit_bytes=VMEM_LIMIT),
        name="finish",
    )(in_all, in_all, out_all, small_all)


class Weights:

    def __init__(self, source, held, sems):
        self.source, self.held, self.sems = source, held, sems
        self.blocks = source.shape[0]
        self.columns = source.shape[2]

    def copies(self):
        out = []
        for k in range(self.blocks):
            if len(self.held.shape) == 3:
                target = self.held.at[k]
            else:
                target = self.held.at[:, pl.ds(k * self.columns, self.columns)]
            out.append(pltpu.make_async_copy(self.source.at[k], target, self.sems.at[k]))
        return out

    def forward(self, rows):
        if len(self.held.shape) == 2:
            return dot(rows, self.held[...], ((1,), (1,)))
        total = 0.0
        for k in range(self.blocks):
            total = total + dot(
                rows[:, k * self.columns : (k + 1) * self.columns], self.held[k], ((1,), (1,))
            )
        return total

    def backward(self, rows):
        if len(self.held.shape) == 2:
            return dot(rows, self.held[...])
        return jnp.concatenate([dot(rows, self.held[k]) for k in range(self.blocks)], axis=1)


def held_shape(w_in):
    blocks, width, columns = w_in.shape
    return (width, blocks * columns) if columns % LANES == 0 else (blocks, width, columns)


def own_steps(steps, turn):
    padded = jnp.concatenate([steps, jnp.zeros((steps.shape[0], LANES - H), F32)], axis=1)
    return pltpu.roll(padded, LANES - turn, 1)


def mix_forward(
    ch, proj_ref, meta_ref, segrow_ref, conv_w_ref, conv_b_ref, dtb_ref, alog_ref, skip_ref,
    gated_ref, square_ref, mixed_ref, pre_ref, state_out_ref, pad, state, sub, turn,
):
    conv_width = ch + 2 * N
    rows = pl.ds(pl.multiple_of(sub * Q, Q), Q)
    meta = meta_ref[rows, :]
    pad[8:, :] = proj_ref[rows, ch : ch + conv_width]
    pre = conv_b_ref[...] + conv_w_ref[3:4, :] * pad[8:, :]
    for lag in range(1, K):
        pre = pre + (conv_w_ref[3 - lag : 4 - lag, :] * meta[:, lag : lag + 1]) * pad[8 - lag : 8 - lag + Q, :]
    pad[0:8, :] = pad[Q : Q + 8, :]
    pre_ref[rows, :] = pre
    conv_out = pre * jax.nn.sigmoid(pre)
    values = conv_out[:, :ch]
    b_part = conv_out[:, ch : ch + N]
    c_part = conv_out[:, ch + N :]
    row, column = triangles()
    tri = jnp.where(row >= column, 1.0, 0.0)
    shifted, step, log_decay, cumulative = decay_tables(
        own_steps(proj_ref[rows, ch + conv_width :], turn), dtb_ref[...], alog_ref[...], tri
    )
    linked = (row >= column) & (meta[:, 0:1] == segrow_ref[sub])
    inner = jnp.where(linked, split_dot(c_part, b_part, ((1,), (1,))), 0.0)
    cum_t = cumulative.T
    step_t = step.T
    last = cumulative[Q - 1 : Q, :]
    entry = meta[:, 4:5] * jnp.exp(cumulative)
    weight = meta[:, 5:6] * jnp.exp(last - cumulative) * step
    state_in = state[...]
    state_out_ref[sub] = state_in
    carried = split_dot(c_part, state_in)
    low_half = lax.broadcasted_iota(jnp.int32, (Q, LANES), 1) < P_SIZE
    squares = jnp.zeros((Q, 1), F32)
    weighted = []
    entries = []
    values_high, values_low = halves(values)
    for pair in range(ch // LANES):
        lanes = slice(pair * LANES, (pair + 1) * LANES)
        values_pair = values[:, lanes]
        mats = []
        for head in (2 * pair, 2 * pair + 1):
            spread = jnp.minimum(cumulative[:, head : head + 1] - cum_t[head : head + 1, :], 0.0)
            mats.append((inner * jnp.exp(spread) * step_t[head : head + 1, :]).astype(BF16))
        parts = [values_high[:, lanes], values_low[:, lanes]]
        zero = jnp.zeros_like(parts[0])
        stacked = jnp.concatenate(
            [
                jnp.concatenate([jnp.where(low_half, part, zero) for part in parts], axis=1),
                jnp.concatenate([jnp.where(low_half, zero, part) for part in parts], axis=1),
            ],
            axis=0,
        )
        both = dot(jnp.concatenate(mats, axis=1), stacked)
        out = both[:, :LANES] + both[:, LANES:]
        entry_pair = pair_lanes(entry, 2 * pair, low_half)
        out = out + entry_pair * carried[:, lanes] + skip_ref[:, lanes] * values_pair
        mixed_ref[rows, lanes] = out
        gate = proj_ref[rows, lanes]
        gated = out * (gate * jax.nn.sigmoid(gate))
        squares = squares + jnp.sum(gated * gated, axis=1, keepdims=True)
        gated_ref[rows, lanes] = gated
        weighted.append(pair_lanes(weight, 2 * pair, low_half) * values_pair)
        entries.append(entry_pair[Q - 1 : Q, :])
    square_ref[0, pl.ds(sub, 1), :] = to_row(squares)
    state[...] = jnp.concatenate(entries, axis=1) * state_in + split_dot(
        b_part.T, jnp.concatenate(weighted, axis=1)
    )


def first_kernel(
    ch, nf, nd,
    x_ref, cot_ref, seg_ref, in_ref, out_ref, conv_w_ref, conv_b_ref, norm_ref, gate_ref, head_ref,
    proj_ref, mixed_ref, pre_ref, state_out_ref, nout_ref, branch_ref, next_ref, ratio_ref,
    conv_w_out, conv_b_out, dtb_out, alog_out, skip_out, gain_out, norm_out, meta_out, segrow_out,
    normed_all, moved_ref, hidden_out, cot_own, w_in0, w_in1, w_out0, w_out1,
    held, w_out, pad, state, gated, partial, landed, squares, low, normed, x_low, table, seg_all, own_block, staged,
    sum_send, sum_recv, tile_send, tile_recv, group_send, group_recv, start_send, start_recv, deal_send, deal_recv,
    in_sems0, in_sems1, out_sems0, out_sems1, local_sem, load_sem, small_sem, swap_sem, own_sem,
):
    step = pl.program_id(0)
    y, z, d = lax.axis_index("section"), lax.axis_index("fsdp"), lax.axis_index("dp")
    block = proj_ref.shape[0]
    subs = block // Q
    rows = block // nd
    length = block * nf
    lines = block // Q * 8
    heads = H // nd
    bits = bits_of(nd)
    twin = {"fsdp": d, "dp": z}
    home = z == d
    away = z != d
    peer = {"section": 1 - y}
    blocks = BlockSum(partial, landed, d, nd, sum_send, sum_recv)
    weights = Weights(w_in0, held, load_sem)
    out_load = pltpu.make_async_copy(w_out0, w_out, local_sem.at[0])
    gathers = [SectionGather(w_in0, 0, nf, y, z, in_sems0, own_block), SectionGather(w_in1, 1, nf, y, z, in_sems1, own_block)]
    outs = [
        OutGather(out_ref, w_out0, 0, nf, y, z, d, out_sems0, staged),
        OutGather(out_ref, w_out1, 1, nf, y, z, d, out_sems1, staged),
    ]
    enter = Deal(x_ref.at[y], x_low, nf, nd, z, d, deal_send.at[0], deal_recv.at[0], False)
    enter_cot = Deal(cot_ref.at[y], cot_own, nf, nd, z, d, deal_send.at[1], deal_recv.at[1], False)
    first_group = GroupRows(lambda device: normed.at[:, device], d, nd, start_send.at[0], start_recv.at[0])
    normed_copy = pltpu.make_async_copy(normed, normed_all, local_sem.at[1])
    hidden_copy = pltpu.make_async_copy(x_low, hidden_out, local_sem.at[2])

    def seg_rows(device):
        return seg_all.at[pl.ds(pl.multiple_of(device * lines, 8), lines)]

    seg_group = GroupRows(seg_rows, d, nd, start_send.at[1], start_recv.at[1])

    def every(place):
        return GroupRows(lambda device: moved_ref.at[place, device], d, nd, group_send.at[place], group_recv.at[place])

    def mine(place):
        return pltpu.make_async_copy(low.at[place], moved_ref.at[place, d], local_sem.at[3 + place])

    def stage(gather, k):
        gather.arrive(k)
        gather.relay(k)

    @pl.when(step == 0)
    def _():
        greet(
            line_neighbours(nf, y, z)
            + [(away, twin)]
            + deal_partners(nf, nd, z, d)
            + [(None, {"dp": flip(d, j)}) for j in range(1, nd)]
        )

        own_copies = [
            pltpu.make_async_copy(
                in_ref.at[pl.ds(pl.multiple_of(begin, 16), count)], own_block.at[pl.ds(spot, count)], own_sem.at[k]
            )
            for k, (begin, spot, count) in enumerate(
                [(d * ch, 0, ch), (DI + d * ch, ch, ch), (2 * DI, 2 * ch, DIN - 2 * DI)]
            )
        ]
        for copy in own_copies:
            copy.start()
        for copy in own_copies:
            copy.wait()
        gathers[0].start_cross()
        gathers[1].start_cross()
        table[y, 0:4, :] = conv_w_ref[...]
        table[y, 4:5, :] = conv_b_ref[...]
        table[y, 5:6, 0:D] = norm_ref[...]
        table[y, 6:7, 0:DI] = gate_ref[...]
        for k in range(3):
            table[y, 7:8, k * LANES : (k + 1) * LANES] = head_ref[k : k + 1, :]
        small_copy = remote(table.at[y], table.at[y], small_sem.at[0], small_sem.at[1], peer)
        small_copy.start()
        seg_swap = remote(seg_ref, seg_rows(z), swap_sem.at[0], swap_sem.at[1], twin)
        seg_stay = pltpu.make_async_copy(seg_ref, seg_rows(d), swap_sem.at[0])

        @pl.when(away)
        def _():
            seg_swap.start()

        @pl.when(home)
        def _():
            seg_stay.start()

        gathers[0].begin()
        enter.start_all()
        outs[0].begin()
        stage(gathers[0], 1)
        outs[0].begin_other()
        outs[0].hops(1)

        small_copy.wait()
        enter.arrive()
        hidden_copy.start()
        values = x_low[...].astype(F32)
        low[...] = (values * rms_parts(values) * table[0, 5:6, 0:D]).astype(BF16)
        for place in range(nf):
            normed[place, d] = low[place]
        first_group.begin(low)

        @pl.when(away)
        def _():
            seg_swap.wait()

        @pl.when(home)
        def _():
            seg_stay.wait()

        seg_group.begin()
        for k in range(2, nf - 1):
            stage(gathers[0], k)
            outs[0].hops(k)

        turn = d * heads
        low_half = lax.broadcasted_iota(jnp.int32, (1, LANES), 1) < P_SIZE
        channels = pl.ds(pl.multiple_of(d * ch, LANES), ch)
        for section in range(2):
            conv_w_out[section, :, 0:ch] = table[section, 0:4, channels]
            conv_w_out[section, :, ch:] = table[section, 0:4, DI:DC]
            conv_b_out[section, :, 0:ch] = table[section, 4:5, channels]
            conv_b_out[section, :, ch:] = table[section, 4:5, DI:DC]
            norm_out[section] = table[section, 5:6, 0:D]
            gain_out[section] = table[section, 6:7, channels]
            head_rows = [
                pltpu.roll(table[section, :, k * LANES : (k + 1) * LANES], LANES - turn, 1)[7:8, :] for k in range(3)
            ]
            dtb_out[section] = head_rows[0]
            alog_out[section] = head_rows[1]
            for pair in range(ch // LANES):
                skip_out[section, :, pair * LANES : (pair + 1) * LANES] = pair_lanes(head_rows[2], 2 * pair, low_half)

        seg_group.finish()

        lane = lax.broadcasted_iota(jnp.int32, (8, LANES), 1)
        sub_lane = lax.broadcasted_iota(jnp.int32, (Q, LANES), 1)
        before = jnp.full((8, LANES), -1.0, F32)
        for chunk in range(length // Q):
            now = seg_all[chunk * 8 : chunk * 8 + 8, :]
            segrow_out[chunk] = now[0:1, :]
            columns = [now[0:1, :]]
            for lag in range(1, K):
                earlier = jnp.where(lane < lag, pltpu.roll(before, lag, 1), pltpu.roll(now, lag, 1))
                columns.append(jnp.where(earlier == now, 1.0, 0.0)[0:1, :])
            columns.append(jnp.where(now == before[:, Q - 1 : Q], 1.0, 0.0)[0:1, :])
            columns.append(jnp.where(now == now[:, Q - 1 : Q], 1.0, 0.0)[0:1, :])
            masks = jnp.zeros((Q, LANES), F32)
            for j, row in enumerate(columns):
                masks = jnp.where(sub_lane == j, to_column(row), masks)
            meta_out[chunk * Q : (chunk + 1) * Q, :] = masks
            before = now

        stage(gathers[0], nf - 1)
        outs[0].hops(nf - 1)
        outs[0].hand_over()
        gathers[1].begin()
        first_group.finish()
        normed_copy.start()
        pad[0:8, :] = jnp.zeros((8, pad.shape[1]), F32)
        state[...] = jnp.zeros_like(state)
        for k in range(1, nf):
            gathers[0].settle(k)
        gathers[0].settle_begin()
        for copy in weights.copies():
            copy.start()
        for copy in weights.copies():
            copy.wait()

    def tile(place):
        return GroupTiles(squares.at[place], tile_send.at[place], tile_recv.at[place], d, nd)

    def project(place):
        ratio = lax.rsqrt(tile(place).finish() * (1.0 / DI) + EPSILON)
        for sub in range(subs):
            piece = place * subs + sub
            ratio_ref[pl.ds(piece, 1), :] = ratio[sub : sub + 1, :]
            normed_out = gated[place % 2, sub * Q : (sub + 1) * Q, :] * to_column(ratio[sub : sub + 1, :])
            nout_ref[pl.ds(pl.multiple_of(piece * Q, Q), Q), :] = (normed_out * gain_out[0]).astype(BF16)
        here_rows = pl.ds(pl.multiple_of(place * block, Q), block)
        product = dot(nout_ref[here_rows, :], w_out[...])
        for o in range(nd):
            partial[place, o] = product[o * rows : (o + 1) * rows, :]
        blocks.send(0, place)

    def pass_on(place):
        for k in range(1, len(bits)):
            blocks.send(k, place)

    def conclude(place):
        branch = blocks.own(place)
        branch_ref[place] = branch
        moved = (x_low[place].astype(F32) + branch).astype(BF16)
        next_ref[place] = moved
        values = moved.astype(F32)
        low[place] = (values * rms_parts(values) * norm_out[1]).astype(BF16)
        mine(place).start()
        every(place).begin(low.at[place])

    proj_ref[...] = weights.forward(normed[step].reshape(block, D))

    @pl.when(step == 0)
    def _():
        stage(gathers[1], 1)

    @pl.when(step == 1)
    def _():
        outs[0].settle()
        out_load.start()
        out_load.wait()

    @pl.when(step >= 1)
    def _():
        project(step - 1)

    meta = meta_out.at[pl.ds(pl.multiple_of(step * block, Q), block)]
    segrow = segrow_out.at[pl.ds(step * subs, subs)]

    def one_chunk(sub, carry):
        mix_forward(
            ch, proj_ref, meta, segrow, conv_w_out.at[0], conv_b_out.at[0], dtb_out.at[0], alog_out.at[0],
            skip_out.at[0], gated.at[step % 2], squares.at[step], mixed_ref, pre_ref, state_out_ref, pad, state, sub,
            d * heads,
        )

        @pl.when(sub == 0)
        def _():
            @pl.when(step >= 2)
            def _():
                conclude(step - 2)

            @pl.when(step >= 1)
            def _():
                pass_on(step - 1)

            @pl.when(step >= 3)
            def _():
                every(step - 3).relay()

            for k in range(2, nf):

                @pl.when(step == k - 1)
                def _():
                    stage(gathers[1], k)


        return carry

    lax.fori_loop(0, subs, one_chunk, 0)
    tile(step).begin()

    @pl.when(step == 1)
    def _():
        outs[1].begin()

    @pl.when(step == nf - 2)
    def _():
        enter_cot.start_all()

    @pl.when(step == 2)
    def _():
        outs[1].begin_other()

    for k in range(1, nf):

        @pl.when(step == min(k + 1, nf - 1))
        def _():
            outs[1].hops(k)
            if k == nf - 1:
                outs[1].hand_over()

    @pl.when(step == nf - 1)
    def _():
        project(nf - 1)
        pass_on(nf - 1)
        conclude(nf - 2)
        every(nf - 3).relay()
        conclude(nf - 1)
        every(nf - 2).relay()
        for k in range(1, nf):
            gathers[1].settle(k)
        gathers[1].settle_begin()
        outs[1].settle()
        enter.settle()
        enter_cot.arrive()
        enter_cot.settle()
        normed_copy.wait()
        hidden_copy.wait()
        every(nf - 1).relay()
        for place in range(nf):
            every(place).close()
            mine(place).wait()
        blocks.settle(nf)


def run_first(ch, nf, nd, x, cot, seg, in_rows, out_rows, conv_w, conv_b, norm_gain, gate_gain, head_table, identity):
    block = x.shape[1]
    length = block * nf
    conv_width = ch + 2 * N
    columns = in_rows.shape[1]
    width = 2 * ch + DIN - 2 * DI
    pieces = length // Q
    subs = block // Q
    bits = len(bits_of(nd))
    own = (nf, block // nd, D)
    every = (nf, nd, block // nd, D)
    w_in = jax.ShapeDtypeStruct((nf, width, columns), BF16)
    anywhere = pl.BlockSpec(memory_space=pl.ANY)
    dma = pltpu.SemaphoreType.DMA
    ordered = lambda s: (s, 0)
    small = [(2, K, conv_width), (2, 1, conv_width), (2, 1, LANES), (2, 1, LANES), (2, 1, ch), (2, 1, ch), (2, 1, D)]
    resident = small + [(length, LANES), (pieces, 1, Q)]
    return pl.pallas_call(
        functools.partial(first_kernel, ch, nf, nd),
        grid=(nf,),
        in_specs=[anywhere] * 5 + [once(part.shape) for part in (conv_w, conv_b, norm_gain, gate_gain, head_table)],
        out_specs=[
            pl.BlockSpec((block, width), ordered),
            pl.BlockSpec((block, ch), ordered),
            pl.BlockSpec((block, conv_width), ordered),
            pl.BlockSpec((subs, N, ch), lambda s: (s, 0, 0)),
            once((length, ch)),
            once(own),
            once(own),
            once((pieces, Q)),
        ]
        + [once(shape) for shape in resident]
        + [anywhere] * 8,
        out_shape=[
            jax.ShapeDtypeStruct((length, width), F32),
            jax.ShapeDtypeStruct((length, ch), F32),
            jax.ShapeDtypeStruct((length, conv_width), F32),
            jax.ShapeDtypeStruct((pieces, N, ch), F32),
            jax.ShapeDtypeStruct((length, ch), BF16),
            jax.ShapeDtypeStruct(own, F32),
            jax.ShapeDtypeStruct(own, BF16),
            jax.ShapeDtypeStruct((pieces, Q), F32),
        ]
        + [jax.ShapeDtypeStruct(shape, F32) for shape in resident]
        + [
            jax.ShapeDtypeStruct(every, BF16),
            jax.ShapeDtypeStruct(every, BF16),
            jax.ShapeDtypeStruct(own, BF16),
            jax.ShapeDtypeStruct(own, BF16),
            w_in,
            w_in,
            jax.ShapeDtypeStruct((ch, D), BF16),
            jax.ShapeDtypeStruct((ch, D), BF16),
        ],
        scratch_shapes=[
            pltpu.VMEM(held_shape(w_in), BF16),
            pltpu.VMEM((ch, D), BF16),
            pltpu.VMEM((Q + 8, conv_width), F32),
            pltpu.VMEM((N, ch), F32),
            pltpu.VMEM((2, block, ch), F32),
            pltpu.VMEM(every, F32),
            pltpu.VMEM((nd - 1, nf, block // nd, D), F32),
            pltpu.VMEM((nf, nd, 8, LANES), F32),
            pltpu.VMEM(own, BF16),
            pltpu.VMEM(every, BF16),
            pltpu.VMEM(own, BF16),
            pltpu.VMEM((2, 8, DC), F32),
            pltpu.VMEM((pieces * 8, LANES), F32),
            pltpu.VMEM((width, columns), BF16),
            pltpu.VMEM((ch, D), BF16),
            dma((bits, nf, nd)),
            dma((bits, nf, nd)),
            dma((nf, nd)),
            dma((nf, nd)),
            dma((nf, nd)),
            dma((nf, nd)),
            dma((2, nd)),
            dma((2, nd)),
            dma((2, nf)),
            dma((2, nf)),
            dma((7, 2 * nf)),
            dma((7, 2 * nf)),
            dma((6, 4)),
            dma((6, 4)),
            dma((3 + nf,)),
            dma((nf,)),
            dma((2,)),
            dma((2,)),
            dma((3,)),
        ],
        compiler_params=pltpu.CompilerParams(
            vmem_limit_bytes=VMEM_LIMIT, collective_id=identity, has_side_effects=True
        ),
        name="layer_first",
    )(x, cot, seg, in_rows, out_rows, conv_w, conv_b, norm_gain, gate_gain, head_table)


def layer_kernel(
    ch, nf, nd,
    normed_ref, meta_ref, segrow_ref, conv_w_ref, conv_b_ref, dtb_ref, alog_ref, skip_ref, gain_ref,
    w_in_ref, w_out_ref, hidden_ref, extra_ref,
    proj_ref, nout_ref, mixed_ref, pre_ref, state_out_ref, branch_ref, next_ref, ratio_ref, pull_ref, cot_all,
    held, w_out, pad, state, gated, partial, landed, squares, pulls,
    sum_send, sum_recv, tile_send, tile_recv, group_send, group_recv, local_sem, load_sem,
):
    step = pl.program_id(0)
    y, z, d = lax.axis_index("section"), lax.axis_index("fsdp"), lax.axis_index("dp")
    block = normed_ref.shape[0]
    subs = block // Q
    rows = block // nd
    bits = bits_of(nd)
    blocks = BlockSum(partial, landed, d, nd, sum_send, sum_recv)
    weights = Weights(w_in_ref, held, load_sem)
    out_load = pltpu.make_async_copy(w_out_ref, w_out, local_sem.at[0])
    cot_group = GroupRows(lambda device: cot_all.at[:, device], d, nd, group_send.at[0], group_recv.at[0])
    cot_keep = pltpu.make_async_copy(extra_ref, cot_group.part(0), local_sem.at[1])

    @pl.when(step == 0)
    def _():
        for copy in weights.copies():
            copy.start()
        out_load.start()
        greet([(None, {"dp": flip(d, j)}) for j in range(1, nd)])
        cot_keep.start()
        cot_group.begin(extra_ref)
        pad[0:8, :] = jnp.zeros((8, pad.shape[1]), F32)
        state[...] = jnp.zeros_like(state)
        pulls[0] = jnp.zeros(pulls.shape[1:], F32)
        for copy in weights.copies():
            copy.wait()
        out_load.wait()

    def tile(place):
        return GroupTiles(squares.at[place], tile_send.at[place], tile_recv.at[place], d, nd)

    def project(place):
        ratio = lax.rsqrt(tile(place).finish() * (1.0 / DI) + EPSILON)
        for sub in range(subs):
            piece = place * subs + sub
            ratio_ref[pl.ds(piece, 1), :] = ratio[sub : sub + 1, :]
            normed_out = gated[place % 2, sub * Q : (sub + 1) * Q, :] * to_column(ratio[sub : sub + 1, :])
            nout_ref[pl.ds(pl.multiple_of(piece * Q, Q), Q), :] = (normed_out * gain_ref[...]).astype(BF16)
        here_rows = pl.ds(pl.multiple_of(place * block, Q), block)
        product = dot(nout_ref[here_rows, :], w_out[...]).astype(partial.dtype)
        for o in range(nd):
            partial[place, o] = product[o * rows : (o + 1) * rows, :]
        blocks.send(0, place)

    def pass_on(place):
        for k in range(1, len(bits)):
            blocks.send(k, place)

    def conclude(place):
        branch = blocks.own(place)
        branch_ref[place] = branch
        moved = (hidden_ref[place].astype(F32) + branch).astype(BF16)
        next_ref[place] = moved
        first = place * block + d * rows
        pulls[0, pl.ds(first // Q, 1), :] += to_row(
            jnp.sum(extra_ref[place].astype(F32) * branch, axis=1, keepdims=True), first % Q
        )

    proj_ref[...] = weights.forward(normed_ref[...])

    @pl.when(step >= 1)
    def _():
        project(step - 1)

    def one_chunk(sub, carry):
        mix_forward(
            ch, proj_ref, meta_ref, segrow_ref, conv_w_ref, conv_b_ref, dtb_ref, alog_ref, skip_ref,
            gated.at[step % 2], squares.at[step], mixed_ref, pre_ref, state_out_ref, pad, state, sub, d * (H // nd),
        )

        @pl.when(sub == 0)
        def _():
            @pl.when(step >= 2)
            def _():
                conclude(step - 2)

            @pl.when(step >= 1)
            def _():
                pass_on(step - 1)

        return carry

    lax.fori_loop(0, subs, one_chunk, 0)
    tile(step).begin()

    @pl.when(step == min(2, nf - 1))
    def _():
        cot_group.relay()

    @pl.when(step == nf - 1)
    def _():
        project(nf - 1)
        pass_on(nf - 1)
        conclude(nf - 2)
        conclude(nf - 1)
        pull_ref[...] = group_tiles(pulls, group_send.at[1], group_recv.at[1], d, nd)
        cot_group.close()
        cot_keep.wait()
        blocks.settle(nf)


def once(shape):
    return pl.BlockSpec(shape, lambda s: (0,) * len(shape), pipeline_mode=pl.Buffered(buffer_count=1))


def pick(part, layer):
    return pl.BlockSpec(
        (None,) + part.shape[1:], lambda s: (layer, 0, 0), pipeline_mode=pl.Buffered(buffer_count=1)
    )


def run_layer(
    ch, rows, nf, nd, normed_all, meta, segrow, small, w_in, w_out, hidden, extra, identity
):
    length, width = normed_all.shape[0], w_in.shape[1]
    layer = 1
    conv_width = ch + 2 * N
    block = rows
    steps = nf
    pieces = length // Q
    subs = block // Q
    own = (nf, rows // nd, D)
    every = (nf, nd, rows // nd, D)
    bits = len(bits_of(nd))
    dma = pltpu.SemaphoreType.DMA
    anywhere = pl.BlockSpec(memory_space=pl.ANY)
    ordered = lambda s: (s, 0)
    ordered3 = lambda s: (s, 0, 0)
    return pl.pallas_call(
        functools.partial(layer_kernel, ch, nf, nd),
        grid=(steps,),
        in_specs=[
            pl.BlockSpec((block, D), ordered),
            pl.BlockSpec((block, LANES), ordered),
            pl.BlockSpec((subs, 1, Q), ordered3),
        ]
        + [pick(part, layer) for part in small]
        + [
            anywhere,
            anywhere,
            once(own),
            once(own),
        ],
        out_specs=[
            pl.BlockSpec((block, width), ordered),
            once((length, ch)),
            pl.BlockSpec((block, ch), ordered),
            pl.BlockSpec((block, conv_width), ordered),
            pl.BlockSpec((subs, N, ch), ordered3),
            once(own),
            once(own),
            once((pieces, Q)),
            once((pieces, Q)),
            anywhere,
        ],
        out_shape=[
            jax.ShapeDtypeStruct((length, width), F32),
            jax.ShapeDtypeStruct((length, ch), BF16),
            jax.ShapeDtypeStruct((length, ch), F32),
            jax.ShapeDtypeStruct((length, conv_width), F32),
            jax.ShapeDtypeStruct((pieces, N, ch), F32),
            jax.ShapeDtypeStruct(own, F32),
            jax.ShapeDtypeStruct(own, BF16),
            jax.ShapeDtypeStruct((pieces, Q), F32),
            jax.ShapeDtypeStruct((pieces, Q), F32),
            jax.ShapeDtypeStruct(every, BF16),
        ],
        scratch_shapes=[
            pltpu.VMEM(held_shape(w_in), BF16),
            pltpu.VMEM((ch, D), BF16),
            pltpu.VMEM((Q + 8, conv_width), F32),
            pltpu.VMEM((N, ch), F32),
            pltpu.VMEM((2, block, ch), F32),
            pltpu.VMEM(every, BF16),
            pltpu.VMEM((nd - 1, nf, rows // nd, D), BF16),
            pltpu.VMEM((steps, nd, 8, LANES), F32),
            pltpu.VMEM((nd, pieces, Q), F32),
            dma((bits, nf, nd)),
            dma((bits, nf, nd)),
            dma((steps, nd)),
            dma((steps, nd)),
            dma((nf, nd)),
            dma((nf, nd)),
            dma((2,)),
            dma((nf,)),
        ],
        compiler_params=pltpu.CompilerParams(
            vmem_limit_bytes=VMEM_LIMIT, collective_id=identity, has_side_effects=True
        ),
        name="layer_last",
    )(normed_all, meta, segrow, *small, w_in, w_out, hidden, extra)


def mix_backward(
    ch, proj_ref, pre_ref, mixed_ref, state_ref, grad_ref, ratio_ref, pull_ref, meta_ref, segrow_ref,
    conv_w_ref, dtb_ref, alog_ref, skip_ref, gain_ref,
    dproj_ref, small_ref, tail, work, dstate, sub, chunk, turn,
):
    conv_width = ch + 2 * N
    rows = pl.ds(pl.multiple_of(sub * Q, Q), Q)
    meta = meta_ref[rows, :]
    pre = pre_ref[rows, :]
    sig = jax.nn.sigmoid(pre)
    conv_out = pre * sig
    values = conv_out[:, :ch]
    b_part = conv_out[:, ch : ch + N]
    c_part = conv_out[:, ch + N :]
    row, column = triangles()
    tri = jnp.where(row >= column, 1.0, 0.0)
    shifted, step, log_decay, cumulative = decay_tables(
        own_steps(proj_ref[rows, ch + conv_width :], turn), dtb_ref[...], alog_ref[...], tri
    )
    linked = (row <= column) & (meta[:, 0:1] == segrow_ref[sub])
    b_low = b_part.astype(BF16)
    c_low = c_part.astype(BF16)
    inner = jnp.where(linked, dot(b_low, c_low, ((1,), (1,))), 0.0)
    cum_t = cumulative.T
    last = cumulative[Q - 1 : Q, :]
    entry = meta[:, 4:5] * jnp.exp(cumulative)
    weight = meta[:, 5:6] * jnp.exp(last - cumulative)
    state_in = state_ref[sub]
    dstate_in = dstate[...]
    state_low = state_in.astype(BF16)
    dstate_low = dstate_in.astype(BF16)
    carried = dot(c_low, state_low)
    carried_back = dot(b_low, dstate_low)
    low_half = lax.broadcasted_iota(jnp.int32, (Q, LANES), 1) < P_SIZE
    lane = lax.broadcasted_iota(jnp.int32, (Q, LANES), 1)
    ratio = to_column(ratio_ref[pl.ds(chunk, 1), :])
    pull = ratio * ratio * to_column(pull_ref[pl.ds(chunk, 1), :]) * (1.0 / DI)
    dinner = jnp.zeros((Q, Q), F32)
    turned_parts = []
    step_parts, exit_parts, entry_parts = [], [], []
    weighted = []
    entered = []
    entry_rows = []
    dpre_parts = []
    for pair in range(ch // LANES):
        lanes = slice(pair * LANES, (pair + 1) * LANES)
        values_pair = values[:, lanes]
        gate = proj_ref[rows, lanes]
        mixed = mixed_ref[rows, lanes]
        gate_sig = jax.nn.sigmoid(gate)
        gate_silu = gate * gate_sig
        gated = mixed * gate_silu
        scaled = grad_ref[rows, lanes] * ratio
        small_ref[5:6, lanes] += jnp.sum(scaled * gated, axis=0, keepdims=True)
        dgated = scaled * gain_ref[:, lanes] - gated * pull
        dproj_ref[rows, lanes] = (dgated * mixed * (gate_sig + gate_silu * (1.0 - gate_sig))).astype(BF16)
        dmixed = dgated * gate_silu
        small_ref[6:7, lanes] += jnp.sum(dmixed * values_pair, axis=0, keepdims=True)
        zero = jnp.zeros_like(values_pair)
        dmixed_halves = [jnp.where(low_half, dmixed, zero).astype(BF16), jnp.where(low_half, zero, dmixed).astype(BF16)]
        values_low = values_pair.astype(BF16)
        step_pair = pair_lanes(step, 2 * pair, low_half)
        mats = []
        for half, head in enumerate((2 * pair, 2 * pair + 1)):
            spread = jnp.minimum(cum_t[head : head + 1, :] - cumulative[:, head : head + 1], 0.0)
            plain = jnp.exp(spread)
            decay = plain * step[:, head : head + 1]
            product = dot(values_low, dmixed_halves[half], ((1,), (1,)))
            mats.append((inner * plain).astype(BF16))
            spreaded = product * decay
            dinner = dinner + spreaded
            turned_parts.append((spreaded * inner).astype(BF16))
        back = dot(jnp.concatenate(mats, axis=1), jnp.concatenate(dmixed_halves, axis=0))
        weight_pair = pair_lanes(weight, 2 * pair, low_half)
        through = weight_pair * carried_back[:, lanes]
        total = back + through
        dvalues = step_pair * total + skip_ref[:, lanes] * dmixed
        step_parts.append((total * values_pair).astype(BF16))
        exit_parts.append((through * values_pair * step_pair).astype(BF16))
        entry_pair = pair_lanes(entry, 2 * pair, low_half)
        entry_grad = entry_pair * dmixed
        entry_parts.append((entry_grad * carried[:, lanes]).astype(BF16))
        weighted.append((weight_pair * step_pair * values_pair).astype(BF16))
        entered.append(entry_grad.astype(BF16))
        entry_rows.append(entry_pair[Q - 1 : Q, :])
        dpre_parts.append(dvalues)
    weighted = jnp.concatenate(weighted, axis=1)
    entered = jnp.concatenate(entered, axis=1)
    entry_rows = jnp.concatenate(entry_rows, axis=1)
    dinner_low = jnp.where(linked, dinner, 0.0).astype(BF16)
    db = dot(dinner_low, c_low) + dot(weighted, dstate_low, ((1,), (1,)))
    dc = dot(dinner_low.T, b_low) + dot(entered, state_low, ((1,), (1,)))
    state_terms = jnp.sum(state_in * dstate_in, axis=0, keepdims=True) * entry_rows
    head_lane = lax.broadcasted_iota(jnp.int32, (1, LANES), 1)
    state_sum = jnp.zeros((1, LANES), F32)
    for head in range(ch // P_SIZE):
        part = jnp.sum(state_terms[:, head * P_SIZE : (head + 1) * P_SIZE], axis=1, keepdims=True)
        state_sum = state_sum + jnp.where(head_lane == head, part, 0.0)
    heads = ch // P_SIZE

    def marks(shape, place, index):
        return jnp.where(place(shape) == index(shape), 1.0, 0.0).astype(BF16)

    rows_of_shape = lambda shape: lax.broadcasted_iota(jnp.int32, shape, 0)
    columns_of_shape = lambda shape: lax.broadcasted_iota(jnp.int32, shape, 1)
    by_head = marks((ch, LANES), lambda shape: rows_of_shape(shape) // P_SIZE, columns_of_shape)
    dstep = dot(jnp.concatenate(step_parts, axis=1), by_head)
    dexit = dot(jnp.concatenate(exit_parts, axis=1), by_head)
    dcum = dot(jnp.concatenate(entry_parts, axis=1), by_head)
    by_target = marks((LANES, heads * Q), rows_of_shape, lambda shape: columns_of_shape(shape) // Q)
    by_source = marks((heads * Q, LANES), lambda shape: rows_of_shape(shape) // Q, columns_of_shape)
    dcum = dcum + dot(by_target, jnp.concatenate(turned_parts, axis=0)).T
    dcum = dcum - dot(jnp.concatenate(turned_parts, axis=1), by_source)
    later = jnp.where(row <= column, 1.0, 0.0)
    before = jnp.where(row > column, 1.0, 0.0)
    dlog = fine_dot(later, dcum) + fine_dot(before, dexit) + state_sum
    growth = jnp.exp(alog_ref[...])
    dstep = dstep - dlog * growth
    ddt = dstep * jax.nn.sigmoid(shifted)
    small_ref[7:8, 0:LANES] += jnp.sum(ddt, axis=0, keepdims=True)
    small_ref[7:8, LANES : 2 * LANES] += jnp.sum(dlog * log_decay, axis=0, keepdims=True)
    dproj_ref[rows, ch + conv_width :] = pltpu.roll(jnp.where(lane < heads, ddt, 0.0), turn, 1)[:, :H].astype(BF16)
    dstate[...] = entry_rows * dstate_in + dot(c_part.T.astype(BF16), entered)
    dconv_out = jnp.concatenate(dpre_parts + [db, dc], axis=1)
    dpre = dconv_out * (sig + conv_out * (1.0 - sig))
    raw = proj_ref[rows, ch : ch + conv_width]
    small_ref[4:5, :] += jnp.sum(dpre, axis=0, keepdims=True)
    draw = conv_w_ref[3:4, :] * dpre
    small_ref[3:4, :] += jnp.sum(raw * dpre, axis=0, keepdims=True)
    for lag in range(1, K):
        kept = meta[:, lag : lag + 1] * dpre
        work[0:Q, :] = kept
        work[Q : Q + 8, :] = tail[lag - 1]
        moved = work[lag : lag + Q, :]
        tail[lag - 1] = kept[0:8, :]
        draw = draw + conv_w_ref[3 - lag : 4 - lag, :] * moved
        small_ref[3 - lag : 4 - lag, :] += jnp.sum(raw * moved, axis=0, keepdims=True)
    dproj_ref[rows, ch : ch + conv_width] = draw.astype(BF16)


def gain_rows(width):
    return [(start, min(width, D - start)) for start in range(0, D, width)]


def layer_back_kernel(
    ch, nf, nd, last, fused,
    grad_all_ref, proj_ref, pre_ref, mixed_ref, state_ref, meta_ref, segrow_ref, ratio_ref, pull_ref,
    conv_w_ref, dtb_ref, alog_ref, skip_ref, gain_ref, w_in_ref, w_out_ref,
    hidden_ref, grad_own_ref, norm_gain_ref, branch_ref, *refs,
):
    count = 2 if last else 1
    sources, refs = refs[: count - fused], refs[count - fused :]
    if not last:
        rows_out, refs = refs[0], refs[1:]
    if fused:
        (normed_ref, nout_ref, grads_ref), refs = refs[:3], refs[3:]
    (
        dproj_ref, small_ref, next_ref, next_pull_ref, moved_ref,
    ) = refs[:5]
    results, refs = refs[5 : 5 + count], refs[5 + count :]
    if not last:
        final_ref, refs = refs[0], refs[1:]
    (
        held, w_out, tail, work, dstate, dnout, partial, landed, pulls, low, dgain,
        sum_send, sum_recv, tile_send, tile_recv, group_send, group_recv, local_sem, load_sem, deal_send, deal_recv,
    ) = refs[:21]
    refs = refs[21:]
    if fused:
        dproj_all, normed, staged, out_grad, normed_sem, staged_sem = refs[-6:]
        refs = refs[:-6]
        nout = dproj_all.at[:, pl.ds(0, ch)]
        block = grad_all_ref.shape[0]
        weight_grad = dproj_ref
        dproj_ref = dproj_all.at[pl.ds(pl.multiple_of((nf - 1 - pl.program_id(0)) * block, Q), block)]
        normed_load = pltpu.make_async_copy(normed_ref, normed, normed_sem.at[0])
        grads_load = pltpu.make_async_copy(grads_ref, normed, normed_sem.at[0])
        nout_load = pltpu.make_async_copy(nout_ref, nout, normed_sem.at[1])
        sources = (out_grad,) + sources
    step = pl.program_id(0)
    y, z, d = lax.axis_index("section"), lax.axis_index("fsdp"), lax.axis_index("dp")
    block = grad_all_ref.shape[0]
    subs = block // Q
    rows = block // nd
    bits = bits_of(nd)
    place = nf - 1 - step
    blocks = BlockSum(partial, landed, d, nd, sum_send, sum_recv)
    sums = [
        SectionSum(make(source, nf), nf, y, z, *refs[5 * k : 5 * k + 5])
        for k, (make, source) in enumerate(zip((out_view, in_view), sources))
    ]
    weights = Weights(w_in_ref, held, load_sem)
    out_load = pltpu.make_async_copy(w_out_ref, w_out, local_sem.at[0])
    if last:
        leave = Deal(moved_ref, low, nf, nd, z, d, deal_send, deal_recv, True)
    else:
        leave = Deal(final_ref, rows_out, nf, nd, z, d, deal_send, deal_recv, True)

    def every(place):
        return GroupRows(lambda device: moved_ref.at[place, device], d, nd, group_send.at[place], group_recv.at[place])

    def mine(place):
        return pltpu.make_async_copy(low.at[place], moved_ref.at[place, d], local_sem.at[2 + place])

    @pl.when(step == 0)
    def _():
        for copy in weights.copies():
            copy.start()
        out_load.start()
        greet(
            [(None, {"dp": flip(d, j)}) for j in range(1, nd)]
            + line_neighbours(nf, y, z)
            + deal_partners(nf, nd, z, d)
        )
        if fused:
            grads_load.start()
            nout_load.start()
        for one in sums[::-1] if not fused else sums[:0:-1]:
            one.begin()
        if not last:
            leave.start_all()
        tail[...] = jnp.zeros_like(tail)
        dstate[...] = jnp.zeros_like(dstate)
        small_ref[...] = jnp.zeros_like(small_ref)
        dgain[...] = jnp.zeros_like(dgain)
        pulls[0] = jnp.zeros(pulls.shape[1:], F32)
        if fused:
            grads_load.wait()
            nout_load.wait()

            def out_tile(i, carry):
                part = pl.ds(pl.multiple_of(i * LANES, LANES), LANES)
                out_grad[part, :] = dot(nout[:, part], normed[...], ((0,), (0,))).astype(BF16)
                return carry

            lax.fori_loop(0, ch // LANES, out_tile, 0)
            sums[0].begin()
            normed_load.start()
        for copy in weights.copies():
            copy.wait()
        out_load.wait()

    def pass_on(place):
        for k in range(1, len(bits)):
            blocks.send(k, place)

    def conclude(place):
        dnormed = blocks.own(place)
        hidden = hidden_ref[place].astype(F32)
        inverse = rms_parts(hidden)
        dgain[...] += jnp.sum(dnormed * hidden * inverse, axis=0, keepdims=True)
        scaled = dnormed * norm_gain_ref[...]
        dhidden = inverse * (
            scaled - hidden * (inverse * inverse) * jnp.mean(scaled * hidden, axis=1, keepdims=True)
        )
        moved = (grad_own_ref[place].astype(F32) + dhidden).astype(BF16)
        low[place] = moved
        if last:
            leave.start(place)
        else:
            next_ref[place] = moved
            first = place * block + d * rows
            pulls[0, pl.ds(first // Q, 1), :] += to_row(
                jnp.sum(moved.astype(F32) * branch_ref[place], axis=1, keepdims=True), first % Q
            )
            mine(place).start()
            every(place).begin(low.at[place])

    dnout[...] = dot(grad_all_ref[...], w_out[...], ((1,), (1,)))

    @pl.when(step >= 1)
    def _():
        pass_on(place + 1)

    def one_chunk(turn, carry):
        sub = subs - 1 - turn
        mix_backward(
            ch, proj_ref, pre_ref, mixed_ref, state_ref, dnout, ratio_ref, pull_ref, meta_ref, segrow_ref,
            conv_w_ref, dtb_ref, alog_ref, skip_ref, gain_ref,
            dproj_ref, small_ref, tail, work, dstate, sub, place * subs + sub, d * (H // nd),
        )

        @pl.when((turn == 0) & (step >= 1))
        def _():
            conclude(place + 1)

        return carry

    lax.fori_loop(0, subs, one_chunk, 0)
    product = weights.backward(dproj_ref[...]).astype(BF16)
    for o in range(nd):
        partial[place, o] = product[o * rows : (o + 1) * rows, :]
    blocks.send(0, place)
    if not last:

        @pl.when(step >= 1)
        def _():
            every(place + 1).relay()

    for k in range(nf - 1, 0, -1):

        @pl.when(step == nf - 1 - k)
        def _():
            for one in sums:
                one.stage(k)

    @pl.when(step == nf - 1)
    def _():
        pass_on(0)
        if fused:
            normed_load.wait()
            width = dproj_all.shape[1]
            wide = staged.shape[1]
            full = width // wide

            def store(i, size):
                rows = pl.ds(pl.multiple_of(i * wide, 16), size)
                return pltpu.make_async_copy(
                    staged.at[i % 2, pl.ds(0, size)], weight_grad.at[rows], staged_sem.at[i % 2]
                )

            def some(i, carry):
                @pl.when(i >= 2)
                def _():
                    store(i - 2, wide).wait()

                columns = dproj_all[:, pl.ds(pl.multiple_of(i * wide, LANES), wide)]
                staged[i % 2] = dot(columns, normed[...], ((0,), (0,))).astype(BF16)
                store(i, wide).start()
                return carry

            lax.fori_loop(0, full // 2, some, 0)
        conclude(0)
        for row, (start, size) in enumerate(gain_rows(small_ref.shape[1])):
            small_ref[8 + row : 9 + row, 0:size] = dgain[:, start : start + size]
        if last:
            next_pull_ref[...] = jnp.zeros_like(next_pull_ref)
        else:
            next_pull_ref[...] = group_tiles(pulls, tile_send, tile_recv, d, nd)
        if fused:
            lax.fori_loop(full // 2, full, some, 0)
            store(full - 2, wide).wait()
            rest = width - full * wide
            if rest:
                staged[full % 2, 0:rest] = dot(dproj_all[:, full * wide :], normed[...], ((0,), (0,))).astype(BF16)
                store(full, rest).start()
                store(full, rest).wait()
            store(full - 1, wide).wait()
        for one, result in zip(sums, results):
            one.finish()
            copy = pltpu.make_async_copy(one.result, result, local_sem.at[1])
            copy.start()
            copy.wait()
            one.settle()
        leave.arrive()
        leave.settle()
        if not last:
            every(0).relay()
            for k in range(nf):
                every(k).close()
                mine(k).wait()
        blocks.settle(nf)


def run_layer_back(
    ch, rows, nf, nd, last, grad_all, proj, pre, mixed, states, meta, segrow, ratio, pull, small, w_in, w_out,
    hidden, grad_own, norm_gain, branch, identity, sums, leaving, more,
):
    length, width = proj.shape
    if more:
        shapes = [out_part_shape(nf, w_out)] + [in_part_shape(nf, g) for g in sums]
    else:
        shapes = [make(nf, g) for make, g in zip((out_part_shape, in_part_shape), sums)]
    conv_width = ch + 2 * N
    block = rows
    steps = nf
    own = (nf, rows // nd, D)
    every = (nf, nd, rows // nd, D)
    pieces = length // Q
    subs = block // Q
    bits = len(bits_of(nd))
    dma = pltpu.SemaphoreType.DMA
    ordered = lambda s: (steps - 1 - s, 0)
    ordered3 = lambda s: (steps - 1 - s, 0, 0)
    layer = 0 if last else 1
    conv_w, conv_b, dtb, alog, skip, gain = small
    return pl.pallas_call(
        functools.partial(layer_back_kernel, ch, nf, nd, last, bool(more)),
        grid=(steps,),
        in_specs=[
            pl.BlockSpec((block, D), ordered),
            pl.BlockSpec((block, width), ordered),
            pl.BlockSpec((block, conv_width), ordered),
            pl.BlockSpec((block, ch), ordered),
            pl.BlockSpec((subs, N, ch), ordered3),
            pl.BlockSpec((block, LANES), ordered),
            pl.BlockSpec((subs, 1, Q), ordered3),
            once((pieces, Q)),
            once((pieces, Q)),
        ]
        + [pick(part, layer) for part in (conv_w, dtb, alog, skip, gain)]
        + [
            pl.BlockSpec(memory_space=pl.ANY),
            pl.BlockSpec(memory_space=pl.ANY),
            once(own),
            once(own),
            pick(norm_gain, layer),
            pl.BlockSpec(memory_space=pl.ANY) if last else once(own),
        ]
        + [pl.BlockSpec(memory_space=pl.ANY)] * (len(sums) + len(leaving) + len(more)),
        out_specs=[
            pl.BlockSpec(memory_space=pl.ANY) if more else pl.BlockSpec((block, width), ordered),
            once((16, conv_width)),
            pl.BlockSpec(memory_space=pl.ANY) if last else once(own),
            once((pieces, Q)),
            pl.BlockSpec(memory_space=pl.ANY),
        ]
        + [pl.BlockSpec(memory_space=pl.ANY)] * (len(shapes) + len(leaving)),
        out_shape=[
            jax.ShapeDtypeStruct((width, D) if more else (length, width), BF16),
            jax.ShapeDtypeStruct((16, conv_width), F32),
            jax.ShapeDtypeStruct(own, BF16),
            jax.ShapeDtypeStruct((pieces, Q), F32),
            jax.ShapeDtypeStruct((rows, D) if last else every, BF16),
        ]
        + [jax.ShapeDtypeStruct(shape, BF16) for shape in shapes]
        + [jax.ShapeDtypeStruct((rows, D), BF16) for part in leaving],
        scratch_shapes=[
            pltpu.VMEM(held_shape(w_in), BF16),
            pltpu.VMEM((ch, D), BF16),
            pltpu.VMEM((K - 1, 8, conv_width), F32),
            pltpu.VMEM((Q + 8, conv_width), F32),
            pltpu.VMEM((N, ch), F32),
            pltpu.VMEM((block, ch), F32),
            pltpu.VMEM(every, BF16),
            pltpu.VMEM((nd - 1, nf, rows // nd, D), BF16),
            pltpu.VMEM((nd, pieces, Q), F32),
            pltpu.VMEM(own, BF16),
            pltpu.VMEM((1, D), F32),
            dma((bits, nf, nd)),
            dma((bits, nf, nd)),
            dma((nd,)),
            dma((nd,)),
            dma((nf, nd)),
            dma((nf, nd)),
            dma((2 + nf,)),
            dma((nf,)),
            dma((nf,)),
            dma((nf,)),
        ]
        + [part for shape in shapes for part in section_sum_scratch(nf, shape)]
        + (
            [
                pltpu.VMEM((length, width), BF16),
                pltpu.VMEM((length, D), BF16),
                pltpu.VMEM((2, LANES, D), BF16),
                pltpu.VMEM((ch, D), BF16),
                dma((2,)),
                dma((2,)),
            ]
            if more
            else []
        ),
        compiler_params=pltpu.CompilerParams(
            vmem_limit_bytes=VMEM_LIMIT, collective_id=identity, has_side_effects=True
        ),
        name="layer_back_last" if last else "layer_back_first",
    )(
        grad_all, proj, pre, mixed, states, meta, segrow, ratio, pull, conv_w, dtb, alog, skip, gain, w_in, w_out,
        hidden, grad_own, norm_gain, branch, *sums, *leaving, *more,
    )


def shards(
    inputs, segment, cotangent, norm_gain, in_weight, conv_weight, conv_bias, dt_bias, a_log, d_skip,
    gate_gain, out_weight,
):
    fsdp, dp = lax.axis_size("fsdp"), lax.axis_size("dp")
    section, here = lax.axis_index("section"), lax.axis_index("dp")
    rows = inputs.shape[2]
    ch = DI // dp
    heads = H // dp
    conv_width = ch + 2 * N
    seg_mine = lax.dynamic_index_in_dim(segment, section, 0, keepdims=False)[0].astype(F32)
    seg_mine = jnp.broadcast_to(seg_mine.reshape(rows // Q, 1, Q), (rows // Q, 8, Q)).reshape(-1, Q)
    head_table = jnp.pad(
        jnp.concatenate([dt_bias[0], a_log[0], d_skip[0]], axis=0), ((0, 0), (0, LANES - H))
    )
    (
        proj, mixed, pre, states, nout, branch, after, ratio, conv_w, conv_b, dtb, alog, skip, gain, gains, meta, segrow,
        normed_all, moved, hidden, cot_own, w_in0, w_in1, w_out0, w_out1,
    ) = run_first(
        ch, fsdp, dp, inputs[:, 0], cotangent[:, 0], seg_mine, in_weight[0, 0].T, out_weight[0, 0], conv_weight[0, 0],
        conv_bias[0], norm_gain[0], gate_gain[0], head_table, 2,
    )
    small = (conv_w, conv_b, dtb, alog, skip, gain)
    length = meta.shape[0]
    saved = [(normed_all.reshape(length, D), hidden, proj, nout, mixed, pre, states, branch, ratio)]
    normed_all, hidden = moved.reshape(length, D), after
    proj, nout, mixed, pre, states, branch, final_rows, ratio, pull, cot_all = run_layer(
        ch, rows, fsdp, dp, normed_all, meta, segrow, small, w_in1, w_out1, hidden, cot_own, 3
    )
    saved.append((normed_all, hidden, proj, nout, mixed, pre, states, branch, ratio))

    grad_all, grad_own = cot_all.reshape(length, D), cot_own
    in_grad, small_grads, parts = (), [None, None], []
    fused = D // fsdp % LANES == 0
    for layer in (1, 0):
        last = layer == 0
        normed_all, hidden, proj, gated, mixed, pre, states, branch, ratio = saved[layer]
        out_grad = () if fused else (dot(gated, grad_all, ((0,), (0,))).astype(BF16),)
        dproj, small_grads[layer], after, next_pull, moved, *done = run_layer_back(
            ch, rows, fsdp, dp, last, grad_all, proj, pre, mixed, states, meta, segrow, ratio, pull, small,
            w_in0 if last else w_in1, w_out0 if last else w_out1, hidden, grad_own, gains, saved[0][7], 4 + layer,
            out_grad + in_grad, () if last else (final_rows,), (normed_all, gated, grad_all) if fused else (),
        )
        if not last:
            *done, final = done
        parts += done
        if fused:
            grad = dproj
        else:
            grad = dot(dproj, normed_all, ((0,), (0,))).astype(BF16)
        if not fused:
            grad = jnp.swapaxes(grad.reshape(-1, fsdp, D // fsdp), 0, 1)
        in_grad = (grad,)
        if not last:
            grad_all, grad_own, pull = moved.reshape(length, D), after, next_pull
    input_grad = moved

    in_all, out_all, small_all = run_end(
        fsdp, dp, in_grad[0], parts[2], parts[1], parts[0], small_grads[0], small_grads[1]
    )
    in_total, out_total, gain_total, convw_total, convb_total, dtb_total, alog_total, skip_total, gate_total = run_finish(
        ch, dp, in_all, out_all, small_all
    )
    return (
        final[None, None],
        input_grad[None, None],
        gain_total[None],
        in_total.T[None, None],
        convw_total[None, None],
        convb_total[None],
        dtb_total[None],
        alog_total[None],
        skip_total[None],
        gate_total[None],
        out_total[None, None],
    )


def solution(mesh):
    return jax.shard_map(
        shards,
        mesh=mesh,
        in_specs=(
            P(None, "dp", "fsdp", None),
            P(None, "dp", "fsdp"),
            P(None, "dp", "fsdp", None),
            P("section", None, None),
            P("section", None, "fsdp", None),
            P("section", None, None, None),
            P("section", None, None),
            P("section", None, None),
            P("section", None, None),
            P("section", None, None),
            P("section", None, None),
            P("section", None, "fsdp", None),
        ),
        out_specs=(
            P("section", "dp", "fsdp", None),
            P("section", "dp", "fsdp", None),
            P("section", None, None),
            P("section", None, "fsdp", None),
            P("section", None, None, None),
            P("section", None, None),
            P("section", None, None),
            P("section", None, None),
            P("section", None, None),
            P("section", None, None),
            P("section", None, "fsdp", None),
        ),
        check_vma=False,
    )
```

```python
import functools

import jax
import jax.numpy as jnp
from jax import lax
from jax.experimental import pallas as pl
from jax.experimental.pallas import tpu as pltpu
from jax.sharding import PartitionSpec as P

D = 1536
H = 48
P_SIZE = 64
N = 128
K = 4
DI = 3072
DC = 3328
DIN = 6448
EPSILON = 1e-05
HIGHEST = lax.Precision.HIGHEST
BF16 = jnp.bfloat16
F32 = jnp.float32
Q = 128
LANES = 128


def dot(a, b, dims=((1,), (0,)), precision=None):
    return lax.dot_general(a, b, (dims, ((), ())), preferred_element_type=F32, precision=precision)


def low_dot(a, b, dims=((1,), (0,))):
    return dot(a.astype(BF16), b.astype(BF16), dims)


def fine_dot(a, b, dims=((1,), (0,))):
    return dot(a, b, dims, HIGHEST)


def halves(value):
    high = value.astype(BF16)
    return high, (value - high.astype(F32)).astype(BF16)


def split_dot(a, b, dims=((1,), (0,))):
    (a_high, a_low), (b_high, b_low) = halves(a), halves(b)
    a_axis, b_axis = dims[0][0], dims[1][0]
    both = dot(
        jnp.concatenate([a_high, a_low], axis=a_axis), jnp.concatenate([b_high, b_high], axis=b_axis), dims
    )
    return both + dot(a_high, b_low, dims)


def pair_lanes(table, first, low_half):
    return jnp.where(low_half, table[:, first : first + 1], table[:, first + 1 : first + 2])


def decay_tables(proj_dt, dt_bias, a_row, tri):
    shifted = proj_dt + dt_bias
    step = jnp.maximum(shifted, 0.0) + jnp.log1p(jnp.exp(-jnp.abs(shifted)))
    log_decay = -step * jnp.exp(a_row)
    cumulative = fine_dot(tri, log_decay)
    return shifted, step, log_decay, cumulative


def triangles():
    row = lax.broadcasted_iota(jnp.int32, (Q, Q), 0)
    column = lax.broadcasted_iota(jnp.int32, (Q, Q), 1)
    return row, column


MESH_ID = pl.DeviceIdType.MESH
VMEM_LIMIT = 60 * 1024 * 1024


def remote(src, dst, send_sem, recv_sem, device):
    return pltpu.make_async_remote_copy(
        src_ref=src, dst_ref=dst, send_sem=send_sem, recv_sem=recv_sem, device_id=device, device_id_type=MESH_ID
    )


def greet(devices):
    barrier = pltpu.get_barrier_semaphore()
    count = 0
    for condition, device in devices:
        if condition is None:
            pl.semaphore_signal(barrier, inc=1, device_id=device, device_id_type=MESH_ID)
            count = count + 1
        else:

            @pl.when(condition)
            def _():
                pl.semaphore_signal(barrier, inc=1, device_id=device, device_id_type=MESH_ID)

            count = count + condition.astype(jnp.int32)
    pl.semaphore_wait(barrier, count)


def bits_of(peers):
    return [1 << k for k in range(peers.bit_length() - 1)]


def has_bit(value, bit):
    return (value // bit) % 2


def flip(value, bits):
    bit = 1
    out = value
    while bit <= bits:
        if bits & bit:
            out = out + bit * (1 - 2 * has_bit(value, bit))
        bit = bit * 2
    return out


def to_column(row):
    down, across = triangles()
    return jnp.sum(jnp.where(down == across, jnp.broadcast_to(row, (Q, Q)), 0.0), axis=1, keepdims=True)


def to_row(column, offset=0):
    shape = (column.shape[0], Q)
    down = lax.broadcasted_iota(jnp.int32, shape, 0)
    across = lax.broadcasted_iota(jnp.int32, shape, 1)
    return jnp.sum(jnp.where(across == down + offset, jnp.broadcast_to(column, shape), 0.0), axis=0, keepdims=True)


class GroupTiles:

    def __init__(self, tiles, send_sem, recv_sem, here, peers):
        self.tiles, self.send_sem, self.recv_sem, self.here, self.peers = tiles, send_sem, recv_sem, here, peers

    def copies(self):
        return [
            remote(
                self.tiles.at[0], self.tiles.at[j], self.send_sem.at[j], self.recv_sem.at[j],
                {"dp": flip(self.here, j)},
            )
            for j in range(1, self.peers)
        ]

    def begin(self):
        for copy in self.copies():
            copy.start()

    def finish(self):
        for copy in self.copies():
            copy.wait()
        total = self.tiles[0]
        for j in range(1, self.peers):
            total = total + self.tiles[j]
        return total


def group_tiles(tiles, send_sem, recv_sem, here, peers):
    group = GroupTiles(tiles, send_sem, recv_sem, here, peers)
    group.begin()
    return group.finish()


class GroupRows:

    def __init__(self, where, here, peers, send_sem, recv_sem):
        self.where, self.here, self.peers = where, here, peers
        self.send_sem, self.recv_sem = send_sem, recv_sem

    def part(self, j):
        return self.where(flip(self.here, j))

    def copy(self, j, bit, source=None):
        part = self.part(j)
        return remote(
            part if source is None else source, part, self.send_sem.at[j ^ bit], self.recv_sem.at[j ^ bit],
            {"dp": flip(self.here, bit)},
        )

    def begin(self, source=None):
        for bit in bits_of(self.peers)[::-1]:
            self.copy(0, bit, source).start()

    def phase(self, bit):
        for j in range(bit, self.peers, 2 * bit):
            self.copy(j ^ bit, bit).wait_send()
            landing = self.part(j)
            remote(
                landing, landing, self.send_sem.at[j], self.recv_sem.at[j], {"dp": flip(self.here, bit)}
            ).wait_recv()
            for lower in bits_of(bit)[::-1]:
                self.copy(j, lower).start()

    def relay(self):
        for bit in bits_of(self.peers)[:0:-1]:
            self.phase(bit)

    def close(self):
        self.phase(1)

    def finish(self):
        self.relay()
        self.close()


def rows_of(whole, rows):
    return lambda device: whole.at[pl.ds(pl.multiple_of(device * rows, 8), rows)]


def rms_parts(values):
    return lax.rsqrt(jnp.mean(values * values, axis=-1, keepdims=True) + EPSILON)


class BlockSum:

    def __init__(self, partial, landed, here, peers, send_sem, recv_sem):
        self.partial, self.landed, self.here, self.peers = partial, landed, here, peers
        self.bits = bits_of(peers)
        self.send_sem, self.recv_sem = send_sem, recv_sem

    def slot(self, k, owner):
        return self.peers - self.peers // self.bits[k] + owner // (2 * self.bits[k])

    def copy(self, k, block, owner):
        return remote(
            self.partial.at[block, owner], self.landed.at[self.slot(k, owner), block], self.send_sem.at[k, block, owner],
            self.recv_sem.at[k, block, owner], {"dp": flip(self.here, self.bits[k])},
        )

    def total(self, block, owner, stages):
        total = self.partial[block, owner].astype(F32)
        for m in range(stages):
            self.copy(m, block, owner).wait_recv()
            total = total + self.landed[self.slot(m, owner), block].astype(F32)
        return total

    def leaving(self, k):
        return [flip(self.here, j) for j in range(self.bits[k], self.peers, 2 * self.bits[k])]

    def send(self, k, block):
        for owner in self.leaving(k):
            if k > 0:
                self.partial[block, owner] = self.total(block, owner, k).astype(self.partial.dtype)
            self.copy(k, block, owner).start()

    def own(self, block):
        return self.total(block, self.here, len(self.bits))

    def settle(self, blocks):
        for block in range(blocks):
            for k in range(len(self.bits)):
                for owner in self.leaving(k):
                    self.copy(k, block, owner).wait_send()


class Deal:

    def __init__(self, chunk, own, nf, nd, z, d, send_sem, recv_sem, outward):
        self.chunk, self.own, self.nf, self.nd, self.z, self.d = chunk, own, nf, nd, z, d
        self.send_sem, self.recv_sem, self.outward = send_sem, recv_sem, outward
        self.rows = chunk.shape[0] // nd

    def part(self, o):
        return self.chunk.at[pl.ds(pl.multiple_of(o * self.rows, 16), self.rows)]

    def holder(self, b):
        return {"fsdp": b, "dp": self.z}

    def worker(self, o):
        return {"fsdp": self.d, "dp": o}

    def at_home(self, k):
        return (self.z == self.d) & (self.z == k)

    def send(self, k):
        if self.outward:
            return remote(
                self.own.at[k], self.part(self.d), self.send_sem.at[k], self.recv_sem.at[self.d], self.holder(k)
            )
        return remote(
            self.part(k), self.own.at[self.z], self.send_sem.at[k], self.recv_sem.at[self.z], self.worker(k)
        )

    def recv(self, k):
        if self.outward:
            part = self.part(k)
            return remote(part, part, self.send_sem.at[k], self.recv_sem.at[k], self.worker(k))
        part = self.own.at[k]
        return remote(part, part, self.send_sem.at[k], self.recv_sem.at[k], self.holder(k))

    def keep(self, k):
        if self.outward:
            return pltpu.make_async_copy(self.own.at[k], self.part(k), self.send_sem.at[k])
        return pltpu.make_async_copy(self.part(k), self.own.at[k], self.send_sem.at[k])

    def start(self, k):
        @pl.when(self.at_home(k))
        def _():
            self.keep(k).start()

        @pl.when(jnp.logical_not(self.at_home(k)))
        def _():
            self.send(k).start()

    def start_all(self):
        for k in range(self.nf):
            self.start(k)

    def arrive(self):
        for k in range(self.nf):

            @pl.when(self.at_home(k))
            def _():
                self.keep(k).wait()

            @pl.when(jnp.logical_not(self.at_home(k)))
            def _():
                self.recv(k).wait_recv()

    def settle(self):
        for k in range(self.nf):

            @pl.when(jnp.logical_not(self.at_home(k)))
            def _():
                self.send(k).wait_send()


def deal_partners(nf, nd, z, d):
    out = []
    for k in range(nf):
        elsewhere = (z != d) | (z != k)
        out += [(elsewhere, {"fsdp": k, "dp": z}), (elsewhere, {"fsdp": d, "dp": k})]
    return out


class SectionGather:

    def __init__(self, held, section, nf, y, z, sems, own=None):
        self.own = own
        self.held, self.section, self.nf, self.y, self.z, self.sems = held, section, nf, y, z, sems
        width = held.shape[1]
        first = -(-width // 32) * 16
        self.spans = [(0, first), (first, width - first)]
        self.peer = {"section": 1 - y}

    def block(self, b, part):
        start, size = self.spans[part]
        return self.held.at[b, pl.ds(start, size)]

    def each(self, body):
        for part in range(2):
            owner = self.y == self.section

            @pl.when(owner if part == 0 else jnp.logical_not(owner))
            def _():
                body(part)

    def own_part(self, part):
        start, size = self.spans[part]
        return self.own.at[pl.ds(start, size)]

    def send(self, b, part, row, k, landed, device, source=None):
        here = self.block(b, part)
        return remote(
            here if source is None else source, here, self.sems.at[row, k], self.sems.at[landed, k], device
        )

    def right(self, k, b, part, source=None):
        return self.send(b, part, 0, k, 2, {"fsdp": self.z + 1}, source)

    def left(self, k, b, part, source=None):
        return self.send(b, part, 1, k, 3, {"fsdp": self.z - 1}, source)

    def over(self, k, b, part, source=None):
        return self.send(b, part, 4, k, 5, self.peer, source)

    def cross(self):
        here = self.block(self.z, 1)
        return remote(self.own_part(1), here, self.sems.at[6, 0], self.sems.at[6, 1], self.peer)

    def keep(self):
        return pltpu.make_async_copy(self.own, self.held.at[self.z], self.sems.at[6, 2])

    def has_right(self):
        return self.z < self.nf - 1

    def has_left(self):
        return self.z > 0

    def start_cross(self):
        @pl.when(self.y == self.section)
        def _():
            self.cross().start()
            self.keep().start()

    def begin(self):
        def body(part):
            source = None
            if part == 1:
                self.cross().wait_recv()
            else:
                source = self.own_part(0)

            @pl.when(self.has_right())
            def _():
                self.right(1, self.z, part, source).start()

            @pl.when(self.has_left())
            def _():
                self.left(1, self.z, part, source).start()

            if part == 0:
                self.cross().wait_send()
                self.over(0, self.z, 0, source).start()

        self.each(body)

    def settle_begin(self):
        def body(part):
            @pl.when(self.has_right())
            def _():
                self.right(1, self.z, part).wait_send()

            @pl.when(self.has_left())
            def _():
                self.left(1, self.z, part).wait_send()

            if part == 0:
                self.over(0, self.z, 0).wait_send()
                self.keep().wait()
            else:
                self.over(0, self.z, 0).wait_recv()

        self.each(body)

    def sides(self, k, body):
        @pl.when(self.z >= k)
        def _():
            body(self.z - k, k, True)

        @pl.when(self.z + k < self.nf)
        def _():
            body(self.z + k, self.nf + k, False)

    def arrive(self, k):
        def body(part):
            def one(b, index, from_left):
                if from_left:
                    self.right(k, b, part).wait_recv()
                else:
                    self.left(k, b, part).wait_recv()

            self.sides(k, one)

        self.each(body)

    def relay(self, k):
        def body(part):
            def one(b, index, from_left):
                if k < self.nf - 1:
                    if from_left:

                        @pl.when(self.has_right())
                        def _():
                            self.right(k + 1, b, part).start()

                    else:

                        @pl.when(self.has_left())
                        def _():
                            self.left(k + 1, b, part).start()

                self.over(index, b, part).start()

            self.sides(k, one)

        self.each(body)

    def settle(self, k):
        def body(part):
            def one(b, index, from_left):
                self.over(index, b, part).wait_send()
                self.over(index, b, 1 - part).wait_recv()
                if k < self.nf - 1:
                    if from_left:

                        @pl.when(self.has_right())
                        def _():
                            self.right(k + 1, b, part).wait_send()

                    else:

                        @pl.when(self.has_left())
                        def _():
                            self.left(k + 1, b, part).wait_send()

            self.sides(k, one)

        self.each(body)


class OutGather:

    def __init__(self, source, held, section, nf, y, z, d, sems, staged):
        self.staged = staged
        self.source, self.held, self.section, self.nf = source, held, section, nf
        self.y, self.z, self.d, self.sems = y, z, d, sems
        self.pieces = sems.shape[1]
        self.rows = source.shape[0] // self.pieces
        self.columns = source.shape[1] // 2
        self.peer = {"section": 1 - y}
        self.source_here = z == d

    def owner(self):
        return self.y == self.section

    def piece(self, ref, part, i):
        return ref.at[pl.ds(i * self.rows, self.rows), pl.ds(part * self.columns, self.columns)]

    def send(self, i, part, row, landed, device, source=None):
        target = self.piece(self.held, part, i)
        return remote(
            target if source is None else self.piece(source, part, i), target, self.sems.at[row, i],
            self.sems.at[landed, i], device,
        )

    def right(self, i, part, source=None):
        return self.send(i, part, 0, 2, {"fsdp": self.z + 1}, source)

    def left(self, i, part, source=None):
        return self.send(i, part, 1, 2, {"fsdp": self.z - 1}, source)

    def over(self, i, part, source=None):
        return self.send(i, part, 3, 4, self.peer, source)

    def cross(self):
        columns = pl.ds(self.columns, self.columns)
        return remote(
            self.source.at[:, columns], self.held.at[:, columns], self.sems.at[5, 0], self.sems.at[5, 1], self.peer
        )

    def stage(self):
        return pltpu.make_async_copy(self.source, self.staged, self.sems.at[5, 2])

    def keep(self):
        return pltpu.make_async_copy(self.staged, self.held, self.sems.at[5, 3])

    def goes_right(self):
        return (self.z >= self.d) & (self.z < self.nf - 1)

    def goes_left(self):
        return (self.z <= self.d) & (self.z > 0)

    def each(self, condition, body):
        for part in range(2):
            mine = self.owner() if part == 0 else jnp.logical_not(self.owner())

            @pl.when(condition & mine)
            def _():
                body(part)

    def along(self, i, part, action, source=None):
        @pl.when(self.goes_right())
        def _():
            action(self.right(i, part, source))

        @pl.when(self.goes_left())
        def _():
            action(self.left(i, part, source))

    def begin(self):
        @pl.when(self.source_here & self.owner())
        def _():
            self.cross().start()
            self.stage().start()
            for i in range(self.pieces):
                self.along(i, 0, lambda copy: copy.start(), self.source)

    def begin_other(self):
        @pl.when(self.source_here & jnp.logical_not(self.owner()))
        def _():
            self.cross().wait_recv()
            for i in range(self.pieces):
                self.along(i, 1, lambda copy: copy.start())

    def hops(self, distance):
        def body(part):
            for i in range(self.pieces):
                self.right(i, part).wait_recv()
                self.along(i, part, lambda copy: copy.start())

        self.each((self.z == self.d + distance) | (self.z == self.d - distance), body)

    def hand_over(self):
        @pl.when(self.source_here & self.owner())
        def _():
            self.stage().wait()
            self.keep().start()
            for i in range(self.pieces):
                self.over(i, 0, self.source).start()

        def body(part):
            for i in range(self.pieces):
                self.over(i, part).start()

        self.each(jnp.logical_not(self.source_here), body)

    def settle(self):
        @pl.when(self.source_here & self.owner())
        def _():
            self.cross().wait_send()
            self.keep().wait()

        def at_source(part):
            for i in range(self.pieces):
                self.along(i, part, lambda copy: copy.wait_send())
                if part == 0:
                    self.over(i, 0).wait_send()
                else:
                    self.over(i, 0).wait_recv()

        def elsewhere(part):
            for i in range(self.pieces):
                self.along(i, part, lambda copy: copy.wait_send())
                self.over(i, part).wait_send()
                self.over(i, 1 - part).wait_recv()

        self.each(self.source_here, at_source)
        self.each(jnp.logical_not(self.source_here), elsewhere)


def line_neighbours(nf, y, z):
    return [
        (None, {"section": 1 - y}),
        (z < nf - 1, {"fsdp": z + 1}),
        (z > 0, {"fsdp": z - 1}),
    ]


class SectionSum:

    def __init__(self, view, nf, y, z, own, landed, chain, sems, result):
        self.view, self.nf, self.y, self.z, self.result = view, nf, y, z, result
        self.own, self.landed, self.chain = own, landed, chain
        self.load_sem, self.over_send, self.over_recv, self.chain_send, self.chain_recv = (
            sems.at[0], sems.at[1], sems.at[2], sems.at[3], sems.at[4]
        )
        self.part_rows = own.shape[1]

    def load(self, block):
        return pltpu.make_async_copy(self.view(block, self.y), self.own.at[block], self.load_sem.at[block])

    def over(self, block):
        return remote(
            self.view(block, 1 - self.y), self.landed.at[block], self.over_send.at[block], self.over_recv.at[block],
            {"section": 1 - self.y},
        )

    def right(self, block):
        return remote(
            self.own.at[block], self.chain.at[block], self.chain_send.at[block], self.chain_recv.at[block],
            {"fsdp": self.z + 1},
        )

    def left(self, block, arrives):
        slot = self.nf if arrives else block
        return remote(
            self.own.at[block], self.chain.at[slot], self.chain_send.at[block], self.chain_recv.at[slot],
            {"fsdp": self.z - 1},
        )

    def at(self, k, body):
        if k == 0:
            body(self.z, False)
            return

        @pl.when(self.z + k < self.nf)
        def _():
            body(self.z + k, True)

        @pl.when(self.z - k >= 0)
        def _():
            body(self.z - k, False)

    def begin(self):
        self.at(self.nf - 1, lambda block, rightward: self.over(block).start())
        for k in range(self.nf - 1, -1, -1):
            self.at(k, lambda block, rightward: self.load(block).start())

    def add(self, block, sources, target):
        step = 32

        def some(i, carry):
            rows = pl.ds(pl.multiple_of(i * step, 16), step)
            total = self.own[block, rows, :].astype(F32)
            for ref, slot in sources:
                total = total + ref[slot, rows, :].astype(F32)
            if target is None:
                self.own[block, rows, :] = total.astype(BF16)
            else:
                target[rows, :] = total.astype(BF16)
            return carry

        lax.fori_loop(0, self.part_rows // step, some, 0)

    def ready(self, block):
        self.load(block).wait()
        self.over(block).wait_recv()

    def stage(self, k):
        z, nf = self.z, self.nf
        self.at(k, lambda block, rightward: self.ready(block))
        self.at(k - 1, lambda block, rightward: self.over(block).start())

        def one(block, rightward):
            far_end = z == 0 if rightward else z == nf - 1
            arrived = self.right(block) if rightward else self.left(block, False)
            leaving = self.right(block) if rightward else self.left(block, k == 1)

            @pl.when(jnp.logical_not(far_end))
            def _():
                arrived.wait_recv()
                self.add(block, [(self.landed, block), (self.chain, block)], None)

            @pl.when(far_end)
            def _():
                self.add(block, [(self.landed, block)], None)

            leaving.start()

        self.at(k, one)

    def finish(self):
        z, nf, target = self.z, self.nf, self.result
        self.ready(z)

        @pl.when(z > 0)
        def _():
            self.right(z).wait_recv()

        @pl.when(z < nf - 1)
        def _():
            self.left(z, True).wait_recv()

        @pl.when(z == 0)
        def _():
            self.add(z, [(self.landed, z), (self.chain, nf)], target)

        @pl.when(z == nf - 1)
        def _():
            self.add(z, [(self.landed, z), (self.chain, z)], target)

        @pl.when((z > 0) & (z < nf - 1))
        def _():
            self.add(z, [(self.landed, z), (self.chain, z), (self.chain, nf)], target)

    def settle(self):
        z, nf = self.z, self.nf
        self.over(z).wait_send()
        for k in range(nf - 1, 0, -1):

            @pl.when(z + k < nf)
            def _():
                self.over(z + k).wait_send()
                self.right(z + k).wait_send()

            @pl.when(z - k >= 0)
            def _():
                self.over(z - k).wait_send()
                self.left(z - k, k == 1).wait_send()


def in_parts(width):
    rows = -(-width // 64) * 32
    return rows, width - rows


def in_view(source, nf):
    rows, second = in_parts(source.shape[-2])

    def view(block, part):
        here = pl.ds(pl.multiple_of(part * second, 16), rows)
        if len(source.shape) == 3:
            return source.at[block, here]
        columns = source.shape[1] // nf
        return source.at[here, pl.ds(pl.multiple_of(block * columns, LANES), columns)]

    return view


def out_view(source, nf):
    rows, columns = source.shape[0] // nf, source.shape[1] // 2

    def view(block, part):
        here = pl.ds(pl.multiple_of(block * rows, 16), rows)
        return source.at[here, pl.ds(pl.multiple_of(part * columns, LANES), columns)]

    return view


def in_part_shape(nf, source):
    columns = source.shape[2] if len(source.shape) == 3 else source.shape[1] // nf
    return in_parts(source.shape[-2])[0], columns


def out_part_shape(nf, source):
    return source.shape[0] // nf, source.shape[1] // 2


def section_sum_scratch(nf, part):
    return [
        pltpu.VMEM((nf,) + part, BF16),
        pltpu.VMEM((nf,) + part, BF16),
        pltpu.VMEM((nf + 1,) + part, BF16),
        pltpu.SemaphoreType.DMA((5, nf + 1)),
        pltpu.VMEM(part, BF16),
    ]


class SectionReturn:

    def __init__(self, piece, place, owner, y, sems):
        self.piece, self.place, self.owner, self.y, self.sems = piece, place, owner, y, sems

    def keep(self):
        return pltpu.make_async_copy(self.piece(self.owner), self.place(self.owner), self.sems.at[2])

    def send(self):
        other = 1 - self.owner
        return remote(
            self.piece(other), self.place(other), self.sems.at[0], self.sems.at[1], {"section": 1 - self.y}
        )

    def begin(self):
        @pl.when(self.y == self.owner)
        def _():
            self.keep().start()

        @pl.when(self.y != self.owner)
        def _():
            self.send().start()

    def finish(self):
        @pl.when(self.y == self.owner)
        def _():
            self.keep().wait()
            self.send().wait_recv()

        @pl.when(self.y != self.owner)
        def _():
            self.send().wait_send()


def end_kernel(
    nf, nd,
    in_ref, in_part1_ref, out_part0_ref, out_part1_ref, small0_ref, small1_ref,
    in_all, out_all, small_all,
    in_own, in_landed, in_chain, in_sems, in_part,
    in_final, out_final, small_slots, small_total, local_sem, swap_sem, back_sem, small_sems, group_send, group_recv,
):
    y, z, d = lax.axis_index("section"), lax.axis_index("fsdp"), lax.axis_index("dp")
    away = z != d
    twin = {"fsdp": d, "dp": z}
    peer = {"section": 1 - y}
    wide = lambda k: {"fsdp": (z + k) % nf}
    greet(
        [(None, peer), (away, twin)]
        + [(None, wide(k)) for k in range(1, nf)]
        + [(None, {"dp": flip(d, bit)}) for bit in bits_of(nd)]
    )
    in_sum = SectionSum(in_view(in_ref, nf), nf, y, z, in_own, in_landed, in_chain, in_sems, in_part)
    width = in_final.shape[0]
    part_rows, second = in_parts(width)
    overlap = part_rows - second
    out_rows, out_columns = out_part0_ref.shape
    in_piece = lambda ref: lambda p: ref if p == 0 else ref.at[pl.ds(overlap, width - part_rows)]
    in_place = lambda p: in_final.at[pl.ds(p * part_rows, width - part_rows if p else part_rows)]
    out_place = lambda p: out_final.at[:, pl.ds(p * out_columns, out_columns)]
    out_returns = [
        SectionReturn(lambda p: out_part0_ref, out_place, 0, y, back_sem.at[0]),
        SectionReturn(lambda p: out_part1_ref, out_place, 1, y, back_sem.at[1]),
    ]
    in_returns = [
        SectionReturn(in_piece(in_part), in_place, 0, y, back_sem.at[2]),
        SectionReturn(in_piece(in_part1_ref), in_place, 1, y, back_sem.at[3]),
    ]
    in_groups = [
        GroupRows(
            lambda device, p=p: in_all.at[device, pl.ds(p * part_rows, width - part_rows if p else part_rows)],
            d, nd, group_send.at[p], group_recv.at[p],
        )
        for p in range(2)
    ]
    out_group = GroupRows(rows_of(out_all, out_rows), d, nd, group_send.at[2], group_recv.at[2])
    small_group = GroupRows(lambda device: small_all.at[device], d, nd, group_send.at[3], group_recv.at[3])

    def small_over(ref):
        return remote(ref, small_slots.at[nf], small_sems.at[0, 0], small_sems.at[1, 0], peer)

    def small_load(ref):
        return pltpu.make_async_copy(ref, small_slots.at[0], local_sem.at[0])

    small_copies = [
        remote(small_slots.at[0], small_slots.at[k], small_sems.at[0, k], small_sems.at[1, k], wide(k))
        for k in range(1, nf)
    ]
    small_own = pltpu.make_async_copy(small_total, small_group.part(0), local_sem.at[0])
    swap_target = out_all.at[pl.ds(pl.multiple_of(z * out_rows, 16), out_rows)]
    swap = remote(out_final, swap_target, swap_sem.at[0], swap_sem.at[1], twin)
    stay = pltpu.make_async_copy(out_final, out_group.part(0), swap_sem.at[2])

    def own_copy(p):
        return pltpu.make_async_copy(in_place(p), in_groups[p].part(0), local_sem.at[1 + p])

    def spread(p):
        own_copy(p).start()
        in_groups[p].begin(in_place(p))

    for back in out_returns:
        back.begin()
    in_sum.begin()
    for section, (mine, other) in enumerate(((small0_ref, small1_ref), (small1_ref, small0_ref))):

        @pl.when(y == section)
        def _():
            small_over(other).start()
            small_load(mine).start()


    @pl.when(y == 1)
    def _():
        in_returns[1].keep().start()
        in_returns[1].keep().wait()
        spread(1)

    for back in out_returns:
        back.finish()

    @pl.when(away)
    def _():
        swap.start()

    @pl.when(jnp.logical_not(away))
    def _():
        stay.start()

    for k in range(nf - 1, 0, -1):
        in_sum.stage(k)
        if k == nf - 1:
            small_load(small0_ref).wait()
            small_over(small0_ref).wait()
            small_slots[0] = small_slots[0] + small_slots[nf]
            for copy in small_copies:
                copy.start()

            @pl.when(away)
            def _():
                swap.wait()

            @pl.when(jnp.logical_not(away))
            def _():
                stay.wait()

            out_group.begin()
        if k == nf - 2:
            for copy in small_copies:
                copy.wait()
            total = small_slots[0]
            for j in range(1, nf):
                total = total + small_slots[j]
            small_total[...] = total
            small_own.start()
            small_group.begin(small_total)
            out_group.relay()
        if k == 1:
            small_group.finish()
            small_own.wait()
            out_group.close()
    in_sum.finish()

    @pl.when(y == 0)
    def _():
        in_returns[0].keep().start()
        in_returns[1].send().start()
        in_returns[0].keep().wait()
        spread(0)
        in_returns[0].send().wait_recv()
        spread(1)
        in_returns[1].send().wait_send()

    @pl.when(y == 1)
    def _():
        in_returns[0].send().start()
        in_returns[1].send().wait_recv()
        spread(0)
        in_returns[0].send().wait_send()

    for p in range(2):
        in_groups[p].finish()
        own_copy(p).wait()
    in_sum.settle()


def run_end(nf, nd, in_grad, in_part1, out_part0, out_part1, small0, small1):
    anywhere = pl.BlockSpec(memory_space=pl.ANY)
    dma = pltpu.SemaphoreType.DMA
    width = in_grad.shape[-2]
    out_rows = out_part0.shape[0]
    return pl.pallas_call(
        functools.partial(end_kernel, nf, nd),
        in_specs=[anywhere] * 6,
        out_specs=[anywhere] * 3,
        out_shape=[
            jax.ShapeDtypeStruct((nd, width, in_part1.shape[1]), BF16),
            jax.ShapeDtypeStruct((nd * out_rows, D), BF16),
            jax.ShapeDtypeStruct((nd,) + small0.shape, F32),
        ],
        scratch_shapes=section_sum_scratch(nf, in_part1.shape)
        + [
            pltpu.VMEM((width, in_part1.shape[1]), BF16),
            pltpu.VMEM((out_rows, D), BF16),
            pltpu.VMEM((nf + 1,) + small0.shape, F32),
            pltpu.VMEM(small0.shape, F32),
            dma((3,)),
            dma((3,)),
            dma((4, 3)),
            dma((2, nf)),
            dma((4, nd)),
            dma((4, nd)),
        ],
        compiler_params=pltpu.CompilerParams(
            vmem_limit_bytes=VMEM_LIMIT, collective_id=6, has_side_effects=True
        ),
        name="sum_end",
    )(in_grad, in_part1, out_part0, out_part1, small0, small1)


def finish_kernel(
    ch, nd, in_ref, shared_ref, out_ref, small_ref,
    in_total, out_total, gain_ref, convw_ref, convb_ref, dtb_ref, alog_ref, skip_ref, gate_ref, shared, sems,
):
    step = pl.program_id(0)
    heads = H // nd
    count = DIN - 2 * DI

    def copy(j):
        return pltpu.make_async_copy(shared_ref.at[j, pl.ds(2 * ch, count)], shared.at[j], sems.at[j])

    @pl.when(step == 0)
    def _():
        for j in range(nd):
            copy(j).start()
        for row, (start, size) in enumerate(gain_rows(small_ref.shape[2])):
            gain_ref[:, start : start + size] = jnp.sum(small_ref[:, 8 + row : 9 + row, 0:size], axis=0)
        both = jnp.sum(small_ref[:, 0:8, ch:], axis=0)
        convw_ref[:, DI:] = both[0:4, :]
        convb_ref[:, DI:] = both[4:5, :]
        rows = lax.broadcasted_iota(jnp.int32, (ch, LANES), 0)
        columns = lax.broadcasted_iota(jnp.int32, (ch, LANES), 1)
        by_head = jnp.where(rows // P_SIZE == columns, 1.0, 0.0)
        decays, skips = [[], []], []
        for j in range(nd):
            here = slice(j * ch, (j + 1) * ch)
            convw_ref[:, here] = small_ref[j, 0:4, :ch]
            convb_ref[:, here] = small_ref[j, 4:5, :ch]
            gate_ref[:, here] = small_ref[j, 5:6, :ch]
            skips.append(fine_dot(small_ref[j, 0:8, :ch], by_head)[6:7, :heads])
            for k in range(2):
                decays[k].append(small_ref[j, 7:8, k * LANES : k * LANES + heads])
        dtb_ref[...] = jnp.concatenate(decays[0], axis=1)
        alog_ref[...] = jnp.concatenate(decays[1], axis=1)
        skip_ref[...] = jnp.concatenate(skips, axis=1)

    @pl.when(step < 2 * nd)
    def _():
        in_total[...] = in_ref[...].astype(F32)
        out_total[...] = out_ref[...].astype(F32)

    @pl.when(step == 2 * nd)
    def _():
        for j in range(nd):
            copy(j).wait()
        total = shared[0].astype(F32)
        for j in range(1, nd):
            total = total + shared[j].astype(F32)
        in_total[0:count, :] = total


def run_finish(ch, nd, in_all, out_all, small_all):
    columns = in_all.shape[2]
    rows = out_all.shape[0]
    piece = rows // (2 * nd)
    final = lambda s: (jnp.minimum(s, 2 * nd - 1), 0)

    def in_block(s):
        s = jnp.minimum(s, 2 * nd - 1)
        return (s % nd, s // nd, 0)

    smalls = [(1, D), (K, DC), (1, DC), (1, H), (1, H), (1, H), (1, DI)]
    return pl.pallas_call(
        functools.partial(finish_kernel, ch, nd),
        grid=(2 * nd + 1,),
        in_specs=[
            pl.BlockSpec((None, ch, columns), in_block),
            pl.BlockSpec(memory_space=pl.ANY),
            pl.BlockSpec((piece, D), final),
            once(small_all.shape),
        ],
        out_specs=[pl.BlockSpec((ch, columns), lambda s: (s, 0)), pl.BlockSpec((piece, D), final)]
        + [once(shape) for shape in smalls],
        out_shape=[jax.ShapeDtypeStruct((DIN, columns), F32), jax.ShapeDtypeStruct((rows, D), F32)]
        + [jax.ShapeDtypeStruct(shape, F32) for shape in smalls],
        scratch_shapes=[pltpu.VMEM((nd, DIN - 2 * DI, columns), BF16), pltpu.SemaphoreType.DMA((nd,))],
        compiler_params=pltpu.CompilerParams(vmem_limit_bytes=VMEM_LIMIT),
        name="finish",
    )(in_all, in_all, out_all, small_all)


class Weights:

    def __init__(self, source, held, sems):
        self.source, self.held, self.sems = source, held, sems
        self.blocks = source.shape[0]
        self.columns = source.shape[2]

    def copies(self):
        out = []
        for k in range(self.blocks):
            if len(self.held.shape) == 3:
                target = self.held.at[k]
            else:
                target = self.held.at[:, pl.ds(k * self.columns, self.columns)]
            out.append(pltpu.make_async_copy(self.source.at[k], target, self.sems.at[k]))
        return out

    def forward(self, rows):
        if len(self.held.shape) == 2:
            return dot(rows, self.held[...], ((1,), (1,)))
        total = 0.0
        for k in range(self.blocks):
            total = total + dot(
                rows[:, k * self.columns : (k + 1) * self.columns], self.held[k], ((1,), (1,))
            )
        return total

    def backward(self, rows):
        if len(self.held.shape) == 2:
            return dot(rows, self.held[...])
        return jnp.concatenate([dot(rows, self.held[k]) for k in range(self.blocks)], axis=1)


def held_shape(w_in):
    blocks, width, columns = w_in.shape
    return (width, blocks * columns) if columns % LANES == 0 else (blocks, width, columns)


def own_steps(steps, turn):
    padded = jnp.concatenate([steps, jnp.zeros((steps.shape[0], LANES - H), F32)], axis=1)
    return pltpu.roll(padded, LANES - turn, 1)


def mix_forward(
    ch, proj_ref, meta_ref, segrow_ref, conv_w_ref, conv_b_ref, dtb_ref, alog_ref, skip_ref,
    gated_ref, square_ref, mixed_ref, pre_ref, state_out_ref, pad, state, sub, turn,
):
    conv_width = ch + 2 * N
    rows = pl.ds(pl.multiple_of(sub * Q, Q), Q)
    meta = meta_ref[rows, :]
    raw = proj_ref[rows, ch : ch + conv_width]
    pre = conv_b_ref[...] + conv_w_ref[3:4, :] * raw
    before = pad[...]
    first_rows = lax.broadcasted_iota(jnp.int32, (8, conv_width), 0)
    for lag in range(1, K):
        earlier = pltpu.roll(raw, lag, 0)
        begin = jnp.where(first_rows >= lag, earlier[0:8, :], pltpu.roll(before, lag, 0))
        shifted = jnp.concatenate([begin, earlier[8:, :]], axis=0)
        pre = pre + (conv_w_ref[3 - lag : 4 - lag, :] * meta[:, lag : lag + 1]) * shifted
    pad[...] = raw[Q - 8 :, :]
    pre_ref[rows, :] = pre
    conv_out = pre * jax.nn.sigmoid(pre)
    values = conv_out[:, :ch]
    b_part = conv_out[:, ch : ch + N]
    c_part = conv_out[:, ch + N :]
    row, column = triangles()
    tri = jnp.where(row >= column, 1.0, 0.0)
    shifted, step, log_decay, cumulative = decay_tables(
        own_steps(proj_ref[rows, ch + conv_width :], turn), dtb_ref[...], alog_ref[...], tri
    )
    linked = (row >= column) & (meta[:, 0:1] == segrow_ref[sub])
    inner = jnp.where(linked, split_dot(c_part, b_part, ((1,), (1,))), 0.0)
    cum_t = cumulative.T
    step_t = step.T
    last = cumulative[Q - 1 : Q, :]
    entry = meta[:, 4:5] * jnp.exp(cumulative)
    weight = meta[:, 5:6] * jnp.exp(last - cumulative) * step
    state_in = state[...]
    state_out_ref[sub] = state_in
    carried = split_dot(c_part, state_in)
    low_half = lax.broadcasted_iota(jnp.int32, (Q, LANES), 1) < P_SIZE
    squares = jnp.zeros((Q, 1), F32)
    weighted = []
    entries = []
    values_high, values_low = halves(values)
    for pair in range(ch // LANES):
        lanes = slice(pair * LANES, (pair + 1) * LANES)
        values_pair = values[:, lanes]
        mats = []
        for head in (2 * pair, 2 * pair + 1):
            spread = jnp.minimum(cumulative[:, head : head + 1] - cum_t[head : head + 1, :], 0.0)
            mats.append((inner * jnp.exp(spread) * step_t[head : head + 1, :]).astype(BF16))
        parts = [values_high[:, lanes], values_low[:, lanes]]
        zero = jnp.zeros_like(parts[0])
        stacked = jnp.concatenate(
            [
                jnp.concatenate([jnp.where(low_half, part, zero) for part in parts], axis=1),
                jnp.concatenate([jnp.where(low_half, zero, part) for part in parts], axis=1),
            ],
            axis=0,
        )
        both = dot(jnp.concatenate(mats, axis=1), stacked)
        out = both[:, :LANES] + both[:, LANES:]
        entry_pair = pair_lanes(entry, 2 * pair, low_half)
        out = out + entry_pair * carried[:, lanes] + skip_ref[:, lanes] * values_pair
        mixed_ref[rows, lanes] = out
        gate = proj_ref[rows, lanes]
        gated = out * (gate * jax.nn.sigmoid(gate))
        squares = squares + jnp.sum(gated * gated, axis=1, keepdims=True)
        gated_ref[rows, lanes] = gated
        weighted.append(pair_lanes(weight, 2 * pair, low_half) * values_pair)
        entries.append(entry_pair[Q - 1 : Q, :])
    square_ref[0, pl.ds(sub, 1), :] = to_row(squares)
    state[...] = jnp.concatenate(entries, axis=1) * state_in + split_dot(
        b_part.T, jnp.concatenate(weighted, axis=1)
    )


def first_kernel(
    ch, nf, nd,
    x_ref, cot_ref, seg_ref, in_ref, out_ref, conv_w_ref, conv_b_ref, norm_ref, gate_ref, head_ref,
    proj_ref, mixed_ref, pre_ref, state_out_ref, nout_ref, branch_ref, next_ref, ratio_ref,
    conv_w_out, conv_b_out, dtb_out, alog_out, skip_out, gain_out, norm_out, meta_out, segrow_out,
    normed_all, moved_ref, hidden_out, cot_own, w_in0, w_in1, w_out0, w_out1,
    held, w_out, pad, state, gated, partial, landed, squares, low, normed, x_low, table, seg_all, own_block, staged,
    sum_send, sum_recv, tile_send, tile_recv, group_send, group_recv, start_send, start_recv, deal_send, deal_recv,
    in_sems0, in_sems1, out_sems0, out_sems1, local_sem, load_sem, small_sem, swap_sem, own_sem,
):
    step = pl.program_id(0)
    y, z, d = lax.axis_index("section"), lax.axis_index("fsdp"), lax.axis_index("dp")
    block = proj_ref.shape[0]
    subs = block // Q
    rows = block // nd
    length = block * nf
    lines = block // Q * 8
    heads = H // nd
    bits = bits_of(nd)
    twin = {"fsdp": d, "dp": z}
    home = z == d
    away = z != d
    peer = {"section": 1 - y}
    blocks = BlockSum(partial, landed, d, nd, sum_send, sum_recv)
    weights = Weights(w_in0, held, load_sem)
    out_load = pltpu.make_async_copy(w_out0, w_out, local_sem.at[0])
    gathers = [SectionGather(w_in0, 0, nf, y, z, in_sems0, own_block), SectionGather(w_in1, 1, nf, y, z, in_sems1, own_block)]
    outs = [
        OutGather(out_ref, w_out0, 0, nf, y, z, d, out_sems0, staged),
        OutGather(out_ref, w_out1, 1, nf, y, z, d, out_sems1, staged),
    ]
    enter = Deal(x_ref.at[y], x_low, nf, nd, z, d, deal_send.at[0], deal_recv.at[0], False)
    enter_cot = Deal(cot_ref.at[y], cot_own, nf, nd, z, d, deal_send.at[1], deal_recv.at[1], False)
    first_group = GroupRows(lambda device: normed.at[:, device], d, nd, start_send.at[0], start_recv.at[0])
    normed_copy = pltpu.make_async_copy(normed, normed_all, local_sem.at[1])
    hidden_copy = pltpu.make_async_copy(x_low, hidden_out, local_sem.at[2])

    def seg_rows(device):
        return seg_all.at[pl.ds(pl.multiple_of(device * lines, 8), lines)]

    seg_group = GroupRows(seg_rows, d, nd, start_send.at[1], start_recv.at[1])

    def every(place):
        return GroupRows(lambda device: moved_ref.at[place, device], d, nd, group_send.at[place], group_recv.at[place])

    def mine(place):
        return pltpu.make_async_copy(low.at[place], moved_ref.at[place, d], local_sem.at[3 + place])

    def stage(gather, k):
        gather.arrive(k)
        gather.relay(k)

    @pl.when(step == 0)
    def _():
        greet(
            line_neighbours(nf, y, z)
            + [(away, twin)]
            + deal_partners(nf, nd, z, d)
            + [(None, {"dp": flip(d, j)}) for j in range(1, nd)]
        )

        own_copies = [
            pltpu.make_async_copy(
                in_ref.at[pl.ds(pl.multiple_of(begin, 16), count)], own_block.at[pl.ds(spot, count)], own_sem.at[k]
            )
            for k, (begin, spot, count) in enumerate(
                [(d * ch, 0, ch), (DI + d * ch, ch, ch), (2 * DI, 2 * ch, DIN - 2 * DI)]
            )
        ]
        for copy in own_copies:
            copy.start()
        for copy in own_copies:
            copy.wait()
        gathers[0].start_cross()
        gathers[1].start_cross()
        table[y, 0:4, :] = conv_w_ref[...]
        table[y, 4:5, :] = conv_b_ref[...]
        table[y, 5:6, 0:D] = norm_ref[...]
        table[y, 6:7, 0:DI] = gate_ref[...]
        for k in range(3):
            table[y, 7:8, k * LANES : (k + 1) * LANES] = head_ref[k : k + 1, :]
        small_copy = remote(table.at[y], table.at[y], small_sem.at[0], small_sem.at[1], peer)
        small_copy.start()
        seg_swap = remote(seg_ref, seg_rows(z), swap_sem.at[0], swap_sem.at[1], twin)
        seg_stay = pltpu.make_async_copy(seg_ref, seg_rows(d), swap_sem.at[0])

        @pl.when(away)
        def _():
            seg_swap.start()

        @pl.when(home)
        def _():
            seg_stay.start()

        gathers[0].begin()
        enter.start_all()
        outs[0].begin()
        stage(gathers[0], 1)
        outs[0].begin_other()
        outs[0].hops(1)

        small_copy.wait()
        enter.arrive()
        hidden_copy.start()
        values = x_low[...].astype(F32)
        low[...] = (values * rms_parts(values) * table[0, 5:6, 0:D]).astype(BF16)
        for place in range(nf):
            normed[place, d] = low[place]
        first_group.begin(low)

        @pl.when(away)
        def _():
            seg_swap.wait()

        @pl.when(home)
        def _():
            seg_stay.wait()

        seg_group.begin()
        for k in range(2, nf - 1):
            stage(gathers[0], k)
            outs[0].hops(k)

        turn = d * heads
        low_half = lax.broadcasted_iota(jnp.int32, (1, LANES), 1) < P_SIZE
        channels = pl.ds(pl.multiple_of(d * ch, LANES), ch)
        for section in range(2):
            conv_w_out[section, :, 0:ch] = table[section, 0:4, channels]
            conv_w_out[section, :, ch:] = table[section, 0:4, DI:DC]
            conv_b_out[section, :, 0:ch] = table[section, 4:5, channels]
            conv_b_out[section, :, ch:] = table[section, 4:5, DI:DC]
            norm_out[section] = table[section, 5:6, 0:D]
            gain_out[section] = table[section, 6:7, channels]
            head_rows = [
                pltpu.roll(table[section, :, k * LANES : (k + 1) * LANES], LANES - turn, 1)[7:8, :] for k in range(3)
            ]
            dtb_out[section] = head_rows[0]
            alog_out[section] = head_rows[1]
            for pair in range(ch // LANES):
                skip_out[section, :, pair * LANES : (pair + 1) * LANES] = pair_lanes(head_rows[2], 2 * pair, low_half)

        seg_group.finish()

        lane = lax.broadcasted_iota(jnp.int32, (8, LANES), 1)
        sub_lane = lax.broadcasted_iota(jnp.int32, (Q, LANES), 1)
        before = jnp.full((8, LANES), -1.0, F32)
        for chunk in range(length // Q):
            now = seg_all[chunk * 8 : chunk * 8 + 8, :]
            segrow_out[chunk] = now[0:1, :]
            columns = [now[0:1, :]]
            for lag in range(1, K):
                earlier = jnp.where(lane < lag, pltpu.roll(before, lag, 1), pltpu.roll(now, lag, 1))
                columns.append(jnp.where(earlier == now, 1.0, 0.0)[0:1, :])
            columns.append(jnp.where(now == before[:, Q - 1 : Q], 1.0, 0.0)[0:1, :])
            columns.append(jnp.where(now == now[:, Q - 1 : Q], 1.0, 0.0)[0:1, :])
            masks = jnp.zeros((Q, LANES), F32)
            for j, row in enumerate(columns):
                masks = jnp.where(sub_lane == j, to_column(row), masks)
            meta_out[chunk * Q : (chunk + 1) * Q, :] = masks
            before = now

        stage(gathers[0], nf - 1)
        outs[0].hops(nf - 1)
        outs[0].hand_over()
        gathers[1].begin()
        first_group.finish()
        normed_copy.start()
        pad[...] = jnp.zeros_like(pad)
        state[...] = jnp.zeros_like(state)
        for k in range(1, nf):
            gathers[0].settle(k)
        gathers[0].settle_begin()
        for copy in weights.copies():
            copy.start()
        for copy in weights.copies():
            copy.wait()

    def tile(place):
        return GroupTiles(squares.at[place], tile_send.at[place], tile_recv.at[place], d, nd)

    def project(place):
        ratio = lax.rsqrt(tile(place).finish() * (1.0 / DI) + EPSILON)
        for sub in range(subs):
            piece = place * subs + sub
            ratio_ref[pl.ds(piece, 1), :] = ratio[sub : sub + 1, :]
            normed_out = gated[place % 2, sub * Q : (sub + 1) * Q, :] * to_column(ratio[sub : sub + 1, :])
            nout_ref[pl.ds(pl.multiple_of(piece * Q, Q), Q), :] = (normed_out * gain_out[0]).astype(BF16)
        here_rows = pl.ds(pl.multiple_of(place * block, Q), block)
        product = dot(nout_ref[here_rows, :], w_out[...])
        for o in range(nd):
            partial[place, o] = product[o * rows : (o + 1) * rows, :]
        blocks.send(0, place)

    def pass_on(place):
        for k in range(1, len(bits)):
            blocks.send(k, place)

    def conclude(place):
        branch = blocks.own(place)
        branch_ref[place] = branch
        moved = (x_low[place].astype(F32) + branch).astype(BF16)
        next_ref[place] = moved
        values = moved.astype(F32)
        low[place] = (values * rms_parts(values) * norm_out[1]).astype(BF16)
        mine(place).start()
        every(place).begin(low.at[place])

    proj_ref[...] = weights.forward(normed[step].reshape(block, D))

    @pl.when(step == 0)
    def _():
        stage(gathers[1], 1)

    @pl.when(step == 1)
    def _():
        outs[0].settle()
        out_load.start()
        out_load.wait()

    @pl.when(step >= 1)
    def _():
        project(step - 1)

    meta = meta_out.at[pl.ds(pl.multiple_of(step * block, Q), block)]
    segrow = segrow_out.at[pl.ds(step * subs, subs)]

    def one_chunk(sub, carry):
        mix_forward(
            ch, proj_ref, meta, segrow, conv_w_out.at[0], conv_b_out.at[0], dtb_out.at[0], alog_out.at[0],
            skip_out.at[0], gated.at[step % 2], squares.at[step], mixed_ref, pre_ref, state_out_ref, pad, state, sub,
            d * heads,
        )

        @pl.when(sub == 0)
        def _():
            @pl.when(step >= 2)
            def _():
                conclude(step - 2)

            @pl.when(step >= 1)
            def _():
                pass_on(step - 1)

            @pl.when(step >= 3)
            def _():
                every(step - 3).relay()

            for k in range(2, nf):

                @pl.when(step == k - 1)
                def _():
                    stage(gathers[1], k)


        return carry

    lax.fori_loop(0, subs, one_chunk, 0)
    tile(step).begin()

    @pl.when(step == 1)
    def _():
        outs[1].begin()

    @pl.when(step == nf - 2)
    def _():
        enter_cot.start_all()

    @pl.when(step == 2)
    def _():
        outs[1].begin_other()

    for k in range(1, nf):

        @pl.when(step == min(k + 1, nf - 1))
        def _():
            outs[1].hops(k)
            if k == nf - 1:
                outs[1].hand_over()

    @pl.when(step == nf - 1)
    def _():
        project(nf - 1)
        pass_on(nf - 1)
        conclude(nf - 2)
        every(nf - 3).relay()
        conclude(nf - 1)
        every(nf - 2).relay()
        for k in range(1, nf):
            gathers[1].settle(k)
        gathers[1].settle_begin()
        outs[1].settle()
        enter.settle()
        enter_cot.arrive()
        enter_cot.settle()
        normed_copy.wait()
        hidden_copy.wait()
        every(nf - 1).relay()
        for place in range(nf):
            every(place).close()
            mine(place).wait()
        blocks.settle(nf)


def run_first(ch, nf, nd, x, cot, seg, in_rows, out_rows, conv_w, conv_b, norm_gain, gate_gain, head_table, identity):
    block = x.shape[1]
    length = block * nf
    conv_width = ch + 2 * N
    columns = in_rows.shape[1]
    width = 2 * ch + DIN - 2 * DI
    pieces = length // Q
    subs = block // Q
    bits = len(bits_of(nd))
    own = (nf, block // nd, D)
    every = (nf, nd, block // nd, D)
    w_in = jax.ShapeDtypeStruct((nf, width, columns), BF16)
    anywhere = pl.BlockSpec(memory_space=pl.ANY)
    dma = pltpu.SemaphoreType.DMA
    ordered = lambda s: (s, 0)
    small = [(2, K, conv_width), (2, 1, conv_width), (2, 1, LANES), (2, 1, LANES), (2, 1, ch), (2, 1, ch), (2, 1, D)]
    resident = small + [(length, LANES), (pieces, 1, Q)]
    return pl.pallas_call(
        functools.partial(first_kernel, ch, nf, nd),
        grid=(nf,),
        in_specs=[anywhere] * 5 + [once(part.shape) for part in (conv_w, conv_b, norm_gain, gate_gain, head_table)],
        out_specs=[
            pl.BlockSpec((block, width), ordered),
            pl.BlockSpec((block, ch), ordered),
            pl.BlockSpec((block, conv_width), ordered),
            pl.BlockSpec((subs, N, ch), lambda s: (s, 0, 0)),
            once((length, ch)),
            once(own),
            once(own),
            once((pieces, Q)),
        ]
        + [once(shape) for shape in resident]
        + [anywhere] * 8,
        out_shape=[
            jax.ShapeDtypeStruct((length, width), F32),
            jax.ShapeDtypeStruct((length, ch), F32),
            jax.ShapeDtypeStruct((length, conv_width), F32),
            jax.ShapeDtypeStruct((pieces, N, ch), F32),
            jax.ShapeDtypeStruct((length, ch), BF16),
            jax.ShapeDtypeStruct(own, F32),
            jax.ShapeDtypeStruct(own, BF16),
            jax.ShapeDtypeStruct((pieces, Q), F32),
        ]
        + [jax.ShapeDtypeStruct(shape, F32) for shape in resident]
        + [
            jax.ShapeDtypeStruct(every, BF16),
            jax.ShapeDtypeStruct(every, BF16),
            jax.ShapeDtypeStruct(own, BF16),
            jax.ShapeDtypeStruct(own, BF16),
            w_in,
            w_in,
            jax.ShapeDtypeStruct((ch, D), BF16),
            jax.ShapeDtypeStruct((ch, D), BF16),
        ],
        scratch_shapes=[
            pltpu.VMEM(held_shape(w_in), BF16),
            pltpu.VMEM((ch, D), BF16),
            pltpu.VMEM((8, conv_width), F32),
            pltpu.VMEM((N, ch), F32),
            pltpu.VMEM((2, block, ch), F32),
            pltpu.VMEM(every, F32),
            pltpu.VMEM((nd - 1, nf, block // nd, D), F32),
            pltpu.VMEM((nf, nd, 8, LANES), F32),
            pltpu.VMEM(own, BF16),
            pltpu.VMEM(every, BF16),
            pltpu.VMEM(own, BF16),
            pltpu.VMEM((2, 8, DC), F32),
            pltpu.VMEM((pieces * 8, LANES), F32),
            pltpu.VMEM((width, columns), BF16),
            pltpu.VMEM((ch, D), BF16),
            dma((bits, nf, nd)),
            dma((bits, nf, nd)),
            dma((nf, nd)),
            dma((nf, nd)),
            dma((nf, nd)),
            dma((nf, nd)),
            dma((2, nd)),
            dma((2, nd)),
            dma((2, nf)),
            dma((2, nf)),
            dma((7, 2 * nf)),
            dma((7, 2 * nf)),
            dma((6, 4)),
            dma((6, 4)),
            dma((3 + nf,)),
            dma((nf,)),
            dma((2,)),
            dma((2,)),
            dma((3,)),
        ],
        compiler_params=pltpu.CompilerParams(
            vmem_limit_bytes=VMEM_LIMIT, collective_id=identity, has_side_effects=True
        ),
        name="layer_first",
    )(x, cot, seg, in_rows, out_rows, conv_w, conv_b, norm_gain, gate_gain, head_table)


def layer_kernel(
    ch, nf, nd,
    normed_ref, meta_ref, segrow_ref, conv_w_ref, conv_b_ref, dtb_ref, alog_ref, skip_ref, gain_ref,
    w_in_ref, w_out_ref, hidden_ref, extra_ref,
    proj_ref, nout_ref, mixed_ref, pre_ref, state_out_ref, branch_ref, next_ref, ratio_ref, pull_ref, cot_all,
    held, w_out, pad, state, gated, partial, landed, squares, pulls,
    sum_send, sum_recv, tile_send, tile_recv, group_send, group_recv, local_sem, load_sem,
):
    step = pl.program_id(0)
    y, z, d = lax.axis_index("section"), lax.axis_index("fsdp"), lax.axis_index("dp")
    block = normed_ref.shape[0]
    subs = block // Q
    rows = block // nd
    bits = bits_of(nd)
    blocks = BlockSum(partial, landed, d, nd, sum_send, sum_recv)
    weights = Weights(w_in_ref, held, load_sem)
    out_load = pltpu.make_async_copy(w_out_ref, w_out, local_sem.at[0])
    cot_group = GroupRows(lambda device: cot_all.at[:, device], d, nd, group_send.at[0], group_recv.at[0])
    cot_keep = pltpu.make_async_copy(extra_ref, cot_group.part(0), local_sem.at[1])

    @pl.when(step == 0)
    def _():
        for copy in weights.copies():
            copy.start()
        out_load.start()
        greet([(None, {"dp": flip(d, j)}) for j in range(1, nd)])
        cot_keep.start()
        cot_group.begin(extra_ref)
        pad[...] = jnp.zeros_like(pad)
        state[...] = jnp.zeros_like(state)
        pulls[0] = jnp.zeros(pulls.shape[1:], F32)
        for copy in weights.copies():
            copy.wait()
        out_load.wait()

    def tile(place):
        return GroupTiles(squares.at[place], tile_send.at[place], tile_recv.at[place], d, nd)

    def project(place):
        ratio = lax.rsqrt(tile(place).finish() * (1.0 / DI) + EPSILON)
        for sub in range(subs):
            piece = place * subs + sub
            ratio_ref[pl.ds(piece, 1), :] = ratio[sub : sub + 1, :]
            normed_out = gated[place % 2, sub * Q : (sub + 1) * Q, :] * to_column(ratio[sub : sub + 1, :])
            nout_ref[pl.ds(pl.multiple_of(piece * Q, Q), Q), :] = (normed_out * gain_ref[...]).astype(BF16)
        here_rows = pl.ds(pl.multiple_of(place * block, Q), block)
        product = dot(nout_ref[here_rows, :], w_out[...]).astype(partial.dtype)
        for o in range(nd):
            partial[place, o] = product[o * rows : (o + 1) * rows, :]
        blocks.send(0, place)

    def pass_on(place):
        for k in range(1, len(bits)):
            blocks.send(k, place)

    def conclude(place):
        branch = blocks.own(place)
        branch_ref[place] = branch
        moved = (hidden_ref[place].astype(F32) + branch).astype(BF16)
        next_ref[place] = moved
        first = place * block + d * rows
        pulls[0, pl.ds(first // Q, 1), :] += to_row(
            jnp.sum(extra_ref[place].astype(F32) * branch, axis=1, keepdims=True), first % Q
        )

    proj_ref[...] = weights.forward(normed_ref[...])

    @pl.when(step >= 1)
    def _():
        project(step - 1)

    def one_chunk(sub, carry):
        mix_forward(
            ch, proj_ref, meta_ref, segrow_ref, conv_w_ref, conv_b_ref, dtb_ref, alog_ref, skip_ref,
            gated.at[step % 2], squares.at[step], mixed_ref, pre_ref, state_out_ref, pad, state, sub, d * (H // nd),
        )

        @pl.when(sub == 0)
        def _():
            @pl.when(step >= 2)
            def _():
                conclude(step - 2)

            @pl.when(step >= 1)
            def _():
                pass_on(step - 1)

        return carry

    lax.fori_loop(0, subs, one_chunk, 0)
    tile(step).begin()

    @pl.when(step == min(2, nf - 1))
    def _():
        cot_group.relay()

    @pl.when(step == nf - 1)
    def _():
        project(nf - 1)
        pass_on(nf - 1)
        conclude(nf - 2)
        conclude(nf - 1)
        pull_ref[...] = group_tiles(pulls, group_send.at[1], group_recv.at[1], d, nd)
        cot_group.close()
        cot_keep.wait()
        blocks.settle(nf)


def once(shape):
    return pl.BlockSpec(shape, lambda s: (0,) * len(shape), pipeline_mode=pl.Buffered(buffer_count=1))


def pick(part, layer):
    return pl.BlockSpec(
        (None,) + part.shape[1:], lambda s: (layer, 0, 0), pipeline_mode=pl.Buffered(buffer_count=1)
    )


def run_layer(
    ch, rows, nf, nd, normed_all, meta, segrow, small, w_in, w_out, hidden, extra, identity
):
    length, width = normed_all.shape[0], w_in.shape[1]
    layer = 1
    conv_width = ch + 2 * N
    block = rows
    steps = nf
    pieces = length // Q
    subs = block // Q
    own = (nf, rows // nd, D)
    every = (nf, nd, rows // nd, D)
    bits = len(bits_of(nd))
    dma = pltpu.SemaphoreType.DMA
    anywhere = pl.BlockSpec(memory_space=pl.ANY)
    ordered = lambda s: (s, 0)
    ordered3 = lambda s: (s, 0, 0)
    return pl.pallas_call(
        functools.partial(layer_kernel, ch, nf, nd),
        grid=(steps,),
        in_specs=[
            pl.BlockSpec((block, D), ordered),
            pl.BlockSpec((block, LANES), ordered),
            pl.BlockSpec((subs, 1, Q), ordered3),
        ]
        + [pick(part, layer) for part in small]
        + [
            anywhere,
            anywhere,
            once(own),
            once(own),
        ],
        out_specs=[
            pl.BlockSpec((block, width), ordered),
            once((length, ch)),
            pl.BlockSpec((block, ch), ordered),
            pl.BlockSpec((block, conv_width), ordered),
            pl.BlockSpec((subs, N, ch), ordered3),
            once(own),
            once(own),
            once((pieces, Q)),
            once((pieces, Q)),
            anywhere,
        ],
        out_shape=[
            jax.ShapeDtypeStruct((length, width), F32),
            jax.ShapeDtypeStruct((length, ch), BF16),
            jax.ShapeDtypeStruct((length, ch), F32),
            jax.ShapeDtypeStruct((length, conv_width), F32),
            jax.ShapeDtypeStruct((pieces, N, ch), F32),
            jax.ShapeDtypeStruct(own, F32),
            jax.ShapeDtypeStruct(own, BF16),
            jax.ShapeDtypeStruct((pieces, Q), F32),
            jax.ShapeDtypeStruct((pieces, Q), F32),
            jax.ShapeDtypeStruct(every, BF16),
        ],
        scratch_shapes=[
            pltpu.VMEM(held_shape(w_in), BF16),
            pltpu.VMEM((ch, D), BF16),
            pltpu.VMEM((8, conv_width), F32),
            pltpu.VMEM((N, ch), F32),
            pltpu.VMEM((2, block, ch), F32),
            pltpu.VMEM(every, BF16),
            pltpu.VMEM((nd - 1, nf, rows // nd, D), BF16),
            pltpu.VMEM((steps, nd, 8, LANES), F32),
            pltpu.VMEM((nd, pieces, Q), F32),
            dma((bits, nf, nd)),
            dma((bits, nf, nd)),
            dma((steps, nd)),
            dma((steps, nd)),
            dma((nf, nd)),
            dma((nf, nd)),
            dma((2,)),
            dma((nf,)),
        ],
        compiler_params=pltpu.CompilerParams(
            vmem_limit_bytes=VMEM_LIMIT, collective_id=identity, has_side_effects=True
        ),
        name="layer_last",
    )(normed_all, meta, segrow, *small, w_in, w_out, hidden, extra)


def mix_backward(
    ch, proj_ref, pre_ref, mixed_ref, state_ref, grad_ref, ratio_ref, pull_ref, meta_ref, segrow_ref,
    conv_w_ref, dtb_ref, alog_ref, skip_ref, gain_ref,
    dproj_ref, small_ref, tail, dstate, sub, chunk, turn,
):
    conv_width = ch + 2 * N
    rows = pl.ds(pl.multiple_of(sub * Q, Q), Q)
    meta = meta_ref[rows, :]
    pre = pre_ref[rows, :]
    sig = jax.nn.sigmoid(pre)
    conv_out = pre * sig
    values = conv_out[:, :ch]
    b_part = conv_out[:, ch : ch + N]
    c_part = conv_out[:, ch + N :]
    row, column = triangles()
    tri = jnp.where(row >= column, 1.0, 0.0)
    shifted, step, log_decay, cumulative = decay_tables(
        own_steps(proj_ref[rows, ch + conv_width :], turn), dtb_ref[...], alog_ref[...], tri
    )
    linked = (row <= column) & (meta[:, 0:1] == segrow_ref[sub])
    b_low = b_part.astype(BF16)
    c_low = c_part.astype(BF16)
    inner = jnp.where(linked, dot(b_low, c_low, ((1,), (1,))), 0.0)
    cum_t = cumulative.T
    last = cumulative[Q - 1 : Q, :]
    entry = meta[:, 4:5] * jnp.exp(cumulative)
    weight = meta[:, 5:6] * jnp.exp(last - cumulative)
    state_in = state_ref[sub]
    dstate_in = dstate[...]
    state_low = state_in.astype(BF16)
    dstate_low = dstate_in.astype(BF16)
    carried = dot(c_low, state_low)
    carried_back = dot(b_low, dstate_low)
    low_half = lax.broadcasted_iota(jnp.int32, (Q, LANES), 1) < P_SIZE
    lane = lax.broadcasted_iota(jnp.int32, (Q, LANES), 1)
    ratio = to_column(ratio_ref[pl.ds(chunk, 1), :])
    pull = ratio * ratio * to_column(pull_ref[pl.ds(chunk, 1), :]) * (1.0 / DI)
    dinner = jnp.zeros((Q, Q), F32)
    turned_parts = []
    step_parts, exit_parts, entry_parts = [], [], []
    weighted = []
    entered = []
    entry_rows = []
    dpre_parts = []
    for pair in range(ch // LANES):
        lanes = slice(pair * LANES, (pair + 1) * LANES)
        values_pair = values[:, lanes]
        gate = proj_ref[rows, lanes]
        mixed = mixed_ref[rows, lanes]
        gate_sig = jax.nn.sigmoid(gate)
        gate_silu = gate * gate_sig
        gated = mixed * gate_silu
        scaled = grad_ref[rows, lanes] * ratio
        small_ref[5:6, lanes] += jnp.sum(scaled * gated, axis=0, keepdims=True)
        dgated = scaled * gain_ref[:, lanes] - gated * pull
        dproj_ref[rows, lanes] = (dgated * mixed * (gate_sig + gate_silu * (1.0 - gate_sig))).astype(BF16)
        dmixed = dgated * gate_silu
        small_ref[6:7, lanes] += jnp.sum(dmixed * values_pair, axis=0, keepdims=True)
        zero = jnp.zeros_like(values_pair)
        dmixed_halves = [jnp.where(low_half, dmixed, zero).astype(BF16), jnp.where(low_half, zero, dmixed).astype(BF16)]
        values_low = values_pair.astype(BF16)
        step_pair = pair_lanes(step, 2 * pair, low_half)
        mats = []
        for half, head in enumerate((2 * pair, 2 * pair + 1)):
            spread = jnp.minimum(cum_t[head : head + 1, :] - cumulative[:, head : head + 1], 0.0)
            plain = jnp.exp(spread)
            decay = plain * step[:, head : head + 1]
            product = dot(values_low, dmixed_halves[half], ((1,), (1,)))
            mats.append((inner * plain).astype(BF16))
            spreaded = product * decay
            dinner = dinner + spreaded
            turned_parts.append((spreaded * inner).astype(BF16))
        back = dot(jnp.concatenate(mats, axis=1), jnp.concatenate(dmixed_halves, axis=0))
        weight_pair = pair_lanes(weight, 2 * pair, low_half)
        through = weight_pair * carried_back[:, lanes]
        total = back + through
        dvalues = step_pair * total + skip_ref[:, lanes] * dmixed
        step_parts.append((total * values_pair).astype(BF16))
        exit_parts.append((through * values_pair * step_pair).astype(BF16))
        entry_pair = pair_lanes(entry, 2 * pair, low_half)
        entry_grad = entry_pair * dmixed
        entry_parts.append((entry_grad * carried[:, lanes]).astype(BF16))
        weighted.append((weight_pair * step_pair * values_pair).astype(BF16))
        entered.append(entry_grad.astype(BF16))
        entry_rows.append(entry_pair[Q - 1 : Q, :])
        dpre_parts.append(dvalues)
    weighted = jnp.concatenate(weighted, axis=1)
    entered = jnp.concatenate(entered, axis=1)
    entry_rows = jnp.concatenate(entry_rows, axis=1)
    dinner_low = jnp.where(linked, dinner, 0.0).astype(BF16)
    db = dot(dinner_low, c_low) + dot(weighted, dstate_low, ((1,), (1,)))
    dc = dot(dinner_low.T, b_low) + dot(entered, state_low, ((1,), (1,)))
    state_terms = jnp.sum(state_in * dstate_in, axis=0, keepdims=True) * entry_rows
    head_lane = lax.broadcasted_iota(jnp.int32, (1, LANES), 1)
    state_sum = jnp.zeros((1, LANES), F32)
    for head in range(ch // P_SIZE):
        part = jnp.sum(state_terms[:, head * P_SIZE : (head + 1) * P_SIZE], axis=1, keepdims=True)
        state_sum = state_sum + jnp.where(head_lane == head, part, 0.0)
    heads = ch // P_SIZE

    def marks(shape, place, index):
        return jnp.where(place(shape) == index(shape), 1.0, 0.0).astype(BF16)

    rows_of_shape = lambda shape: lax.broadcasted_iota(jnp.int32, shape, 0)
    columns_of_shape = lambda shape: lax.broadcasted_iota(jnp.int32, shape, 1)
    by_head = marks((ch, LANES), lambda shape: rows_of_shape(shape) // P_SIZE, columns_of_shape)
    dstep = dot(jnp.concatenate(step_parts, axis=1), by_head)
    dexit = dot(jnp.concatenate(exit_parts, axis=1), by_head)
    dcum = dot(jnp.concatenate(entry_parts, axis=1), by_head)
    by_target = marks((LANES, heads * Q), rows_of_shape, lambda shape: columns_of_shape(shape) // Q)
    by_source = marks((heads * Q, LANES), lambda shape: rows_of_shape(shape) // Q, columns_of_shape)
    dcum = dcum + dot(by_target, jnp.concatenate(turned_parts, axis=0)).T
    dcum = dcum - dot(jnp.concatenate(turned_parts, axis=1), by_source)
    later = jnp.where(row <= column, 1.0, 0.0)
    before = jnp.where(row > column, 1.0, 0.0)
    dlog = fine_dot(later, dcum) + fine_dot(before, dexit) + state_sum
    growth = jnp.exp(alog_ref[...])
    dstep = dstep - dlog * growth
    ddt = dstep * jax.nn.sigmoid(shifted)
    small_ref[7:8, 0:LANES] += jnp.sum(ddt, axis=0, keepdims=True)
    small_ref[7:8, LANES : 2 * LANES] += jnp.sum(dlog * log_decay, axis=0, keepdims=True)
    dproj_ref[rows, ch + conv_width :] = pltpu.roll(jnp.where(lane < heads, ddt, 0.0), turn, 1)[:, :H].astype(BF16)
    dstate[...] = entry_rows * dstate_in + dot(c_part.T.astype(BF16), entered)
    dconv_out = jnp.concatenate(dpre_parts + [db, dc], axis=1)
    dpre = dconv_out * (sig + conv_out * (1.0 - sig))
    raw = proj_ref[rows, ch : ch + conv_width]
    small_ref[4:5, :] += jnp.sum(dpre, axis=0, keepdims=True)
    draw = conv_w_ref[3:4, :] * dpre
    last_rows = lax.broadcasted_iota(jnp.int32, (8, conv_width), 0)
    small_ref[3:4, :] += jnp.sum(raw * dpre, axis=0, keepdims=True)
    for lag in range(1, K):
        kept = meta[:, lag : lag + 1] * dpre
        later = pltpu.roll(kept, Q - lag, 0)
        end = jnp.where(last_rows < 8 - lag, later[Q - 8 :, :], pltpu.roll(tail[lag - 1], 8 - lag, 0))
        moved = jnp.concatenate([later[: Q - 8, :], end], axis=0)
        tail[lag - 1] = kept[0:8, :]
        draw = draw + conv_w_ref[3 - lag : 4 - lag, :] * moved
        small_ref[3 - lag : 4 - lag, :] += jnp.sum(raw * moved, axis=0, keepdims=True)
    dproj_ref[rows, ch : ch + conv_width] = draw.astype(BF16)


def gain_rows(width):
    return [(start, min(width, D - start)) for start in range(0, D, width)]


def layer_back_kernel(
    ch, nf, nd, last, fused,
    grad_all_ref, proj_ref, pre_ref, mixed_ref, state_ref, meta_ref, segrow_ref, ratio_ref, pull_ref,
    conv_w_ref, dtb_ref, alog_ref, skip_ref, gain_ref, w_in_ref, w_out_ref,
    hidden_ref, grad_own_ref, norm_gain_ref, branch_ref, *refs,
):
    count = 2 if last else 1
    sources, refs = refs[: count - fused], refs[count - fused :]
    if not last:
        rows_out, refs = refs[0], refs[1:]
    if fused:
        (normed_ref, nout_ref, grads_ref), refs = refs[:3], refs[3:]
    (
        dproj_ref, small_ref, next_ref, next_pull_ref, moved_ref,
    ) = refs[:5]
    results, refs = refs[5 : 5 + count], refs[5 + count :]
    if not last:
        final_ref, refs = refs[0], refs[1:]
    (
        held, w_out, tail, dstate, dnout, partial, landed, pulls, low, dgain,
        sum_send, sum_recv, tile_send, tile_recv, group_send, group_recv, local_sem, load_sem, deal_send, deal_recv,
    ) = refs[:20]
    refs = refs[20:]
    if fused:
        dproj_all, normed, staged, out_grad, normed_sem, staged_sem = refs[-6:]
        refs = refs[:-6]
        nout = dproj_all.at[:, pl.ds(0, ch)]
        block = grad_all_ref.shape[0]
        weight_grad = dproj_ref
        dproj_ref = dproj_all.at[pl.ds(pl.multiple_of((nf - 1 - pl.program_id(0)) * block, Q), block)]
        normed_load = pltpu.make_async_copy(normed_ref, normed, normed_sem.at[0])
        grads_load = pltpu.make_async_copy(grads_ref, normed, normed_sem.at[0])
        nout_load = pltpu.make_async_copy(nout_ref, nout, normed_sem.at[1])
        sources = (out_grad,) + sources
    step = pl.program_id(0)
    y, z, d = lax.axis_index("section"), lax.axis_index("fsdp"), lax.axis_index("dp")
    block = grad_all_ref.shape[0]
    subs = block // Q
    rows = block // nd
    bits = bits_of(nd)
    place = nf - 1 - step
    blocks = BlockSum(partial, landed, d, nd, sum_send, sum_recv)
    sums = [
        SectionSum(make(source, nf), nf, y, z, *refs[5 * k : 5 * k + 5])
        for k, (make, source) in enumerate(zip((out_view, in_view), sources))
    ]
    weights = Weights(w_in_ref, held, load_sem)
    out_load = pltpu.make_async_copy(w_out_ref, w_out, local_sem.at[0])
    if last:
        leave = Deal(moved_ref, low, nf, nd, z, d, deal_send, deal_recv, True)
    else:
        leave = Deal(final_ref, rows_out, nf, nd, z, d, deal_send, deal_recv, True)

    def every(place):
        return GroupRows(lambda device: moved_ref.at[place, device], d, nd, group_send.at[place], group_recv.at[place])

    def mine(place):
        return pltpu.make_async_copy(low.at[place], moved_ref.at[place, d], local_sem.at[2 + place])

    @pl.when(step == 0)
    def _():
        for copy in weights.copies():
            copy.start()
        out_load.start()
        greet(
            [(None, {"dp": flip(d, j)}) for j in range(1, nd)]
            + line_neighbours(nf, y, z)
            + deal_partners(nf, nd, z, d)
        )
        if fused:
            grads_load.start()
            nout_load.start()
        for one in sums[::-1] if not fused else sums[:0:-1]:
            one.begin()
        if not last:
            leave.start_all()
        tail[...] = jnp.zeros_like(tail)
        dstate[...] = jnp.zeros_like(dstate)
        small_ref[...] = jnp.zeros_like(small_ref)
        dgain[...] = jnp.zeros_like(dgain)
        pulls[0] = jnp.zeros(pulls.shape[1:], F32)
        if fused:
            grads_load.wait()
            nout_load.wait()

            def out_tile(i, carry):
                part = pl.ds(pl.multiple_of(i * LANES, LANES), LANES)
                out_grad[part, :] = dot(nout[:, part], normed[...], ((0,), (0,))).astype(BF16)
                return carry

            lax.fori_loop(0, ch // LANES, out_tile, 0)
            sums[0].begin()
            normed_load.start()
        for copy in weights.copies():
            copy.wait()
        out_load.wait()

    def pass_on(place):
        for k in range(1, len(bits)):
            blocks.send(k, place)

    def conclude(place):
        dnormed = blocks.own(place)
        hidden = hidden_ref[place].astype(F32)
        inverse = rms_parts(hidden)
        dgain[...] += jnp.sum(dnormed * hidden * inverse, axis=0, keepdims=True)
        scaled = dnormed * norm_gain_ref[...]
        dhidden = inverse * (
            scaled - hidden * (inverse * inverse) * jnp.mean(scaled * hidden, axis=1, keepdims=True)
        )
        moved = (grad_own_ref[place].astype(F32) + dhidden).astype(BF16)
        low[place] = moved
        if last:
            leave.start(place)
        else:
            next_ref[place] = moved
            first = place * block + d * rows
            pulls[0, pl.ds(first // Q, 1), :] += to_row(
                jnp.sum(moved.astype(F32) * branch_ref[place], axis=1, keepdims=True), first % Q
            )
            mine(place).start()
            every(place).begin(low.at[place])

    dnout[...] = dot(grad_all_ref[...], w_out[...], ((1,), (1,)))

    @pl.when(step >= 1)
    def _():
        pass_on(place + 1)

    def one_chunk(turn, carry):
        sub = subs - 1 - turn
        mix_backward(
            ch, proj_ref, pre_ref, mixed_ref, state_ref, dnout, ratio_ref, pull_ref, meta_ref, segrow_ref,
            conv_w_ref, dtb_ref, alog_ref, skip_ref, gain_ref,
            dproj_ref, small_ref, tail, dstate, sub, place * subs + sub, d * (H // nd),
        )

        @pl.when((turn == 0) & (step >= 1))
        def _():
            conclude(place + 1)

        return carry

    lax.fori_loop(0, subs, one_chunk, 0)
    product = weights.backward(dproj_ref[...]).astype(BF16)
    for o in range(nd):
        partial[place, o] = product[o * rows : (o + 1) * rows, :]
    blocks.send(0, place)
    if not last:

        @pl.when(step >= 1)
        def _():
            every(place + 1).relay()

    for k in range(nf - 1, 0, -1):

        @pl.when(step == nf - 1 - k)
        def _():
            for one in sums:
                one.stage(k)

    @pl.when(step == nf - 1)
    def _():
        pass_on(0)
        if fused:
            normed_load.wait()
            width = dproj_all.shape[1]
            wide = staged.shape[1]
            full = width // wide

            def store(i, size):
                rows = pl.ds(pl.multiple_of(i * wide, 16), size)
                return pltpu.make_async_copy(
                    staged.at[i % 2, pl.ds(0, size)], weight_grad.at[rows], staged_sem.at[i % 2]
                )

            def some(i, carry):
                @pl.when(i >= 2)
                def _():
                    store(i - 2, wide).wait()

                columns = dproj_all[:, pl.ds(pl.multiple_of(i * wide, LANES), wide)]
                staged[i % 2] = dot(columns, normed[...], ((0,), (0,))).astype(BF16)
                store(i, wide).start()
                return carry

            lax.fori_loop(0, full // 2, some, 0)
        conclude(0)
        for row, (start, size) in enumerate(gain_rows(small_ref.shape[1])):
            small_ref[8 + row : 9 + row, 0:size] = dgain[:, start : start + size]
        if last:
            next_pull_ref[...] = jnp.zeros_like(next_pull_ref)
        else:
            next_pull_ref[...] = group_tiles(pulls, tile_send, tile_recv, d, nd)
        if fused:
            lax.fori_loop(full // 2, full, some, 0)
            store(full - 2, wide).wait()
            rest = width - full * wide
            if rest:
                staged[full % 2, 0:rest] = dot(dproj_all[:, full * wide :], normed[...], ((0,), (0,))).astype(BF16)
                store(full, rest).start()
                store(full, rest).wait()
            store(full - 1, wide).wait()
        for one, result in zip(sums, results):
            one.finish()
            copy = pltpu.make_async_copy(one.result, result, local_sem.at[1])
            copy.start()
            copy.wait()
            one.settle()
        leave.arrive()
        leave.settle()
        if not last:
            every(0).relay()
            for k in range(nf):
                every(k).close()
                mine(k).wait()
        blocks.settle(nf)


def run_layer_back(
    ch, rows, nf, nd, last, grad_all, proj, pre, mixed, states, meta, segrow, ratio, pull, small, w_in, w_out,
    hidden, grad_own, norm_gain, branch, identity, sums, leaving, more,
):
    length, width = proj.shape
    if more:
        shapes = [out_part_shape(nf, w_out)] + [in_part_shape(nf, g) for g in sums]
    else:
        shapes = [make(nf, g) for make, g in zip((out_part_shape, in_part_shape), sums)]
    conv_width = ch + 2 * N
    block = rows
    steps = nf
    own = (nf, rows // nd, D)
    every = (nf, nd, rows // nd, D)
    pieces = length // Q
    subs = block // Q
    bits = len(bits_of(nd))
    dma = pltpu.SemaphoreType.DMA
    ordered = lambda s: (steps - 1 - s, 0)
    ordered3 = lambda s: (steps - 1 - s, 0, 0)
    layer = 0 if last else 1
    conv_w, conv_b, dtb, alog, skip, gain = small
    return pl.pallas_call(
        functools.partial(layer_back_kernel, ch, nf, nd, last, bool(more)),
        grid=(steps,),
        in_specs=[
            pl.BlockSpec((block, D), ordered),
            pl.BlockSpec((block, width), ordered),
            pl.BlockSpec((block, conv_width), ordered),
            pl.BlockSpec((block, ch), ordered),
            pl.BlockSpec((subs, N, ch), ordered3),
            pl.BlockSpec((block, LANES), ordered),
            pl.BlockSpec((subs, 1, Q), ordered3),
            once((pieces, Q)),
            once((pieces, Q)),
        ]
        + [pick(part, layer) for part in (conv_w, dtb, alog, skip, gain)]
        + [
            pl.BlockSpec(memory_space=pl.ANY),
            pl.BlockSpec(memory_space=pl.ANY),
            once(own),
            once(own),
            pick(norm_gain, layer),
            pl.BlockSpec(memory_space=pl.ANY) if last else once(own),
        ]
        + [pl.BlockSpec(memory_space=pl.ANY)] * (len(sums) + len(leaving) + len(more)),
        out_specs=[
            pl.BlockSpec(memory_space=pl.ANY) if more else pl.BlockSpec((block, width), ordered),
            once((16, conv_width)),
            pl.BlockSpec(memory_space=pl.ANY) if last else once(own),
            once((pieces, Q)),
            pl.BlockSpec(memory_space=pl.ANY),
        ]
        + [pl.BlockSpec(memory_space=pl.ANY)] * (len(shapes) + len(leaving)),
        out_shape=[
            jax.ShapeDtypeStruct((width, D) if more else (length, width), BF16),
            jax.ShapeDtypeStruct((16, conv_width), F32),
            jax.ShapeDtypeStruct(own, BF16),
            jax.ShapeDtypeStruct((pieces, Q), F32),
            jax.ShapeDtypeStruct((rows, D) if last else every, BF16),
        ]
        + [jax.ShapeDtypeStruct(shape, BF16) for shape in shapes]
        + [jax.ShapeDtypeStruct((rows, D), BF16) for part in leaving],
        scratch_shapes=[
            pltpu.VMEM(held_shape(w_in), BF16),
            pltpu.VMEM((ch, D), BF16),
            pltpu.VMEM((K - 1, 8, conv_width), F32),
            pltpu.VMEM((N, ch), F32),
            pltpu.VMEM((block, ch), F32),
            pltpu.VMEM(every, BF16),
            pltpu.VMEM((nd - 1, nf, rows // nd, D), BF16),
            pltpu.VMEM((nd, pieces, Q), F32),
            pltpu.VMEM(own, BF16),
            pltpu.VMEM((1, D), F32),
            dma((bits, nf, nd)),
            dma((bits, nf, nd)),
            dma((nd,)),
            dma((nd,)),
            dma((nf, nd)),
            dma((nf, nd)),
            dma((2 + nf,)),
            dma((nf,)),
            dma((nf,)),
            dma((nf,)),
        ]
        + [part for shape in shapes for part in section_sum_scratch(nf, shape)]
        + (
            [
                pltpu.VMEM((length, width), BF16),
                pltpu.VMEM((length, D), BF16),
                pltpu.VMEM((2, LANES, D), BF16),
                pltpu.VMEM((ch, D), BF16),
                dma((2,)),
                dma((2,)),
            ]
            if more
            else []
        ),
        compiler_params=pltpu.CompilerParams(
            vmem_limit_bytes=VMEM_LIMIT, collective_id=identity, has_side_effects=True
        ),
        name="layer_back_last" if last else "layer_back_first",
    )(
        grad_all, proj, pre, mixed, states, meta, segrow, ratio, pull, conv_w, dtb, alog, skip, gain, w_in, w_out,
        hidden, grad_own, norm_gain, branch, *sums, *leaving, *more,
    )


def shards(
    inputs, segment, cotangent, norm_gain, in_weight, conv_weight, conv_bias, dt_bias, a_log, d_skip,
    gate_gain, out_weight,
):
    fsdp, dp = lax.axis_size("fsdp"), lax.axis_size("dp")
    section, here = lax.axis_index("section"), lax.axis_index("dp")
    rows = inputs.shape[2]
    ch = DI // dp
    heads = H // dp
    conv_width = ch + 2 * N
    seg_mine = lax.dynamic_index_in_dim(segment, section, 0, keepdims=False)[0].astype(F32)
    seg_mine = jnp.broadcast_to(seg_mine.reshape(rows // Q, 1, Q), (rows // Q, 8, Q)).reshape(-1, Q)
    head_table = jnp.pad(
        jnp.concatenate([dt_bias[0], a_log[0], d_skip[0]], axis=0), ((0, 0), (0, LANES - H))
    )
    (
        proj, mixed, pre, states, nout, branch, after, ratio, conv_w, conv_b, dtb, alog, skip, gain, gains, meta, segrow,
        normed_all, moved, hidden, cot_own, w_in0, w_in1, w_out0, w_out1,
    ) = run_first(
        ch, fsdp, dp, inputs[:, 0], cotangent[:, 0], seg_mine, in_weight[0, 0].T, out_weight[0, 0], conv_weight[0, 0],
        conv_bias[0], norm_gain[0], gate_gain[0], head_table, 2,
    )
    small = (conv_w, conv_b, dtb, alog, skip, gain)
    length = meta.shape[0]
    saved = [(normed_all.reshape(length, D), hidden, proj, nout, mixed, pre, states, branch, ratio)]
    normed_all, hidden = moved.reshape(length, D), after
    proj, nout, mixed, pre, states, branch, final_rows, ratio, pull, cot_all = run_layer(
        ch, rows, fsdp, dp, normed_all, meta, segrow, small, w_in1, w_out1, hidden, cot_own, 3
    )
    saved.append((normed_all, hidden, proj, nout, mixed, pre, states, branch, ratio))

    grad_all, grad_own = cot_all.reshape(length, D), cot_own
    in_grad, small_grads, parts = (), [None, None], []
    fused = D // fsdp % LANES == 0
    for layer in (1, 0):
        last = layer == 0
        normed_all, hidden, proj, gated, mixed, pre, states, branch, ratio = saved[layer]
        out_grad = () if fused else (dot(gated, grad_all, ((0,), (0,))).astype(BF16),)
        dproj, small_grads[layer], after, next_pull, moved, *done = run_layer_back(
            ch, rows, fsdp, dp, last, grad_all, proj, pre, mixed, states, meta, segrow, ratio, pull, small,
            w_in0 if last else w_in1, w_out0 if last else w_out1, hidden, grad_own, gains, saved[0][7], 4 + layer,
            out_grad + in_grad, () if last else (final_rows,), (normed_all, gated, grad_all) if fused else (),
        )
        if not last:
            *done, final = done
        parts += done
        if fused:
            grad = dproj
        else:
            grad = dot(dproj, normed_all, ((0,), (0,))).astype(BF16)
        if not fused:
            grad = jnp.swapaxes(grad.reshape(-1, fsdp, D // fsdp), 0, 1)
        in_grad = (grad,)
        if not last:
            grad_all, grad_own, pull = moved.reshape(length, D), after, next_pull
    input_grad = moved

    in_all, out_all, small_all = run_end(
        fsdp, dp, in_grad[0], parts[2], parts[1], parts[0], small_grads[0], small_grads[1]
    )
    in_total, out_total, gain_total, convw_total, convb_total, dtb_total, alog_total, skip_total, gate_total = run_finish(
        ch, dp, in_all, out_all, small_all
    )
    return (
        final[None, None],
        input_grad[None, None],
        gain_total[None],
        in_total.T[None, None],
        convw_total[None, None],
        convb_total[None],
        dtb_total[None],
        alog_total[None],
        skip_total[None],
        gate_total[None],
        out_total[None, None],
    )


def solution(mesh):
    return jax.shard_map(
        shards,
        mesh=mesh,
        in_specs=(
            P(None, "dp", "fsdp", None),
            P(None, "dp", "fsdp"),
            P(None, "dp", "fsdp", None),
            P("section", None, None),
            P("section", None, "fsdp", None),
            P("section", None, None, None),
            P("section", None, None),
            P("section", None, None),
            P("section", None, None),
            P("section", None, None),
            P("section", None, None),
            P("section", None, "fsdp", None),
        ),
        out_specs=(
            P("section", "dp", "fsdp", None),
            P("section", "dp", "fsdp", None),
            P("section", None, None),
            P("section", None, "fsdp", None),
            P("section", None, None, None),
            P("section", None, None),
            P("section", None, None),
            P("section", None, None),
            P("section", None, None),
            P("section", None, None),
            P("section", None, "fsdp", None),
        ),
        check_vma=False,
    )
```

```python
import functools

import jax
import jax.numpy as jnp
from jax import lax
from jax.experimental import pallas as pl
from jax.experimental.pallas import tpu as pltpu
from jax.sharding import PartitionSpec as P

D = 1536
H = 48
P_SIZE = 64
N = 128
K = 4
DI = 3072
DC = 3328
DIN = 6448
EPSILON = 1e-05
HIGHEST = lax.Precision.HIGHEST
BF16 = jnp.bfloat16
F32 = jnp.float32
Q = 128
LANES = 128


def dot(a, b, dims=((1,), (0,)), precision=None):
    return lax.dot_general(a, b, (dims, ((), ())), preferred_element_type=F32, precision=precision)


def low_dot(a, b, dims=((1,), (0,))):
    return dot(a.astype(BF16), b.astype(BF16), dims)


def fine_dot(a, b, dims=((1,), (0,))):
    return dot(a, b, dims, HIGHEST)


def halves(value):
    high = value.astype(BF16)
    return high, (value - high.astype(F32)).astype(BF16)


def split_dot(a, b, dims=((1,), (0,))):
    (a_high, a_low), (b_high, b_low) = halves(a), halves(b)
    a_axis, b_axis = dims[0][0], dims[1][0]
    both = dot(
        jnp.concatenate([a_high, a_low], axis=a_axis), jnp.concatenate([b_high, b_high], axis=b_axis), dims
    )
    return both + dot(a_high, b_low, dims)


def pair_lanes(table, first, low_half):
    return jnp.where(low_half, table[:, first : first + 1], table[:, first + 1 : first + 2])


def decay_tables(proj_dt, dt_bias, a_row, tri):
    shifted = proj_dt + dt_bias
    step = jnp.maximum(shifted, 0.0) + jnp.log1p(jnp.exp(-jnp.abs(shifted)))
    log_decay = -step * jnp.exp(a_row)
    cumulative = fine_dot(tri, log_decay)
    return shifted, step, log_decay, cumulative


def triangles():
    row = lax.broadcasted_iota(jnp.int32, (Q, Q), 0)
    column = lax.broadcasted_iota(jnp.int32, (Q, Q), 1)
    return row, column


MESH_ID = pl.DeviceIdType.MESH
VMEM_LIMIT = 60 * 1024 * 1024


def remote(src, dst, send_sem, recv_sem, device):
    return pltpu.make_async_remote_copy(
        src_ref=src, dst_ref=dst, send_sem=send_sem, recv_sem=recv_sem, device_id=device, device_id_type=MESH_ID
    )


def greet(devices):
    barrier = pltpu.get_barrier_semaphore()
    count = 0
    for condition, device in devices:
        if condition is None:
            pl.semaphore_signal(barrier, inc=1, device_id=device, device_id_type=MESH_ID)
            count = count + 1
        else:

            @pl.when(condition)
            def _():
                pl.semaphore_signal(barrier, inc=1, device_id=device, device_id_type=MESH_ID)

            count = count + condition.astype(jnp.int32)
    pl.semaphore_wait(barrier, count)


def bits_of(peers):
    return [1 << k for k in range(peers.bit_length() - 1)]


def has_bit(value, bit):
    return (value // bit) % 2


def flip(value, bits):
    bit = 1
    out = value
    while bit <= bits:
        if bits & bit:
            out = out + bit * (1 - 2 * has_bit(value, bit))
        bit = bit * 2
    return out


def to_column(row):
    down, across = triangles()
    return jnp.sum(jnp.where(down == across, jnp.broadcast_to(row, (Q, Q)), 0.0), axis=1, keepdims=True)


def to_row(column, offset=0):
    shape = (column.shape[0], Q)
    down = lax.broadcasted_iota(jnp.int32, shape, 0)
    across = lax.broadcasted_iota(jnp.int32, shape, 1)
    return jnp.sum(jnp.where(across == down + offset, jnp.broadcast_to(column, shape), 0.0), axis=0, keepdims=True)


class GroupTiles:

    def __init__(self, tiles, send_sem, recv_sem, here, peers):
        self.tiles, self.send_sem, self.recv_sem, self.here, self.peers = tiles, send_sem, recv_sem, here, peers

    def copies(self):
        return [
            remote(
                self.tiles.at[0], self.tiles.at[j], self.send_sem.at[j], self.recv_sem.at[j],
                {"dp": flip(self.here, j)},
            )
            for j in range(1, self.peers)
        ]

    def begin(self):
        for copy in self.copies():
            copy.start()

    def finish(self):
        for copy in self.copies():
            copy.wait()
        total = self.tiles[0]
        for j in range(1, self.peers):
            total = total + self.tiles[j]
        return total


def group_tiles(tiles, send_sem, recv_sem, here, peers):
    group = GroupTiles(tiles, send_sem, recv_sem, here, peers)
    group.begin()
    return group.finish()


class GroupRows:

    def __init__(self, where, here, peers, send_sem, recv_sem):
        self.where, self.here, self.peers = where, here, peers
        self.send_sem, self.recv_sem = send_sem, recv_sem

    def part(self, j):
        return self.where(flip(self.here, j))

    def copy(self, j, bit, source=None):
        part = self.part(j)
        return remote(
            part if source is None else source, part, self.send_sem.at[j ^ bit], self.recv_sem.at[j ^ bit],
            {"dp": flip(self.here, bit)},
        )

    def begin(self, source=None):
        for bit in bits_of(self.peers)[::-1]:
            self.copy(0, bit, source).start()

    def phase(self, bit):
        for j in range(bit, self.peers, 2 * bit):
            self.copy(j ^ bit, bit).wait_send()
            landing = self.part(j)
            remote(
                landing, landing, self.send_sem.at[j], self.recv_sem.at[j], {"dp": flip(self.here, bit)}
            ).wait_recv()
            for lower in bits_of(bit)[::-1]:
                self.copy(j, lower).start()

    def relay(self):
        for bit in bits_of(self.peers)[:0:-1]:
            self.phase(bit)

    def close(self):
        self.phase(1)

    def finish(self):
        self.relay()
        self.close()


def rows_of(whole, rows):
    return lambda device: whole.at[pl.ds(pl.multiple_of(device * rows, 8), rows)]


def rms_parts(values):
    return lax.rsqrt(jnp.mean(values * values, axis=-1, keepdims=True) + EPSILON)


class BlockSum:

    def __init__(self, partial, landed, here, peers, send_sem, recv_sem):
        self.partial, self.landed, self.here, self.peers = partial, landed, here, peers
        self.bits = bits_of(peers)
        self.send_sem, self.recv_sem = send_sem, recv_sem

    def slot(self, k, owner):
        return self.peers - self.peers // self.bits[k] + owner // (2 * self.bits[k])

    def copy(self, k, block, owner):
        return remote(
            self.partial.at[block, owner], self.landed.at[self.slot(k, owner), block], self.send_sem.at[k, block, owner],
            self.recv_sem.at[k, block, owner], {"dp": flip(self.here, self.bits[k])},
        )

    def total(self, block, owner, stages):
        total = self.partial[block, owner].astype(F32)
        for m in range(stages):
            self.copy(m, block, owner).wait_recv()
            total = total + self.landed[self.slot(m, owner), block].astype(F32)
        return total

    def leaving(self, k):
        return [flip(self.here, j) for j in range(self.bits[k], self.peers, 2 * self.bits[k])]

    def send(self, k, block):
        for owner in self.leaving(k):
            if k > 0:
                self.partial[block, owner] = self.total(block, owner, k).astype(self.partial.dtype)
            self.copy(k, block, owner).start()

    def own(self, block):
        return self.total(block, self.here, len(self.bits))

    def settle(self, blocks):
        for block in range(blocks):
            for k in range(len(self.bits)):
                for owner in self.leaving(k):
                    self.copy(k, block, owner).wait_send()


class Deal:

    def __init__(self, chunk, own, nf, nd, z, d, send_sem, recv_sem, outward):
        self.chunk, self.own, self.nf, self.nd, self.z, self.d = chunk, own, nf, nd, z, d
        self.send_sem, self.recv_sem, self.outward = send_sem, recv_sem, outward
        self.rows = chunk.shape[0] // nd

    def part(self, o):
        return self.chunk.at[pl.ds(pl.multiple_of(o * self.rows, 16), self.rows)]

    def holder(self, b):
        return {"fsdp": b, "dp": self.z}

    def worker(self, o):
        return {"fsdp": self.d, "dp": o}

    def at_home(self, k):
        return (self.z == self.d) & (self.z == k)

    def send(self, k):
        if self.outward:
            return remote(
                self.own.at[k], self.part(self.d), self.send_sem.at[k], self.recv_sem.at[self.d], self.holder(k)
            )
        return remote(
            self.part(k), self.own.at[self.z], self.send_sem.at[k], self.recv_sem.at[self.z], self.worker(k)
        )

    def recv(self, k):
        if self.outward:
            part = self.part(k)
            return remote(part, part, self.send_sem.at[k], self.recv_sem.at[k], self.worker(k))
        part = self.own.at[k]
        return remote(part, part, self.send_sem.at[k], self.recv_sem.at[k], self.holder(k))

    def keep(self, k):
        if self.outward:
            return pltpu.make_async_copy(self.own.at[k], self.part(k), self.send_sem.at[k])
        return pltpu.make_async_copy(self.part(k), self.own.at[k], self.send_sem.at[k])

    def start(self, k):
        @pl.when(self.at_home(k))
        def _():
            self.keep(k).start()

        @pl.when(jnp.logical_not(self.at_home(k)))
        def _():
            self.send(k).start()

    def start_all(self):
        for k in range(self.nf):
            self.start(k)

    def arrive(self):
        for k in range(self.nf):

            @pl.when(self.at_home(k))
            def _():
                self.keep(k).wait()

            @pl.when(jnp.logical_not(self.at_home(k)))
            def _():
                self.recv(k).wait_recv()

    def settle(self):
        for k in range(self.nf):

            @pl.when(jnp.logical_not(self.at_home(k)))
            def _():
                self.send(k).wait_send()


def deal_partners(nf, nd, z, d):
    out = []
    for k in range(nf):
        elsewhere = (z != d) | (z != k)
        out += [(elsewhere, {"fsdp": k, "dp": z}), (elsewhere, {"fsdp": d, "dp": k})]
    return out


class SectionGather:

    def __init__(self, held, section, nf, y, z, sems, own=None):
        self.own = own
        self.held, self.section, self.nf, self.y, self.z, self.sems = held, section, nf, y, z, sems
        width = held.shape[1]
        first = -(-width // 32) * 16
        self.spans = [(0, first), (first, width - first)]
        self.peer = {"section": 1 - y}

    def block(self, b, part):
        start, size = self.spans[part]
        return self.held.at[b, pl.ds(start, size)]

    def each(self, body):
        for part in range(2):
            owner = self.y == self.section

            @pl.when(owner if part == 0 else jnp.logical_not(owner))
            def _():
                body(part)

    def own_part(self, part):
        start, size = self.spans[part]
        return self.own.at[pl.ds(start, size)]

    def send(self, b, part, row, k, landed, device, source=None):
        here = self.block(b, part)
        return remote(
            here if source is None else source, here, self.sems.at[row, k], self.sems.at[landed, k], device
        )

    def right(self, k, b, part, source=None):
        return self.send(b, part, 0, k, 2, {"fsdp": (self.z + 1) % self.nf}, source)

    def left(self, k, b, part, source=None):
        return self.send(b, part, 1, k, 3, {"fsdp": (self.z + self.nf - 1) % self.nf}, source)

    def over(self, k, b, part, source=None):
        return self.send(b, part, 4, k, 5, self.peer, source)

    def cross(self):
        here = self.block(self.z, 1)
        return remote(self.own_part(1), here, self.sems.at[6, 0], self.sems.at[6, 1], self.peer)

    def keep(self):
        return pltpu.make_async_copy(self.own, self.held.at[self.z], self.sems.at[6, 2])

    def has_right(self):
        return self.z < self.nf - 1

    def has_left(self):
        return self.z > 0

    def start_cross(self):
        @pl.when(self.y == self.section)
        def _():
            self.cross().start()
            self.keep().start()

    def begin(self):
        def body(part):
            source = None
            if part == 1:
                self.cross().wait_recv()
            else:
                source = self.own_part(0)

            @pl.when(self.has_right())
            def _():
                self.right(1, self.z, part, source).start()

            @pl.when(self.has_left())
            def _():
                self.left(1, self.z, part, source).start()

            if part == 0:
                self.cross().wait_send()
                self.over(0, self.z, 0, source).start()

        self.each(body)

    def settle_begin(self):
        def body(part):
            @pl.when(self.has_right())
            def _():
                self.right(1, self.z, part).wait_send()

            @pl.when(self.has_left())
            def _():
                self.left(1, self.z, part).wait_send()

            if part == 0:
                self.over(0, self.z, 0).wait_send()
                self.keep().wait()
            else:
                self.over(0, self.z, 0).wait_recv()

        self.each(body)

    def sides(self, k, body):
        @pl.when(self.z >= k)
        def _():
            body(self.z - k, k, True)

        @pl.when(self.z + k < self.nf)
        def _():
            body(self.z + k, self.nf + k, False)

    def arrive(self, k):
        def body(part):
            def one(b, index, from_left):
                if from_left:
                    self.right(k, b, part).wait_recv()
                else:
                    self.left(k, b, part).wait_recv()

            self.sides(k, one)

        self.each(body)

    def relay(self, k):
        def body(part):
            def one(b, index, from_left):
                if k < self.nf - 1:
                    if from_left:

                        @pl.when(self.has_right())
                        def _():
                            self.right(k + 1, b, part).start()

                    else:

                        @pl.when(self.has_left())
                        def _():
                            self.left(k + 1, b, part).start()

                self.over(index, b, part).start()

            self.sides(k, one)

        self.each(body)

    def settle(self, k):
        def body(part):
            def one(b, index, from_left):
                self.over(index, b, part).wait_send()
                self.over(index, b, 1 - part).wait_recv()
                if k < self.nf - 1:
                    if from_left:

                        @pl.when(self.has_right())
                        def _():
                            self.right(k + 1, b, part).wait_send()

                    else:

                        @pl.when(self.has_left())
                        def _():
                            self.left(k + 1, b, part).wait_send()

            self.sides(k, one)

        self.each(body)


class OutGather:

    def __init__(self, source, held, section, nf, y, z, d, sems, staged):
        self.staged = staged
        self.source, self.held, self.section, self.nf = source, held, section, nf
        self.y, self.z, self.d, self.sems = y, z, d, sems
        self.pieces = sems.shape[1]
        self.rows = source.shape[0] // self.pieces
        self.columns = source.shape[1] // 2
        self.peer = {"section": 1 - y}
        self.source_here = z == d

    def owner(self):
        return self.y == self.section

    def piece(self, ref, part, i):
        return ref.at[pl.ds(i * self.rows, self.rows), pl.ds(part * self.columns, self.columns)]

    def send(self, i, part, row, landed, device, source=None):
        target = self.piece(self.held, part, i)
        return remote(
            target if source is None else self.piece(source, part, i), target, self.sems.at[row, i],
            self.sems.at[landed, i], device,
        )

    def right(self, i, part, source=None):
        return self.send(i, part, 0, 2, {"fsdp": (self.z + 1) % self.nf}, source)

    def left(self, i, part, source=None):
        return self.send(i, part, 1, 2, {"fsdp": (self.z + self.nf - 1) % self.nf}, source)

    def over(self, i, part, source=None):
        return self.send(i, part, 3, 4, self.peer, source)

    def cross(self):
        columns = pl.ds(self.columns, self.columns)
        return remote(
            self.source.at[:, columns], self.held.at[:, columns], self.sems.at[5, 0], self.sems.at[5, 1], self.peer
        )

    def stage(self):
        return pltpu.make_async_copy(self.source, self.staged, self.sems.at[5, 2])

    def keep(self):
        return pltpu.make_async_copy(self.staged, self.held, self.sems.at[5, 3])

    def goes_right(self):
        return (self.z >= self.d) & (self.z < self.nf - 1)

    def goes_left(self):
        return (self.z <= self.d) & (self.z > 0)

    def each(self, condition, body):
        for part in range(2):
            mine = self.owner() if part == 0 else jnp.logical_not(self.owner())

            @pl.when(condition & mine)
            def _():
                body(part)

    def along(self, i, part, action, source=None):
        @pl.when(self.goes_right())
        def _():
            action(self.right(i, part, source))

        @pl.when(self.goes_left())
        def _():
            action(self.left(i, part, source))

    def begin(self):
        @pl.when(self.source_here & self.owner())
        def _():
            self.cross().start()
            self.stage().start()
            for i in range(self.pieces):
                self.along(i, 0, lambda copy: copy.start(), self.source)

    def begin_other(self):
        @pl.when(self.source_here & jnp.logical_not(self.owner()))
        def _():
            self.cross().wait_recv()
            for i in range(self.pieces):
                self.along(i, 1, lambda copy: copy.start())

    def hops(self, distance):
        def body(part):
            for i in range(self.pieces):
                self.right(i, part).wait_recv()
                self.along(i, part, lambda copy: copy.start())

        self.each((self.z == self.d + distance) | (self.z == self.d - distance), body)

    def hand_over(self):
        @pl.when(self.source_here & self.owner())
        def _():
            self.stage().wait()
            self.keep().start()
            for i in range(self.pieces):
                self.over(i, 0, self.source).start()

        def body(part):
            for i in range(self.pieces):
                self.over(i, part).start()

        self.each(jnp.logical_not(self.source_here), body)

    def settle(self):
        @pl.when(self.source_here & self.owner())
        def _():
            self.cross().wait_send()
            self.keep().wait()

        def at_source(part):
            for i in range(self.pieces):
                self.along(i, part, lambda copy: copy.wait_send())
                if part == 0:
                    self.over(i, 0).wait_send()
                else:
                    self.over(i, 0).wait_recv()

        def elsewhere(part):
            for i in range(self.pieces):
                self.along(i, part, lambda copy: copy.wait_send())
                self.over(i, part).wait_send()
                self.over(i, 1 - part).wait_recv()

        self.each(self.source_here, at_source)
        self.each(jnp.logical_not(self.source_here), elsewhere)


def line_neighbours(nf, y, z):
    return [
        (None, {"section": 1 - y}),
        (z < nf - 1, {"fsdp": z + 1}),
        (z > 0, {"fsdp": z - 1}),
    ]


class SectionSum:

    def __init__(self, view, nf, y, z, own, landed, chain, sems, result):
        self.view, self.nf, self.y, self.z, self.result = view, nf, y, z, result
        self.own, self.landed, self.chain = own, landed, chain
        self.load_sem, self.over_send, self.over_recv, self.chain_send, self.chain_recv = (
            sems.at[0], sems.at[1], sems.at[2], sems.at[3], sems.at[4]
        )
        self.part_rows = own.shape[1]

    def load(self, block):
        return pltpu.make_async_copy(self.view(block, self.y), self.own.at[block], self.load_sem.at[block])

    def over(self, block):
        return remote(
            self.view(block, 1 - self.y), self.landed.at[block], self.over_send.at[block], self.over_recv.at[block],
            {"section": 1 - self.y},
        )

    def right(self, block):
        return remote(
            self.own.at[block], self.chain.at[block], self.chain_send.at[block], self.chain_recv.at[block],
            {"fsdp": (self.z + 1) % self.nf},
        )

    def left(self, block, arrives):
        slot = self.nf if arrives else block
        return remote(
            self.own.at[block], self.chain.at[slot], self.chain_send.at[block], self.chain_recv.at[slot],
            {"fsdp": (self.z + self.nf - 1) % self.nf},
        )

    def at(self, k, body):
        if k == 0:
            body(self.z, False)
            return

        @pl.when(self.z + k < self.nf)
        def _():
            body(self.z + k, True)

        @pl.when(self.z - k >= 0)
        def _():
            body(self.z - k, False)

    def begin(self):
        self.at(self.nf - 1, lambda block, rightward: self.over(block).start())
        for k in range(self.nf - 1, -1, -1):
            self.at(k, lambda block, rightward: self.load(block).start())

    def add(self, block, sources, target):
        step = 32

        def some(i, carry):
            rows = pl.ds(pl.multiple_of(i * step, 16), step)
            total = self.own[block, rows, :].astype(F32)
            for ref, slot in sources:
                total = total + ref[slot, rows, :].astype(F32)
            if target is None:
                self.own[block, rows, :] = total.astype(BF16)
            else:
                target[rows, :] = total.astype(BF16)
            return carry

        lax.fori_loop(0, self.part_rows // step, some, 0)

    def ready(self, block):
        self.load(block).wait()
        self.over(block).wait_recv()

    def stage(self, k):
        z, nf = self.z, self.nf
        self.at(k, lambda block, rightward: self.ready(block))
        self.at(k - 1, lambda block, rightward: self.over(block).start())

        def one(block, rightward):
            far_end = z == 0 if rightward else z == nf - 1
            arrived = self.right(block) if rightward else self.left(block, False)
            leaving = self.right(block) if rightward else self.left(block, k == 1)

            @pl.when(jnp.logical_not(far_end))
            def _():
                arrived.wait_recv()
                self.add(block, [(self.landed, block), (self.chain, block)], None)

            @pl.when(far_end)
            def _():
                self.add(block, [(self.landed, block)], None)

            leaving.start()

        self.at(k, one)

    def finish(self):
        z, nf, target = self.z, self.nf, self.result
        self.ready(z)

        @pl.when(z > 0)
        def _():
            self.right(z).wait_recv()

        @pl.when(z < nf - 1)
        def _():
            self.left(z, True).wait_recv()

        @pl.when(z == 0)
        def _():
            self.add(z, [(self.landed, z), (self.chain, nf)], target)

        @pl.when(z == nf - 1)
        def _():
            self.add(z, [(self.landed, z), (self.chain, z)], target)

        @pl.when((z > 0) & (z < nf - 1))
        def _():
            self.add(z, [(self.landed, z), (self.chain, z), (self.chain, nf)], target)

    def settle(self):
        z, nf = self.z, self.nf
        self.over(z).wait_send()
        for k in range(nf - 1, 0, -1):

            @pl.when(z + k < nf)
            def _():
                self.over(z + k).wait_send()
                self.right(z + k).wait_send()

            @pl.when(z - k >= 0)
            def _():
                self.over(z - k).wait_send()
                self.left(z - k, k == 1).wait_send()


def in_parts(width):
    rows = -(-width // 64) * 32
    return rows, width - rows


def in_view(source, nf):
    rows, second = in_parts(source.shape[-2])

    def view(block, part):
        here = pl.ds(pl.multiple_of(part * second, 16), rows)
        if len(source.shape) == 3:
            return source.at[block, here]
        columns = source.shape[1] // nf
        return source.at[here, pl.ds(pl.multiple_of(block * columns, LANES), columns)]

    return view


def out_view(source, nf):
    rows, columns = source.shape[0] // nf, source.shape[1] // 2

    def view(block, part):
        here = pl.ds(pl.multiple_of(block * rows, 16), rows)
        return source.at[here, pl.ds(pl.multiple_of(part * columns, LANES), columns)]

    return view


def in_part_shape(nf, source):
    columns = source.shape[2] if len(source.shape) == 3 else source.shape[1] // nf
    return in_parts(source.shape[-2])[0], columns


def out_part_shape(nf, source):
    return source.shape[0] // nf, source.shape[1] // 2


def section_sum_scratch(nf, part):
    return [
        pltpu.VMEM((nf,) + part, BF16),
        pltpu.VMEM((nf,) + part, BF16),
        pltpu.VMEM((nf + 1,) + part, BF16),
        pltpu.SemaphoreType.DMA((5, nf + 1)),
        pltpu.VMEM(part, BF16),
    ]


class SectionReturn:

    def __init__(self, piece, place, owner, y, sems):
        self.piece, self.place, self.owner, self.y, self.sems = piece, place, owner, y, sems

    def keep(self):
        return pltpu.make_async_copy(self.piece(self.owner), self.place(self.owner), self.sems.at[2])

    def send(self):
        other = 1 - self.owner
        return remote(
            self.piece(other), self.place(other), self.sems.at[0], self.sems.at[1], {"section": 1 - self.y}
        )

    def begin(self):
        @pl.when(self.y == self.owner)
        def _():
            self.keep().start()

        @pl.when(self.y != self.owner)
        def _():
            self.send().start()

    def finish(self):
        @pl.when(self.y == self.owner)
        def _():
            self.keep().wait()
            self.send().wait_recv()

        @pl.when(self.y != self.owner)
        def _():
            self.send().wait_send()


def end_kernel(
    nf, nd,
    in_ref, in_part1_ref, out_part0_ref, out_part1_ref, small0_ref, small1_ref,
    in_all, out_all, small_all,
    in_own, in_landed, in_chain, in_sems, in_part,
    in_final, out_final, small_slots, small_total, local_sem, swap_sem, back_sem, small_sems, group_send, group_recv,
):
    y, z, d = lax.axis_index("section"), lax.axis_index("fsdp"), lax.axis_index("dp")
    away = z != d
    twin = {"fsdp": d, "dp": z}
    peer = {"section": 1 - y}
    wide = lambda k: {"fsdp": (z + k) % nf}
    greet(
        [(None, peer), (away, twin)]
        + [(None, wide(k)) for k in range(1, nf)]
        + [(None, {"dp": flip(d, bit)}) for bit in bits_of(nd)]
    )
    in_sum = SectionSum(in_view(in_ref, nf), nf, y, z, in_own, in_landed, in_chain, in_sems, in_part)
    width = in_final.shape[0]
    part_rows, second = in_parts(width)
    overlap = part_rows - second
    out_rows, out_columns = out_part0_ref.shape
    in_piece = lambda ref: lambda p: ref if p == 0 else ref.at[pl.ds(overlap, width - part_rows)]
    in_place = lambda p: in_final.at[pl.ds(p * part_rows, width - part_rows if p else part_rows)]
    out_place = lambda p: out_final.at[:, pl.ds(p * out_columns, out_columns)]
    out_returns = [
        SectionReturn(lambda p: out_part0_ref, out_place, 0, y, back_sem.at[0]),
        SectionReturn(lambda p: out_part1_ref, out_place, 1, y, back_sem.at[1]),
    ]
    in_returns = [
        SectionReturn(in_piece(in_part), in_place, 0, y, back_sem.at[2]),
        SectionReturn(in_piece(in_part1_ref), in_place, 1, y, back_sem.at[3]),
    ]
    in_groups = [
        GroupRows(
            lambda device, p=p: in_all.at[device, pl.ds(p * part_rows, width - part_rows if p else part_rows)],
            d, nd, group_send.at[p], group_recv.at[p],
        )
        for p in range(2)
    ]
    out_group = GroupRows(rows_of(out_all, out_rows), d, nd, group_send.at[2], group_recv.at[2])
    small_group = GroupRows(lambda device: small_all.at[device], d, nd, group_send.at[3], group_recv.at[3])

    def small_over(ref):
        return remote(ref, small_slots.at[nf], small_sems.at[0, 0], small_sems.at[1, 0], peer)

    def small_load(ref):
        return pltpu.make_async_copy(ref, small_slots.at[0], local_sem.at[0])

    small_copies = [
        remote(small_slots.at[0], small_slots.at[k], small_sems.at[0, k], small_sems.at[1, k], wide(k))
        for k in range(1, nf)
    ]
    small_own = pltpu.make_async_copy(small_total, small_group.part(0), local_sem.at[0])
    swap_target = out_all.at[pl.ds(pl.multiple_of(z * out_rows, 16), out_rows)]
    swap = remote(out_final, swap_target, swap_sem.at[0], swap_sem.at[1], twin)
    stay = pltpu.make_async_copy(out_final, out_group.part(0), swap_sem.at[2])

    def own_copy(p):
        return pltpu.make_async_copy(in_place(p), in_groups[p].part(0), local_sem.at[1 + p])

    def spread(p):
        own_copy(p).start()
        in_groups[p].begin(in_place(p))

    for back in out_returns:
        back.begin()
    in_sum.begin()
    for section, (mine, other) in enumerate(((small0_ref, small1_ref), (small1_ref, small0_ref))):

        @pl.when(y == section)
        def _():
            small_over(other).start()
            small_load(mine).start()


    @pl.when(y == 1)
    def _():
        in_returns[1].keep().start()
        in_returns[1].keep().wait()
        spread(1)

    for back in out_returns:
        back.finish()

    @pl.when(away)
    def _():
        swap.start()

    @pl.when(jnp.logical_not(away))
    def _():
        stay.start()

    for k in range(nf - 1, 0, -1):
        in_sum.stage(k)
        if k == nf - 1:
            small_load(small0_ref).wait()
            small_over(small0_ref).wait()
            small_slots[0] = small_slots[0] + small_slots[nf]
            for copy in small_copies:
                copy.start()

            @pl.when(away)
            def _():
                swap.wait()

            @pl.when(jnp.logical_not(away))
            def _():
                stay.wait()

            out_group.begin()
        if k == nf - 2:
            for copy in small_copies:
                copy.wait()
            total = small_slots[0]
            for j in range(1, nf):
                total = total + small_slots[j]
            small_total[...] = total
            small_own.start()
            small_group.begin(small_total)
            out_group.relay()
        if k == 1:
            small_group.finish()
            small_own.wait()
            out_group.close()
    in_sum.finish()

    @pl.when(y == 0)
    def _():
        in_returns[0].keep().start()
        in_returns[1].send().start()
        in_returns[0].keep().wait()
        spread(0)
        in_returns[0].send().wait_recv()
        spread(1)
        in_returns[1].send().wait_send()

    @pl.when(y == 1)
    def _():
        in_returns[0].send().start()
        in_returns[1].send().wait_recv()
        spread(0)
        in_returns[0].send().wait_send()

    for p in range(2):
        in_groups[p].finish()
        own_copy(p).wait()
    in_sum.settle()


def run_end(nf, nd, in_grad, in_part1, out_part0, out_part1, small0, small1):
    anywhere = pl.BlockSpec(memory_space=pl.ANY)
    dma = pltpu.SemaphoreType.DMA
    width = in_grad.shape[-2]
    out_rows = out_part0.shape[0]
    return pl.pallas_call(
        functools.partial(end_kernel, nf, nd),
        in_specs=[anywhere] * 6,
        out_specs=[anywhere] * 3,
        out_shape=[
            jax.ShapeDtypeStruct((nd, width, in_part1.shape[1]), BF16),
            jax.ShapeDtypeStruct((nd * out_rows, D), BF16),
            jax.ShapeDtypeStruct((nd,) + small0.shape, F32),
        ],
        scratch_shapes=section_sum_scratch(nf, in_part1.shape)
        + [
            pltpu.VMEM((width, in_part1.shape[1]), BF16),
            pltpu.VMEM((out_rows, D), BF16),
            pltpu.VMEM((nf + 1,) + small0.shape, F32),
            pltpu.VMEM(small0.shape, F32),
            dma((3,)),
            dma((3,)),
            dma((4, 3)),
            dma((2, nf)),
            dma((4, nd)),
            dma((4, nd)),
        ],
        compiler_params=pltpu.CompilerParams(
            vmem_limit_bytes=VMEM_LIMIT, collective_id=6, has_side_effects=True
        ),
        name="sum_end",
    )(in_grad, in_part1, out_part0, out_part1, small0, small1)


def finish_kernel(
    ch, nd, in_ref, shared_ref, out_ref, small_ref,
    in_total, out_total, gain_ref, convw_ref, convb_ref, dtb_ref, alog_ref, skip_ref, gate_ref, shared, sems,
):
    step = pl.program_id(0)
    heads = H // nd
    count = DIN - 2 * DI

    def copy(j):
        return pltpu.make_async_copy(shared_ref.at[j, pl.ds(2 * ch, count)], shared.at[j], sems.at[j])

    @pl.when(step == 0)
    def _():
        for j in range(nd):
            copy(j).start()
        for row, (start, size) in enumerate(gain_rows(small_ref.shape[2])):
            gain_ref[:, start : start + size] = jnp.sum(small_ref[:, 8 + row : 9 + row, 0:size], axis=0)
        both = jnp.sum(small_ref[:, 0:8, ch:], axis=0)
        convw_ref[:, DI:] = both[0:4, :]
        convb_ref[:, DI:] = both[4:5, :]
        rows = lax.broadcasted_iota(jnp.int32, (ch, LANES), 0)
        columns = lax.broadcasted_iota(jnp.int32, (ch, LANES), 1)
        by_head = jnp.where(rows // P_SIZE == columns, 1.0, 0.0)
        decays, skips = [[], []], []
        for j in range(nd):
            here = slice(j * ch, (j + 1) * ch)
            convw_ref[:, here] = small_ref[j, 0:4, :ch]
            convb_ref[:, here] = small_ref[j, 4:5, :ch]
            gate_ref[:, here] = small_ref[j, 5:6, :ch]
            skips.append(fine_dot(small_ref[j, 0:8, :ch], by_head)[6:7, :heads])
            for k in range(2):
                decays[k].append(small_ref[j, 7:8, k * LANES : k * LANES + heads])
        dtb_ref[...] = jnp.concatenate(decays[0], axis=1)
        alog_ref[...] = jnp.concatenate(decays[1], axis=1)
        skip_ref[...] = jnp.concatenate(skips, axis=1)

    @pl.when(step < 2 * nd)
    def _():
        in_total[...] = in_ref[...].astype(F32)
        out_total[...] = out_ref[...].astype(F32)

    @pl.when(step == 2 * nd)
    def _():
        for j in range(nd):
            copy(j).wait()
        total = shared[0].astype(F32)
        for j in range(1, nd):
            total = total + shared[j].astype(F32)
        in_total[0:count, :] = total


def run_finish(ch, nd, in_all, out_all, small_all):
    columns = in_all.shape[2]
    rows = out_all.shape[0]
    piece = rows // (2 * nd)
    final = lambda s: (jnp.minimum(s, 2 * nd - 1), 0)

    def in_block(s):
        s = jnp.minimum(s, 2 * nd - 1)
        return (s % nd, s // nd, 0)

    smalls = [(1, D), (K, DC), (1, DC), (1, H), (1, H), (1, H), (1, DI)]
    return pl.pallas_call(
        functools.partial(finish_kernel, ch, nd),
        grid=(2 * nd + 1,),
        in_specs=[
            pl.BlockSpec((None, ch, columns), in_block),
            pl.BlockSpec(memory_space=pl.ANY),
            pl.BlockSpec((piece, D), final),
            once(small_all.shape),
        ],
        out_specs=[pl.BlockSpec((ch, columns), lambda s: (s, 0)), pl.BlockSpec((piece, D), final)]
        + [once(shape) for shape in smalls],
        out_shape=[jax.ShapeDtypeStruct((DIN, columns), F32), jax.ShapeDtypeStruct((rows, D), F32)]
        + [jax.ShapeDtypeStruct(shape, F32) for shape in smalls],
        scratch_shapes=[pltpu.VMEM((nd, DIN - 2 * DI, columns), BF16), pltpu.SemaphoreType.DMA((nd,))],
        compiler_params=pltpu.CompilerParams(vmem_limit_bytes=VMEM_LIMIT),
        name="finish",
    )(in_all, in_all, out_all, small_all)


class Weights:

    def __init__(self, source, held, sems):
        self.source, self.held, self.sems = source, held, sems
        self.blocks = source.shape[0]
        self.columns = source.shape[2]

    def copies(self):
        out = []
        for k in range(self.blocks):
            if len(self.held.shape) == 3:
                target = self.held.at[k]
            else:
                target = self.held.at[:, pl.ds(k * self.columns, self.columns)]
            out.append(pltpu.make_async_copy(self.source.at[k], target, self.sems.at[k]))
        return out

    def forward(self, rows):
        if len(self.held.shape) == 2:
            return dot(rows, self.held[...], ((1,), (1,)))
        total = 0.0
        for k in range(self.blocks):
            total = total + dot(
                rows[:, k * self.columns : (k + 1) * self.columns], self.held[k], ((1,), (1,))
            )
        return total

    def backward(self, rows):
        if len(self.held.shape) == 2:
            return dot(rows, self.held[...])
        return jnp.concatenate([dot(rows, self.held[k]) for k in range(self.blocks)], axis=1)


def held_shape(w_in):
    blocks, width, columns = w_in.shape
    return (width, blocks * columns) if columns % LANES == 0 else (blocks, width, columns)


def own_steps(steps, turn):
    padded = jnp.concatenate([steps, jnp.zeros((steps.shape[0], LANES - H), F32)], axis=1)
    return pltpu.roll(padded, LANES - turn, 1)


def mix_forward(
    ch, proj_ref, meta_ref, segrow_ref, conv_w_ref, conv_b_ref, dtb_ref, alog_ref, skip_ref,
    gated_ref, square_ref, mixed_ref, pre_ref, state_out_ref, pad, state, sub, turn,
):
    conv_width = ch + 2 * N
    rows = pl.ds(pl.multiple_of(sub * Q, Q), Q)
    meta = meta_ref[rows, :]
    raw = proj_ref[rows, ch : ch + conv_width]
    pre = conv_b_ref[...] + conv_w_ref[3:4, :] * raw
    before = pad[...]
    first_rows = lax.broadcasted_iota(jnp.int32, (8, conv_width), 0)
    for lag in range(1, K):
        earlier = pltpu.roll(raw, lag, 0)
        begin = jnp.where(first_rows >= lag, earlier[0:8, :], pltpu.roll(before, lag, 0))
        shifted = jnp.concatenate([begin, earlier[8:, :]], axis=0)
        pre = pre + (conv_w_ref[3 - lag : 4 - lag, :] * meta[:, lag : lag + 1]) * shifted
    pad[...] = raw[Q - 8 :, :]
    pre_ref[rows, :] = pre
    conv_out = pre * jax.nn.sigmoid(pre)
    values = conv_out[:, :ch]
    b_part = conv_out[:, ch : ch + N]
    c_part = conv_out[:, ch + N :]
    row, column = triangles()
    tri = jnp.where(row >= column, 1.0, 0.0)
    shifted, step, log_decay, cumulative = decay_tables(
        own_steps(proj_ref[rows, ch + conv_width :], turn), dtb_ref[...], alog_ref[...], tri
    )
    linked = (row >= column) & (meta[:, 0:1] == segrow_ref[sub])
    inner = jnp.where(linked, split_dot(c_part, b_part, ((1,), (1,))), 0.0)
    cum_t = cumulative.T
    step_t = step.T
    last = cumulative[Q - 1 : Q, :]
    entry = meta[:, 4:5] * jnp.exp(cumulative)
    weight = meta[:, 5:6] * jnp.exp(last - cumulative) * step
    state_in = state[...]
    state_out_ref[sub] = state_in
    carried = split_dot(c_part, state_in)
    low_half = lax.broadcasted_iota(jnp.int32, (Q, LANES), 1) < P_SIZE
    squares = jnp.zeros((Q, 1), F32)
    weighted = []
    entries = []
    values_high, values_low = halves(values)
    for pair in range(ch // LANES):
        lanes = slice(pair * LANES, (pair + 1) * LANES)
        values_pair = values[:, lanes]
        mats = []
        for head in (2 * pair, 2 * pair + 1):
            spread = jnp.minimum(cumulative[:, head : head + 1] - cum_t[head : head + 1, :], 0.0)
            mats.append((inner * jnp.exp(spread) * step_t[head : head + 1, :]).astype(BF16))
        parts = [values_high[:, lanes], values_low[:, lanes]]
        zero = jnp.zeros_like(parts[0])
        stacked = jnp.concatenate(
            [
                jnp.concatenate([jnp.where(low_half, part, zero) for part in parts], axis=1),
                jnp.concatenate([jnp.where(low_half, zero, part) for part in parts], axis=1),
            ],
            axis=0,
        )
        both = dot(jnp.concatenate(mats, axis=1), stacked)
        out = both[:, :LANES] + both[:, LANES:]
        entry_pair = pair_lanes(entry, 2 * pair, low_half)
        out = out + entry_pair * carried[:, lanes] + skip_ref[:, lanes] * values_pair
        mixed_ref[rows, lanes] = out
        gate = proj_ref[rows, lanes]
        gated = out * (gate * jax.nn.sigmoid(gate))
        squares = squares + jnp.sum(gated * gated, axis=1, keepdims=True)
        gated_ref[rows, lanes] = gated
        weighted.append(pair_lanes(weight, 2 * pair, low_half) * values_pair)
        entries.append(entry_pair[Q - 1 : Q, :])
    square_ref[0, pl.ds(sub, 1), :] = to_row(squares)
    state[...] = jnp.concatenate(entries, axis=1) * state_in + split_dot(
        b_part.T, jnp.concatenate(weighted, axis=1)
    )


def first_kernel(
    ch, nf, nd,
    x_ref, cot_ref, seg_ref, in_ref, out_ref, conv_w_ref, conv_b_ref, norm_ref, gate_ref, head_ref,
    proj_ref, mixed_ref, pre_ref, state_out_ref, nout_ref, branch_ref, next_ref, ratio_ref,
    conv_w_out, conv_b_out, dtb_out, alog_out, skip_out, gain_out, norm_out, meta_out, segrow_out,
    normed_all, moved_ref, hidden_out, cot_own, w_in0, w_in1, w_out0, w_out1,
    held, w_out, pad, state, gated, partial, landed, squares, low, normed, x_low, table, seg_all, own_block, staged,
    sum_send, sum_recv, tile_send, tile_recv, group_send, group_recv, start_send, start_recv, deal_send, deal_recv,
    in_sems0, in_sems1, out_sems0, out_sems1, local_sem, load_sem, small_sem, swap_sem, own_sem,
):
    step = pl.program_id(0)
    y, z, d = lax.axis_index("section"), lax.axis_index("fsdp"), lax.axis_index("dp")
    block = proj_ref.shape[0]
    subs = block // Q
    rows = block // nd
    length = block * nf
    lines = block // Q * 8
    heads = H // nd
    bits = bits_of(nd)
    twin = {"fsdp": d, "dp": z}
    home = z == d
    away = z != d
    peer = {"section": 1 - y}
    blocks = BlockSum(partial, landed, d, nd, sum_send, sum_recv)
    weights = Weights(w_in0, held, load_sem)
    out_load = pltpu.make_async_copy(w_out0, w_out, local_sem.at[0])
    gathers = [SectionGather(w_in0, 0, nf, y, z, in_sems0, own_block), SectionGather(w_in1, 1, nf, y, z, in_sems1, own_block)]
    outs = [
        OutGather(out_ref, w_out0, 0, nf, y, z, d, out_sems0, staged),
        OutGather(out_ref, w_out1, 1, nf, y, z, d, out_sems1, staged),
    ]
    enter = Deal(x_ref.at[y], x_low, nf, nd, z, d, deal_send.at[0], deal_recv.at[0], False)
    enter_cot = Deal(cot_ref.at[y], cot_own, nf, nd, z, d, deal_send.at[1], deal_recv.at[1], False)
    first_group = GroupRows(lambda device: normed.at[:, device], d, nd, start_send.at[0], start_recv.at[0])
    normed_copy = pltpu.make_async_copy(normed, normed_all, local_sem.at[1])
    hidden_copy = pltpu.make_async_copy(x_low, hidden_out, local_sem.at[2])

    def seg_rows(device):
        return seg_all.at[pl.ds(pl.multiple_of(device * lines, 8), lines)]

    seg_group = GroupRows(seg_rows, d, nd, start_send.at[1], start_recv.at[1])

    def every(place):
        return GroupRows(lambda device: moved_ref.at[place, device], d, nd, group_send.at[place], group_recv.at[place])

    def mine(place):
        return pltpu.make_async_copy(low.at[place], moved_ref.at[place, d], local_sem.at[3 + place])

    def stage(gather, k):
        gather.arrive(k)
        gather.relay(k)

    @pl.when(step == 0)
    def _():
        greet(
            line_neighbours(nf, y, z)
            + [(away, twin)]
            + deal_partners(nf, nd, z, d)
            + [(None, {"dp": flip(d, j)}) for j in range(1, nd)]
        )

        own_copies = [
            pltpu.make_async_copy(
                in_ref.at[pl.ds(pl.multiple_of(begin, 16), count)], own_block.at[pl.ds(spot, count)], own_sem.at[k]
            )
            for k, (begin, spot, count) in enumerate(
                [(d * ch, 0, ch), (DI + d * ch, ch, ch), (2 * DI, 2 * ch, DIN - 2 * DI)]
            )
        ]
        for copy in own_copies:
            copy.start()
        for copy in own_copies:
            copy.wait()
        gathers[0].start_cross()
        gathers[1].start_cross()
        table[y, 0:4, :] = conv_w_ref[...]
        table[y, 4:5, :] = conv_b_ref[...]
        table[y, 5:6, 0:D] = norm_ref[...]
        table[y, 6:7, 0:DI] = gate_ref[...]
        for k in range(3):
            table[y, 7:8, k * LANES : (k + 1) * LANES] = head_ref[k : k + 1, :]
        small_copy = remote(table.at[y], table.at[y], small_sem.at[0], small_sem.at[1], peer)
        small_copy.start()
        seg_swap = remote(seg_ref, seg_rows(z), swap_sem.at[0], swap_sem.at[1], twin)
        seg_stay = pltpu.make_async_copy(seg_ref, seg_rows(d), swap_sem.at[0])

        @pl.when(away)
        def _():
            seg_swap.start()

        @pl.when(home)
        def _():
            seg_stay.start()

        gathers[0].begin()
        enter.start_all()
        outs[0].begin()
        stage(gathers[0], 1)
        outs[0].begin_other()
        outs[0].hops(1)

        small_copy.wait()
        enter.arrive()
        hidden_copy.start()
        values = x_low[...].astype(F32)
        low[...] = (values * rms_parts(values) * table[0, 5:6, 0:D]).astype(BF16)
        for place in range(nf):
            normed[place, d] = low[place]
        first_group.begin(low)

        @pl.when(away)
        def _():
            seg_swap.wait()

        @pl.when(home)
        def _():
            seg_stay.wait()

        seg_group.begin()
        for k in range(2, nf - 1):
            stage(gathers[0], k)
            outs[0].hops(k)

        turn = d * heads
        low_half = lax.broadcasted_iota(jnp.int32, (1, LANES), 1) < P_SIZE
        channels = pl.ds(pl.multiple_of(d * ch, LANES), ch)
        for section in range(2):
            conv_w_out[section, :, 0:ch] = table[section, 0:4, channels]
            conv_w_out[section, :, ch:] = table[section, 0:4, DI:DC]
            conv_b_out[section, :, 0:ch] = table[section, 4:5, channels]
            conv_b_out[section, :, ch:] = table[section, 4:5, DI:DC]
            norm_out[section] = table[section, 5:6, 0:D]
            gain_out[section] = table[section, 6:7, channels]
            head_rows = [
                pltpu.roll(table[section, :, k * LANES : (k + 1) * LANES], LANES - turn, 1)[7:8, :] for k in range(3)
            ]
            dtb_out[section] = head_rows[0]
            alog_out[section] = head_rows[1]
            for pair in range(ch // LANES):
                skip_out[section, :, pair * LANES : (pair + 1) * LANES] = pair_lanes(head_rows[2], 2 * pair, low_half)

        seg_group.finish()

        lane = lax.broadcasted_iota(jnp.int32, (8, LANES), 1)
        sub_lane = lax.broadcasted_iota(jnp.int32, (Q, LANES), 1)
        before = jnp.full((8, LANES), -1.0, F32)
        for chunk in range(length // Q):
            now = seg_all[chunk * 8 : chunk * 8 + 8, :]
            segrow_out[chunk] = now[0:1, :]
            columns = [now[0:1, :]]
            for lag in range(1, K):
                earlier = jnp.where(lane < lag, pltpu.roll(before, lag, 1), pltpu.roll(now, lag, 1))
                columns.append(jnp.where(earlier == now, 1.0, 0.0)[0:1, :])
            columns.append(jnp.where(now == before[:, Q - 1 : Q], 1.0, 0.0)[0:1, :])
            columns.append(jnp.where(now == now[:, Q - 1 : Q], 1.0, 0.0)[0:1, :])
            masks = jnp.zeros((Q, LANES), F32)
            for j, row in enumerate(columns):
                masks = jnp.where(sub_lane == j, to_column(row), masks)
            meta_out[chunk * Q : (chunk + 1) * Q, :] = masks
            before = now

        stage(gathers[0], nf - 1)
        outs[0].hops(nf - 1)
        outs[0].hand_over()
        gathers[1].begin()
        first_group.finish()
        normed_copy.start()
        pad[...] = jnp.zeros_like(pad)
        state[...] = jnp.zeros_like(state)
        for k in range(1, nf):
            gathers[0].settle(k)
        gathers[0].settle_begin()
        for copy in weights.copies():
            copy.start()
        for copy in weights.copies():
            copy.wait()

    def tile(place):
        return GroupTiles(squares.at[place], tile_send.at[place], tile_recv.at[place], d, nd)

    def project(place):
        ratio = lax.rsqrt(tile(place).finish() * (1.0 / DI) + EPSILON)
        for sub in range(subs):
            piece = place * subs + sub
            ratio_ref[pl.ds(piece, 1), :] = ratio[sub : sub + 1, :]
            normed_out = gated[place % 2, sub * Q : (sub + 1) * Q, :] * to_column(ratio[sub : sub + 1, :])
            nout_ref[pl.ds(pl.multiple_of(piece * Q, Q), Q), :] = (normed_out * gain_out[0]).astype(BF16)
        here_rows = pl.ds(pl.multiple_of(place * block, Q), block)
        product = dot(nout_ref[here_rows, :], w_out[...])
        for o in range(nd):
            partial[place, o] = product[o * rows : (o + 1) * rows, :]
        blocks.send(0, place)

    def pass_on(place):
        for k in range(1, len(bits)):
            blocks.send(k, place)

    def conclude(place):
        branch = blocks.own(place)
        branch_ref[place] = branch
        moved = (x_low[place].astype(F32) + branch).astype(BF16)
        next_ref[place] = moved
        values = moved.astype(F32)
        low[place] = (values * rms_parts(values) * norm_out[1]).astype(BF16)
        mine(place).start()
        every(place).begin(low.at[place])

    proj_ref[...] = weights.forward(normed[step].reshape(block, D))

    @pl.when(step == 0)
    def _():
        stage(gathers[1], 1)

    @pl.when(step == 1)
    def _():
        outs[0].settle()
        out_load.start()
        out_load.wait()

    @pl.when(step >= 1)
    def _():
        project(step - 1)

    meta = meta_out.at[pl.ds(pl.multiple_of(step * block, Q), block)]
    segrow = segrow_out.at[pl.ds(step * subs, subs)]

    def one_chunk(sub, carry):
        mix_forward(
            ch, proj_ref, meta, segrow, conv_w_out.at[0], conv_b_out.at[0], dtb_out.at[0], alog_out.at[0],
            skip_out.at[0], gated.at[step % 2], squares.at[step], mixed_ref, pre_ref, state_out_ref, pad, state, sub,
            d * heads,
        )

        @pl.when(sub == 0)
        def _():
            @pl.when(step >= 2)
            def _():
                conclude(step - 2)

            @pl.when(step >= 1)
            def _():
                pass_on(step - 1)

            @pl.when(step >= 3)
            def _():
                every(step - 3).relay()

            for k in range(2, nf):

                @pl.when(step == k - 1)
                def _():
                    stage(gathers[1], k)


        return carry

    lax.fori_loop(0, subs, one_chunk, 0)
    tile(step).begin()

    @pl.when(step == 1)
    def _():
        outs[1].begin()

    @pl.when(step == nf - 2)
    def _():
        enter_cot.start_all()

    @pl.when(step == 2)
    def _():
        outs[1].begin_other()

    for k in range(1, nf):

        @pl.when(step == min(k + 1, nf - 1))
        def _():
            outs[1].hops(k)
            if k == nf - 1:
                outs[1].hand_over()

    @pl.when(step == nf - 1)
    def _():
        project(nf - 1)
        pass_on(nf - 1)
        conclude(nf - 2)
        every(nf - 3).relay()
        conclude(nf - 1)
        every(nf - 2).relay()
        for k in range(1, nf):
            gathers[1].settle(k)
        gathers[1].settle_begin()
        outs[1].settle()
        enter.settle()
        enter_cot.arrive()
        enter_cot.settle()
        normed_copy.wait()
        hidden_copy.wait()
        every(nf - 1).relay()
        for place in range(nf):
            every(place).close()
            mine(place).wait()
        blocks.settle(nf)


def run_first(ch, nf, nd, x, cot, seg, in_rows, out_rows, conv_w, conv_b, norm_gain, gate_gain, head_table, identity):
    block = x.shape[1]
    length = block * nf
    conv_width = ch + 2 * N
    columns = in_rows.shape[1]
    width = 2 * ch + DIN - 2 * DI
    pieces = length // Q
    subs = block // Q
    bits = len(bits_of(nd))
    own = (nf, block // nd, D)
    every = (nf, nd, block // nd, D)
    w_in = jax.ShapeDtypeStruct((nf, width, columns), BF16)
    anywhere = pl.BlockSpec(memory_space=pl.ANY)
    dma = pltpu.SemaphoreType.DMA
    ordered = lambda s: (s, 0)
    small = [(2, K, conv_width), (2, 1, conv_width), (2, 1, LANES), (2, 1, LANES), (2, 1, ch), (2, 1, ch), (2, 1, D)]
    resident = small + [(length, LANES), (pieces, 1, Q)]
    return pl.pallas_call(
        functools.partial(first_kernel, ch, nf, nd),
        grid=(nf,),
        in_specs=[anywhere] * 5 + [once(part.shape) for part in (conv_w, conv_b, norm_gain, gate_gain, head_table)],
        out_specs=[
            pl.BlockSpec((block, width), ordered),
            pl.BlockSpec((block, ch), ordered),
            pl.BlockSpec((block, conv_width), ordered),
            pl.BlockSpec((subs, N, ch), lambda s: (s, 0, 0)),
            once((length, ch)),
            once(own),
            once(own),
            once((pieces, Q)),
        ]
        + [once(shape) for shape in resident]
        + [anywhere] * 8,
        out_shape=[
            jax.ShapeDtypeStruct((length, width), F32),
            jax.ShapeDtypeStruct((length, ch), F32),
            jax.ShapeDtypeStruct((length, conv_width), F32),
            jax.ShapeDtypeStruct((pieces, N, ch), F32),
            jax.ShapeDtypeStruct((length, ch), BF16),
            jax.ShapeDtypeStruct(own, F32),
            jax.ShapeDtypeStruct(own, BF16),
            jax.ShapeDtypeStruct((pieces, Q), F32),
        ]
        + [jax.ShapeDtypeStruct(shape, F32) for shape in resident]
        + [
            jax.ShapeDtypeStruct(every, BF16),
            jax.ShapeDtypeStruct(every, BF16),
            jax.ShapeDtypeStruct(own, BF16),
            jax.ShapeDtypeStruct(own, BF16),
            w_in,
            w_in,
            jax.ShapeDtypeStruct((ch, D), BF16),
            jax.ShapeDtypeStruct((ch, D), BF16),
        ],
        scratch_shapes=[
            pltpu.VMEM(held_shape(w_in), BF16),
            pltpu.VMEM((ch, D), BF16),
            pltpu.VMEM((8, conv_width), F32),
            pltpu.VMEM((N, ch), F32),
            pltpu.VMEM((2, block, ch), F32),
            pltpu.VMEM(every, F32),
            pltpu.VMEM((nd - 1, nf, block // nd, D), F32),
            pltpu.VMEM((nf, nd, 8, LANES), F32),
            pltpu.VMEM(own, BF16),
            pltpu.VMEM(every, BF16),
            pltpu.VMEM(own, BF16),
            pltpu.VMEM((2, 8, DC), F32),
            pltpu.VMEM((pieces * 8, LANES), F32),
            pltpu.VMEM((width, columns), BF16),
            pltpu.VMEM((ch, D), BF16),
            dma((bits, nf, nd)),
            dma((bits, nf, nd)),
            dma((nf, nd)),
            dma((nf, nd)),
            dma((nf, nd)),
            dma((nf, nd)),
            dma((2, nd)),
            dma((2, nd)),
            dma((2, nf)),
            dma((2, nf)),
            dma((7, 2 * nf)),
            dma((7, 2 * nf)),
            dma((6, 4)),
            dma((6, 4)),
            dma((3 + nf,)),
            dma((nf,)),
            dma((2,)),
            dma((2,)),
            dma((3,)),
        ],
        compiler_params=pltpu.CompilerParams(
            vmem_limit_bytes=VMEM_LIMIT, collective_id=identity, has_side_effects=True
        ),
        name="layer_first",
    )(x, cot, seg, in_rows, out_rows, conv_w, conv_b, norm_gain, gate_gain, head_table)


def layer_kernel(
    ch, nf, nd,
    normed_ref, meta_ref, segrow_ref, conv_w_ref, conv_b_ref, dtb_ref, alog_ref, skip_ref, gain_ref,
    w_in_ref, w_out_ref, hidden_ref, extra_ref,
    proj_ref, nout_ref, mixed_ref, pre_ref, state_out_ref, branch_ref, next_ref, ratio_ref, pull_ref, cot_all,
    held, w_out, pad, state, gated, partial, landed, squares, pulls,
    sum_send, sum_recv, tile_send, tile_recv, group_send, group_recv, local_sem, load_sem,
):
    step = pl.program_id(0)
    y, z, d = lax.axis_index("section"), lax.axis_index("fsdp"), lax.axis_index("dp")
    block = normed_ref.shape[0]
    subs = block // Q
    rows = block // nd
    bits = bits_of(nd)
    blocks = BlockSum(partial, landed, d, nd, sum_send, sum_recv)
    weights = Weights(w_in_ref, held, load_sem)
    out_load = pltpu.make_async_copy(w_out_ref, w_out, local_sem.at[0])
    cot_group = GroupRows(lambda device: cot_all.at[:, device], d, nd, group_send.at[0], group_recv.at[0])
    cot_keep = pltpu.make_async_copy(extra_ref, cot_group.part(0), local_sem.at[1])

    @pl.when(step == 0)
    def _():
        for copy in weights.copies():
            copy.start()
        out_load.start()
        greet([(None, {"dp": flip(d, j)}) for j in range(1, nd)])
        cot_keep.start()
        cot_group.begin(extra_ref)
        pad[...] = jnp.zeros_like(pad)
        state[...] = jnp.zeros_like(state)
        pulls[0] = jnp.zeros(pulls.shape[1:], F32)
        for copy in weights.copies():
            copy.wait()
        out_load.wait()

    def tile(place):
        return GroupTiles(squares.at[place], tile_send.at[place], tile_recv.at[place], d, nd)

    def project(place):
        ratio = lax.rsqrt(tile(place).finish() * (1.0 / DI) + EPSILON)
        for sub in range(subs):
            piece = place * subs + sub
            ratio_ref[pl.ds(piece, 1), :] = ratio[sub : sub + 1, :]
            normed_out = gated[place % 2, sub * Q : (sub + 1) * Q, :] * to_column(ratio[sub : sub + 1, :])
            nout_ref[pl.ds(pl.multiple_of(piece * Q, Q), Q), :] = (normed_out * gain_ref[...]).astype(BF16)
        here_rows = pl.ds(pl.multiple_of(place * block, Q), block)
        product = dot(nout_ref[here_rows, :], w_out[...]).astype(partial.dtype)
        for o in range(nd):
            partial[place, o] = product[o * rows : (o + 1) * rows, :]
        blocks.send(0, place)

    def pass_on(place):
        for k in range(1, len(bits)):
            blocks.send(k, place)

    def conclude(place):
        branch = blocks.own(place)
        branch_ref[place] = branch
        moved = (hidden_ref[place].astype(F32) + branch).astype(BF16)
        next_ref[place] = moved
        first = place * block + d * rows
        pulls[0, pl.ds(first // Q, 1), :] += to_row(
            jnp.sum(extra_ref[place].astype(F32) * branch, axis=1, keepdims=True), first % Q
        )

    proj_ref[...] = weights.forward(normed_ref[...])

    @pl.when(step >= 1)
    def _():
        project(step - 1)

    def one_chunk(sub, carry):
        mix_forward(
            ch, proj_ref, meta_ref, segrow_ref, conv_w_ref, conv_b_ref, dtb_ref, alog_ref, skip_ref,
            gated.at[step % 2], squares.at[step], mixed_ref, pre_ref, state_out_ref, pad, state, sub, d * (H // nd),
        )

        @pl.when(sub == 0)
        def _():
            @pl.when(step >= 2)
            def _():
                conclude(step - 2)

            @pl.when(step >= 1)
            def _():
                pass_on(step - 1)

        return carry

    lax.fori_loop(0, subs, one_chunk, 0)
    tile(step).begin()

    @pl.when(step == min(2, nf - 1))
    def _():
        cot_group.relay()

    @pl.when(step == nf - 1)
    def _():
        project(nf - 1)
        pass_on(nf - 1)
        conclude(nf - 2)
        conclude(nf - 1)
        pull_ref[...] = group_tiles(pulls, group_send.at[1], group_recv.at[1], d, nd)
        cot_group.close()
        cot_keep.wait()
        blocks.settle(nf)


def once(shape):
    return pl.BlockSpec(shape, lambda s: (0,) * len(shape), pipeline_mode=pl.Buffered(buffer_count=1))


def pick(part, layer):
    return pl.BlockSpec(
        (None,) + part.shape[1:], lambda s: (layer, 0, 0), pipeline_mode=pl.Buffered(buffer_count=1)
    )


def run_layer(
    ch, rows, nf, nd, normed_all, meta, segrow, small, w_in, w_out, hidden, extra, identity
):
    length, width = normed_all.shape[0], w_in.shape[1]
    layer = 1
    conv_width = ch + 2 * N
    block = rows
    steps = nf
    pieces = length // Q
    subs = block // Q
    own = (nf, rows // nd, D)
    every = (nf, nd, rows // nd, D)
    bits = len(bits_of(nd))
    dma = pltpu.SemaphoreType.DMA
    anywhere = pl.BlockSpec(memory_space=pl.ANY)
    ordered = lambda s: (s, 0)
    ordered3 = lambda s: (s, 0, 0)
    return pl.pallas_call(
        functools.partial(layer_kernel, ch, nf, nd),
        grid=(steps,),
        in_specs=[
            pl.BlockSpec((block, D), ordered),
            pl.BlockSpec((block, LANES), ordered),
            pl.BlockSpec((subs, 1, Q), ordered3),
        ]
        + [pick(part, layer) for part in small]
        + [
            anywhere,
            anywhere,
            once(own),
            once(own),
        ],
        out_specs=[
            pl.BlockSpec((block, width), ordered),
            once((length, ch)),
            pl.BlockSpec((block, ch), ordered),
            pl.BlockSpec((block, conv_width), ordered),
            pl.BlockSpec((subs, N, ch), ordered3),
            once(own),
            once(own),
            once((pieces, Q)),
            once((pieces, Q)),
            anywhere,
        ],
        out_shape=[
            jax.ShapeDtypeStruct((length, width), F32),
            jax.ShapeDtypeStruct((length, ch), BF16),
            jax.ShapeDtypeStruct((length, ch), F32),
            jax.ShapeDtypeStruct((length, conv_width), F32),
            jax.ShapeDtypeStruct((pieces, N, ch), F32),
            jax.ShapeDtypeStruct(own, F32),
            jax.ShapeDtypeStruct(own, BF16),
            jax.ShapeDtypeStruct((pieces, Q), F32),
            jax.ShapeDtypeStruct((pieces, Q), F32),
            jax.ShapeDtypeStruct(every, BF16),
        ],
        scratch_shapes=[
            pltpu.VMEM(held_shape(w_in), BF16),
            pltpu.VMEM((ch, D), BF16),
            pltpu.VMEM((8, conv_width), F32),
            pltpu.VMEM((N, ch), F32),
            pltpu.VMEM((2, block, ch), F32),
            pltpu.VMEM(every, BF16),
            pltpu.VMEM((nd - 1, nf, rows // nd, D), BF16),
            pltpu.VMEM((steps, nd, 8, LANES), F32),
            pltpu.VMEM((nd, pieces, Q), F32),
            dma((bits, nf, nd)),
            dma((bits, nf, nd)),
            dma((steps, nd)),
            dma((steps, nd)),
            dma((nf, nd)),
            dma((nf, nd)),
            dma((2,)),
            dma((nf,)),
        ],
        compiler_params=pltpu.CompilerParams(
            vmem_limit_bytes=VMEM_LIMIT, collective_id=identity, has_side_effects=True
        ),
        name="layer_last",
    )(normed_all, meta, segrow, *small, w_in, w_out, hidden, extra)


def mix_backward(
    ch, proj_ref, pre_ref, mixed_ref, state_ref, grad_ref, ratio_ref, pull_ref, meta_ref, segrow_ref,
    conv_w_ref, dtb_ref, alog_ref, skip_ref, gain_ref,
    dproj_ref, small_ref, tail, dstate, sub, chunk, turn,
):
    conv_width = ch + 2 * N
    rows = pl.ds(pl.multiple_of(sub * Q, Q), Q)
    meta = meta_ref[rows, :]
    pre = pre_ref[rows, :]
    sig = jax.nn.sigmoid(pre)
    conv_out = pre * sig
    values = conv_out[:, :ch]
    b_part = conv_out[:, ch : ch + N]
    c_part = conv_out[:, ch + N :]
    row, column = triangles()
    tri = jnp.where(row >= column, 1.0, 0.0)
    shifted, step, log_decay, cumulative = decay_tables(
        own_steps(proj_ref[rows, ch + conv_width :], turn), dtb_ref[...], alog_ref[...], tri
    )
    linked = (row <= column) & (meta[:, 0:1] == segrow_ref[sub])
    b_low = b_part.astype(BF16)
    c_low = c_part.astype(BF16)
    inner = jnp.where(linked, dot(b_low, c_low, ((1,), (1,))), 0.0)
    cum_t = cumulative.T
    last = cumulative[Q - 1 : Q, :]
    entry = meta[:, 4:5] * jnp.exp(cumulative)
    weight = meta[:, 5:6] * jnp.exp(last - cumulative)
    state_in = state_ref[sub]
    dstate_in = dstate[...]
    state_low = state_in.astype(BF16)
    dstate_low = dstate_in.astype(BF16)
    carried = dot(c_low, state_low)
    carried_back = dot(b_low, dstate_low)
    low_half = lax.broadcasted_iota(jnp.int32, (Q, LANES), 1) < P_SIZE
    lane = lax.broadcasted_iota(jnp.int32, (Q, LANES), 1)
    ratio = to_column(ratio_ref[pl.ds(chunk, 1), :])
    pull = ratio * ratio * to_column(pull_ref[pl.ds(chunk, 1), :]) * (1.0 / DI)
    dinner = jnp.zeros((Q, Q), F32)
    turned_parts = []
    step_parts, exit_parts, entry_parts = [], [], []
    weighted = []
    entered = []
    entry_rows = []
    dpre_parts = []
    for pair in range(ch // LANES):
        lanes = slice(pair * LANES, (pair + 1) * LANES)
        values_pair = values[:, lanes]
        gate = proj_ref[rows, lanes]
        mixed = mixed_ref[rows, lanes]
        gate_sig = jax.nn.sigmoid(gate)
        gate_silu = gate * gate_sig
        gated = mixed * gate_silu
        scaled = grad_ref[rows, lanes] * ratio
        small_ref[5:6, lanes] += jnp.sum(scaled * gated, axis=0, keepdims=True)
        dgated = scaled * gain_ref[:, lanes] - gated * pull
        dproj_ref[rows, lanes] = (dgated * mixed * (gate_sig + gate_silu * (1.0 - gate_sig))).astype(BF16)
        dmixed = dgated * gate_silu
        small_ref[6:7, lanes] += jnp.sum(dmixed * values_pair, axis=0, keepdims=True)
        zero = jnp.zeros_like(values_pair)
        dmixed_halves = [jnp.where(low_half, dmixed, zero).astype(BF16), jnp.where(low_half, zero, dmixed).astype(BF16)]
        values_low = values_pair.astype(BF16)
        step_pair = pair_lanes(step, 2 * pair, low_half)
        mats = []
        for half, head in enumerate((2 * pair, 2 * pair + 1)):
            spread = jnp.minimum(cum_t[head : head + 1, :] - cumulative[:, head : head + 1], 0.0)
            plain = jnp.exp(spread)
            decay = plain * step[:, head : head + 1]
            product = dot(values_low, dmixed_halves[half], ((1,), (1,)))
            mats.append((inner * plain).astype(BF16))
            spreaded = product * decay
            dinner = dinner + spreaded
            turned_parts.append((spreaded * inner).astype(BF16))
        back = dot(jnp.concatenate(mats, axis=1), jnp.concatenate(dmixed_halves, axis=0))
        weight_pair = pair_lanes(weight, 2 * pair, low_half)
        through = weight_pair * carried_back[:, lanes]
        total = back + through
        dvalues = step_pair * total + skip_ref[:, lanes] * dmixed
        step_parts.append((total * values_pair).astype(BF16))
        exit_parts.append((through * values_pair * step_pair).astype(BF16))
        entry_pair = pair_lanes(entry, 2 * pair, low_half)
        entry_grad = entry_pair * dmixed
        entry_parts.append((entry_grad * carried[:, lanes]).astype(BF16))
        weighted.append((weight_pair * step_pair * values_pair).astype(BF16))
        entered.append(entry_grad.astype(BF16))
        entry_rows.append(entry_pair[Q - 1 : Q, :])
        dpre_parts.append(dvalues)
    weighted = jnp.concatenate(weighted, axis=1)
    entered = jnp.concatenate(entered, axis=1)
    entry_rows = jnp.concatenate(entry_rows, axis=1)
    dinner_low = jnp.where(linked, dinner, 0.0).astype(BF16)
    db = dot(dinner_low, c_low) + dot(weighted, dstate_low, ((1,), (1,)))
    dc = dot(dinner_low.T, b_low) + dot(entered, state_low, ((1,), (1,)))
    state_terms = jnp.sum(state_in * dstate_in, axis=0, keepdims=True) * entry_rows
    head_lane = lax.broadcasted_iota(jnp.int32, (1, LANES), 1)
    state_sum = jnp.zeros((1, LANES), F32)
    for head in range(ch // P_SIZE):
        part = jnp.sum(state_terms[:, head * P_SIZE : (head + 1) * P_SIZE], axis=1, keepdims=True)
        state_sum = state_sum + jnp.where(head_lane == head, part, 0.0)
    heads = ch // P_SIZE

    def marks(shape, place, index):
        return jnp.where(place(shape) == index(shape), 1.0, 0.0).astype(BF16)

    rows_of_shape = lambda shape: lax.broadcasted_iota(jnp.int32, shape, 0)
    columns_of_shape = lambda shape: lax.broadcasted_iota(jnp.int32, shape, 1)
    by_head = marks((ch, LANES), lambda shape: rows_of_shape(shape) // P_SIZE, columns_of_shape)
    dstep = dot(jnp.concatenate(step_parts, axis=1), by_head)
    dexit = dot(jnp.concatenate(exit_parts, axis=1), by_head)
    dcum = dot(jnp.concatenate(entry_parts, axis=1), by_head)
    by_target = marks((LANES, heads * Q), rows_of_shape, lambda shape: columns_of_shape(shape) // Q)
    by_source = marks((heads * Q, LANES), lambda shape: rows_of_shape(shape) // Q, columns_of_shape)
    dcum = dcum + dot(by_target, jnp.concatenate(turned_parts, axis=0)).T
    dcum = dcum - dot(jnp.concatenate(turned_parts, axis=1), by_source)
    later = jnp.where(row <= column, 1.0, 0.0)
    before = jnp.where(row > column, 1.0, 0.0)
    dlog = fine_dot(later, dcum) + fine_dot(before, dexit) + state_sum
    growth = jnp.exp(alog_ref[...])
    dstep = dstep - dlog * growth
    ddt = dstep * jax.nn.sigmoid(shifted)
    small_ref[7:8, 0:LANES] += jnp.sum(ddt, axis=0, keepdims=True)
    small_ref[7:8, LANES : 2 * LANES] += jnp.sum(dlog * log_decay, axis=0, keepdims=True)
    dproj_ref[rows, ch + conv_width :] = pltpu.roll(jnp.where(lane < heads, ddt, 0.0), turn, 1)[:, :H].astype(BF16)
    dstate[...] = entry_rows * dstate_in + dot(c_part.T.astype(BF16), entered)
    dconv_out = jnp.concatenate(dpre_parts + [db, dc], axis=1)
    dpre = dconv_out * (sig + conv_out * (1.0 - sig))
    raw = proj_ref[rows, ch : ch + conv_width]
    small_ref[4:5, :] += jnp.sum(dpre, axis=0, keepdims=True)
    draw = conv_w_ref[3:4, :] * dpre
    last_rows = lax.broadcasted_iota(jnp.int32, (8, conv_width), 0)
    small_ref[3:4, :] += jnp.sum(raw * dpre, axis=0, keepdims=True)
    for lag in range(1, K):
        kept = meta[:, lag : lag + 1] * dpre
        later = pltpu.roll(kept, Q - lag, 0)
        end = jnp.where(last_rows < 8 - lag, later[Q - 8 :, :], pltpu.roll(tail[lag - 1], 8 - lag, 0))
        moved = jnp.concatenate([later[: Q - 8, :], end], axis=0)
        tail[lag - 1] = kept[0:8, :]
        draw = draw + conv_w_ref[3 - lag : 4 - lag, :] * moved
        small_ref[3 - lag : 4 - lag, :] += jnp.sum(raw * moved, axis=0, keepdims=True)
    dproj_ref[rows, ch : ch + conv_width] = draw.astype(BF16)


def gain_rows(width):
    return [(start, min(width, D - start)) for start in range(0, D, width)]


def layer_back_kernel(
    ch, nf, nd, last, fused,
    grad_all_ref, proj_ref, pre_ref, mixed_ref, state_ref, meta_ref, segrow_ref, ratio_ref, pull_ref,
    conv_w_ref, dtb_ref, alog_ref, skip_ref, gain_ref, w_in_ref, w_out_ref,
    hidden_ref, grad_own_ref, norm_gain_ref, branch_ref, *refs,
):
    count = 2 if last else 1
    sources, refs = refs[: count - fused], refs[count - fused :]
    if not last:
        rows_out, refs = refs[0], refs[1:]
    if fused:
        (normed_ref, nout_ref, grads_ref), refs = refs[:3], refs[3:]
    (
        dproj_ref, small_ref, next_ref, next_pull_ref, moved_ref,
    ) = refs[:5]
    results, refs = refs[5 : 5 + count], refs[5 + count :]
    if not last:
        final_ref, refs = refs[0], refs[1:]
    (
        held, w_out, tail, dstate, dnout, partial, landed, pulls, low, dgain,
        sum_send, sum_recv, tile_send, tile_recv, group_send, group_recv, local_sem, load_sem, deal_send, deal_recv,
    ) = refs[:20]
    refs = refs[20:]
    if fused:
        dproj_all, normed, staged, out_grad, normed_sem, staged_sem = refs[-6:]
        refs = refs[:-6]
        nout = dproj_all.at[:, pl.ds(0, ch)]
        block = grad_all_ref.shape[0]
        weight_grad = dproj_ref
        dproj_ref = dproj_all.at[pl.ds(pl.multiple_of((nf - 1 - pl.program_id(0)) * block, Q), block)]
        normed_load = pltpu.make_async_copy(normed_ref, normed, normed_sem.at[0])
        grads_load = pltpu.make_async_copy(grads_ref, normed, normed_sem.at[0])
        nout_load = pltpu.make_async_copy(nout_ref, nout, normed_sem.at[1])
        sources = (out_grad,) + sources
    step = pl.program_id(0)
    y, z, d = lax.axis_index("section"), lax.axis_index("fsdp"), lax.axis_index("dp")
    block = grad_all_ref.shape[0]
    subs = block // Q
    rows = block // nd
    bits = bits_of(nd)
    place = nf - 1 - step
    blocks = BlockSum(partial, landed, d, nd, sum_send, sum_recv)
    sums = [
        SectionSum(make(source, nf), nf, y, z, *refs[5 * k : 5 * k + 5])
        for k, (make, source) in enumerate(zip((out_view, in_view), sources))
    ]
    weights = Weights(w_in_ref, held, load_sem)
    out_load = pltpu.make_async_copy(w_out_ref, w_out, local_sem.at[0])
    if last:
        leave = Deal(moved_ref, low, nf, nd, z, d, deal_send, deal_recv, True)
    else:
        leave = Deal(final_ref, rows_out, nf, nd, z, d, deal_send, deal_recv, True)

    def every(place):
        return GroupRows(lambda device: moved_ref.at[place, device], d, nd, group_send.at[place], group_recv.at[place])

    def mine(place):
        return pltpu.make_async_copy(low.at[place], moved_ref.at[place, d], local_sem.at[2 + place])

    @pl.when(step == 0)
    def _():
        for copy in weights.copies():
            copy.start()
        out_load.start()
        greet(
            [(None, {"dp": flip(d, j)}) for j in range(1, nd)]
            + line_neighbours(nf, y, z)
            + deal_partners(nf, nd, z, d)
        )
        if fused:
            grads_load.start()
            nout_load.start()
        for one in sums[::-1] if not fused else sums[:0:-1]:
            one.begin()
        if not last:
            leave.start_all()
        tail[...] = jnp.zeros_like(tail)
        dstate[...] = jnp.zeros_like(dstate)
        small_ref[...] = jnp.zeros_like(small_ref)
        dgain[...] = jnp.zeros_like(dgain)
        pulls[0] = jnp.zeros(pulls.shape[1:], F32)
        if fused:
            grads_load.wait()
            nout_load.wait()

            def out_tile(i, carry):
                part = pl.ds(pl.multiple_of(i * LANES, LANES), LANES)
                out_grad[part, :] = dot(nout[:, part], normed[...], ((0,), (0,))).astype(BF16)
                return carry

            lax.fori_loop(0, ch // LANES, out_tile, 0)
            sums[0].begin()
            normed_load.start()
        for copy in weights.copies():
            copy.wait()
        out_load.wait()

    def pass_on(place):
        for k in range(1, len(bits)):
            blocks.send(k, place)

    def conclude(place):
        dnormed = blocks.own(place)
        hidden = hidden_ref[place].astype(F32)
        inverse = rms_parts(hidden)
        dgain[...] += jnp.sum(dnormed * hidden * inverse, axis=0, keepdims=True)
        scaled = dnormed * norm_gain_ref[...]
        dhidden = inverse * (
            scaled - hidden * (inverse * inverse) * jnp.mean(scaled * hidden, axis=1, keepdims=True)
        )
        moved = (grad_own_ref[place].astype(F32) + dhidden).astype(BF16)
        low[place] = moved
        if last:
            leave.start(place)
        else:
            next_ref[place] = moved
            first = place * block + d * rows
            pulls[0, pl.ds(first // Q, 1), :] += to_row(
                jnp.sum(moved.astype(F32) * branch_ref[place], axis=1, keepdims=True), first % Q
            )
            mine(place).start()
            every(place).begin(low.at[place])

    dnout[...] = dot(grad_all_ref[...], w_out[...], ((1,), (1,)))

    @pl.when(step >= 1)
    def _():
        pass_on(place + 1)

    def one_chunk(turn, carry):
        sub = subs - 1 - turn
        mix_backward(
            ch, proj_ref, pre_ref, mixed_ref, state_ref, dnout, ratio_ref, pull_ref, meta_ref, segrow_ref,
            conv_w_ref, dtb_ref, alog_ref, skip_ref, gain_ref,
            dproj_ref, small_ref, tail, dstate, sub, place * subs + sub, d * (H // nd),
        )

        @pl.when((turn == 0) & (step >= 1))
        def _():
            conclude(place + 1)

        return carry

    lax.fori_loop(0, subs, one_chunk, 0)
    product = weights.backward(dproj_ref[...]).astype(BF16)
    for o in range(nd):
        partial[place, o] = product[o * rows : (o + 1) * rows, :]
    blocks.send(0, place)
    if not last:

        @pl.when(step >= 1)
        def _():
            every(place + 1).relay()

    for k in range(nf - 1, 0, -1):

        @pl.when(step == nf - 1 - k)
        def _():
            for one in sums:
                one.stage(k)

    @pl.when(step == nf - 1)
    def _():
        pass_on(0)
        if fused:
            normed_load.wait()
            width = dproj_all.shape[1]
            wide = staged.shape[1]
            full = width // wide

            def store(i, size):
                rows = pl.ds(pl.multiple_of(i * wide, 16), size)
                return pltpu.make_async_copy(
                    staged.at[i % 2, pl.ds(0, size)], weight_grad.at[rows], staged_sem.at[i % 2]
                )

            def some(i, carry):
                @pl.when(i >= 2)
                def _():
                    store(i - 2, wide).wait()

                columns = dproj_all[:, pl.ds(pl.multiple_of(i * wide, LANES), wide)]
                staged[i % 2] = dot(columns, normed[...], ((0,), (0,))).astype(BF16)
                store(i, wide).start()
                return carry

            lax.fori_loop(0, full // 2, some, 0)
        conclude(0)
        for row, (start, size) in enumerate(gain_rows(small_ref.shape[1])):
            small_ref[8 + row : 9 + row, 0:size] = dgain[:, start : start + size]
        if last:
            next_pull_ref[...] = jnp.zeros_like(next_pull_ref)
        else:
            next_pull_ref[...] = group_tiles(pulls, tile_send, tile_recv, d, nd)
        if fused:
            lax.fori_loop(full // 2, full, some, 0)
            store(full - 2, wide).wait()
            rest = width - full * wide
            if rest:
                staged[full % 2, 0:rest] = dot(dproj_all[:, full * wide :], normed[...], ((0,), (0,))).astype(BF16)
                store(full, rest).start()
                store(full, rest).wait()
            store(full - 1, wide).wait()
        for one, result in zip(sums, results):
            one.finish()
            copy = pltpu.make_async_copy(one.result, result, local_sem.at[1])
            copy.start()
            copy.wait()
            one.settle()
        leave.arrive()
        leave.settle()
        if not last:
            every(0).relay()
            for k in range(nf):
                every(k).close()
                mine(k).wait()
        blocks.settle(nf)


def run_layer_back(
    ch, rows, nf, nd, last, grad_all, proj, pre, mixed, states, meta, segrow, ratio, pull, small, w_in, w_out,
    hidden, grad_own, norm_gain, branch, identity, sums, leaving, more,
):
    length, width = proj.shape
    if more:
        shapes = [out_part_shape(nf, w_out)] + [in_part_shape(nf, g) for g in sums]
    else:
        shapes = [make(nf, g) for make, g in zip((out_part_shape, in_part_shape), sums)]
    conv_width = ch + 2 * N
    block = rows
    steps = nf
    own = (nf, rows // nd, D)
    every = (nf, nd, rows // nd, D)
    pieces = length // Q
    subs = block // Q
    bits = len(bits_of(nd))
    dma = pltpu.SemaphoreType.DMA
    ordered = lambda s: (steps - 1 - s, 0)
    ordered3 = lambda s: (steps - 1 - s, 0, 0)
    layer = 0 if last else 1
    conv_w, conv_b, dtb, alog, skip, gain = small
    return pl.pallas_call(
        functools.partial(layer_back_kernel, ch, nf, nd, last, bool(more)),
        grid=(steps,),
        in_specs=[
            pl.BlockSpec((block, D), ordered),
            pl.BlockSpec((block, width), ordered),
            pl.BlockSpec((block, conv_width), ordered),
            pl.BlockSpec((block, ch), ordered),
            pl.BlockSpec((subs, N, ch), ordered3),
            pl.BlockSpec((block, LANES), ordered),
            pl.BlockSpec((subs, 1, Q), ordered3),
            once((pieces, Q)),
            once((pieces, Q)),
        ]
        + [pick(part, layer) for part in (conv_w, dtb, alog, skip, gain)]
        + [
            pl.BlockSpec(memory_space=pl.ANY),
            pl.BlockSpec(memory_space=pl.ANY),
            once(own),
            once(own),
            pick(norm_gain, layer),
            pl.BlockSpec(memory_space=pl.ANY) if last else once(own),
        ]
        + [pl.BlockSpec(memory_space=pl.ANY)] * (len(sums) + len(leaving) + len(more)),
        out_specs=[
            pl.BlockSpec(memory_space=pl.ANY) if more else pl.BlockSpec((block, width), ordered),
            once((16, conv_width)),
            pl.BlockSpec(memory_space=pl.ANY) if last else once(own),
            once((pieces, Q)),
            pl.BlockSpec(memory_space=pl.ANY),
        ]
        + [pl.BlockSpec(memory_space=pl.ANY)] * (len(shapes) + len(leaving)),
        out_shape=[
            jax.ShapeDtypeStruct((width, D) if more else (length, width), BF16),
            jax.ShapeDtypeStruct((16, conv_width), F32),
            jax.ShapeDtypeStruct(own, BF16),
            jax.ShapeDtypeStruct((pieces, Q), F32),
            jax.ShapeDtypeStruct((rows, D) if last else every, BF16),
        ]
        + [jax.ShapeDtypeStruct(shape, BF16) for shape in shapes]
        + [jax.ShapeDtypeStruct((rows, D), BF16) for part in leaving],
        scratch_shapes=[
            pltpu.VMEM(held_shape(w_in), BF16),
            pltpu.VMEM((ch, D), BF16),
            pltpu.VMEM((K - 1, 8, conv_width), F32),
            pltpu.VMEM((N, ch), F32),
            pltpu.VMEM((block, ch), F32),
            pltpu.VMEM(every, BF16),
            pltpu.VMEM((nd - 1, nf, rows // nd, D), BF16),
            pltpu.VMEM((nd, pieces, Q), F32),
            pltpu.VMEM(own, BF16),
            pltpu.VMEM((1, D), F32),
            dma((bits, nf, nd)),
            dma((bits, nf, nd)),
            dma((nd,)),
            dma((nd,)),
            dma((nf, nd)),
            dma((nf, nd)),
            dma((2 + nf,)),
            dma((nf,)),
            dma((nf,)),
            dma((nf,)),
        ]
        + [part for shape in shapes for part in section_sum_scratch(nf, shape)]
        + (
            [
                pltpu.VMEM((length, width), BF16),
                pltpu.VMEM((length, D), BF16),
                pltpu.VMEM((2, LANES, D), BF16),
                pltpu.VMEM((ch, D), BF16),
                dma((2,)),
                dma((2,)),
            ]
            if more
            else []
        ),
        compiler_params=pltpu.CompilerParams(
            vmem_limit_bytes=VMEM_LIMIT, collective_id=identity, has_side_effects=True
        ),
        name="layer_back_last" if last else "layer_back_first",
    )(
        grad_all, proj, pre, mixed, states, meta, segrow, ratio, pull, conv_w, dtb, alog, skip, gain, w_in, w_out,
        hidden, grad_own, norm_gain, branch, *sums, *leaving, *more,
    )


def shards(
    inputs, segment, cotangent, norm_gain, in_weight, conv_weight, conv_bias, dt_bias, a_log, d_skip,
    gate_gain, out_weight,
):
    fsdp, dp = lax.axis_size("fsdp"), lax.axis_size("dp")
    section, here = lax.axis_index("section"), lax.axis_index("dp")
    rows = inputs.shape[2]
    ch = DI // dp
    heads = H // dp
    conv_width = ch + 2 * N
    seg_mine = lax.dynamic_index_in_dim(segment, section, 0, keepdims=False)[0].astype(F32)
    seg_mine = jnp.broadcast_to(seg_mine.reshape(rows // Q, 1, Q), (rows // Q, 8, Q)).reshape(-1, Q)
    head_table = jnp.pad(
        jnp.concatenate([dt_bias[0], a_log[0], d_skip[0]], axis=0), ((0, 0), (0, LANES - H))
    )
    (
        proj, mixed, pre, states, nout, branch, after, ratio, conv_w, conv_b, dtb, alog, skip, gain, gains, meta, segrow,
        normed_all, moved, hidden, cot_own, w_in0, w_in1, w_out0, w_out1,
    ) = run_first(
        ch, fsdp, dp, inputs[:, 0], cotangent[:, 0], seg_mine, in_weight[0, 0].T, out_weight[0, 0], conv_weight[0, 0],
        conv_bias[0], norm_gain[0], gate_gain[0], head_table, 2,
    )
    small = (conv_w, conv_b, dtb, alog, skip, gain)
    length = meta.shape[0]
    saved = [(normed_all.reshape(length, D), hidden, proj, nout, mixed, pre, states, branch, ratio)]
    normed_all, hidden = moved.reshape(length, D), after
    proj, nout, mixed, pre, states, branch, final_rows, ratio, pull, cot_all = run_layer(
        ch, rows, fsdp, dp, normed_all, meta, segrow, small, w_in1, w_out1, hidden, cot_own, 3
    )
    saved.append((normed_all, hidden, proj, nout, mixed, pre, states, branch, ratio))

    grad_all, grad_own = cot_all.reshape(length, D), cot_own
    in_grad, small_grads, parts = (), [None, None], []
    fused = D // fsdp % LANES == 0
    for layer in (1, 0):
        last = layer == 0
        normed_all, hidden, proj, gated, mixed, pre, states, branch, ratio = saved[layer]
        out_grad = () if fused else (dot(gated, grad_all, ((0,), (0,))).astype(BF16),)
        dproj, small_grads[layer], after, next_pull, moved, *done = run_layer_back(
            ch, rows, fsdp, dp, last, grad_all, proj, pre, mixed, states, meta, segrow, ratio, pull, small,
            w_in0 if last else w_in1, w_out0 if last else w_out1, hidden, grad_own, gains, saved[0][7], 4 + layer,
            out_grad + in_grad, () if last else (final_rows,), (normed_all, gated, grad_all) if fused else (),
        )
        if not last:
            *done, final = done
        parts += done
        if fused:
            grad = dproj
        else:
            grad = dot(dproj, normed_all, ((0,), (0,))).astype(BF16)
        if not fused:
            grad = jnp.swapaxes(grad.reshape(-1, fsdp, D // fsdp), 0, 1)
        in_grad = (grad,)
        if not last:
            grad_all, grad_own, pull = moved.reshape(length, D), after, next_pull
    input_grad = moved

    in_all, out_all, small_all = run_end(
        fsdp, dp, in_grad[0], parts[2], parts[1], parts[0], small_grads[0], small_grads[1]
    )
    in_total, out_total, gain_total, convw_total, convb_total, dtb_total, alog_total, skip_total, gate_total = run_finish(
        ch, dp, in_all, out_all, small_all
    )
    return (
        final[None, None],
        input_grad[None, None],
        gain_total[None],
        in_total.T[None, None],
        convw_total[None, None],
        convb_total[None],
        dtb_total[None],
        alog_total[None],
        skip_total[None],
        gate_total[None],
        out_total[None, None],
    )


def solution(mesh):
    return jax.shard_map(
        shards,
        mesh=mesh,
        in_specs=(
            P(None, "dp", "fsdp", None),
            P(None, "dp", "fsdp"),
            P(None, "dp", "fsdp", None),
            P("section", None, None),
            P("section", None, "fsdp", None),
            P("section", None, None, None),
            P("section", None, None),
            P("section", None, None),
            P("section", None, None),
            P("section", None, None),
            P("section", None, None),
            P("section", None, "fsdp", None),
        ),
        out_specs=(
            P("section", "dp", "fsdp", None),
            P("section", "dp", "fsdp", None),
            P("section", None, None),
            P("section", None, "fsdp", None),
            P("section", None, None, None),
            P("section", None, None),
            P("section", None, None),
            P("section", None, None),
            P("section", None, None),
            P("section", None, None),
            P("section", None, "fsdp", None),
        ),
        check_vma=False,
    )
```
